32 devices in a mesh: grp: 4 (over y, core), seq: 2 (over x), head: 4 (over z).
Axes of the slice: x: 2, y: 2, z: 4, core: 2. Of those that a mesh axis runs over, the one named last changes fastest.
Arguments:
- keys: bfloat16 [32, 1024, 1536], P('grp', 'seq', 'head'), may hold values from -6 to 6
- values: bfloat16 [32, 1024, 1536], P('grp', 'seq', 'head'), may hold values from -6 to 6
- log_forget: float32 [32, 24, 1024], P('grp', 'head', 'seq'), may hold values from -0.6 to 0, as said below
- keep: int32 [32, 1024], P('grp', 'seq'), may hold values from 0 to 1, as said below
- merge_weight: float32 [32, 1024], P('grp', 'seq'), may hold values from 0.1 to 10
- lengths: int32 [32], P('grp'), may hold values from 64 to 1024, as said below
- route: int32 [32], P('grp'), may hold values from 0 to 31, as said below
- fresh: bfloat16 [3, 32, 1536], P(None, 'grp', 'head'), may hold values from -7.5 to 7.5
- new_forget: bfloat16 [32, 24], P('grp', 'head'), may hold values from -1 to -0.049804688
- out_weight: bfloat16 [1536, 1536], P('head', 'seq'), may hold values from -0.15625 to 0.15625
Outputs:
- compact_keys: bfloat16 [32, 512, 1536], P('grp', 'seq', 'head')
- compact_values: bfloat16 [32, 512, 1536], P('grp', 'seq', 'head')
- compact_decay: float32 [32, 24, 512], P('grp', 'head', 'seq')
- layer_out: bfloat16 [32, 1536], P('grp', 'seq')
The draws below stay inside these ranges and needn't reach their ends.
Inputs may be any that keep to these rules, and one draw needn't show every extreme that they name: `keep`: within every aligned block of 64 positions of a request, between 16 and 31 entries are 1, and some block has exactly 31. `lengths`: multiples of 64; the first request of every 8 in order has 1024. `route`: A permutation of the requests. `log_forget`: Negative.
All inputs are finite; a program needn't handle non-finite values.
Results may differ from the reference program's by a relative error of at most 0.0085.
Values may be sent and summed in bfloat16 or wider, within the bound.
No kernel may reach another device: no remote copies, remote signals or barrier semaphores. Data moves between devices by JAX's collectives and lax.ppermute only.
A program may use at most 64 MiB of HBM per device.

```python
import math
import jax
import jax.numpy as jnp
from jax import lax

D = 1536
HEAD_COUNT = 24
HD = 64
BLOCK = 64
SLOTS = 32
R_GRP = 8
CACHE_LENGTH = 1024
REQUEST_COUNT = 32
NBLK = 16
ROWS = 512
CROWS = 256
PIECE = 128
N_SEQ = 2


def pattern_parts(key):
    baseline_level = jax.random.fold_in(key, 31)
    key_head = jax.random.fold_in(baseline_level, 1)
    chosen_head = jax.random.randint(key_head, (REQUEST_COUNT,), 0, HEAD_COUNT)
    aligned = jnp.arange(REQUEST_COUNT) % 3 == 0
    return (chosen_head, aligned)


def route_common(key):
    return jax.random.permutation(jax.random.fold_in(key, 11), REQUEST_COUNT).astype(jnp.int32)


def draw_route(key, part):
    return route_common(key)


def draw_lengths(key, part):
    blocks = jax.random.randint(jax.random.fold_in(key, 5), (REQUEST_COUNT,), 1, NBLK + 1)
    full = jnp.arange(REQUEST_COUNT) % R_GRP == 0
    blocks = jnp.where(full, NBLK, blocks)
    return (blocks * BLOCK).astype(jnp.int32)


def draw_keep(key, part):
    key_count, key_order = jax.random.split(jax.random.fold_in(key, 7))
    counts = jax.random.randint(key_count, (REQUEST_COUNT, NBLK), 16, SLOTS)
    counts = counts.at[0, 0].set(SLOTS - 1)
    scores = jax.random.randint(key_order, (REQUEST_COUNT, NBLK, BLOCK), 0, 2 ** 20) * BLOCK + jnp.arange(BLOCK)[None, None, :]
    ranks = jnp.argsort(jnp.argsort(scores, axis=2), axis=2)
    flags = (ranks < counts[:, :, None]).astype(jnp.int32)
    return flags.reshape(REQUEST_COUNT, CACHE_LENGTH)


def draw_log_forget(key, part):
    baseline_level = jax.random.fold_in(key, 13)
    variety_random_key, quick_random_key, gradual_random_key, noise_random_key, spike_random_key, removal_random_key = jax.random.split(baseline_level, 6)
    chosen_head, aligned = pattern_parts(key)
    fast_share = 0.5
    fast = jax.random.uniform(variety_random_key, (REQUEST_COUNT, HEAD_COUNT)) < fast_share
    forced = aligned[:, None] & (jnp.arange(HEAD_COUNT)[None, :] == chosen_head[:, None])
    fast = fast & jnp.logical_not(forced)
    fast_rate = jnp.exp(jax.random.uniform(quick_random_key, (REQUEST_COUNT, HEAD_COUNT), jnp.float32, math.log(1.0 / 50.0), math.log(1.0 / 30.0)))
    slow_rate = jnp.exp(jax.random.uniform(gradual_random_key, (REQUEST_COUNT, HEAD_COUNT), jnp.float32, math.log(0.1), math.log(0.8))) / CACHE_LENGTH
    decay_speed = jnp.where(fast, fast_rate, slow_rate)
    noisy_part = jnp.exp(jax.random.uniform(noise_random_key, (REQUEST_COUNT, HEAD_COUNT, CACHE_LENGTH), jnp.float32, math.log(0.5), math.log(2.0)))
    sudden_spike = jax.random.uniform(spike_random_key, (REQUEST_COUNT, HEAD_COUNT, CACHE_LENGTH)) < 2.0 / CACHE_LENGTH
    removal_flags = jax.random.uniform(removal_random_key, (REQUEST_COUNT, HEAD_COUNT, CACHE_LENGTH), jnp.float32, math.log(0.6), math.log(0.85))
    return -decay_speed[:, :, None] * noisy_part + jnp.where(sudden_spike, removal_flags, 0.0)


def draw_keys(key, part):
    base_key = jax.random.fold_in(key, 17)
    key_base = jax.random.fold_in(base_key, 0)
    baseline_level = jnp.clip(jax.random.normal(key_base, (REQUEST_COUNT, CACHE_LENGTH, D), jnp.float32), -6.0, 6.0)
    return baseline_level.astype(jnp.bfloat16)


def draw_fresh(key, part):
    key_base = jax.random.fold_in(key, 19)
    baseline_level = jnp.clip(jax.random.normal(key_base, (3, REQUEST_COUNT, D), jnp.float32), -6.0, 6.0)
    return baseline_level.astype(jnp.bfloat16)


def steps_of(key, shape, pieces, smallest, largest):
    level, own = 1.0, jax.random.fold_in(key, 6)
    for dim, shards_of in pieces:
        draws = jnp.exp(jax.random.uniform(jax.random.fold_in(own, dim), (shards_of,), jnp.float32, smallest / len(pieces), largest / len(pieces)))
        level = level * jnp.repeat(draws, shape[dim] // shards_of).reshape([-1 if axis == dim else 1 for axis in range(len(shape))])
    return level


def normal_values(key, dims, width, most, pieces=(), held_as=jnp.bfloat16):
    entries = jax.random.normal(key, dims, jnp.float32) * width
    if len(pieces) > 0:
        entries = steps_of(key, dims, pieces, -0.22, 0.18) * entries
    return jnp.clip(entries, min=-most, max=most).astype(held_as)


def setup_inputs(seed: int = 0) -> dict:
    streams_of = jax.random.split(jax.random.key(seed), 11)
    keys = draw_keys(jax.random.fold_in(streams_of[10], 71), 0)
    values = normal_values(streams_of[1], (REQUEST_COUNT, CACHE_LENGTH, D), 1.0, 6.0, ((0, 4), (1, 2), (2, 4)))
    log_forget = draw_log_forget(jax.random.fold_in(streams_of[10], 71), 0)
    keep = draw_keep(jax.random.fold_in(streams_of[10], 71), 0)
    merge_weight = jnp.clip(jnp.exp(math.log(10.0) - 4.6051702 * jax.random.uniform(streams_of[4], (REQUEST_COUNT, CACHE_LENGTH), jnp.float32) ** steps_of(streams_of[4], (REQUEST_COUNT, CACHE_LENGTH), ((0, 4), (1, 2)), -0.2, 0.2)), 0.1, 10.0)
    lengths = draw_lengths(jax.random.fold_in(streams_of[10], 71), 0)
    route = draw_route(jax.random.fold_in(streams_of[10], 71), 0)
    fresh = draw_fresh(jax.random.fold_in(streams_of[10], 71), 0)
    new_forget = jnp.clip(-1.0 + 0.9501953 * jax.random.uniform(streams_of[8], (REQUEST_COUNT, HEAD_COUNT), jnp.float32) ** steps_of(streams_of[8], (REQUEST_COUNT, HEAD_COUNT), ((0, 4), (1, 4)), -0.2, 0.2), -1.0, -0.049804688).astype(jnp.bfloat16)
    out_weight = normal_values(streams_of[9], (D, D), D ** -0.5, 0.15625, ((0, 4), (1, 2)))
    return {"keys": keys, "values": values, "log_forget": log_forget, "keep": keep, "merge_weight": merge_weight, "lengths": lengths, "route": route, "fresh": fresh, "new_forget": new_forget, "out_weight": out_weight}


EMPTY_LOG = -1.0e4


def reference(keys, values, log_forget, keep, merge_weight, lengths, route, fresh, new_forget, out_weight):
    scale = HD ** -0.5

    def one_request(index):
        length = lengths[index]
        position = jnp.arange(CACHE_LENGTH, dtype=jnp.int32)
        live = position < length
        forget = jnp.where(live[None, :], log_forget[index], 0.0)
        log_decay = jnp.sum(forget, axis=1, keepdims=True) - jnp.cumsum(forget, axis=1)
        flags = keep[index].reshape(NBLK, BLOCK)
        rank = jnp.cumsum(flags, axis=1) - 1
        slot_ids = jnp.arange(SLOTS - 1, dtype=jnp.int32)
        block_live = (jnp.arange(NBLK, dtype=jnp.int32) * BLOCK < length).astype(jnp.float32)
        chosen = ((flags[:, None, :] == 1) & (rank[:, None, :] == slot_ids[None, :, None])).astype(jnp.float32)
        chosen = chosen * block_live[:, None, None]
        dropped = flags == 0
        weighted = jnp.where(dropped, merge_weight[index].reshape(NBLK, BLOCK), 0.0)
        share = (weighted / jnp.sum(weighted, axis=1, keepdims=True)).astype(jnp.bfloat16).astype(jnp.float32)
        select = jnp.concatenate([chosen, (share * block_live[:, None])[:, None, :]], axis=1)
        key_blocks = keys[index].reshape(NBLK, BLOCK, D).astype(jnp.float32)
        value_blocks = values[index].reshape(NBLK, BLOCK, D).astype(jnp.float32)
        packed_keys = jnp.einsum("bej,bjc->bec", select, key_blocks, precision=lax.Precision.HIGHEST).astype(jnp.bfloat16).reshape(ROWS, D)
        packed_values = jnp.einsum("bej,bjc->bec", select, value_blocks, precision=lax.Precision.HIGHEST).astype(jnp.bfloat16).reshape(ROWS, D)
        decay_blocks = log_decay.reshape(HEAD_COUNT, NBLK, BLOCK)
        kept_log = jnp.einsum("bej,hbj->hbe", chosen, decay_blocks, precision=lax.Precision.HIGHEST)
        filled = jnp.sum(chosen, axis=2)
        kept_log = kept_log + (1.0 - filled)[None, :, :] * EMPTY_LOG
        drop_mask = dropped[None, :, :]
        drop_peak = jnp.max(jnp.where(drop_mask, decay_blocks, -jnp.inf), axis=2)
        spread = jnp.where(drop_mask, jnp.exp(decay_blocks - drop_peak[:, :, None]), 0.0)
        merged_log = drop_peak + jnp.log(jnp.sum(share[None, :, :] * spread, axis=2))
        merged_log = jnp.where(block_live[None, :] > 0, merged_log, EMPTY_LOG)
        slot_log = jnp.concatenate([kept_log, merged_log[:, :, None]], axis=2).reshape(HEAD_COUNT, ROWS)
        arrival = route[index]
        query = fresh[0, arrival].reshape(HEAD_COUNT, HD).astype(jnp.float32)
        own_key = fresh[1, arrival].reshape(HEAD_COUNT, HD).astype(jnp.float32)
        own_value = fresh[2, arrival].reshape(HEAD_COUNT, HD).astype(jnp.float32)
        new_log = new_forget[arrival].astype(jnp.float32)
        key_rows = packed_keys.reshape(ROWS, HEAD_COUNT, HD).astype(jnp.float32)
        value_rows = packed_values.reshape(N_SEQ, CROWS, HEAD_COUNT, HD).astype(jnp.float32)
        scores = jnp.einsum("hd,nhd->hn", query, key_rows, precision=lax.Precision.HIGHEST) * scale + slot_log
        runs = scores.reshape(HEAD_COUNT, N_SEQ, CROWS)
        run_top = jnp.max(runs, axis=2)
        weights = jnp.exp(runs - run_top[:, :, None]).astype(jnp.bfloat16).astype(jnp.float32)
        run_sum = jnp.sum(weights, axis=2)
        run_acc = jnp.einsum("hsn,snhd->hsd", weights, value_rows, precision=lax.Precision.HIGHEST)
        top = jnp.max(run_top, axis=1)
        rescale = jnp.exp(run_top - top[:, None])
        total_sum = jnp.sum(rescale * run_sum, axis=1)
        total_acc = jnp.sum(rescale[:, :, None] * run_acc, axis=1)
        own_score = jnp.sum(query * own_key, axis=1) * scale
        cache_top = top + new_log
        joint = jnp.maximum(cache_top, own_score)
        cache_scale = jnp.exp(cache_top - joint)
        self_weight = jnp.exp(own_score - joint)
        attended = (cache_scale[:, None] * total_acc + self_weight[:, None] * own_value) / (cache_scale * total_sum + self_weight)[:, None]
        attended = attended.reshape(D).astype(jnp.bfloat16)
        dealt_keys = packed_keys.reshape(N_SEQ, N_SEQ, PIECE, D).transpose(1, 0, 2, 3).reshape(ROWS, D)
        dealt_values = packed_values.reshape(N_SEQ, N_SEQ, PIECE, D).transpose(1, 0, 2, 3).reshape(ROWS, D)
        return dealt_keys, dealt_values, jnp.exp(slot_log), attended

    compact_keys, compact_values, compact_decay, attended = lax.map(one_request, jnp.arange(REQUEST_COUNT, dtype=jnp.int32))
    layer_out = jnp.dot(attended, out_weight, preferred_element_type=jnp.float32).astype(jnp.bfloat16)
    return compact_keys, compact_values, compact_decay, layer_out
```

```python
import functools

import jax
import jax.numpy as jnp
from jax import lax
from jax.experimental import pallas as pl
from jax.experimental.pallas import tpu as pltpu
from jax.sharding import PartitionSpec as P

BLOCK = 64
SLOTS = 32
EMPTY_LOG = -10000.0
CHUNKS = 4
VMEM_LIMIT = 48 * 1024 * 1024


def dot(a, b):
    return lax.dot_general(a, b, (((1,), (0,)), ((), ())), preferred_element_type=jnp.float32)


def dot_nt(a, b):
    return lax.dot_general(a, b, (((1,), (1,)), ((), ())), preferred_element_type=jnp.float32)


def iota(shape, dim):
    return lax.broadcasted_iota(jnp.int32, shape, dim)


def three(x):
    hi = x.astype(jnp.bfloat16).astype(jnp.float32)
    rest = x - hi
    mid = rest.astype(jnp.bfloat16).astype(jnp.float32)
    return hi, mid, rest - mid


def split_dot(x, ones):
    rows = x.shape[0]
    parts = dot(jnp.concatenate(three(x), axis=0).astype(jnp.bfloat16), ones)
    return parts[:rows] + parts[rows : 2 * rows] + parts[2 * rows :]


def half_of(axis, count):
    own = lax.axis_index(axis) if count == 2 else jnp.int32(0)
    return own, 1 - own


def plan(keep, weight, start, len_ref):
    rows, width = keep.shape
    one, two = iota((width, width), 0), iota((width, width), 1)
    same = (one // BLOCK) == (two // BLOCK)
    upto = (same & (one <= two)).astype(jnp.float32).astype(jnp.bfloat16)
    block = same.astype(jnp.float32).astype(jnp.bfloat16)
    kept = keep == 1
    rank = dot(keep.astype(jnp.float32).astype(jnp.bfloat16), upto) - 1.0
    weighted = jnp.where(kept, 0.0, weight)
    share = (weighted / split_dot(weighted, block)).astype(jnp.bfloat16).astype(jnp.float32)
    lane, row = iota((rows, width), 1), iota((rows, width), 0)
    slot = jnp.where(kept, rank.astype(jnp.int32), SLOTS - 1) + (lane // BLOCK) * SLOTS
    length = jnp.zeros((rows, width), jnp.int32)
    for r in range(rows):
        length = jnp.where(row == r, len_ref[r], length)
    slot = jnp.where(start + lane < length, slot, -1)
    return slot, jnp.where(kept, 1.0, share)


def select(slot, factor, r):
    width = slot.shape[1]
    shape = (width // 2, width)
    hit = iota(shape, 0) == slot[r : r + 1, :]
    return jnp.where(hit, jnp.broadcast_to(factor[r : r + 1, :], shape), 0.0).astype(jnp.bfloat16)


def lanes(half, width):
    return pl.ds(pl.multiple_of(half * width, width), width)


def send_kernel(n_seq, first, count, len_ref, keep_ref, weight_ref, keys, values, out, buf, sem):
    _, sent = half_of("seq", n_seq)
    width = buf.shape[2]
    copies = []
    for i, source in enumerate((keys, values)):
        for j in range(count):
            copies.append(
                pltpu.make_async_copy(
                    source.at[first + j, lanes(sent, width), :], buf.at[i, j], sem.at[i, j]
                )
            )
    for copy in copies:
        copy.start()
    start = lax.axis_index("seq") * (2 * width) + sent * width
    slot, factor = plan(
        keep_ref[:, lanes(sent, width)], weight_ref[:, lanes(sent, width)], start, len_ref
    )
    chosen = [select(slot, factor, first + j) for j in range(count)]
    for i in range(2):
        for j in range(count):
            copies[i * count + j].wait()
            out[i, j] = dot(chosen[j], buf[i, j]).astype(jnp.bfloat16)


def send_part(n_seq, first, count, lengths, keep, weight, keys, values):
    req, pos, width = keys.shape
    half = pos // 2
    vmem = pl.BlockSpec(memory_space=pltpu.VMEM)
    hbm = pl.BlockSpec(memory_space=pl.ANY)
    return pl.pallas_call(
        functools.partial(send_kernel, n_seq, first, count),
        out_shape=jax.ShapeDtypeStruct((2, count, half // 2, width), jnp.bfloat16),
        in_specs=[pl.BlockSpec(memory_space=pltpu.SMEM), vmem, vmem, hbm, hbm],
        out_specs=vmem,
        scratch_shapes=[
            pltpu.VMEM((2, count, half, width), jnp.bfloat16),
            pltpu.SemaphoreType.DMA((2, count)),
        ],
        compiler_params=pltpu.CompilerParams(vmem_limit_bytes=VMEM_LIMIT),
        cost_estimate=pl.CostEstimate(
            flops=4 * count * half * half * width,
            bytes_accessed=6 * count * half * width,
            transcendentals=0,
        ),
        name="compact_sent",
    )(lengths, keep, weight, keys, values)


def main_kernel(
    n_seq, n_grp, n_chunk, len_ref, route_ref, keep_ref, weight_ref, forget_ref, keys, values, *rest
):
    chunks, rest = rest[:n_chunk], rest[n_chunk:]
    fresh, rest = rest[:n_grp], rest[n_grp:]
    out_k, out_v, log_ref, stats_ref, picked_ref = rest[:5]
    raw, own_rows, sent_rows, forget, logs, scores, sem_raw, sem_sent, sem_out = rest[5:]
    own, sent = half_of("seq", n_seq)
    seq = lax.axis_index("seq")
    req, heads, pos = forget_ref.shape
    half = pos // 2
    rows = half // 2
    width = keys.shape[2]
    size = width // heads
    pad = forget.shape[0] // req

    raw_copies = [
        [
            pltpu.make_async_copy(source.at[r, lanes(own, half), :], raw.at[i, r], sem_raw.at[i, r])
            for i, source in enumerate((keys, values))
        ]
        for r in range(req)
    ]
    for pair in raw_copies:
        for copy in pair:
            copy.start()
    count = req // n_chunk
    sent_copies = [
        pltpu.make_async_copy(
            chunks[c], sent_rows.at[:, pl.ds(c * count, count)], sem_sent.at[c]
        )
        for c in range(n_chunk)
    ]
    for copy in sent_copies:
        copy.start()

    kinds = 4 * req
    shape = (kinds, kinds)
    to, frm = iota(shape, 0), iota(shape, 1)
    wanted = jnp.zeros(shape, jnp.int32)
    for r in range(req):
        wanted = jnp.where(to % req == r, route_ref[r], wanted)
    me = lax.axis_index("grp")
    picked = jnp.zeros((kinds, width), jnp.float32)
    for k in range(n_grp):
        source = lax.rem(me + n_grp - k, n_grp)
        hit = (to // req == frm // req) & (wanted == source * req + frm % req)
        picked = picked + dot(hit.astype(jnp.float32).astype(jnp.bfloat16), fresh[k][...])
    picked_ref[...] = picked

    forget[...] = jnp.zeros_like(forget)
    lane = iota((heads, pos), 1)
    for r in range(req):
        live = seq * pos + lane < len_ref[r]
        forget[r * pad : r * pad + heads, :] = jnp.where(live, forget_ref[r], 0.0)
    gates = forget[...]
    total = jnp.sum(gates, axis=1, keepdims=True)
    one, two = iota((half, half), 0), iota((half, half), 1)
    after = ((one // BLOCK == two // BLOCK) & (one > two)).astype(jnp.float32).astype(jnp.bfloat16)
    ends = iota((pos, rows), 1) // SLOTS
    begins = iota((pos, rows), 0) // BLOCK
    last = iota((req * pad, rows), 1) % SLOTS == SLOTS - 1

    for i, h in enumerate((own, sent)):
        slot, factor = plan(
            keep_ref[:, lanes(h, half)], weight_ref[:, lanes(h, half)], seq * pos + h * half, len_ref
        )
        inner = split_dot(forget[:, lanes(h, half)], after)
        beyond = split_dot(
            gates, (begins > ends + h * (half // BLOCK)).astype(jnp.float32).astype(jnp.bfloat16)
        )
        spread = jnp.exp(inner)
        high = spread.astype(jnp.bfloat16).astype(jnp.float32)
        planes = three(inner) + (high, spread - high, jnp.ones_like(inner))
        found = []
        for r in range(req):
            chosen = select(slot, factor, r)
            stack = jnp.concatenate([x[r * pad : (r + 1) * pad] for x in planes], axis=0)
            found.append(dot_nt(stack.astype(jnp.bfloat16), chosen))
            if i == 0:
                for copy in raw_copies[r]:
                    copy.wait()
                own_rows[0, r] = dot(chosen, raw[0, r]).astype(jnp.bfloat16)
                own_rows[1, r] = dot(chosen, raw[1, r]).astype(jnp.bfloat16)
        at = [
            jnp.concatenate([x[p * pad : (p + 1) * pad] for x in found], axis=0) for p in range(6)
        ]
        filled = at[5] > 0.5
        kept = at[0] + at[1] + at[2]
        merged = jnp.log(jnp.where(filled, at[3] + at[4], 1.0))
        level = jnp.where(filled, jnp.where(last, merged, kept) + beyond, EMPTY_LOG)
        logs[:, i * rows : (i + 1) * rows] = level
        for r in range(req):
            log_ref[r, :, lanes(h, rows)] = level[r * pad : r * pad + heads]

    out_copies = [
        pltpu.make_async_copy(own_rows.at[i], out.at[:, lanes(own, rows), :], sem_out.at[i])
        for i, out in enumerate((out_k, out_v))
    ]
    for copy in out_copies:
        copy.start()
    for copy in sent_copies:
        copy.wait()

    mine = iota((pad, width), 0) == iota((pad, width), 1) // size
    for r in range(req):
        query = jnp.where(mine, picked[r : r + 1, :], 0.0).astype(jnp.bfloat16)
        here = slice(r * pad, (r + 1) * pad)
        scores[here, :rows] = dot_nt(query, own_rows[0, r])
        scores[here, rows:] = dot_nt(query, sent_rows[0, r])
    level = scores[...] * (size**-0.5) + logs[...]
    top = jnp.max(level, axis=1, keepdims=True)
    weights = jnp.exp(level - top).astype(jnp.bfloat16).astype(jnp.float32)
    mass = jnp.sum(weights, axis=1, keepdims=True)

    def spread_out(column, r):
        return jnp.sum(
            jnp.where(mine, column[r * pad : (r + 1) * pad], 0.0), axis=0, keepdims=True
        )

    for r in range(req):
        w = weights[r * pad : (r + 1) * pad].astype(jnp.bfloat16)
        acc = dot(w[:, :rows], own_rows[1, r]) + dot(w[:, rows:], sent_rows[1, r])
        acc = jnp.sum(jnp.where(mine, acc, 0.0), axis=0, keepdims=True)
        for p, row in enumerate(
            (spread_out(top, r), spread_out(mass, r), spread_out(total, r), acc)
        ):
            stats_ref[p * req + r : p * req + r + 1, :] = row
    for copy in out_copies:
        copy.wait()


def main_part(n_seq, n_grp, lengths, route, keep, weight, forget, keys, values, chunks, fresh):
    req, pos, width = keys.shape
    heads = forget.shape[1]
    half, rows, pad = pos // 2, pos // 4, -(-heads // 8) * 8
    n_chunk = len(chunks)
    vmem = pl.BlockSpec(memory_space=pltpu.VMEM)
    hbm = pl.BlockSpec(memory_space=pl.ANY)
    smem = pl.BlockSpec(memory_space=pltpu.SMEM)
    whole = jax.ShapeDtypeStruct((req, 2 * rows, width), jnp.bfloat16)
    return pl.pallas_call(
        functools.partial(main_kernel, n_seq, n_grp, n_chunk),
        out_shape=(
            whole,
            whole,
            jax.ShapeDtypeStruct((req, heads, 2 * rows), jnp.float32),
            jax.ShapeDtypeStruct((4 * req, width), jnp.float32),
            jax.ShapeDtypeStruct((4 * req, width), jnp.float32),
        ),
        in_specs=[smem, smem, vmem, vmem, vmem, hbm, hbm] + [hbm] * n_chunk + [vmem] * n_grp,
        out_specs=(hbm, hbm, vmem, vmem, vmem),
        scratch_shapes=[
            pltpu.VMEM((2, req, half, width), jnp.bfloat16),
            pltpu.VMEM((2, req, rows, width), jnp.bfloat16),
            pltpu.VMEM((2, req, rows, width), jnp.bfloat16),
            pltpu.VMEM((req * pad, pos), jnp.float32),
            pltpu.VMEM((req * pad, 2 * rows), jnp.float32),
            pltpu.VMEM((req * pad, 2 * rows), jnp.float32),
            pltpu.SemaphoreType.DMA((2, req)),
            pltpu.SemaphoreType.DMA((n_chunk,)),
            pltpu.SemaphoreType.DMA((2,)),
        ],
        compiler_params=pltpu.CompilerParams(vmem_limit_bytes=VMEM_LIMIT),
        cost_estimate=pl.CostEstimate(
            flops=8 * req * half * half * width,
            bytes_accessed=8 * req * half * width,
            transcendentals=4 * req * heads * pos,
        ),
        name="compact_own_and_attend",
    )(lengths, route, keep, weight, forget, keys, values, *chunks, *fresh)


def merge_kernel(count, relative, size, *refs):
    stats, (picked_ref, weight_ref, log_ref, decay_ref, out_ref) = refs[:count], refs[count:]
    req, heads, rows = log_ref.shape
    width = picked_ref.shape[1]
    seq = lax.axis_index("seq")
    places = [lax.rem(seq + count - k, count) if relative else jnp.int32(k) for k in range(count)]
    tops, masses, totals, accs = [
        [ref[p * req : (p + 1) * req, :] for ref in stats] for p in range(4)
    ]

    def later(place):
        total = jnp.zeros_like(totals[0])
        for k in range(count):
            total = total + jnp.where(places[k] > place, totals[k], 0.0)
        return total

    tops = [tops[k] + later(places[k]) for k in range(count)]
    top = functools.reduce(jnp.maximum, tops)
    scales = [jnp.exp(t - top) for t in tops]
    mass = sum(s * x for s, x in zip(scales, masses))
    acc = sum(s * x for s, x in zip(scales, accs))
    query, key, value, gate = [picked_ref[p * req : (p + 1) * req, :] for p in range(4)]
    one, two = iota((width, width), 0), iota((width, width), 1)
    same = (one // size == two // size).astype(jnp.float32).astype(jnp.bfloat16)
    own = split_dot(query * key, same) * (size**-0.5)
    past = top + gate
    joint = jnp.maximum(past, own)
    scale, self_weight = jnp.exp(past - joint), jnp.exp(own - joint)
    attended = (scale * acc + self_weight * value) / (scale * mass + self_weight)
    out_ref[...] = dot(attended.astype(jnp.bfloat16), weight_ref[...])

    beyond = later(seq)
    head = iota((heads, width), 0)
    first = head * size == iota((heads, width), 1)
    for r in range(req):
        column = jnp.sum(jnp.where(first, beyond[r : r + 1, :], 0.0), axis=1, keepdims=True)
        decay_ref[r] = jnp.exp(log_ref[r] + column)


def merge_part(stats, relative, picked, out_weight, logs, size):
    req = logs.shape[0]
    vmem = pl.BlockSpec(memory_space=pltpu.VMEM)
    return pl.pallas_call(
        functools.partial(merge_kernel, len(stats), relative, size),
        out_shape=(
            jax.ShapeDtypeStruct(logs.shape, jnp.float32),
            jax.ShapeDtypeStruct((req, out_weight.shape[1]), jnp.float32),
        ),
        in_specs=[vmem] * (len(stats) + 3),
        out_specs=(vmem, vmem),
        compiler_params=pltpu.CompilerParams(vmem_limit_bytes=VMEM_LIMIT),
        name="merge_and_project",
    )(*stats, picked, out_weight, logs)


def sum_kernel(count, *refs):
    parts, out = refs[:count], refs[count]
    me = lax.axis_index("head")
    total = jnp.zeros(out.shape, jnp.float32)
    for place in range(count):
        for k in range(count):
            total = total + jnp.where(lax.rem(me + count - k, count) == place, parts[k][...], 0.0)
    out[...] = total.astype(out.dtype)


def sum_part(parts):
    return pl.pallas_call(
        functools.partial(sum_kernel, len(parts)),
        out_shape=jax.ShapeDtypeStruct(parts[0].shape, jnp.bfloat16),
        in_specs=[pl.BlockSpec(memory_space=pltpu.VMEM)] * len(parts),
        out_specs=pl.BlockSpec(memory_space=pltpu.VMEM),
        name="sum_heads",
    )(*parts)


def place_kernel(n_seq, first, part, old_k, old_v, out_k, out_v, sem):
    _, sent = half_of("seq", n_seq)
    _, count, rows, _ = part.shape
    copies = [
        pltpu.make_async_copy(
            part.at[i, j], out.at[first + j, lanes(sent, rows), :], sem.at[i, j]
        )
        for i, out in enumerate((out_k, out_v))
        for j in range(count)
    ]
    for copy in copies:
        copy.start()
    for copy in copies:
        copy.wait()


def place_part(n_seq, first, part, out_k, out_v):
    hbm = pl.BlockSpec(memory_space=pl.ANY)
    shape = jax.ShapeDtypeStruct(out_k.shape, out_k.dtype)
    return pl.pallas_call(
        functools.partial(place_kernel, n_seq, first),
        out_shape=(shape, shape),
        in_specs=[hbm] * 3,
        out_specs=(hbm, hbm),
        scratch_shapes=[pltpu.SemaphoreType.DMA((2, part.shape[1]))],
        input_output_aliases={1: 0, 2: 1},
        name="place_received",
    )(part, out_k, out_v)


def others(value, axis):
    count = lax.axis_size(axis)
    return [value] + [
        lax.ppermute(value, axis, [(i, (i + k) % count) for i in range(count)])
        for k in range(1, count)
    ]


def shards(
    keys, values, log_forget, keep, merge_weight, lengths, route, fresh, new_forget, out_weight
):
    req, pos, width = keys.shape
    heads = log_forget.shape[1]
    size = width // heads
    n_seq, n_grp = lax.axis_size("seq"), lax.axis_size("grp")
    gates = jnp.repeat(new_forget, size, axis=1)
    tokens = others(jnp.concatenate([fresh.reshape(3 * req, width), gates], axis=0), "grp")
    count = req // CHUNKS
    chunks = [
        send_part(n_seq, c * count, count, lengths, keep, merge_weight, keys, values)
        for c in range(CHUNKS)
    ]
    if n_seq == 2:
        received = [lax.ppermute(x, "seq", [(0, 1), (1, 0)]) for x in chunks]
    else:
        received = chunks
    out_k, out_v, logs, stats, picked = main_part(
        n_seq, n_grp, lengths, route, keep, merge_weight, log_forget, keys, values, chunks, tokens
    )
    if n_seq == 2:
        all_stats = others(stats, "seq")
    else:
        gathered = lax.all_gather(stats, "seq")
        all_stats = [gathered[i] for i in range(n_seq)]
    decay, partial = merge_part(all_stats, n_seq == 2, picked, out_weight, logs, size)
    layer_out = sum_part(others(partial, "head"))
    for c in range(CHUNKS):
        out_k, out_v = place_part(n_seq, c * count, received[c], out_k, out_v)
    if n_seq != 2:
        out_k, out_v = (
            lax.all_to_all(x, "seq", split_axis=1, concat_axis=1, tiled=True) for x in (out_k, out_v)
        )
    return out_k, out_v, decay, layer_out


def solution(mesh):
    return jax.shard_map(
        shards,
        mesh=mesh,
        in_specs=(
            P("grp", "seq", "head"),
            P("grp", "seq", "head"),
            P("grp", "head", "seq"),
            P("grp", "seq"),
            P("grp", "seq"),
            P("grp"),
            P("grp"),
            P(None, "grp", "head"),
            P("grp", "head"),
            P("head", "seq"),
        ),
        out_specs=(
            P("grp", "seq", "head"),
            P("grp", "seq", "head"),
            P("grp", "head", "seq"),
            P("grp", "seq"),
        ),
        check_vma=False,
    )
```

```python
import functools

import jax
import jax.numpy as jnp
from jax import lax
from jax.experimental import pallas as pl
from jax.experimental.pallas import tpu as pltpu
from jax.sharding import PartitionSpec as P

BLOCK = 64
SLOTS = 32
LANES = 128
BLOCK_LOG = BLOCK.bit_length() - 1
SLOT_LOG = SLOTS.bit_length() - 1
EMPTY_LOG = -10000.0
FIRST = 4
VMEM_LIMIT = 63 * 1024 * 1024
MAIN_LIMIT = 63 * 1024 * 1024
SMALL_LIMIT = 8 * 1024 * 1024


LIGHT = pl.CostEstimate(flops=1, bytes_accessed=1, transcendentals=0)


def dot(a, b):
    return lax.dot_general(a, b, (((1,), (0,)), ((), ())), preferred_element_type=jnp.float32)


def dot_nt(a, b):
    return lax.dot_general(a, b, (((1,), (1,)), ((), ())), preferred_element_type=jnp.float32)


def iota(shape, dim):
    return lax.broadcasted_iota(jnp.int32, shape, dim)


def three(x):
    hi = x.astype(jnp.bfloat16).astype(jnp.float32)
    rest = x - hi
    mid = rest.astype(jnp.bfloat16).astype(jnp.float32)
    return hi, mid, rest - mid


def split_dot(x, ones):
    rows = x.shape[0]
    parts = dot(jnp.concatenate(three(x), axis=0).astype(jnp.bfloat16), ones)
    return parts[:rows] + parts[rows : 2 * rows] + parts[2 * rows :]


def half_of(axis, count):
    own = lax.axis_index(axis) if count == 2 else jnp.int32(0)
    return own, 1 - own


def by_row(ref, row):
    picked = jnp.zeros_like(row)
    for r in range(ref.shape[0]):
        picked = jnp.where(row == r, ref[r], picked)
    return picked


def plan(keep, weight, start, len_ref):
    rows, width = keep.shape
    one, two = iota((width, width), 0), iota((width, width), 1)
    same = (one ^ two) < BLOCK
    upto = (same & (one <= two)).astype(jnp.float32).astype(jnp.bfloat16)
    block = same.astype(jnp.float32).astype(jnp.bfloat16)
    kept = keep == 1
    rank = dot(keep.astype(jnp.float32).astype(jnp.bfloat16), upto) - 1.0
    weighted = jnp.where(kept, 0.0, weight)
    share = (weighted / split_dot(weighted, block)).astype(jnp.bfloat16).astype(jnp.float32)
    lane, row = iota((rows, width), 1), iota((rows, width), 0)
    slot = jnp.where(kept, rank.astype(jnp.int32), SLOTS - 1) + (lane >> BLOCK_LOG) * SLOTS
    slot = jnp.where(start + lane < by_row(len_ref, row), slot, -1)
    return slot, jnp.where(kept, 1.0, share)


def select(slot, factor, r):
    width = slot.shape[1]
    shape = (width // 2, width)
    hit = iota(shape, 0) == slot[r : r + 1, :]
    return jnp.where(hit, jnp.broadcast_to(factor[r : r + 1, :], shape), 0.0).astype(jnp.bfloat16)


def lanes(half, width):
    return pl.ds(pl.multiple_of(half * width, width), width)


def send_kernel(n_seq, first, count, len_ref, keep_ref, weight_ref, keys, values, *rest):
    if first == 0:
        *tokens, out, packed, buf, sem = rest
    else:
        _, out, buf, sem = rest
    _, sent = half_of("seq", n_seq)
    width = buf.shape[2]
    copies = []
    for j in range(count):
        for i, source in enumerate((keys, values)):
            copies.append(
                pltpu.make_async_copy(
                    source.at[first + j, lanes(sent, width), :], buf.at[i, j], sem.at[i, j]
                )
            )
    for copy in copies:
        copy.start()
    start = lax.axis_index("seq") * (2 * width) + sent * width
    slot, factor = plan(
        keep_ref[:, lanes(sent, width)], weight_ref[:, lanes(sent, width)], start, len_ref
    )
    if first == 0:
        fresh, gates = tokens[0][...].astype(jnp.float32), tokens[1][...].astype(jnp.float32)
        req, heads = gates.shape
        lane = iota((req, fresh.shape[1]), 1)
        size = fresh.shape[1] // heads
        spread = jnp.zeros((req, fresh.shape[1]), jnp.float32)
        for h in range(heads):
            inside = (lane >= h * size) & (lane < (h + 1) * size)
            spread = jnp.where(inside, gates[:, h : h + 1], spread)
        packed[...] = jnp.concatenate([fresh, spread], axis=0).astype(jnp.bfloat16)
    for j in range(count):
        chosen = select(slot, factor, first + j)
        for i in range(2):
            copies[j * 2 + i].wait()
            out[i, j] = dot(chosen, buf[i, j]).astype(jnp.bfloat16)


def send_part(n_seq, first, count, lengths, keep, weight, keys, values, extra):
    req, pos, width = keys.shape
    half = pos // 2
    vmem = pl.BlockSpec(memory_space=pltpu.VMEM)
    hbm = pl.BlockSpec(memory_space=pl.ANY)
    shapes = [jax.ShapeDtypeStruct((2, count, half // 2, width), jnp.bfloat16)]
    if first == 0:
        shapes.append(jax.ShapeDtypeStruct((extra[0].shape[0] + req, width), jnp.bfloat16))
    return pl.pallas_call(
        functools.partial(send_kernel, n_seq, first, count),
        out_shape=tuple(shapes),
        in_specs=[pl.BlockSpec(memory_space=pltpu.SMEM), vmem, vmem, hbm, hbm]
        + ([vmem] * 2 if first == 0 else [hbm]),
        out_specs=(vmem,) * len(shapes),
        scratch_shapes=[
            pltpu.VMEM((2, count, half, width), jnp.bfloat16),
            pltpu.SemaphoreType.DMA((2, count)),
        ],
        compiler_params=pltpu.CompilerParams(vmem_limit_bytes=VMEM_LIMIT),
        cost_estimate=LIGHT,
        name="compact_sent",
    )(lengths, keep, weight, keys, values, *extra)


def main_kernel(
    n_seq, n_grp, n_chunk, len_ref, route_ref, keep_ref, weight_ref, forget_ref, keys, values, *rest
):
    chunks, rest = rest[:n_chunk], rest[n_chunk:]
    fresh, rest = rest[:n_grp], rest[n_grp:]
    out_k, out_v, log_ref, stats_ref, picked_ref = rest[:5]
    raw, own_rows, sent_rows, forget, logs, scores, sem_raw, sem_sent, sem_out = rest[5:]
    own, sent = half_of("seq", n_seq)
    seq = lax.axis_index("seq")
    heads, req, pos = forget_ref.shape
    half = pos // 2
    rows = half // 2
    width = keys.shape[2]
    size = width // heads
    pad = forget.shape[1] // req

    raw_copies = [
        [
            pltpu.make_async_copy(source.at[r, lanes(own, half), :], raw.at[i, r], sem_raw.at[i, r])
            for i, source in enumerate((keys, values))
        ]
        for r in range(req)
    ]
    for pair in raw_copies:
        for copy in pair:
            copy.start()
    firsts = [sum(x.shape[1] for x in chunks[:c]) for c in range(n_chunk)]
    sent_copies = [
        pltpu.make_async_copy(
            chunk, sent_rows.at[:, pl.ds(firsts[c], chunk.shape[1])], sem_sent.at[c]
        )
        for c, chunk in enumerate(chunks)
    ]
    for copy in sent_copies:
        copy.start()

    kinds = 4 * req
    shape = (kinds, kinds)
    to, frm = iota(shape, 0), iota(shape, 1)
    wanted = by_row(route_ref, to % req)
    me = lax.axis_index("grp")
    picked = jnp.zeros((kinds, width), jnp.float32)
    for k in range(n_grp):
        source = lax.rem(me + n_grp - k, n_grp)
        hit = (to // req == frm // req) & (wanted == source * req + frm % req)
        picked = picked + dot(hit.astype(jnp.float32).astype(jnp.bfloat16), fresh[k][...])
    picked_ref[...] = picked

    forget[...] = jnp.zeros_like(forget)
    live = seq * pos + iota((req, pos), 1) < by_row(len_ref, iota((req, pos), 0))
    for h in range(heads):
        gate = jnp.where(live, forget_ref[h], 0.0)
        for c in range(pos // LANES):
            forget[c, pl.ds(h, req, stride=pad), :] = gate[:, c * LANES : (c + 1) * LANES]
    gates = jnp.concatenate([forget[c] for c in range(pos // LANES)], axis=1)
    total = jnp.sum(gates, axis=1, keepdims=True)
    one, two = iota((half, half), 0), iota((half, half), 1)
    after = (((one ^ two) < BLOCK) & (one > two)).astype(jnp.float32).astype(jnp.bfloat16)
    ends = iota((pos, rows), 1) >> SLOT_LOG
    begins = iota((pos, rows), 0) >> BLOCK_LOG
    last = iota((req * pad, rows), 1) & (SLOTS - 1) == SLOTS - 1

    for i, h in enumerate((own, sent)):
        slot, factor = plan(
            keep_ref[:, lanes(h, half)], weight_ref[:, lanes(h, half)], seq * pos + h * half, len_ref
        )
        near = half // LANES
        inner = split_dot(
            jnp.concatenate([forget[h * near + c] for c in range(near)], axis=1), after
        )
        beyond = split_dot(
            gates, (begins > ends + h * (half // BLOCK)).astype(jnp.float32).astype(jnp.bfloat16)
        )
        spread = jnp.exp(inner)
        high = spread.astype(jnp.bfloat16).astype(jnp.float32)
        planes = three(inner) + (high, spread - high, jnp.ones_like(inner))
        found = []
        for r in range(req):
            chosen = select(slot, factor, r)
            stack = jnp.concatenate([x[r * pad : (r + 1) * pad] for x in planes], axis=0)
            found.append(dot_nt(stack.astype(jnp.bfloat16), chosen))
            if i == 0:
                for copy in raw_copies[r]:
                    copy.wait()
                own_rows[0, r] = dot(chosen, raw[0, r]).astype(jnp.bfloat16)
                own_rows[1, r] = dot(chosen, raw[1, r]).astype(jnp.bfloat16)
        at = [
            jnp.concatenate([x[p * pad : (p + 1) * pad] for x in found], axis=0) for p in range(6)
        ]
        filled = at[5] > 0.5
        kept = at[0] + at[1] + at[2]
        merged = jnp.log(jnp.where(filled, at[3] + at[4], 1.0))
        level = jnp.where(filled, jnp.where(last, merged, kept) + beyond, EMPTY_LOG)
        logs[i] = level
        for k in range(heads):
            log_ref[k, :, lanes(h, rows)] = logs[i, pl.ds(k, req, stride=pad), :]

    out_copies = [
        pltpu.make_async_copy(own_rows.at[i], out.at[:, lanes(own, rows), :], sem_out.at[i])
        for i, out in enumerate((out_k, out_v))
    ]
    for copy in out_copies:
        copy.start()
    for copy in sent_copies:
        copy.wait()

    lane, row = iota((pad, width), 1), iota((pad, width), 0)
    mine = (lane >= row * size) & (lane < (row + 1) * size)
    for r in range(req):
        query = jnp.where(mine, picked[r : r + 1, :], 0.0).astype(jnp.bfloat16)
        here = slice(r * pad, (r + 1) * pad)
        scores[here, :rows] = dot_nt(query, own_rows[0, r])
        scores[here, rows:] = dot_nt(query, sent_rows[0, r])
    level = scores[...] * (size**-0.5) + jnp.concatenate([logs[0], logs[1]], axis=1)
    top = jnp.max(level, axis=1, keepdims=True)
    weights = jnp.exp(level - top).astype(jnp.bfloat16).astype(jnp.float32)
    mass = jnp.sum(weights, axis=1, keepdims=True)

    def spread_out(column, r):
        return jnp.sum(
            jnp.where(mine, column[r * pad : (r + 1) * pad], 0.0), axis=0, keepdims=True
        )

    for r in range(req):
        w = weights[r * pad : (r + 1) * pad].astype(jnp.bfloat16)
        acc = dot(w[:, :rows], own_rows[1, r]) + dot(w[:, rows:], sent_rows[1, r])
        acc = jnp.sum(jnp.where(mine, acc, 0.0), axis=0, keepdims=True)
        for p, row in enumerate(
            (spread_out(top, r), spread_out(mass, r), spread_out(total, r), acc)
        ):
            stats_ref[p * req + r : p * req + r + 1, :] = row
    for copy in out_copies:
        copy.wait()


def main_part(n_seq, n_grp, lengths, route, keep, weight, forget, keys, values, chunks, fresh):
    req, pos, width = keys.shape
    heads = forget.shape[0]
    half, rows, pad = pos // 2, pos // 4, -(-heads // 8) * 8
    n_chunk = len(chunks)
    vmem = pl.BlockSpec(memory_space=pltpu.VMEM)
    hbm = pl.BlockSpec(memory_space=pl.ANY)
    smem = pl.BlockSpec(memory_space=pltpu.SMEM)
    whole = jax.ShapeDtypeStruct((req, 2 * rows, width), jnp.bfloat16)
    return pl.pallas_call(
        functools.partial(main_kernel, n_seq, n_grp, n_chunk),
        out_shape=(
            whole,
            whole,
            jax.ShapeDtypeStruct((heads, req, 2 * rows), jnp.float32),
            jax.ShapeDtypeStruct((4 * req, width), jnp.float32),
            jax.ShapeDtypeStruct((4 * req, width), jnp.float32),
        ),
        in_specs=[smem, smem, vmem, vmem, vmem, hbm, hbm] + [hbm] * n_chunk + [vmem] * n_grp,
        out_specs=(hbm, hbm, vmem, vmem, vmem),
        scratch_shapes=[
            pltpu.VMEM((2, req, half, width), jnp.bfloat16),
            pltpu.VMEM((2, req, rows, width), jnp.bfloat16),
            pltpu.VMEM((2, req, rows, width), jnp.bfloat16),
            pltpu.VMEM((pos // LANES, req * pad, LANES), jnp.float32),
            pltpu.VMEM((2, req * pad, rows), jnp.float32),
            pltpu.VMEM((req * pad, 2 * rows), jnp.float32),
            pltpu.SemaphoreType.DMA((2, req)),
            pltpu.SemaphoreType.DMA((n_chunk,)),
            pltpu.SemaphoreType.DMA((2,)),
        ],
        compiler_params=pltpu.CompilerParams(vmem_limit_bytes=MAIN_LIMIT),
        cost_estimate=LIGHT,
        name="compact_own_and_attend",
    )(lengths, route, keep, weight, forget, keys, values, *chunks, *fresh)


def merge_kernel(count, relative, size, *refs):
    stats, (picked_ref, weight_ref, log_ref, decay_ref, out_ref) = refs[:count], refs[count:]
    heads, req, rows = log_ref.shape
    width = picked_ref.shape[1]
    seq = lax.axis_index("seq")
    places = [lax.rem(seq + count - k, count) if relative else jnp.int32(k) for k in range(count)]
    tops, masses, totals, accs = [
        [ref[p * req : (p + 1) * req, :] for ref in stats] for p in range(4)
    ]

    def later(place):
        total = jnp.zeros_like(totals[0])
        for k in range(count):
            total = total + jnp.where(places[k] > place, totals[k], 0.0)
        return total

    tops = [tops[k] + later(places[k]) for k in range(count)]
    top = functools.reduce(jnp.maximum, tops)
    scales = [jnp.exp(t - top) for t in tops]
    mass = sum(s * x for s, x in zip(scales, masses))
    acc = sum(s * x for s, x in zip(scales, accs))
    query, key, value, gate = [picked_ref[p * req : (p + 1) * req, :] for p in range(4)]
    one, two = iota((width, width), 0), iota((width, width), 1)
    same = (one // size == two // size).astype(jnp.float32).astype(jnp.bfloat16)
    own = split_dot(query * key, same) * (size**-0.5)
    past = top + gate
    joint = jnp.maximum(past, own)
    scale, self_weight = jnp.exp(past - joint), jnp.exp(own - joint)
    attended = (scale * acc + self_weight * value) / (scale * mass + self_weight)
    out_ref[...] = dot(attended.astype(jnp.bfloat16), weight_ref[...])

    beyond = later(seq)
    for h in range(heads):
        decay_ref[h] = jnp.exp(log_ref[h] + beyond[:, h * size : h * size + 1])


def merge_part(stats, relative, picked, out_weight, logs, size):
    req = logs.shape[1]
    vmem = pl.BlockSpec(memory_space=pltpu.VMEM)
    return pl.pallas_call(
        functools.partial(merge_kernel, len(stats), relative, size),
        out_shape=(
            jax.ShapeDtypeStruct(logs.shape, jnp.float32),
            jax.ShapeDtypeStruct((req, out_weight.shape[1]), jnp.float32),
        ),
        in_specs=[vmem] * (len(stats) + 3),
        out_specs=(vmem, vmem),
        compiler_params=pltpu.CompilerParams(vmem_limit_bytes=SMALL_LIMIT),
        cost_estimate=LIGHT,
        name="merge_and_project",
    )(*stats, picked, out_weight, logs)


def sum_kernel(count, *refs):
    parts, out = refs[:count], refs[count]
    me = lax.axis_index("head")
    total = jnp.zeros(out.shape, jnp.float32)
    for place in range(count):
        for k in range(count):
            total = total + jnp.where(lax.rem(me + count - k, count) == place, parts[k][...], 0.0)
    out[...] = total.astype(out.dtype)


def sum_part(parts):
    return pl.pallas_call(
        functools.partial(sum_kernel, len(parts)),
        out_shape=jax.ShapeDtypeStruct(parts[0].shape, jnp.bfloat16),
        in_specs=[pl.BlockSpec(memory_space=pltpu.VMEM)] * len(parts),
        out_specs=pl.BlockSpec(memory_space=pltpu.VMEM),
        compiler_params=pltpu.CompilerParams(vmem_limit_bytes=SMALL_LIMIT),
        cost_estimate=LIGHT,
        name="sum_heads",
    )(*parts)


def place_kernel(n_seq, first, part, old_k, old_v, out_k, out_v, buf, sem_in, sem_out):
    _, sent = half_of("seq", n_seq)
    _, count, rows, _ = part.shape
    pairs = [
        (
            pltpu.make_async_copy(part.at[i, j], buf.at[i, j], sem_in.at[i, j]),
            pltpu.make_async_copy(
                buf.at[i, j], out.at[first + j, lanes(sent, rows), :], sem_out.at[i, j]
            ),
        )
        for j in range(count)
        for i, out in enumerate((out_k, out_v))
    ]
    for load, _ in pairs:
        load.start()
    for load, store in pairs:
        load.wait()
        store.start()
    for _, store in pairs:
        store.wait()


def place_part(n_seq, first, part, out_k, out_v):
    hbm = pl.BlockSpec(memory_space=pl.ANY)
    shape = jax.ShapeDtypeStruct(out_k.shape, out_k.dtype)
    return pl.pallas_call(
        functools.partial(place_kernel, n_seq, first),
        out_shape=(shape, shape),
        in_specs=[hbm] * 3,
        out_specs=(hbm, hbm),
        scratch_shapes=[
            pltpu.VMEM(part.shape, part.dtype),
            pltpu.SemaphoreType.DMA((2, part.shape[1])),
            pltpu.SemaphoreType.DMA((2, part.shape[1])),
        ],
        input_output_aliases={1: 0, 2: 1},
        compiler_params=pltpu.CompilerParams(vmem_limit_bytes=SMALL_LIMIT),
        cost_estimate=LIGHT,
        name="place_received",
    )(part, out_k, out_v)


def others(value, axis):
    count = lax.axis_size(axis)
    return [value] + [
        lax.ppermute(value, axis, [(i, (i + k) % count) for i in range(count)])
        for k in range(1, count)
    ]


def shards(
    keys, values, log_forget, keep, merge_weight, lengths, route, fresh, new_forget, out_weight
):
    req, pos, width = keys.shape
    heads = log_forget.shape[1]
    size = width // heads
    n_seq, n_grp = lax.axis_size("seq"), lax.axis_size("grp")
    cache = (lengths, keep, merge_weight, keys, values)
    chunk, packed = send_part(
        n_seq, 0, FIRST, *cache, (fresh.reshape(3 * req, width), new_forget)
    )
    chunks = [chunk, send_part(n_seq, FIRST, req - FIRST, *cache, (chunk,))[0]]
    if n_seq == 2:
        received = [lax.ppermute(x, "seq", [(0, 1), (1, 0)]) for x in chunks]
    else:
        received = chunks
    tokens = others(packed, "grp")
    out_k, out_v, logs, stats, picked = main_part(
        n_seq,
        n_grp,
        lengths,
        route,
        keep,
        merge_weight,
        log_forget.transpose(1, 0, 2),
        keys,
        values,
        chunks,
        tokens,
    )
    if n_seq == 2:
        all_stats = others(stats, "seq")
    else:
        gathered = lax.all_gather(stats, "seq")
        all_stats = [gathered[i] for i in range(n_seq)]
    decay, partial = merge_part(all_stats, n_seq == 2, picked, out_weight, logs, size)
    layer_out = sum_part(others(partial, "head"))
    out_k, out_v = place_part(n_seq, 0, received[0], out_k, out_v)
    out_k, out_v = place_part(n_seq, FIRST, received[1], out_k, out_v)
    if n_seq != 2:
        out_k, out_v = (
            lax.all_to_all(x, "seq", split_axis=1, concat_axis=1, tiled=True) for x in (out_k, out_v)
        )
    return out_k, out_v, decay.transpose(1, 0, 2), layer_out


def solution(mesh):
    return jax.shard_map(
        shards,
        mesh=mesh,
        in_specs=(
            P("grp", "seq", "head"),
            P("grp", "seq", "head"),
            P("grp", "head", "seq"),
            P("grp", "seq"),
            P("grp", "seq"),
            P("grp"),
            P("grp"),
            P(None, "grp", "head"),
            P("grp", "head"),
            P("head", "seq"),
        ),
        out_specs=(
            P("grp", "seq", "head"),
            P("grp", "seq", "head"),
            P("grp", "head", "seq"),
            P("grp", "seq"),
        ),
        check_vma=False,
    )
```

```python
import functools

import jax
import jax.numpy as jnp
from jax import lax
from jax.experimental import pallas as pl
from jax.experimental.pallas import tpu as pltpu
from jax.sharding import PartitionSpec as P

BLOCK = 64
SLOTS = 32
LANES = 128
BLOCK_LOG = BLOCK.bit_length() - 1
SLOT_LOG = SLOTS.bit_length() - 1
EMPTY_LOG = -10000.0
FIRST = 4
VMEM_LIMIT = 63 * 1024 * 1024
SMALL_LIMIT = 8 * 1024 * 1024


LIGHT = pl.CostEstimate(flops=1, bytes_accessed=1, transcendentals=0)
MERGE = pl.CostEstimate(flops=1 << 36, bytes_accessed=1, transcendentals=0)


def dot(a, b):
    return lax.dot_general(a, b, (((1,), (0,)), ((), ())), preferred_element_type=jnp.float32)


def dot_nt(a, b):
    return lax.dot_general(a, b, (((1,), (1,)), ((), ())), preferred_element_type=jnp.float32)


def iota(shape, dim):
    return lax.broadcasted_iota(jnp.int32, shape, dim)


def three(x):
    hi = x.astype(jnp.bfloat16).astype(jnp.float32)
    rest = x - hi
    mid = rest.astype(jnp.bfloat16).astype(jnp.float32)
    return hi, mid, rest - mid


def split_dot(x, ones):
    rows = x.shape[0]
    parts = dot(jnp.concatenate(three(x), axis=0).astype(jnp.bfloat16), ones)
    return parts[:rows] + parts[rows : 2 * rows] + parts[2 * rows :]


def half_of(axis, count):
    own = lax.axis_index(axis) if count == 2 else jnp.int32(0)
    return own, 1 - own


def by_row(ref, row):
    picked = jnp.zeros_like(row)
    for r in range(ref.shape[0]):
        picked = jnp.where(row == r, ref[r], picked)
    return picked


def plan(keep, weight, start, len_ref):
    rows, width = keep.shape
    one, two = iota((width, width), 0), iota((width, width), 1)
    same = (one ^ two) < BLOCK
    upto = (same & (one <= two)).astype(jnp.float32).astype(jnp.bfloat16)
    block = same.astype(jnp.float32).astype(jnp.bfloat16)
    kept = keep == 1
    rank = dot(keep.astype(jnp.float32).astype(jnp.bfloat16), upto) - 1.0
    weighted = jnp.where(kept, 0.0, weight)
    share = (weighted / split_dot(weighted, block)).astype(jnp.bfloat16).astype(jnp.float32)
    lane, row = iota((rows, width), 1), iota((rows, width), 0)
    slot = jnp.where(kept, rank.astype(jnp.int32), SLOTS - 1) + (lane >> BLOCK_LOG) * SLOTS
    slot = jnp.where(start + lane < by_row(len_ref, row), slot, -1)
    return slot, jnp.where(kept, 1.0, share)


def select(slot, factor, r):
    width = slot.shape[1]
    shape = (width // 2, width)
    hit = iota(shape, 0) == slot[r : r + 1, :]
    return jnp.where(hit, jnp.broadcast_to(factor[r : r + 1, :], shape), 0.0).astype(jnp.bfloat16)


def lanes(half, width):
    return pl.ds(pl.multiple_of(half * width, width), width)


def fetch(pairs, sem):
    copies = [pltpu.make_async_copy(src, dst, sem.at[i]) for i, (src, dst) in enumerate(pairs)]
    for copy in copies:
        copy.start()
    return copies


def first_kernel(n_seq, len_hbm, keep_hbm, weight_hbm, fresh_hbm, gate_hbm, keys, values, *rest):
    out, packed, lengths, keep, weight, fresh, gates, raw, rows, sem_s, sem_r, sem_o = rest
    _, sent = half_of("seq", n_seq)
    width = raw.shape[2]
    count = raw.shape[1]
    small = fetch(
        [
            (len_hbm, lengths),
            (keep_hbm.at[:, lanes(sent, width)], keep),
            (weight_hbm.at[:, lanes(sent, width)], weight),
            (fresh_hbm, fresh),
            (gate_hbm, gates),
        ],
        sem_s,
    )
    slabs = fetch(
        [
            (source.at[j, lanes(sent, width), :], raw.at[i, j])
            for j in range(count)
            for i, source in enumerate((keys, values))
        ],
        sem_r,
    )
    for copy in small:
        copy.wait()
    start = lax.axis_index("seq") * (2 * width) + sent * width
    slot, factor = plan(keep[...], weight[...], start, lengths)

    new, gate = fresh[...].astype(jnp.float32), gates[...].astype(jnp.float32)
    req, heads = gate.shape
    lane = iota((req, new.shape[1]), 1)
    size = new.shape[1] // heads
    spread = jnp.zeros((req, new.shape[1]), jnp.float32)
    for h in range(heads):
        inside = (lane >= h * size) & (lane < (h + 1) * size)
        spread = jnp.where(inside, gate[:, h : h + 1], spread)
    packed[...] = jnp.concatenate([new, spread], axis=0).astype(jnp.bfloat16)

    stores = []
    for j in range(count):
        chosen = select(slot, factor, j)
        for i in range(2):
            slabs[j * 2 + i].wait()
            rows[i, j] = dot(chosen, raw[i, j]).astype(jnp.bfloat16)
        stores.append(pltpu.make_async_copy(rows.at[:, j], out.at[:, j], sem_o.at[j]))
        stores[-1].start()
    for copy in stores:
        copy.wait()


def first_part(n_seq, count, lengths, keep, weight, fresh, gates, keys, values):
    req, pos, width = keys.shape
    half = pos // 2
    hbm = pl.BlockSpec(memory_space=pl.ANY)
    vmem = pl.BlockSpec(memory_space=pltpu.VMEM)
    rows = (2, count, half // 2, width)
    return pl.pallas_call(
        functools.partial(first_kernel, n_seq),
        out_shape=(
            jax.ShapeDtypeStruct(rows, jnp.bfloat16),
            jax.ShapeDtypeStruct((fresh.shape[0] + req, width), jnp.bfloat16),
        ),
        in_specs=[hbm] * 7,
        out_specs=(hbm, vmem),
        scratch_shapes=[
            pltpu.SMEM(lengths.shape, jnp.int32),
            pltpu.VMEM((req, half), jnp.int32),
            pltpu.VMEM((req, half), jnp.float32),
            pltpu.VMEM(fresh.shape, fresh.dtype),
            pltpu.VMEM(gates.shape, gates.dtype),
            pltpu.VMEM((2, count, half, width), jnp.bfloat16),
            pltpu.VMEM(rows, jnp.bfloat16),
            pltpu.SemaphoreType.DMA((5,)),
            pltpu.SemaphoreType.DMA((2 * count,)),
            pltpu.SemaphoreType.DMA((count,)),
        ],
        compiler_params=pltpu.CompilerParams(vmem_limit_bytes=VMEM_LIMIT),
        cost_estimate=LIGHT,
        name="compact_first_sent",
    )(lengths, keep, weight, fresh, gates, keys, values)


def own_kernel(
    n_seq, first, len_hbm, keep_hbm, weight_hbm, forget_hbm, keys, values, packed_hbm, *rest
):
    out_k, out_v, chunk, log_ref, level_ref, total_ref = rest[:6]
    lengths, keep, weight, gates, raw, late, forget, rows, rows_late = rest[6:15]
    sem_s, sem_l, sem_r, sem_c, sem_o = rest[15:]
    own, sent = half_of("seq", n_seq)
    seq = lax.axis_index("seq")
    heads, req, pos = forget_hbm.shape
    half = pos // 2
    slots = half // 2
    pad = forget.shape[1] // req
    small = fetch(
        [(len_hbm, lengths), (keep_hbm, keep), (weight_hbm, weight), (forget_hbm, gates)], sem_s
    )
    both = ((0, keys), (1, values))
    late_slabs = fetch(
        [
            (source.at[r, lanes(sent, half), :], late.at[i, r - first])
            for r in range(first, req)
            for i, source in both
        ],
        sem_l,
    )
    slabs = fetch(
        [
            (source.at[r, lanes(own, half), :], raw.at[i, r])
            for r in range(req)
            for i, source in both
        ],
        sem_r,
    )
    for copy in small:
        copy.wait()

    forget[...] = jnp.zeros_like(forget)
    live = seq * pos + iota((req, pos), 1) < by_row(lengths, iota((req, pos), 0))
    for h in range(heads):
        gate = jnp.where(live, gates[h], 0.0)
        for c in range(pos // LANES):
            forget[c, pl.ds(h, req, stride=pad), :] = gate[:, c * LANES : (c + 1) * LANES]
    flat = jnp.concatenate([forget[c] for c in range(pos // LANES)], axis=1)
    total_ref[...] = jnp.broadcast_to(jnp.sum(flat, axis=1, keepdims=True), total_ref.shape)
    one, two = iota((half, half), 0), iota((half, half), 1)
    after = (((one ^ two) < BLOCK) & (one > two)).astype(jnp.float32).astype(jnp.bfloat16)
    ends = iota((pos, slots), 1) >> SLOT_LOG
    begins = iota((pos, slots), 0) >> BLOCK_LOG
    last = iota((req * pad, slots), 1) & (SLOTS - 1) == SLOTS - 1

    stores = []
    for i, h in enumerate((own, sent)):
        slot, factor = plan(
            keep[:, lanes(h, half)], weight[:, lanes(h, half)], seq * pos + h * half, lengths
        )
        near = half // LANES
        inner = split_dot(
            jnp.concatenate([forget[h * near + c] for c in range(near)], axis=1), after
        )
        beyond = split_dot(
            flat, (begins > ends + h * (half // BLOCK)).astype(jnp.float32).astype(jnp.bfloat16)
        )
        spread = jnp.exp(inner)
        high = spread.astype(jnp.bfloat16).astype(jnp.float32)
        planes = three(inner) + (high, spread - high, jnp.ones_like(inner))
        found = []
        for r in range(req):
            chosen = select(slot, factor, r)
            stack = jnp.concatenate([x[r * pad : (r + 1) * pad] for x in planes], axis=0)
            found.append(dot_nt(stack.astype(jnp.bfloat16), chosen))
            if i == 0:
                for k, out in enumerate((out_k, out_v)):
                    slabs[2 * r + k].wait()
                    rows[k, r] = dot(chosen, raw[k, r]).astype(jnp.bfloat16)
                    stores.append(
                        pltpu.make_async_copy(
                            rows.at[k, r], out.at[r, lanes(own, slots), :], sem_o.at[2 * r + k]
                        )
                    )
                    stores[-1].start()
            elif r >= first:
                for k in range(2):
                    late_slabs[2 * (r - first) + k].wait()
                    rows_late[k, r - first] = dot(chosen, late[k, r - first]).astype(jnp.bfloat16)
                stores.append(
                    pltpu.make_async_copy(
                        rows_late.at[:, r - first], chunk.at[:, r - first], sem_c.at[r - first]
                    )
                )
                stores[-1].start()
        at = [
            jnp.concatenate([x[p * pad : (p + 1) * pad] for x in found], axis=0) for p in range(6)
        ]
        filled = at[5] > 0.5
        kept = at[0] + at[1] + at[2]
        merged = jnp.log(jnp.where(filled, at[3] + at[4], 1.0))
        level_ref[i] = jnp.where(filled, jnp.where(last, merged, kept) + beyond, EMPTY_LOG)
        for k in range(heads):
            log_ref[k, :, lanes(h, slots)] = level_ref[i, pl.ds(k, req, stride=pad), :]
    for copy in stores:
        copy.wait()


def own_part(n_seq, first, lengths, keep, weight, forget, keys, values, packed):
    req, pos, width = keys.shape
    heads = forget.shape[0]
    half, slots, pad = pos // 2, pos // 4, -(-heads // 8) * 8
    late = req - first
    hbm = pl.BlockSpec(memory_space=pl.ANY)
    vmem = pl.BlockSpec(memory_space=pltpu.VMEM)
    whole = jax.ShapeDtypeStruct((req, 2 * slots, width), jnp.bfloat16)
    return pl.pallas_call(
        functools.partial(own_kernel, n_seq, first),
        out_shape=(
            whole,
            whole,
            jax.ShapeDtypeStruct((2, late, slots, width), jnp.bfloat16),
            jax.ShapeDtypeStruct((heads, req, 2 * slots), jnp.float32),
            jax.ShapeDtypeStruct((2, req * pad, slots), jnp.float32),
            jax.ShapeDtypeStruct((req * pad, LANES), jnp.float32),
        ),
        in_specs=[hbm] * 7,
        out_specs=(hbm, hbm, hbm, vmem, vmem, vmem),
        scratch_shapes=[
            pltpu.SMEM(lengths.shape, jnp.int32),
            pltpu.VMEM(keep.shape, keep.dtype),
            pltpu.VMEM(weight.shape, weight.dtype),
            pltpu.VMEM(forget.shape, forget.dtype),
            pltpu.VMEM((2, req, half, width), jnp.bfloat16),
            pltpu.VMEM((2, late, half, width), jnp.bfloat16),
            pltpu.VMEM((pos // LANES, req * pad, LANES), jnp.float32),
            pltpu.VMEM((2, req, slots, width), jnp.bfloat16),
            pltpu.VMEM((2, late, slots, width), jnp.bfloat16),
            pltpu.SemaphoreType.DMA((4,)),
            pltpu.SemaphoreType.DMA((2 * late,)),
            pltpu.SemaphoreType.DMA((2 * req,)),
            pltpu.SemaphoreType.DMA((late,)),
            pltpu.SemaphoreType.DMA((2 * req,)),
        ],
        compiler_params=pltpu.CompilerParams(vmem_limit_bytes=VMEM_LIMIT),
        cost_estimate=LIGHT,
        name="compact_own",
    )(lengths, keep, weight, forget, keys, values, packed)


def attend_kernel(n_seq, n_grp, heads, first, *refs):
    route_hbm, out_k, out_v, early, late, level_hbm, total_hbm = refs[:7]
    tokens, rest = refs[7 : 7 + n_grp], refs[7 + n_grp :]
    _, _, _, stats_ref, picked_ref = rest[:5]
    route, own_rows, sent_rows, level, total, fresh, scores, sem_s, sem_r = rest[5:]
    own, _ = half_of("seq", n_seq)
    kinds, width = picked_ref.shape
    req = kinds // 4
    size = width // heads
    slots = own_rows.shape[2]
    pad = total.shape[0] // req
    small = fetch(
        [(route_hbm, route), (level_hbm, level), (total_hbm, total)]
        + [(x, fresh.at[k]) for k, x in enumerate(tokens)],
        sem_s,
    )
    slabs = fetch(
        [
            (out_k.at[:, lanes(own, slots), :], own_rows.at[0]),
            (early, sent_rows.at[:, pl.ds(0, first)]),
            (late, sent_rows.at[:, pl.ds(first, req - first)]),
            (out_v.at[:, lanes(own, slots), :], own_rows.at[1]),
        ],
        sem_r,
    )
    for copy in small:
        copy.wait()

    shape = (kinds, kinds)
    to, frm = iota(shape, 0), iota(shape, 1)
    wanted = by_row(route, to % req)
    me = lax.axis_index("grp")
    picked = jnp.zeros((kinds, width), jnp.float32)
    for k in range(n_grp):
        source = lax.rem(me + n_grp - k, n_grp)
        hit = (to // req == frm // req) & (wanted == source * req + frm % req)
        picked = picked + dot(hit.astype(jnp.float32).astype(jnp.bfloat16), fresh[k])
    picked_ref[...] = picked
    for copy in slabs:
        copy.wait()

    lane, row = iota((pad, width), 1), iota((pad, width), 0)
    mine = (lane >= row * size) & (lane < (row + 1) * size)
    for r in range(req):
        query = jnp.where(mine, picked[r : r + 1, :], 0.0).astype(jnp.bfloat16)
        here = slice(r * pad, (r + 1) * pad)
        scores[here, :slots] = dot_nt(query, own_rows[0, r])
        scores[here, slots:] = dot_nt(query, sent_rows[0, r])
    logit = scores[...] * (size**-0.5) + jnp.concatenate([level[0], level[1]], axis=1)
    top = jnp.max(logit, axis=1, keepdims=True)
    weights = jnp.exp(logit - top).astype(jnp.bfloat16).astype(jnp.float32)
    mass = jnp.sum(weights, axis=1, keepdims=True)

    def spread_out(column, r):
        return jnp.sum(
            jnp.where(mine, column[r * pad : (r + 1) * pad], 0.0), axis=0, keepdims=True
        )

    for r in range(req):
        w = weights[r * pad : (r + 1) * pad].astype(jnp.bfloat16)
        acc = dot(w[:, :slots], own_rows[1, r]) + dot(w[:, slots:], sent_rows[1, r])
        acc = jnp.sum(jnp.where(mine, acc, 0.0), axis=0, keepdims=True)
        for p, x in enumerate((top, mass, total[:, :1])):
            stats_ref[p * req + r : p * req + r + 1, :] = spread_out(x, r)
        stats_ref[3 * req + r : 3 * req + r + 1, :] = acc


def attend_part(n_seq, n_grp, heads, route, out_k, out_v, early, late, level, total, tokens):
    req, rows, width = out_k.shape
    slots, first = rows // 2, early.shape[1]
    hbm = pl.BlockSpec(memory_space=pl.ANY)
    vmem = pl.BlockSpec(memory_space=pltpu.VMEM)
    whole = jax.ShapeDtypeStruct(out_k.shape, out_k.dtype)
    small = jax.ShapeDtypeStruct((4 * req, width), jnp.float32)
    return pl.pallas_call(
        functools.partial(attend_kernel, n_seq, n_grp, heads, first),
        out_shape=(whole, whole, jax.ShapeDtypeStruct(late.shape, late.dtype), small, small),
        in_specs=[hbm] * (7 + n_grp),
        out_specs=(hbm, hbm, hbm, vmem, vmem),
        scratch_shapes=[
            pltpu.SMEM(route.shape, jnp.int32),
            pltpu.VMEM((2, req, slots, width), jnp.bfloat16),
            pltpu.VMEM((2, req, slots, width), jnp.bfloat16),
            pltpu.VMEM(level.shape, level.dtype),
            pltpu.VMEM(total.shape, total.dtype),
            pltpu.VMEM((n_grp,) + tokens[0].shape, tokens[0].dtype),
            pltpu.VMEM((total.shape[0], rows), jnp.float32),
            pltpu.SemaphoreType.DMA((3 + n_grp,)),
            pltpu.SemaphoreType.DMA((4,)),
        ],
        input_output_aliases={1: 0, 2: 1, 4: 2},
        compiler_params=pltpu.CompilerParams(vmem_limit_bytes=VMEM_LIMIT),
        cost_estimate=LIGHT,
        name="attend",
    )(route, out_k, out_v, early, late, level, total, *tokens)


def place(n_seq, first, part, out_k, out_v, sem):
    _, sent = half_of("seq", n_seq)
    _, count, rows, _ = part.shape
    return fetch(
        [
            (part.at[i], out.at[pl.ds(first, count), lanes(sent, rows), :])
            for i, out in enumerate((out_k, out_v))
        ],
        sem,
    )


def merge_kernel(n_seq, count, relative, size, *refs):
    stats, refs = refs[:count], refs[count:]
    picked_ref, weight_hbm, log_ref, part, _, _, decay_ref, out_ref, out_k, out_v = refs[:10]
    weight_ref, sem, sem_w = refs[10:]
    (load,) = fetch([(weight_hbm, weight_ref)], sem_w)
    placed = place(n_seq, 0, part, out_k, out_v, sem)
    heads, req, rows = log_ref.shape
    width = picked_ref.shape[1]
    seq = lax.axis_index("seq")
    places = [lax.rem(seq + count - k, count) if relative else jnp.int32(k) for k in range(count)]
    tops, masses, totals, accs = [
        [ref[p * req : (p + 1) * req, :] for ref in stats] for p in range(4)
    ]

    def later(place):
        total = jnp.zeros_like(totals[0])
        for k in range(count):
            total = total + jnp.where(places[k] > place, totals[k], 0.0)
        return total

    tops = [tops[k] + later(places[k]) for k in range(count)]
    top = functools.reduce(jnp.maximum, tops)
    scales = [jnp.exp(t - top) for t in tops]
    mass = sum(s * x for s, x in zip(scales, masses))
    acc = sum(s * x for s, x in zip(scales, accs))
    query, key, value, gate = [picked_ref[p * req : (p + 1) * req, :] for p in range(4)]
    one, two = iota((width, width), 0), iota((width, width), 1)
    same = (one // size == two // size).astype(jnp.float32).astype(jnp.bfloat16)
    own = split_dot(query * key, same) * (size**-0.5)
    past = top + gate
    joint = jnp.maximum(past, own)
    scale, self_weight = jnp.exp(past - joint), jnp.exp(own - joint)
    attended = (scale * acc + self_weight * value) / (scale * mass + self_weight)
    beyond = later(seq)
    for h in range(heads):
        decay_ref[h] = jnp.exp(log_ref[h] + beyond[:, h * size : h * size + 1])
    load.wait()
    out_ref[...] = dot(attended.astype(jnp.bfloat16), weight_ref[...])
    for copy in placed:
        copy.wait()


def merge_part(n_seq, stats, relative, picked, out_weight, logs, size, part, out_k, out_v):
    req = logs.shape[1]
    vmem = pl.BlockSpec(memory_space=pltpu.VMEM)
    hbm = pl.BlockSpec(memory_space=pl.ANY)
    whole = jax.ShapeDtypeStruct(out_k.shape, out_k.dtype)
    count = len(stats)
    return pl.pallas_call(
        functools.partial(merge_kernel, n_seq, count, relative, size),
        out_shape=(
            jax.ShapeDtypeStruct(logs.shape, jnp.float32),
            jax.ShapeDtypeStruct((req, out_weight.shape[1]), jnp.float32),
            whole,
            whole,
        ),
        in_specs=[vmem] * (count + 1) + [hbm] + [vmem] * 2 + [hbm] * 2,
        out_specs=(vmem, vmem, hbm, hbm),
        scratch_shapes=[
            pltpu.VMEM(out_weight.shape, out_weight.dtype),
            pltpu.SemaphoreType.DMA((2,)),
            pltpu.SemaphoreType.DMA((1,)),
        ],
        input_output_aliases={count + 4: 2, count + 5: 3},
        compiler_params=pltpu.CompilerParams(vmem_limit_bytes=VMEM_LIMIT),
        cost_estimate=MERGE,
        name="merge_and_project",
    )(*stats, picked, out_weight, logs, part, out_k, out_v)


def sum_kernel(count, *refs):
    parts, out = refs[:count], refs[count]
    me = lax.axis_index("head")
    total = jnp.zeros(out.shape, jnp.float32)
    for place in range(count):
        for k in range(count):
            total = total + jnp.where(lax.rem(me + count - k, count) == place, parts[k][...], 0.0)
    out[...] = total.astype(out.dtype)


def sum_part(parts):
    return pl.pallas_call(
        functools.partial(sum_kernel, len(parts)),
        out_shape=jax.ShapeDtypeStruct(parts[0].shape, jnp.bfloat16),
        in_specs=[pl.BlockSpec(memory_space=pltpu.VMEM)] * len(parts),
        out_specs=pl.BlockSpec(memory_space=pltpu.VMEM),
        compiler_params=pltpu.CompilerParams(vmem_limit_bytes=SMALL_LIMIT),
        cost_estimate=LIGHT,
        name="sum_heads",
    )(*parts)


def place_kernel(n_seq, first, part, old_k, old_v, out_k, out_v, sem):
    for copy in place(n_seq, first, part, out_k, out_v, sem):
        copy.wait()


def place_part(n_seq, first, part, out_k, out_v):
    hbm = pl.BlockSpec(memory_space=pl.ANY)
    vmem = pl.BlockSpec(memory_space=pltpu.VMEM)
    shape = jax.ShapeDtypeStruct(out_k.shape, out_k.dtype)
    return pl.pallas_call(
        functools.partial(place_kernel, n_seq, first),
        out_shape=(shape, shape),
        in_specs=[vmem, hbm, hbm],
        out_specs=(hbm, hbm),
        scratch_shapes=[pltpu.SemaphoreType.DMA((2,))],
        input_output_aliases={1: 0, 2: 1},
        compiler_params=pltpu.CompilerParams(vmem_limit_bytes=SMALL_LIMIT),
        cost_estimate=LIGHT,
        name="place_received",
    )(part, out_k, out_v)


def others(value, axis):
    count = lax.axis_size(axis)
    return [value] + [
        lax.ppermute(value, axis, [(i, (i + k) % count) for i in range(count)])
        for k in range(1, count)
    ]


def swap(value, n_seq):
    return lax.ppermute(value, "seq", [(0, 1), (1, 0)]) if n_seq == 2 else value


def shards(
    keys, values, log_forget, keep, merge_weight, lengths, route, fresh, new_forget, out_weight
):
    req, pos, width = keys.shape
    heads = log_forget.shape[1]
    size = width // heads
    n_seq, n_grp = lax.axis_size("seq"), lax.axis_size("grp")
    early, packed = first_part(
        n_seq,
        FIRST,
        lengths,
        keep,
        merge_weight,
        fresh.reshape(3 * req, width),
        new_forget,
        keys,
        values,
    )
    exchange = functools.partial(swap, n_seq=n_seq)
    first_received = exchange(early)
    tokens = others(packed, "grp")
    out_k, out_v, late, logs, level, total = own_part(
        n_seq,
        FIRST,
        lengths,
        keep,
        merge_weight,
        log_forget.transpose(1, 0, 2),
        keys,
        values,
        packed,
    )
    out_k, out_v, late, stats, picked = attend_part(
        n_seq, n_grp, heads, route, out_k, out_v, early, late, level, total, tokens
    )
    if n_seq == 2:
        all_stats = others(stats, "seq")
    else:
        gathered = lax.all_gather(stats, "seq")
        all_stats = [gathered[i] for i in range(n_seq)]
    late_received = exchange(late)
    decay, partial, out_k, out_v = merge_part(
        n_seq,
        all_stats,
        n_seq == 2,
        picked,
        out_weight,
        logs,
        size,
        first_received,
        out_k,
        out_v,
    )
    layer_out = sum_part(others(partial, "head"))
    out_k, out_v = place_part(n_seq, FIRST, late_received, out_k, out_v)
    if n_seq != 2:
        out_k, out_v = (
            lax.all_to_all(x, "seq", split_axis=1, concat_axis=1, tiled=True) for x in (out_k, out_v)
        )
    return out_k, out_v, decay.transpose(1, 0, 2), layer_out


def solution(mesh):
    return jax.shard_map(
        shards,
        mesh=mesh,
        in_specs=(
            P("grp", "seq", "head"),
            P("grp", "seq", "head"),
            P("grp", "head", "seq"),
            P("grp", "seq"),
            P("grp", "seq"),
            P("grp"),
            P("grp"),
            P(None, "grp", "head"),
            P("grp", "head"),
            P("head", "seq"),
        ),
        out_specs=(
            P("grp", "seq", "head"),
            P("grp", "seq", "head"),
            P("grp", "head", "seq"),
            P("grp", "seq"),
        ),
        check_vma=False,
    )
```

```python
import functools

import jax
import jax.numpy as jnp
from jax import lax
from jax.experimental import pallas as pl
from jax.experimental.pallas import tpu as pltpu
from jax.sharding import PartitionSpec as P

BLOCK = 64
SLOTS = 32
LANES = 128
BLOCK_LOG = BLOCK.bit_length() - 1
SLOT_LOG = SLOTS.bit_length() - 1
EMPTY_LOG = -10000.0
FIRST = 4
STEP = 2
VMEM_LIMIT = 63 * 1024 * 1024
SMALL_LIMIT = 8 * 1024 * 1024


LIGHT = pl.CostEstimate(flops=1, bytes_accessed=1, transcendentals=0)
MERGE = pl.CostEstimate(flops=1 << 36, bytes_accessed=1, transcendentals=0)


def dot(a, b):
    return lax.dot_general(a, b, (((1,), (0,)), ((), ())), preferred_element_type=jnp.float32)


def dot_nt(a, b):
    return lax.dot_general(a, b, (((1,), (1,)), ((), ())), preferred_element_type=jnp.float32)


def iota(shape, dim):
    return lax.broadcasted_iota(jnp.int32, shape, dim)


def three(x):
    hi = x.astype(jnp.bfloat16).astype(jnp.float32)
    rest = x - hi
    mid = rest.astype(jnp.bfloat16).astype(jnp.float32)
    return hi, mid, rest - mid


def split_dot(x, ones):
    rows = x.shape[0]
    parts = dot(jnp.concatenate(three(x), axis=0).astype(jnp.bfloat16), ones)
    return parts[:rows] + parts[rows : 2 * rows] + parts[2 * rows :]


def half_of(axis, count):
    own = lax.axis_index(axis) if count == 2 else jnp.int32(0)
    return own, 1 - own


def by_row(ref, row):
    picked = jnp.zeros_like(row)
    for r in range(ref.shape[0]):
        picked = jnp.where(row == r, ref[r], picked)
    return picked


def live_blocks(lengths, r, start, most):
    return jnp.clip((lengths[r] - start) >> BLOCK_LOG, 0, most)


def offsets(lengths, first, start, most):
    total = jnp.int32(0)
    ahead = []
    for r in range(first, lengths.shape[0]):
        ahead.append(total)
        total = total + live_blocks(lengths, r, start, most)
    return ahead, total


def plan(keep, weight, start, len_ref):
    rows, width = keep.shape
    one, two = iota((width, width), 0), iota((width, width), 1)
    same = (one ^ two) < BLOCK
    upto = (same & (one <= two)).astype(jnp.float32).astype(jnp.bfloat16)
    block = same.astype(jnp.float32).astype(jnp.bfloat16)
    kept = keep == 1
    rank = dot(keep.astype(jnp.float32).astype(jnp.bfloat16), upto) - 1.0
    weighted = jnp.where(kept, 0.0, weight)
    share = (weighted / split_dot(weighted, block)).astype(jnp.bfloat16).astype(jnp.float32)
    lane, row = iota((rows, width), 1), iota((rows, width), 0)
    slot = jnp.where(kept, rank.astype(jnp.int32), SLOTS - 1) + (lane >> BLOCK_LOG) * SLOTS
    slot = jnp.where(start + lane < by_row(len_ref, row), slot, -1)
    return slot, jnp.where(kept, 1.0, share)


def select(slot, factor, r):
    width = slot.shape[1]
    shape = (width // 2, width)
    hit = iota(shape, 0) == slot[r : r + 1, :]
    return jnp.where(hit, jnp.broadcast_to(factor[r : r + 1, :], shape), 0.0).astype(jnp.bfloat16)


def lanes(half, width):
    return pl.ds(pl.multiple_of(half * width, width), width)


def fetch(pairs, sem):
    copies = [pltpu.make_async_copy(src, dst, sem.at[i]) for i, (src, dst) in enumerate(pairs)]
    for copy in copies:
        copy.start()
    return copies


def first_kernel(n_seq, len_hbm, keep_hbm, weight_hbm, fresh_hbm, gate_hbm, keys, values, *rest):
    out, packed, size_ref, lengths, keep, weight, fresh, gates, raw, rows = rest[:10]
    sem_s, sem_r, sem_o = rest[10:]
    _, sent = half_of("seq", n_seq)
    width = raw.shape[2]
    count = raw.shape[1]
    small = fetch(
        [
            (len_hbm, lengths),
            (keep_hbm.at[:, lanes(sent, width)], keep),
            (weight_hbm.at[:, lanes(sent, width)], weight),
            (fresh_hbm, fresh),
            (gate_hbm, gates),
        ],
        sem_s,
    )
    slabs = fetch(
        [
            (source.at[j, lanes(sent, width), :], raw.at[i, j])
            for j in range(count)
            for i, source in enumerate((keys, values))
        ],
        sem_r,
    )
    for copy in small:
        copy.wait()
    start = lax.axis_index("seq") * (2 * width) + sent * width
    slot, factor = plan(keep[...], weight[...], start, lengths)
    most = width // BLOCK
    _, total = offsets(lengths, count, width, most)
    sizes = most * (lengths.shape[0] - count) // STEP
    size_ref[0] = jnp.clip((total - 1) >> (STEP.bit_length() - 1), 0, sizes - 1)

    new, gate = fresh[...].astype(jnp.float32), gates[...].astype(jnp.float32)
    req, heads = gate.shape
    lane = iota((req, new.shape[1]), 1)
    size = new.shape[1] // heads
    spread = jnp.zeros((req, new.shape[1]), jnp.float32)
    for h in range(heads):
        inside = (lane >= h * size) & (lane < (h + 1) * size)
        spread = jnp.where(inside, gate[:, h : h + 1], spread)
    packed[...] = jnp.concatenate([new, spread], axis=0).astype(jnp.bfloat16)

    stores = []
    for j in range(count):
        chosen = select(slot, factor, j)
        for i in range(2):
            slabs[j * 2 + i].wait()
            rows[i, j] = dot(chosen, raw[i, j]).astype(jnp.bfloat16)
        stores.append(pltpu.make_async_copy(rows.at[:, j], out.at[:, j], sem_o.at[j]))
        stores[-1].start()
    for copy in stores:
        copy.wait()


def first_part(n_seq, count, lengths, keep, weight, fresh, gates, keys, values):
    req, pos, width = keys.shape
    half = pos // 2
    hbm = pl.BlockSpec(memory_space=pl.ANY)
    vmem = pl.BlockSpec(memory_space=pltpu.VMEM)
    rows = (2, count, half // 2, width)
    return pl.pallas_call(
        functools.partial(first_kernel, n_seq),
        out_shape=(
            jax.ShapeDtypeStruct(rows, jnp.bfloat16),
            jax.ShapeDtypeStruct((fresh.shape[0] + req, width), jnp.bfloat16),
            jax.ShapeDtypeStruct((1,), jnp.int32),
        ),
        in_specs=[hbm] * 7,
        out_specs=(hbm, vmem, pl.BlockSpec(memory_space=pltpu.SMEM)),
        scratch_shapes=[
            pltpu.SMEM(lengths.shape, jnp.int32),
            pltpu.VMEM((req, half), jnp.int32),
            pltpu.VMEM((req, half), jnp.float32),
            pltpu.VMEM(fresh.shape, fresh.dtype),
            pltpu.VMEM(gates.shape, gates.dtype),
            pltpu.VMEM((2, count, half, width), jnp.bfloat16),
            pltpu.VMEM(rows, jnp.bfloat16),
            pltpu.SemaphoreType.DMA((5,)),
            pltpu.SemaphoreType.DMA((2 * count,)),
            pltpu.SemaphoreType.DMA((count,)),
        ],
        compiler_params=pltpu.CompilerParams(vmem_limit_bytes=VMEM_LIMIT),
        cost_estimate=LIGHT,
        name="compact_first_sent",
    )(lengths, keep, weight, fresh, gates, keys, values)


def own_kernel(
    n_seq, first, len_hbm, keep_hbm, weight_hbm, forget_hbm, keys, values, packed_hbm, *rest
):
    out_k, out_v, chunk, log_ref, level_ref, total_ref = rest[:6]
    lengths, keep, weight, gates, raw, late, forget, rows, rows_late, zeros = rest[6:16]
    sem_s, sem_l, sem_r, sem_c, sem_o, sem_z = rest[16:]
    own, sent = half_of("seq", n_seq)
    seq = lax.axis_index("seq")
    heads, req, pos = forget_hbm.shape
    half = pos // 2
    slots = half // 2
    pad = forget.shape[1] // req
    small = fetch(
        [(len_hbm, lengths), (keep_hbm, keep), (weight_hbm, weight), (forget_hbm, gates)], sem_s
    )
    both = ((0, keys), (1, values))
    late_slabs = fetch(
        [
            (source.at[r, lanes(sent, half), :], late.at[i, r - first])
            for r in range(first, req)
            for i, source in both
        ],
        sem_l,
    )
    slabs = fetch(
        [
            (source.at[r, lanes(own, half), :], raw.at[i, r])
            for r in range(req)
            for i, source in both
        ],
        sem_r,
    )
    zeros[...] = jnp.zeros_like(zeros)
    stores = fetch(
        [
            (zeros, out.at[r, lanes(sent, slots), :])
            for r in range(first, req)
            for out in (out_k, out_v)
        ],
        sem_z,
    )
    for copy in small:
        copy.wait()
    ahead, _ = offsets(lengths, first, seq * pos + sent * half, half // BLOCK)

    forget[...] = jnp.zeros_like(forget)
    live = seq * pos + iota((req, pos), 1) < by_row(lengths, iota((req, pos), 0))
    for h in range(heads):
        gate = jnp.where(live, gates[h], 0.0)
        for c in range(pos // LANES):
            forget[c, pl.ds(h, req, stride=pad), :] = gate[:, c * LANES : (c + 1) * LANES]
    flat = jnp.concatenate([forget[c] for c in range(pos // LANES)], axis=1)
    total_ref[...] = jnp.broadcast_to(jnp.sum(flat, axis=1, keepdims=True), total_ref.shape)
    one, two = iota((half, half), 0), iota((half, half), 1)
    after = (((one ^ two) < BLOCK) & (one > two)).astype(jnp.float32).astype(jnp.bfloat16)
    ends = iota((pos, slots), 1) >> SLOT_LOG
    begins = iota((pos, slots), 0) >> BLOCK_LOG
    last = iota((req * pad, slots), 1) & (SLOTS - 1) == SLOTS - 1

    for i, h in enumerate((own, sent)):
        slot, factor = plan(
            keep[:, lanes(h, half)], weight[:, lanes(h, half)], seq * pos + h * half, lengths
        )
        near = half // LANES
        inner = split_dot(
            jnp.concatenate([forget[h * near + c] for c in range(near)], axis=1), after
        )
        beyond = split_dot(
            flat, (begins > ends + h * (half // BLOCK)).astype(jnp.float32).astype(jnp.bfloat16)
        )
        spread = jnp.exp(inner)
        high = spread.astype(jnp.bfloat16).astype(jnp.float32)
        planes = three(inner) + (high, spread - high, jnp.ones_like(inner))
        found = []
        for r in range(req):
            chosen = select(slot, factor, r)
            stack = jnp.concatenate([x[r * pad : (r + 1) * pad] for x in planes], axis=0)
            found.append(dot_nt(stack.astype(jnp.bfloat16), chosen))
            if i == 0:
                for k, out in enumerate((out_k, out_v)):
                    slabs[2 * r + k].wait()
                    rows[k, r] = dot(chosen, raw[k, r]).astype(jnp.bfloat16)
                    stores.append(
                        pltpu.make_async_copy(
                            rows.at[k, r], out.at[r, lanes(own, slots), :], sem_o.at[2 * r + k]
                        )
                    )
                    stores[-1].start()
            elif r >= first:
                at = pl.ds(pl.multiple_of(ahead[r - first] * SLOTS, SLOTS), slots)
                for k in range(2):
                    late_slabs[2 * (r - first) + k].wait()
                    rows_late[k, at, :] = dot(chosen, late[k, r - first]).astype(jnp.bfloat16)
        if i == 1:
            stores += fetch([(rows_late, chunk)], sem_c)
        at = [
            jnp.concatenate([x[p * pad : (p + 1) * pad] for x in found], axis=0) for p in range(6)
        ]
        filled = at[5] > 0.5
        kept = at[0] + at[1] + at[2]
        merged = jnp.log(jnp.where(filled, at[3] + at[4], 1.0))
        level_ref[i] = jnp.where(filled, jnp.where(last, merged, kept) + beyond, EMPTY_LOG)
        for k in range(heads):
            log_ref[k, :, lanes(h, slots)] = level_ref[i, pl.ds(k, req, stride=pad), :]
    for copy in stores:
        copy.wait()


def own_part(n_seq, first, lengths, keep, weight, forget, keys, values, packed):
    req, pos, width = keys.shape
    heads = forget.shape[0]
    half, slots, pad = pos // 2, pos // 4, -(-heads // 8) * 8
    late = req - first
    hbm = pl.BlockSpec(memory_space=pl.ANY)
    vmem = pl.BlockSpec(memory_space=pltpu.VMEM)
    whole = jax.ShapeDtypeStruct((req, 2 * slots, width), jnp.bfloat16)
    return pl.pallas_call(
        functools.partial(own_kernel, n_seq, first),
        out_shape=(
            whole,
            whole,
            jax.ShapeDtypeStruct((2, late * slots, width), jnp.bfloat16),
            jax.ShapeDtypeStruct((heads, req, 2 * slots), jnp.float32),
            jax.ShapeDtypeStruct((2, req * pad, slots), jnp.float32),
            jax.ShapeDtypeStruct((req * pad, LANES), jnp.float32),
        ),
        in_specs=[hbm] * 7,
        out_specs=(hbm, hbm, hbm, vmem, vmem, vmem),
        scratch_shapes=[
            pltpu.SMEM(lengths.shape, jnp.int32),
            pltpu.VMEM(keep.shape, keep.dtype),
            pltpu.VMEM(weight.shape, weight.dtype),
            pltpu.VMEM(forget.shape, forget.dtype),
            pltpu.VMEM((2, req, half, width), jnp.bfloat16),
            pltpu.VMEM((2, late, half, width), jnp.bfloat16),
            pltpu.VMEM((pos // LANES, req * pad, LANES), jnp.float32),
            pltpu.VMEM((2, req, slots, width), jnp.bfloat16),
            pltpu.VMEM((2, late * slots, width), jnp.bfloat16),
            pltpu.VMEM((slots, width), jnp.bfloat16),
            pltpu.SemaphoreType.DMA((4,)),
            pltpu.SemaphoreType.DMA((2 * late,)),
            pltpu.SemaphoreType.DMA((2 * req,)),
            pltpu.SemaphoreType.DMA((1,)),
            pltpu.SemaphoreType.DMA((2 * req,)),
            pltpu.SemaphoreType.DMA((2 * late,)),
        ],
        compiler_params=pltpu.CompilerParams(vmem_limit_bytes=VMEM_LIMIT),
        cost_estimate=LIGHT,
        name="compact_own",
    )(lengths, keep, weight, forget, keys, values, packed)


def attend_kernel(n_seq, n_grp, heads, first, *refs):
    len_hbm, route_hbm, out_k, out_v, early, late, level_hbm, total_hbm = refs[:8]
    tokens, rest = refs[8 : 8 + n_grp], refs[8 + n_grp :]
    _, _, _, stats_ref, picked_ref = rest[:5]
    lengths, route, own_rows, sent_rows, late_rows, level, total, fresh, scores = rest[5:14]
    sem_s, sem_r = rest[14:]
    own, sent = half_of("seq", n_seq)
    kinds, width = picked_ref.shape
    req = kinds // 4
    size = width // heads
    slots = own_rows.shape[2]
    pad = total.shape[0] // req
    small = fetch(
        [(len_hbm, lengths), (route_hbm, route), (level_hbm, level), (total_hbm, total)]
        + [(x, fresh.at[k]) for k, x in enumerate(tokens)],
        sem_s,
    )
    slabs = fetch(
        [
            (out_k.at[:, lanes(own, slots), :], own_rows.at[0]),
            (early, sent_rows),
            (late, late_rows),
            (out_v.at[:, lanes(own, slots), :], own_rows.at[1]),
        ],
        sem_r,
    )
    for copy in small:
        copy.wait()
    start = lax.axis_index("seq") * (4 * slots) + sent * (2 * slots)
    ahead, _ = offsets(lengths, first, start, slots // SLOTS)

    def sent_part(i, r):
        if r < first:
            return sent_rows[i, r]
        at = pl.multiple_of(ahead[r - first] * SLOTS, SLOTS)
        return late_rows[i, pl.ds(at, slots), :]

    shape = (kinds, kinds)
    to, frm = iota(shape, 0), iota(shape, 1)
    wanted = by_row(route, to % req)
    me = lax.axis_index("grp")
    picked = jnp.zeros((kinds, width), jnp.float32)
    for k in range(n_grp):
        source = lax.rem(me + n_grp - k, n_grp)
        hit = (to // req == frm // req) & (wanted == source * req + frm % req)
        picked = picked + dot(hit.astype(jnp.float32).astype(jnp.bfloat16), fresh[k])
    picked_ref[...] = picked
    for copy in slabs:
        copy.wait()

    lane, row = iota((pad, width), 1), iota((pad, width), 0)
    mine = (lane >= row * size) & (lane < (row + 1) * size)
    for r in range(req):
        query = jnp.where(mine, picked[r : r + 1, :], 0.0).astype(jnp.bfloat16)
        here = slice(r * pad, (r + 1) * pad)
        scores[here, :slots] = dot_nt(query, own_rows[0, r])
        scores[here, slots:] = dot_nt(query, sent_part(0, r))
    logit = scores[...] * (size**-0.5) + jnp.concatenate([level[0], level[1]], axis=1)
    top = jnp.max(logit, axis=1, keepdims=True)
    weights = jnp.exp(logit - top).astype(jnp.bfloat16).astype(jnp.float32)
    mass = jnp.sum(weights, axis=1, keepdims=True)

    def spread_out(column, r):
        return jnp.sum(
            jnp.where(mine, column[r * pad : (r + 1) * pad], 0.0), axis=0, keepdims=True
        )

    for r in range(req):
        w = weights[r * pad : (r + 1) * pad].astype(jnp.bfloat16)
        acc = dot(w[:, :slots], own_rows[1, r]) + dot(w[:, slots:], sent_part(1, r))
        acc = jnp.sum(jnp.where(mine, acc, 0.0), axis=0, keepdims=True)
        for p, x in enumerate((top, mass, total[:, :1])):
            stats_ref[p * req + r : p * req + r + 1, :] = spread_out(x, r)
        stats_ref[3 * req + r : 3 * req + r + 1, :] = acc


def attend_part(n_seq, n_grp, heads, lengths, route, out_k, out_v, early, late, level, total, tokens):
    req, rows, width = out_k.shape
    slots, first = rows // 2, early.shape[1]
    hbm = pl.BlockSpec(memory_space=pl.ANY)
    vmem = pl.BlockSpec(memory_space=pltpu.VMEM)
    whole = jax.ShapeDtypeStruct(out_k.shape, out_k.dtype)
    small = jax.ShapeDtypeStruct((4 * req, width), jnp.float32)
    return pl.pallas_call(
        functools.partial(attend_kernel, n_seq, n_grp, heads, first),
        out_shape=(whole, whole, jax.ShapeDtypeStruct(late.shape, late.dtype), small, small),
        in_specs=[hbm] * (8 + n_grp),
        out_specs=(hbm, hbm, hbm, vmem, vmem),
        scratch_shapes=[
            pltpu.SMEM(lengths.shape, jnp.int32),
            pltpu.SMEM(route.shape, jnp.int32),
            pltpu.VMEM((2, req, slots, width), jnp.bfloat16),
            pltpu.VMEM(early.shape, early.dtype),
            pltpu.VMEM(late.shape, late.dtype),
            pltpu.VMEM(level.shape, level.dtype),
            pltpu.VMEM(total.shape, total.dtype),
            pltpu.VMEM((n_grp,) + tokens[0].shape, tokens[0].dtype),
            pltpu.VMEM((total.shape[0], rows), jnp.float32),
            pltpu.SemaphoreType.DMA((4 + n_grp,)),
            pltpu.SemaphoreType.DMA((4,)),
        ],
        input_output_aliases={2: 0, 3: 1, 5: 2},
        compiler_params=pltpu.CompilerParams(vmem_limit_bytes=VMEM_LIMIT),
        cost_estimate=LIGHT,
        name="attend",
    )(lengths, route, out_k, out_v, early, late, level, total, *tokens)


def place(n_seq, first, part, out_k, out_v, sem):
    _, sent = half_of("seq", n_seq)
    _, count, rows, _ = part.shape
    return fetch(
        [
            (part.at[i], out.at[pl.ds(first, count), lanes(sent, rows), :])
            for i, out in enumerate((out_k, out_v))
        ],
        sem,
    )


def merge_kernel(count, relative, size, *refs):
    stats, refs = refs[:count], refs[count:]
    picked_ref, weight_ref, log_ref, decay_ref, out_ref = refs
    heads, req, rows = log_ref.shape
    width = picked_ref.shape[1]
    seq = lax.axis_index("seq")
    places = [lax.rem(seq + count - k, count) if relative else jnp.int32(k) for k in range(count)]
    tops, masses, totals, accs = [
        [ref[p * req : (p + 1) * req, :] for ref in stats] for p in range(4)
    ]

    def later(place):
        total = jnp.zeros_like(totals[0])
        for k in range(count):
            total = total + jnp.where(places[k] > place, totals[k], 0.0)
        return total

    tops = [tops[k] + later(places[k]) for k in range(count)]
    top = functools.reduce(jnp.maximum, tops)
    scales = [jnp.exp(t - top) for t in tops]
    mass = sum(s * x for s, x in zip(scales, masses))
    acc = sum(s * x for s, x in zip(scales, accs))
    query, key, value, gate = [picked_ref[p * req : (p + 1) * req, :] for p in range(4)]
    one, two = iota((width, width), 0), iota((width, width), 1)
    same = (one // size == two // size).astype(jnp.float32).astype(jnp.bfloat16)
    own = split_dot(query * key, same) * (size**-0.5)
    past = top + gate
    joint = jnp.maximum(past, own)
    scale, self_weight = jnp.exp(past - joint), jnp.exp(own - joint)
    attended = (scale * acc + self_weight * value) / (scale * mass + self_weight)
    beyond = later(seq)
    for h in range(heads):
        decay_ref[h] = jnp.exp(log_ref[h] + beyond[:, h * size : h * size + 1])
    out_ref[...] = dot(attended.astype(jnp.bfloat16), weight_ref[...])


def merge_part(stats, relative, picked, out_weight, logs, size):
    req = logs.shape[1]
    vmem = pl.BlockSpec(memory_space=pltpu.VMEM)
    return pl.pallas_call(
        functools.partial(merge_kernel, len(stats), relative, size),
        out_shape=(
            jax.ShapeDtypeStruct(logs.shape, jnp.float32),
            jax.ShapeDtypeStruct((req, out_weight.shape[1]), jnp.float32),
        ),
        in_specs=[vmem] * (len(stats) + 3),
        out_specs=(vmem, vmem),
        compiler_params=pltpu.CompilerParams(vmem_limit_bytes=SMALL_LIMIT),
        cost_estimate=MERGE,
        name="merge_and_project",
    )(*stats, picked, out_weight, logs)


def sum_kernel(count, *refs):
    parts, out = refs[:count], refs[count]
    me = lax.axis_index("head")
    total = jnp.zeros(out.shape, jnp.float32)
    for place in range(count):
        for k in range(count):
            total = total + jnp.where(lax.rem(me + count - k, count) == place, parts[k][...], 0.0)
    out[...] = total.astype(out.dtype)


def sum_part(parts):
    return pl.pallas_call(
        functools.partial(sum_kernel, len(parts)),
        out_shape=jax.ShapeDtypeStruct(parts[0].shape, jnp.bfloat16),
        in_specs=[pl.BlockSpec(memory_space=pltpu.VMEM)] * len(parts),
        out_specs=pl.BlockSpec(memory_space=pltpu.VMEM),
        compiler_params=pltpu.CompilerParams(vmem_limit_bytes=SMALL_LIMIT),
        cost_estimate=LIGHT,
        name="sum_heads",
    )(*parts)


def place_kernel(n_seq, first, part, old_k, old_v, out_k, out_v, sem):
    for copy in place(n_seq, first, part, out_k, out_v, sem):
        copy.wait()


def place_part(n_seq, first, part, out_k, out_v):
    hbm = pl.BlockSpec(memory_space=pl.ANY)
    vmem = pl.BlockSpec(memory_space=pltpu.VMEM)
    shape = jax.ShapeDtypeStruct(out_k.shape, out_k.dtype)
    return pl.pallas_call(
        functools.partial(place_kernel, n_seq, first),
        out_shape=(shape, shape),
        in_specs=[vmem, hbm, hbm],
        out_specs=(hbm, hbm),
        scratch_shapes=[pltpu.SemaphoreType.DMA((2,))],
        input_output_aliases={1: 0, 2: 1},
        compiler_params=pltpu.CompilerParams(vmem_limit_bytes=VMEM_LIMIT),
        cost_estimate=LIGHT,
        name="place_received",
    )(part, out_k, out_v)


def place_late_kernel(n_seq, first, part, len_hbm, old_k, old_v, out_k, out_v, lengths, sem_s, sem):
    _, sent = half_of("seq", n_seq)
    (load,) = fetch([(len_hbm, lengths)], sem_s)
    load.wait()
    req, rows, _ = out_k.shape
    slots = rows // 2
    most = slots // SLOTS
    seq = lax.axis_index("seq")
    if n_seq == 2:
        start = (1 - seq) * (4 * slots) + seq * (2 * slots)
    else:
        start = seq * (4 * slots) + sent * (2 * slots)
    ahead, _ = offsets(lengths, first, start, most)
    for phase in ("start", "wait"):
        for j, skip in enumerate(ahead):
            live = live_blocks(lengths, first + j, start, most)
            for blocks in range(1, most + 1):
                size = blocks * SLOTS

                @pl.when(live == blocks)
                def _(j=j, skip=skip, size=size):
                    for i, out in enumerate((out_k, out_v)):
                        source = pl.ds(pl.multiple_of(skip * SLOTS, SLOTS), size)
                        target = pl.ds(pl.multiple_of(sent * slots, SLOTS), size)
                        copy = pltpu.make_async_copy(
                            part.at[i, source, :], out.at[first + j, target, :], sem.at[i, j]
                        )
                        getattr(copy, phase)()


def place_late_part(n_seq, first, part, lengths, out_k, out_v):
    hbm = pl.BlockSpec(memory_space=pl.ANY)
    vmem = pl.BlockSpec(memory_space=pltpu.VMEM)
    shape = jax.ShapeDtypeStruct(out_k.shape, out_k.dtype)
    return pl.pallas_call(
        functools.partial(place_late_kernel, n_seq, first),
        out_shape=(shape, shape),
        in_specs=[vmem, hbm, hbm, hbm],
        out_specs=(hbm, hbm),
        scratch_shapes=[
            pltpu.SMEM(lengths.shape, jnp.int32),
            pltpu.SemaphoreType.DMA((1,)),
            pltpu.SemaphoreType.DMA((2, lengths.shape[0] - first)),
        ],
        input_output_aliases={2: 0, 3: 1},
        compiler_params=pltpu.CompilerParams(vmem_limit_bytes=VMEM_LIMIT),
        cost_estimate=LIGHT,
        name="place_live",
    )(part, lengths, out_k, out_v)


def others(value, axis):
    count = lax.axis_size(axis)
    return [value] + [
        lax.ppermute(value, axis, [(i, (i + k) % count) for i in range(count)])
        for k in range(1, count)
    ]


def swap(value, n_seq):
    return lax.ppermute(value, "seq", [(0, 1), (1, 0)]) if n_seq == 2 else value


def shards(
    keys, values, log_forget, keep, merge_weight, lengths, route, fresh, new_forget, out_weight
):
    req, pos, width = keys.shape
    heads = log_forget.shape[1]
    size = width // heads
    n_seq, n_grp = lax.axis_size("seq"), lax.axis_size("grp")
    early, packed, choice = first_part(
        n_seq,
        FIRST,
        lengths,
        keep,
        merge_weight,
        fresh.reshape(3 * req, width),
        new_forget,
        keys,
        values,
    )
    exchange = functools.partial(swap, n_seq=n_seq)
    first_received = exchange(early)
    tokens = others(packed, "grp")
    out_k, out_v, late, logs, level, total = own_part(
        n_seq,
        FIRST,
        lengths,
        keep,
        merge_weight,
        log_forget.transpose(1, 0, 2),
        keys,
        values,
        packed,
    )
    out_k, out_v, late, stats, picked = attend_part(
        n_seq, n_grp, heads, lengths, route, out_k, out_v, early, late, level, total, tokens
    )

    def finish(rows, late, stats, picked, out_weight, logs, lengths, out_k, out_v):
        if n_seq == 2:
            all_stats = others(stats, "seq")
        else:
            gathered = lax.all_gather(stats, "seq")
            all_stats = [gathered[i] for i in range(n_seq)]
        received = exchange(late[:, :rows])
        decay, partial = merge_part(all_stats, n_seq == 2, picked, out_weight, logs, size)
        layer_out = sum_part(others(partial, "head"))
        out_k, out_v = place_late_part(n_seq, FIRST, received, lengths, out_k, out_v)
        return decay, layer_out, out_k, out_v

    operands = (late, stats, picked, out_weight, logs, lengths, out_k, out_v)
    if n_seq == 2:
        step = STEP * SLOTS
        branches = [
            functools.partial(finish, rows) for rows in range(step, late.shape[1] + 1, step)
        ]
        decay, layer_out, out_k, out_v = lax.switch(choice[0], branches, *operands)
    else:
        decay, layer_out, out_k, out_v = finish(late.shape[1], *operands)
    out_k, out_v = place_part(n_seq, 0, first_received, out_k, out_v)
    if n_seq != 2:
        out_k, out_v = (
            lax.all_to_all(x, "seq", split_axis=1, concat_axis=1, tiled=True) for x in (out_k, out_v)
        )
    return out_k, out_v, decay.transpose(1, 0, 2), layer_out


def solution(mesh):
    return jax.shard_map(
        shards,
        mesh=mesh,
        in_specs=(
            P("grp", "seq", "head"),
            P("grp", "seq", "head"),
            P("grp", "head", "seq"),
            P("grp", "seq"),
            P("grp", "seq"),
            P("grp"),
            P("grp"),
            P(None, "grp", "head"),
            P("grp", "head"),
            P("head", "seq"),
        ),
        out_specs=(
            P("grp", "seq", "head"),
            P("grp", "seq", "head"),
            P("grp", "head", "seq"),
            P("grp", "seq"),
        ),
        check_vma=False,
    )
```

```python
import functools

import jax
import jax.numpy as jnp
from jax import lax
from jax.experimental import pallas as pl
from jax.experimental.pallas import tpu as pltpu
from jax.sharding import PartitionSpec as P

BLOCK = 64
SLOTS = 32
LANES = 128
BLOCK_LOG = BLOCK.bit_length() - 1
SLOT_LOG = SLOTS.bit_length() - 1
EMPTY_LOG = -10000.0
FIRST = 4
STEP = 2
VMEM_LIMIT = 63 * 1024 * 1024
LAST_LIMIT = 60 * 1024 * 1024
SMALL_LIMIT = 8 * 1024 * 1024


LIGHT = pl.CostEstimate(flops=1, bytes_accessed=1, transcendentals=0)
MERGE = pl.CostEstimate(flops=1 << 36, bytes_accessed=1, transcendentals=0)


def dot(a, b):
    return lax.dot_general(a, b, (((1,), (0,)), ((), ())), preferred_element_type=jnp.float32)


def dot_nt(a, b):
    return lax.dot_general(a, b, (((1,), (1,)), ((), ())), preferred_element_type=jnp.float32)


def iota(shape, dim):
    return lax.broadcasted_iota(jnp.int32, shape, dim)


def three(x):
    hi = x.astype(jnp.bfloat16).astype(jnp.float32)
    rest = x - hi
    mid = rest.astype(jnp.bfloat16).astype(jnp.float32)
    return hi, mid, rest - mid


def split_dot(x, ones):
    rows = x.shape[0]
    parts = dot(jnp.concatenate(three(x), axis=0).astype(jnp.bfloat16), ones)
    return parts[:rows] + parts[rows : 2 * rows] + parts[2 * rows :]


def half_of(axis, count):
    own = lax.axis_index(axis) if count == 2 else jnp.int32(0)
    return own, 1 - own


def by_row(ref, row):
    picked = jnp.zeros_like(row)
    for r in range(ref.shape[0]):
        picked = jnp.where(row == r, ref[r], picked)
    return picked


def live_blocks(lengths, r, start, most):
    return jnp.clip((lengths[r] - start) >> BLOCK_LOG, 0, most)


def offsets(lengths, first, start, most):
    total = jnp.int32(0)
    ahead = []
    for r in range(first, lengths.shape[0]):
        ahead.append(total)
        total = total + live_blocks(lengths, r, start, most)
    return ahead, total


def plan(keep, weight, start, len_ref):
    rows, width = keep.shape
    one, two = iota((width, width), 0), iota((width, width), 1)
    same = (one ^ two) < BLOCK
    upto = (same & (one <= two)).astype(jnp.float32).astype(jnp.bfloat16)
    block = same.astype(jnp.float32).astype(jnp.bfloat16)
    kept = keep == 1
    rank = dot(keep.astype(jnp.float32).astype(jnp.bfloat16), upto) - 1.0
    weighted = jnp.where(kept, 0.0, weight)
    share = (weighted / split_dot(weighted, block)).astype(jnp.bfloat16).astype(jnp.float32)
    lane, row = iota((rows, width), 1), iota((rows, width), 0)
    slot = jnp.where(kept, rank.astype(jnp.int32), SLOTS - 1) + (lane >> BLOCK_LOG) * SLOTS
    slot = jnp.where(start + lane < by_row(len_ref, row), slot, -1)
    return slot, jnp.where(kept, 1.0, share)


def select(slot, factor, r):
    width = slot.shape[1]
    shape = (width // 2, width)
    hit = iota(shape, 0) == slot[r : r + 1, :]
    return jnp.where(hit, jnp.broadcast_to(factor[r : r + 1, :], shape), 0.0).astype(jnp.bfloat16)


def lanes(half, width):
    return pl.ds(pl.multiple_of(half * width, width), width)


def fetch(pairs, sem):
    copies = [pltpu.make_async_copy(src, dst, sem.at[i]) for i, (src, dst) in enumerate(pairs)]
    for copy in copies:
        copy.start()
    return copies


def first_kernel(n_seq, len_hbm, keep_hbm, weight_hbm, fresh_hbm, gate_hbm, keys, values, *rest):
    out, packed, size_ref, lengths, keep, weight, fresh, gates, raw, rows = rest[:10]
    sem_s, sem_r, sem_o = rest[10:]
    _, sent = half_of("seq", n_seq)
    width = raw.shape[2]
    count = raw.shape[1]
    small = fetch(
        [
            (len_hbm, lengths),
            (keep_hbm.at[:, lanes(sent, width)], keep),
            (weight_hbm.at[:, lanes(sent, width)], weight),
            (fresh_hbm, fresh),
            (gate_hbm, gates),
        ],
        sem_s,
    )
    slabs = fetch(
        [
            (source.at[j, lanes(sent, width), :], raw.at[i, j])
            for j in range(count)
            for i, source in enumerate((keys, values))
        ],
        sem_r,
    )
    for copy in small:
        copy.wait()
    start = lax.axis_index("seq") * (2 * width) + sent * width
    slot, factor = plan(keep[...], weight[...], start, lengths)
    most = width // BLOCK
    _, total = offsets(lengths, count, width, most)
    sizes = most * (lengths.shape[0] - count) // STEP
    size_ref[0] = jnp.clip((total - 1) >> (STEP.bit_length() - 1), 0, sizes - 1)

    new, gate = fresh[...].astype(jnp.float32), gates[...].astype(jnp.float32)
    req, heads = gate.shape
    lane = iota((req, new.shape[1]), 1)
    size = new.shape[1] // heads
    spread = jnp.zeros((req, new.shape[1]), jnp.float32)
    for h in range(heads):
        inside = (lane >= h * size) & (lane < (h + 1) * size)
        spread = jnp.where(inside, gate[:, h : h + 1], spread)
    packed[...] = jnp.concatenate([new, spread], axis=0).astype(jnp.bfloat16)

    stores = []
    for j in range(count):
        chosen = select(slot, factor, j)
        for i in range(2):
            slabs[j * 2 + i].wait()
            rows[i, j] = dot(chosen, raw[i, j]).astype(jnp.bfloat16)
        stores.append(pltpu.make_async_copy(rows.at[:, j], out.at[:, j], sem_o.at[j]))
        stores[-1].start()
    for copy in stores:
        copy.wait()


def first_part(n_seq, count, lengths, keep, weight, fresh, gates, keys, values):
    req, pos, width = keys.shape
    half = pos // 2
    hbm = pl.BlockSpec(memory_space=pl.ANY)
    vmem = pl.BlockSpec(memory_space=pltpu.VMEM)
    rows = (2, count, half // 2, width)
    return pl.pallas_call(
        functools.partial(first_kernel, n_seq),
        out_shape=(
            jax.ShapeDtypeStruct(rows, jnp.bfloat16),
            jax.ShapeDtypeStruct((fresh.shape[0] + req, width), jnp.bfloat16),
            jax.ShapeDtypeStruct((1,), jnp.int32),
        ),
        in_specs=[hbm] * 7,
        out_specs=(hbm, vmem, pl.BlockSpec(memory_space=pltpu.SMEM)),
        scratch_shapes=[
            pltpu.SMEM(lengths.shape, jnp.int32),
            pltpu.VMEM((req, half), jnp.int32),
            pltpu.VMEM((req, half), jnp.float32),
            pltpu.VMEM(fresh.shape, fresh.dtype),
            pltpu.VMEM(gates.shape, gates.dtype),
            pltpu.VMEM((2, count, half, width), jnp.bfloat16),
            pltpu.VMEM(rows, jnp.bfloat16),
            pltpu.SemaphoreType.DMA((5,)),
            pltpu.SemaphoreType.DMA((2 * count,)),
            pltpu.SemaphoreType.DMA((count,)),
        ],
        compiler_params=pltpu.CompilerParams(vmem_limit_bytes=VMEM_LIMIT),
        cost_estimate=LIGHT,
        name="compact_first_sent",
    )(lengths, keep, weight, fresh, gates, keys, values)


def own_kernel(
    n_seq, first, len_hbm, keep_hbm, weight_hbm, forget_hbm, keys, values, packed_hbm, *rest
):
    out_k, out_v, chunk, log_ref, level_ref, total_ref = rest[:6]
    lengths, keep, weight, gates, raw, late, forget, rows, rows_late, zeros = rest[6:16]
    sem_s, sem_l, sem_r, sem_c, sem_o, sem_z = rest[16:]
    own, sent = half_of("seq", n_seq)
    seq = lax.axis_index("seq")
    heads, req, pos = forget_hbm.shape
    half = pos // 2
    slots = half // 2
    pad = forget.shape[1] // req
    small = fetch(
        [(len_hbm, lengths), (keep_hbm, keep), (weight_hbm, weight), (forget_hbm, gates)], sem_s
    )
    both = ((0, keys), (1, values))
    late_slabs = fetch(
        [
            (source.at[r, lanes(sent, half), :], late.at[i, r - first])
            for r in range(first, req)
            for i, source in both
        ],
        sem_l,
    )
    slabs = fetch(
        [
            (source.at[r, lanes(own, half), :], raw.at[i, r])
            for r in range(req)
            for i, source in both
        ],
        sem_r,
    )
    zeros[...] = jnp.zeros_like(zeros)
    stores = fetch(
        [
            (zeros, out.at[r, lanes(sent, slots), :])
            for r in range(first, req)
            for out in (out_k, out_v)
        ],
        sem_z,
    )
    for copy in small:
        copy.wait()
    ahead, _ = offsets(lengths, first, seq * pos + sent * half, half // BLOCK)

    forget[...] = jnp.zeros_like(forget)
    live = seq * pos + iota((req, pos), 1) < by_row(lengths, iota((req, pos), 0))
    for h in range(heads):
        gate = jnp.where(live, gates[h], 0.0)
        for c in range(pos // LANES):
            forget[c, pl.ds(h, req, stride=pad), :] = gate[:, c * LANES : (c + 1) * LANES]
    flat = jnp.concatenate([forget[c] for c in range(pos // LANES)], axis=1)
    total_ref[...] = jnp.broadcast_to(jnp.sum(flat, axis=1, keepdims=True), total_ref.shape)
    one, two = iota((half, half), 0), iota((half, half), 1)
    after = (((one ^ two) < BLOCK) & (one > two)).astype(jnp.float32).astype(jnp.bfloat16)
    ends = iota((pos, slots), 1) >> SLOT_LOG
    begins = iota((pos, slots), 0) >> BLOCK_LOG
    last = iota((req * pad, slots), 1) & (SLOTS - 1) == SLOTS - 1

    for i, h in enumerate((own, sent)):
        slot, factor = plan(
            keep[:, lanes(h, half)], weight[:, lanes(h, half)], seq * pos + h * half, lengths
        )
        near = half // LANES
        inner = split_dot(
            jnp.concatenate([forget[h * near + c] for c in range(near)], axis=1), after
        )
        beyond = split_dot(
            flat, (begins > ends + h * (half // BLOCK)).astype(jnp.float32).astype(jnp.bfloat16)
        )
        spread = jnp.exp(inner)
        high = spread.astype(jnp.bfloat16).astype(jnp.float32)
        planes = three(inner) + (high, spread - high, jnp.ones_like(inner))
        found = []
        for r in range(req):
            chosen = select(slot, factor, r)
            stack = jnp.concatenate([x[r * pad : (r + 1) * pad] for x in planes], axis=0)
            found.append(dot_nt(stack.astype(jnp.bfloat16), chosen))
            if i == 0:
                for k, out in enumerate((out_k, out_v)):
                    slabs[2 * r + k].wait()
                    rows[k, r] = dot(chosen, raw[k, r]).astype(jnp.bfloat16)
                    stores.append(
                        pltpu.make_async_copy(
                            rows.at[k, r], out.at[r, lanes(own, slots), :], sem_o.at[2 * r + k]
                        )
                    )
                    stores[-1].start()
            elif r >= first:
                at = pl.ds(pl.multiple_of(ahead[r - first] * SLOTS, SLOTS), slots)
                for k in range(2):
                    late_slabs[2 * (r - first) + k].wait()
                    rows_late[k, at, :] = dot(chosen, late[k, r - first]).astype(jnp.bfloat16)
        if i == 1:
            stores += fetch([(rows_late, chunk)], sem_c)
        at = [
            jnp.concatenate([x[p * pad : (p + 1) * pad] for x in found], axis=0) for p in range(6)
        ]
        filled = at[5] > 0.5
        kept = at[0] + at[1] + at[2]
        merged = jnp.log(jnp.where(filled, at[3] + at[4], 1.0))
        level_ref[i] = jnp.where(filled, jnp.where(last, merged, kept) + beyond, EMPTY_LOG)
        for k in range(heads):
            log_ref[k, :, lanes(h, slots)] = level_ref[i, pl.ds(k, req, stride=pad), :]
    for copy in stores:
        copy.wait()


def own_part(n_seq, first, lengths, keep, weight, forget, keys, values, packed):
    req, pos, width = keys.shape
    heads = forget.shape[0]
    half, slots, pad = pos // 2, pos // 4, -(-heads // 8) * 8
    late = req - first
    hbm = pl.BlockSpec(memory_space=pl.ANY)
    vmem = pl.BlockSpec(memory_space=pltpu.VMEM)
    whole = jax.ShapeDtypeStruct((req, 2 * slots, width), jnp.bfloat16)
    return pl.pallas_call(
        functools.partial(own_kernel, n_seq, first),
        out_shape=(
            whole,
            whole,
            jax.ShapeDtypeStruct((2, late * slots, width), jnp.bfloat16),
            jax.ShapeDtypeStruct((heads, req, 2 * slots), jnp.float32),
            jax.ShapeDtypeStruct((2, req * pad, slots), jnp.float32),
            jax.ShapeDtypeStruct((req * pad, LANES), jnp.float32),
        ),
        in_specs=[hbm] * 7,
        out_specs=(hbm, hbm, hbm, vmem, vmem, vmem),
        scratch_shapes=[
            pltpu.SMEM(lengths.shape, jnp.int32),
            pltpu.VMEM(keep.shape, keep.dtype),
            pltpu.VMEM(weight.shape, weight.dtype),
            pltpu.VMEM(forget.shape, forget.dtype),
            pltpu.VMEM((2, req, half, width), jnp.bfloat16),
            pltpu.VMEM((2, late, half, width), jnp.bfloat16),
            pltpu.VMEM((pos // LANES, req * pad, LANES), jnp.float32),
            pltpu.VMEM((2, req, slots, width), jnp.bfloat16),
            pltpu.VMEM((2, late * slots, width), jnp.bfloat16),
            pltpu.VMEM((slots, width), jnp.bfloat16),
            pltpu.SemaphoreType.DMA((4,)),
            pltpu.SemaphoreType.DMA((2 * late,)),
            pltpu.SemaphoreType.DMA((2 * req,)),
            pltpu.SemaphoreType.DMA((1,)),
            pltpu.SemaphoreType.DMA((2 * req,)),
            pltpu.SemaphoreType.DMA((2 * late,)),
        ],
        compiler_params=pltpu.CompilerParams(vmem_limit_bytes=VMEM_LIMIT),
        cost_estimate=LIGHT,
        name="compact_own",
    )(lengths, keep, weight, forget, keys, values, packed)


def attend_kernel(n_seq, n_grp, heads, first, *refs):
    len_hbm, route_hbm, out_k, out_v, early, late, level_hbm, total_hbm = refs[:8]
    tokens, rest = refs[8 : 8 + n_grp], refs[8 + n_grp :]
    _, _, _, stats_ref, picked_ref = rest[:5]
    lengths, route, own_rows, sent_rows, late_rows, level, total, fresh, scores = rest[5:14]
    sem_s, sem_r = rest[14:]
    own, sent = half_of("seq", n_seq)
    kinds, width = picked_ref.shape
    req = kinds // 4
    size = width // heads
    slots = own_rows.shape[2]
    pad = total.shape[0] // req
    small = fetch(
        [(len_hbm, lengths), (route_hbm, route), (level_hbm, level), (total_hbm, total)]
        + [(x, fresh.at[k]) for k, x in enumerate(tokens)],
        sem_s,
    )
    slabs = fetch(
        [
            (out_k.at[:, lanes(own, slots), :], own_rows.at[0]),
            (early, sent_rows),
            (late, late_rows),
            (out_v.at[:, lanes(own, slots), :], own_rows.at[1]),
        ],
        sem_r,
    )
    for copy in small:
        copy.wait()
    start = lax.axis_index("seq") * (4 * slots) + sent * (2 * slots)
    ahead, _ = offsets(lengths, first, start, slots // SLOTS)

    def sent_part(i, r):
        if r < first:
            return sent_rows[i, r]
        at = pl.multiple_of(ahead[r - first] * SLOTS, SLOTS)
        return late_rows[i, pl.ds(at, slots), :]

    shape = (kinds, kinds)
    to, frm = iota(shape, 0), iota(shape, 1)
    wanted = by_row(route, to % req)
    me = lax.axis_index("grp")
    picked = jnp.zeros((kinds, width), jnp.float32)
    for k in range(n_grp):
        source = lax.rem(me + n_grp - k, n_grp)
        hit = (to // req == frm // req) & (wanted == source * req + frm % req)
        picked = picked + dot(hit.astype(jnp.float32).astype(jnp.bfloat16), fresh[k])
    picked_ref[...] = picked
    for copy in slabs:
        copy.wait()

    lane, row = iota((pad, width), 1), iota((pad, width), 0)
    mine = (lane >= row * size) & (lane < (row + 1) * size)
    for r in range(req):
        query = jnp.where(mine, picked[r : r + 1, :], 0.0).astype(jnp.bfloat16)
        here = slice(r * pad, (r + 1) * pad)
        scores[here, :slots] = dot_nt(query, own_rows[0, r])
        scores[here, slots:] = dot_nt(query, sent_part(0, r))
    logit = scores[...] * (size**-0.5) + jnp.concatenate([level[0], level[1]], axis=1)
    top = jnp.max(logit, axis=1, keepdims=True)
    weights = jnp.exp(logit - top).astype(jnp.bfloat16).astype(jnp.float32)
    mass = jnp.sum(weights, axis=1, keepdims=True)

    def spread_out(column, r):
        return jnp.sum(
            jnp.where(mine, column[r * pad : (r + 1) * pad], 0.0), axis=0, keepdims=True
        )

    for r in range(req):
        w = weights[r * pad : (r + 1) * pad].astype(jnp.bfloat16)
        acc = dot(w[:, :slots], own_rows[1, r]) + dot(w[:, slots:], sent_part(1, r))
        acc = jnp.sum(jnp.where(mine, acc, 0.0), axis=0, keepdims=True)
        for p, x in enumerate((top, mass, total[:, :1])):
            stats_ref[p * req + r : p * req + r + 1, :] = spread_out(x, r)
        stats_ref[3 * req + r : 3 * req + r + 1, :] = acc


def attend_part(n_seq, n_grp, heads, lengths, route, out_k, out_v, early, late, level, total, tokens):
    req, rows, width = out_k.shape
    slots, first = rows // 2, early.shape[1]
    hbm = pl.BlockSpec(memory_space=pl.ANY)
    vmem = pl.BlockSpec(memory_space=pltpu.VMEM)
    whole = jax.ShapeDtypeStruct(out_k.shape, out_k.dtype)
    small = jax.ShapeDtypeStruct((4 * req, width), jnp.float32)
    return pl.pallas_call(
        functools.partial(attend_kernel, n_seq, n_grp, heads, first),
        out_shape=(whole, whole, jax.ShapeDtypeStruct(late.shape, late.dtype), small, small),
        in_specs=[hbm] * (8 + n_grp),
        out_specs=(hbm, hbm, hbm, vmem, vmem),
        scratch_shapes=[
            pltpu.SMEM(lengths.shape, jnp.int32),
            pltpu.SMEM(route.shape, jnp.int32),
            pltpu.VMEM((2, req, slots, width), jnp.bfloat16),
            pltpu.VMEM(early.shape, early.dtype),
            pltpu.VMEM(late.shape, late.dtype),
            pltpu.VMEM(level.shape, level.dtype),
            pltpu.VMEM(total.shape, total.dtype),
            pltpu.VMEM((n_grp,) + tokens[0].shape, tokens[0].dtype),
            pltpu.VMEM((total.shape[0], rows), jnp.float32),
            pltpu.SemaphoreType.DMA((4 + n_grp,)),
            pltpu.SemaphoreType.DMA((4,)),
        ],
        input_output_aliases={2: 0, 3: 1, 5: 2},
        compiler_params=pltpu.CompilerParams(vmem_limit_bytes=VMEM_LIMIT),
        cost_estimate=LIGHT,
        name="attend",
    )(lengths, route, out_k, out_v, early, late, level, total, *tokens)


def place(n_seq, first, part, out_k, out_v, sem):
    _, sent = half_of("seq", n_seq)
    _, count, rows, _ = part.shape
    return fetch(
        [
            (part.at[i], out.at[pl.ds(first, count), lanes(sent, rows), :])
            for i, out in enumerate((out_k, out_v))
        ],
        sem,
    )


def merge_kernel(count, relative, size, *refs):
    stats, refs = refs[:count], refs[count:]
    picked_ref, weight_ref, log_ref, decay_ref, out_ref = refs
    heads, req, rows = log_ref.shape
    width = picked_ref.shape[1]
    seq = lax.axis_index("seq")
    places = [lax.rem(seq + count - k, count) if relative else jnp.int32(k) for k in range(count)]
    tops, masses, totals, accs = [
        [ref[p * req : (p + 1) * req, :] for ref in stats] for p in range(4)
    ]

    def later(place):
        total = jnp.zeros_like(totals[0])
        for k in range(count):
            total = total + jnp.where(places[k] > place, totals[k], 0.0)
        return total

    tops = [tops[k] + later(places[k]) for k in range(count)]
    top = functools.reduce(jnp.maximum, tops)
    scales = [jnp.exp(t - top) for t in tops]
    mass = sum(s * x for s, x in zip(scales, masses))
    acc = sum(s * x for s, x in zip(scales, accs))
    query, key, value, gate = [picked_ref[p * req : (p + 1) * req, :] for p in range(4)]
    one, two = iota((width, width), 0), iota((width, width), 1)
    same = (one // size == two // size).astype(jnp.float32).astype(jnp.bfloat16)
    own = split_dot(query * key, same) * (size**-0.5)
    past = top + gate
    joint = jnp.maximum(past, own)
    scale, self_weight = jnp.exp(past - joint), jnp.exp(own - joint)
    attended = (scale * acc + self_weight * value) / (scale * mass + self_weight)
    beyond = later(seq)
    for h in range(heads):
        decay_ref[h] = jnp.exp(log_ref[h] + beyond[:, h * size : h * size + 1])
    out_ref[...] = dot(attended.astype(jnp.bfloat16), weight_ref[...])


def merge_part(stats, relative, picked, out_weight, logs, size):
    req = logs.shape[1]
    vmem = pl.BlockSpec(memory_space=pltpu.VMEM)
    return pl.pallas_call(
        functools.partial(merge_kernel, len(stats), relative, size),
        out_shape=(
            jax.ShapeDtypeStruct(logs.shape, jnp.float32),
            jax.ShapeDtypeStruct((req, out_weight.shape[1]), jnp.float32),
        ),
        in_specs=[vmem] * (len(stats) + 3),
        out_specs=(vmem, vmem),
        compiler_params=pltpu.CompilerParams(vmem_limit_bytes=SMALL_LIMIT),
        cost_estimate=MERGE,
        name="merge_and_project",
    )(*stats, picked, out_weight, logs)


def sum_kernel(count, *refs):
    parts, out = refs[:count], refs[-1]
    me = lax.axis_index("head")
    total = jnp.zeros(out.shape, jnp.float32)
    for place in range(count):
        for k in range(count):
            total = total + jnp.where(lax.rem(me + count - k, count) == place, parts[k][...], 0.0)
    out[...] = total.astype(out.dtype)


def sum_part(parts, placed):
    return pl.pallas_call(
        functools.partial(sum_kernel, len(parts)),
        out_shape=jax.ShapeDtypeStruct(parts[0].shape, jnp.bfloat16),
        in_specs=[pl.BlockSpec(memory_space=pltpu.VMEM)] * (len(parts) + 1),
        out_specs=pl.BlockSpec(memory_space=pltpu.VMEM),
        compiler_params=pltpu.CompilerParams(vmem_limit_bytes=SMALL_LIMIT),
        cost_estimate=LIGHT,
        name="sum_heads",
    )(*parts, placed)


def place_kernel(n_seq, first, part, old_k, old_v, out_k, out_v, placed_ref, sem):
    copies = place(n_seq, first, part, out_k, out_v, sem)
    placed_ref[...] = jnp.zeros_like(placed_ref)
    for copy in copies:
        copy.wait()


def place_part(n_seq, first, part, out_k, out_v):
    hbm = pl.BlockSpec(memory_space=pl.ANY)
    vmem = pl.BlockSpec(memory_space=pltpu.VMEM)
    shape = jax.ShapeDtypeStruct(out_k.shape, out_k.dtype)
    return pl.pallas_call(
        functools.partial(place_kernel, n_seq, first),
        out_shape=(shape, shape, jax.ShapeDtypeStruct((8, LANES), jnp.float32)),
        in_specs=[vmem, hbm, hbm],
        out_specs=(hbm, hbm, vmem),
        scratch_shapes=[pltpu.SemaphoreType.DMA((2,))],
        input_output_aliases={1: 0, 2: 1},
        compiler_params=pltpu.CompilerParams(vmem_limit_bytes=LAST_LIMIT),
        cost_estimate=LIGHT,
        name="place_received",
    )(part, out_k, out_v)


def place_late_kernel(n_seq, first, part, len_hbm, old_k, old_v, out_k, out_v, lengths, sem_s, sem):
    _, sent = half_of("seq", n_seq)
    (load,) = fetch([(len_hbm, lengths)], sem_s)
    load.wait()
    req, rows, _ = out_k.shape
    slots = rows // 2
    most = slots // SLOTS
    seq = lax.axis_index("seq")
    if n_seq == 2:
        start = (1 - seq) * (4 * slots) + seq * (2 * slots)
    else:
        start = seq * (4 * slots) + sent * (2 * slots)
    ahead, _ = offsets(lengths, first, start, most)
    for phase in ("start", "wait"):
        for j, skip in enumerate(ahead):
            live = live_blocks(lengths, first + j, start, most)
            for blocks in range(1, most + 1):
                size = blocks * SLOTS

                @pl.when(live == blocks)
                def _(j=j, skip=skip, size=size):
                    for i, out in enumerate((out_k, out_v)):
                        source = pl.ds(pl.multiple_of(skip * SLOTS, SLOTS), size)
                        target = pl.ds(pl.multiple_of(sent * slots, SLOTS), size)
                        copy = pltpu.make_async_copy(
                            part.at[i, source, :], out.at[first + j, target, :], sem.at[i, j]
                        )
                        getattr(copy, phase)()


def place_late_part(n_seq, first, part, lengths, out_k, out_v):
    hbm = pl.BlockSpec(memory_space=pl.ANY)
    vmem = pl.BlockSpec(memory_space=pltpu.VMEM)
    shape = jax.ShapeDtypeStruct(out_k.shape, out_k.dtype)
    return pl.pallas_call(
        functools.partial(place_late_kernel, n_seq, first),
        out_shape=(shape, shape),
        in_specs=[vmem, hbm, hbm, hbm],
        out_specs=(hbm, hbm),
        scratch_shapes=[
            pltpu.SMEM(lengths.shape, jnp.int32),
            pltpu.SemaphoreType.DMA((1,)),
            pltpu.SemaphoreType.DMA((2, lengths.shape[0] - first)),
        ],
        input_output_aliases={2: 0, 3: 1},
        compiler_params=pltpu.CompilerParams(vmem_limit_bytes=LAST_LIMIT),
        cost_estimate=LIGHT,
        name="place_live",
    )(part, lengths, out_k, out_v)


def others(value, axis):
    count = lax.axis_size(axis)
    return [value] + [
        lax.ppermute(value, axis, [(i, (i + k) % count) for i in range(count)])
        for k in range(1, count)
    ]


def swap(value, n_seq):
    return lax.ppermute(value, "seq", [(0, 1), (1, 0)]) if n_seq == 2 else value


def shards(
    keys, values, log_forget, keep, merge_weight, lengths, route, fresh, new_forget, out_weight
):
    req, pos, width = keys.shape
    heads = log_forget.shape[1]
    size = width // heads
    n_seq, n_grp = lax.axis_size("seq"), lax.axis_size("grp")
    early, packed, choice = first_part(
        n_seq,
        FIRST,
        lengths,
        keep,
        merge_weight,
        fresh.reshape(3 * req, width),
        new_forget,
        keys,
        values,
    )
    exchange = functools.partial(swap, n_seq=n_seq)
    first_received = exchange(early)
    tokens = others(packed, "grp")
    out_k, out_v, late, logs, level, total = own_part(
        n_seq,
        FIRST,
        lengths,
        keep,
        merge_weight,
        log_forget.transpose(1, 0, 2),
        keys,
        values,
        packed,
    )
    out_k, out_v, late, stats, picked = attend_part(
        n_seq, n_grp, heads, lengths, route, out_k, out_v, early, late, level, total, tokens
    )

    def finish(rows, early, late, stats, picked, out_weight, logs, lengths, out_k, out_v):
        if n_seq == 2:
            all_stats = others(stats, "seq")
        else:
            gathered = lax.all_gather(stats, "seq")
            all_stats = [gathered[i] for i in range(n_seq)]
        received = exchange(late[:, :rows])
        decay, partial = merge_part(all_stats, n_seq == 2, picked, out_weight, logs, size)
        out_k, out_v, placed = place_part(n_seq, 0, early, out_k, out_v)
        layer_out = sum_part(others(partial, "head"), placed)
        out_k, out_v = place_late_part(n_seq, FIRST, received, lengths, out_k, out_v)
        return decay, layer_out, out_k, out_v

    operands = (first_received, late, stats, picked, out_weight, logs, lengths, out_k, out_v)
    if n_seq == 2:
        step = STEP * SLOTS
        branches = [
            functools.partial(finish, rows) for rows in range(step, late.shape[1] + 1, step)
        ]
        decay, layer_out, out_k, out_v = lax.switch(choice[0], branches, *operands)
    else:
        decay, layer_out, out_k, out_v = finish(late.shape[1], *operands)
    if n_seq != 2:
        out_k, out_v = (
            lax.all_to_all(x, "seq", split_axis=1, concat_axis=1, tiled=True) for x in (out_k, out_v)
        )
    return out_k, out_v, decay.transpose(1, 0, 2), layer_out


def solution(mesh):
    return jax.shard_map(
        shards,
        mesh=mesh,
        in_specs=(
            P("grp", "seq", "head"),
            P("grp", "seq", "head"),
            P("grp", "head", "seq"),
            P("grp", "seq"),
            P("grp", "seq"),
            P("grp"),
            P("grp"),
            P(None, "grp", "head"),
            P("grp", "head"),
            P("head", "seq"),
        ),
        out_specs=(
            P("grp", "seq", "head"),
            P("grp", "seq", "head"),
            P("grp", "head", "seq"),
            P("grp", "seq"),
        ),
        check_vma=False,
    )
```

```python
import functools

import jax
import jax.numpy as jnp
from jax import lax
from jax.experimental import pallas as pl
from jax.experimental.pallas import tpu as pltpu
from jax.sharding import PartitionSpec as P

BLOCK = 64
SLOTS = 32
LANES = 128
BLOCK_LOG = BLOCK.bit_length() - 1
SLOT_LOG = SLOTS.bit_length() - 1
EMPTY_LOG = -10000.0
FIRST = 4
STEP = 2
VMEM_LIMIT = 16 * 1024 * 1024


LIGHT = pl.CostEstimate(flops=1, bytes_accessed=1, transcendentals=0)
MERGE = pl.CostEstimate(flops=1 << 36, bytes_accessed=1, transcendentals=0)


def dot(a, b):
    return lax.dot_general(a, b, (((1,), (0,)), ((), ())), preferred_element_type=jnp.float32)


def dot_nt(a, b):
    return lax.dot_general(a, b, (((1,), (1,)), ((), ())), preferred_element_type=jnp.float32)


def iota(shape, dim):
    return lax.broadcasted_iota(jnp.int32, shape, dim)


def three(x):
    hi = x.astype(jnp.bfloat16).astype(jnp.float32)
    rest = x - hi
    mid = rest.astype(jnp.bfloat16).astype(jnp.float32)
    return hi, mid, rest - mid


def split_dot(x, ones):
    rows = x.shape[0]
    parts = dot(jnp.concatenate(three(x), axis=0).astype(jnp.bfloat16), ones)
    return parts[:rows] + parts[rows : 2 * rows] + parts[2 * rows :]


def half_of(axis, count):
    own = lax.axis_index(axis) if count == 2 else jnp.int32(0)
    return own, 1 - own


def by_row(ref, row):
    picked = jnp.zeros_like(row)
    for r in range(ref.shape[0]):
        picked = jnp.where(row == r, ref[r], picked)
    return picked


def live_blocks(lengths, r, start, most):
    return jnp.clip((lengths[r] - start) >> BLOCK_LOG, 0, most)


def offsets(lengths, first, start, most):
    total = jnp.int32(0)
    ahead = []
    for r in range(first, lengths.shape[0]):
        ahead.append(total)
        total = total + live_blocks(lengths, r, start, most)
    return ahead, total


def plan(keep, weight, start, len_ref):
    rows, width = keep.shape
    one, two = iota((width, width), 0), iota((width, width), 1)
    same = (one ^ two) < BLOCK
    upto = (same & (one <= two)).astype(jnp.float32).astype(jnp.bfloat16)
    block = same.astype(jnp.float32).astype(jnp.bfloat16)
    kept = keep == 1
    rank = dot(keep.astype(jnp.float32).astype(jnp.bfloat16), upto) - 1.0
    weighted = jnp.where(kept, 0.0, weight)
    share = (weighted / split_dot(weighted, block)).astype(jnp.bfloat16).astype(jnp.float32)
    lane, row = iota((rows, width), 1), iota((rows, width), 0)
    slot = jnp.where(kept, rank.astype(jnp.int32), SLOTS - 1) + (lane >> BLOCK_LOG) * SLOTS
    slot = jnp.where(start + lane < by_row(len_ref, row), slot, -1)
    return slot, jnp.where(kept, 1.0, share)


def select(slot, factor, r):
    width = slot.shape[1]
    shape = (width // 2, width)
    hit = iota(shape, 0) == slot[r : r + 1, :]
    return jnp.where(hit, jnp.broadcast_to(factor[r : r + 1, :], shape), 0.0).astype(jnp.bfloat16)


def lanes(half, width):
    return pl.ds(pl.multiple_of(half * width, width), width)


def far(*arrays):
    return [pltpu.with_memory_space_constraint(x, pltpu.HBM) for x in arrays]


def near(*arrays):
    return [pltpu.with_memory_space_constraint(x, pltpu.VMEM) for x in arrays]


def fetch(pairs, sem):
    copies = [pltpu.make_async_copy(src, dst, sem.at[i]) for i, (src, dst) in enumerate(pairs)]
    for copy in copies:
        copy.start()
    return copies


def first_kernel(n_seq, len_hbm, keep_hbm, weight_hbm, fresh_hbm, gate_hbm, keys, values, *rest):
    out, packed, size_ref, lengths, keep, weight, fresh, gates, raw, sem_s, sem_r = rest
    _, sent = half_of("seq", n_seq)
    width = raw.shape[2]
    count = raw.shape[1]
    small = fetch(
        [
            (len_hbm, lengths),
            (keep_hbm.at[:, lanes(sent, width)], keep),
            (weight_hbm.at[:, lanes(sent, width)], weight),
            (fresh_hbm, fresh),
            (gate_hbm, gates),
        ],
        sem_s,
    )
    slabs = fetch(
        [
            (source.at[j, lanes(sent, width), :], raw.at[i, j])
            for j in range(count)
            for i, source in enumerate((keys, values))
        ],
        sem_r,
    )
    for copy in small:
        copy.wait()
    start = lax.axis_index("seq") * (2 * width) + sent * width
    slot, factor = plan(keep[...], weight[...], start, lengths)
    most = width // BLOCK
    _, total = offsets(lengths, count, width, most)
    sizes = most * (lengths.shape[0] - count) // STEP
    size_ref[0] = jnp.clip((total - 1) >> (STEP.bit_length() - 1), 0, sizes - 1)

    new, gate = fresh[...].astype(jnp.float32), gates[...].astype(jnp.float32)
    req, heads = gate.shape
    lane = iota((req, new.shape[1]), 1)
    size = new.shape[1] // heads
    spread = jnp.zeros((req, new.shape[1]), jnp.float32)
    for h in range(heads):
        inside = (lane >= h * size) & (lane < (h + 1) * size)
        spread = jnp.where(inside, gate[:, h : h + 1], spread)
    packed[...] = jnp.concatenate([new, spread], axis=0).astype(jnp.bfloat16)

    for j in range(count):
        chosen = select(slot, factor, j)
        for i in range(2):
            slabs[j * 2 + i].wait()
            out[i, j] = dot(chosen, raw[i, j]).astype(jnp.bfloat16)


def first_part(n_seq, count, lengths, keep, weight, fresh, gates, keys, values):
    req, pos, width = keys.shape
    half = pos // 2
    hbm = pl.BlockSpec(memory_space=pl.ANY)
    vmem = pl.BlockSpec(memory_space=pltpu.VMEM)
    rows = (2, count, half // 2, width)
    return pl.pallas_call(
        functools.partial(first_kernel, n_seq),
        out_shape=(
            pltpu.VMEM(rows, jnp.bfloat16),
            pltpu.VMEM((fresh.shape[0] + req, width), jnp.bfloat16),
            jax.ShapeDtypeStruct((1,), jnp.int32),
        ),
        in_specs=[hbm] * 7,
        out_specs=(vmem, vmem, pl.BlockSpec(memory_space=pltpu.SMEM)),
        scratch_shapes=[
            pltpu.SMEM(lengths.shape, jnp.int32),
            pltpu.VMEM((req, half), jnp.int32),
            pltpu.VMEM((req, half), jnp.float32),
            pltpu.VMEM(fresh.shape, fresh.dtype),
            pltpu.VMEM(gates.shape, gates.dtype),
            pltpu.VMEM((2, count, half, width), jnp.bfloat16),
            pltpu.SemaphoreType.DMA((5,)),
            pltpu.SemaphoreType.DMA((2 * count,)),
        ],
        compiler_params=pltpu.CompilerParams(vmem_limit_bytes=VMEM_LIMIT),
        cost_estimate=LIGHT,
        name="compact_first_sent",
    )(*far(lengths, keep, weight, fresh, gates, keys, values))


def own_kernel(
    n_seq, first, len_hbm, keep_hbm, weight_hbm, forget_hbm, keys, values, packed_hbm, *rest
):
    out_k, out_v, chunk, log_ref, level_ref, total_ref = rest[:6]
    lengths, keep, weight, gates, raw, late, forget, rows, zeros = rest[6:15]
    sem_s, sem_l, sem_r, sem_o, sem_z = rest[15:]
    own, sent = half_of("seq", n_seq)
    seq = lax.axis_index("seq")
    heads, req, pos = forget_hbm.shape
    half = pos // 2
    slots = half // 2
    pad = forget.shape[1] // req
    small = fetch(
        [(len_hbm, lengths), (keep_hbm, keep), (weight_hbm, weight), (forget_hbm, gates)], sem_s
    )
    both = ((0, keys), (1, values))
    late_slabs = fetch(
        [
            (source.at[r, lanes(sent, half), :], late.at[i, r - first])
            for r in range(first, req)
            for i, source in both
        ],
        sem_l,
    )
    slabs = fetch(
        [
            (source.at[r, lanes(own, half), :], raw.at[i, r])
            for r in range(req)
            for i, source in both
        ],
        sem_r,
    )
    zeros[...] = jnp.zeros_like(zeros)
    stores = fetch(
        [
            (zeros, out.at[r, lanes(sent, slots), :])
            for r in range(first, req)
            for out in (out_k, out_v)
        ],
        sem_z,
    )
    for copy in small:
        copy.wait()
    ahead, _ = offsets(lengths, first, seq * pos + sent * half, half // BLOCK)

    forget[...] = jnp.zeros_like(forget)
    live = seq * pos + iota((req, pos), 1) < by_row(lengths, iota((req, pos), 0))
    for h in range(heads):
        gate = jnp.where(live, gates[h], 0.0)
        for c in range(pos // LANES):
            forget[c, pl.ds(h, req, stride=pad), :] = gate[:, c * LANES : (c + 1) * LANES]
    flat = jnp.concatenate([forget[c] for c in range(pos // LANES)], axis=1)
    total_ref[...] = jnp.broadcast_to(jnp.sum(flat, axis=1, keepdims=True), total_ref.shape)
    one, two = iota((half, half), 0), iota((half, half), 1)
    after = (((one ^ two) < BLOCK) & (one > two)).astype(jnp.float32).astype(jnp.bfloat16)
    ends = iota((pos, slots), 1) >> SLOT_LOG
    begins = iota((pos, slots), 0) >> BLOCK_LOG
    last = iota((req * pad, slots), 1) & (SLOTS - 1) == SLOTS - 1

    for i, h in enumerate((own, sent)):
        slot, factor = plan(
            keep[:, lanes(h, half)], weight[:, lanes(h, half)], seq * pos + h * half, lengths
        )
        near = half // LANES
        inner = split_dot(
            jnp.concatenate([forget[h * near + c] for c in range(near)], axis=1), after
        )
        beyond = split_dot(
            flat, (begins > ends + h * (half // BLOCK)).astype(jnp.float32).astype(jnp.bfloat16)
        )
        spread = jnp.exp(inner)
        high = spread.astype(jnp.bfloat16).astype(jnp.float32)
        planes = three(inner) + (high, spread - high, jnp.ones_like(inner))
        found = []
        for r in range(req):
            chosen = select(slot, factor, r)
            stack = jnp.concatenate([x[r * pad : (r + 1) * pad] for x in planes], axis=0)
            found.append(dot_nt(stack.astype(jnp.bfloat16), chosen))
            if i == 0:
                for k, out in enumerate((out_k, out_v)):
                    slabs[2 * r + k].wait()
                    rows[k, r] = dot(chosen, raw[k, r]).astype(jnp.bfloat16)
                    stores.append(
                        pltpu.make_async_copy(
                            rows.at[k, r], out.at[r, lanes(own, slots), :], sem_o.at[2 * r + k]
                        )
                    )
                    stores[-1].start()
            elif r >= first:
                at = pl.ds(pl.multiple_of(ahead[r - first] * SLOTS, SLOTS), slots)
                for k in range(2):
                    late_slabs[2 * (r - first) + k].wait()
                    chunk[k, at, :] = dot(chosen, late[k, r - first]).astype(jnp.bfloat16)
        at = [
            jnp.concatenate([x[p * pad : (p + 1) * pad] for x in found], axis=0) for p in range(6)
        ]
        filled = at[5] > 0.5
        kept = at[0] + at[1] + at[2]
        merged = jnp.log(jnp.where(filled, at[3] + at[4], 1.0))
        level_ref[i] = jnp.where(filled, jnp.where(last, merged, kept) + beyond, EMPTY_LOG)
        for k in range(heads):
            log_ref[k, :, lanes(h, slots)] = level_ref[i, pl.ds(k, req, stride=pad), :]
    for copy in stores:
        copy.wait()


def own_part(n_seq, first, lengths, keep, weight, forget, keys, values, packed):
    req, pos, width = keys.shape
    heads = forget.shape[0]
    half, slots, pad = pos // 2, pos // 4, -(-heads // 8) * 8
    late = req - first
    hbm = pl.BlockSpec(memory_space=pl.ANY)
    vmem = pl.BlockSpec(memory_space=pltpu.VMEM)
    whole = pltpu.HBM((req, 2 * slots, width), jnp.bfloat16)
    return pl.pallas_call(
        functools.partial(own_kernel, n_seq, first),
        out_shape=(
            whole,
            whole,
            pltpu.VMEM((2, late * slots, width), jnp.bfloat16),
            pltpu.VMEM((heads, req, 2 * slots), jnp.float32),
            pltpu.VMEM((2, req * pad, slots), jnp.float32),
            pltpu.VMEM((req * pad, LANES), jnp.float32),
        ),
        in_specs=[hbm] * 7,
        out_specs=(hbm, hbm, vmem, vmem, vmem, vmem),
        scratch_shapes=[
            pltpu.SMEM(lengths.shape, jnp.int32),
            pltpu.VMEM(keep.shape, keep.dtype),
            pltpu.VMEM(weight.shape, weight.dtype),
            pltpu.VMEM(forget.shape, forget.dtype),
            pltpu.VMEM((2, req, half, width), jnp.bfloat16),
            pltpu.VMEM((2, late, half, width), jnp.bfloat16),
            pltpu.VMEM((pos // LANES, req * pad, LANES), jnp.float32),
            pltpu.VMEM((2, req, slots, width), jnp.bfloat16),
            pltpu.VMEM((slots, width), jnp.bfloat16),
            pltpu.SemaphoreType.DMA((4,)),
            pltpu.SemaphoreType.DMA((2 * late,)),
            pltpu.SemaphoreType.DMA((2 * req,)),
            pltpu.SemaphoreType.DMA((2 * req,)),
            pltpu.SemaphoreType.DMA((2 * late,)),
        ],
        compiler_params=pltpu.CompilerParams(vmem_limit_bytes=VMEM_LIMIT),
        cost_estimate=LIGHT,
        name="compact_own",
    )(*far(lengths, keep, weight, forget, keys, values), packed)


def attend_kernel(n_seq, n_grp, heads, first, *refs):
    len_hbm, route_hbm, out_k, out_v, early, late, level, total = refs[:8]
    tokens, rest = refs[8 : 8 + n_grp], refs[8 + n_grp :]
    _, _, _, stats_ref, picked_ref = rest[:5]
    lengths, route, own_rows, scores, sem_s, sem_r = rest[5:]
    own, sent = half_of("seq", n_seq)
    kinds, width = picked_ref.shape
    req = kinds // 4
    size = width // heads
    slots = own_rows.shape[2]
    pad = total.shape[0] // req
    small = fetch([(len_hbm, lengths), (route_hbm, route)], sem_s)
    slabs = fetch(
        [
            (out_k.at[:, lanes(own, slots), :], own_rows.at[0]),
            (out_v.at[:, lanes(own, slots), :], own_rows.at[1]),
        ],
        sem_r,
    )
    for copy in small:
        copy.wait()
    start = lax.axis_index("seq") * (4 * slots) + sent * (2 * slots)
    ahead, _ = offsets(lengths, first, start, slots // SLOTS)

    def sent_part(i, r):
        if r < first:
            return early[i, r]
        at = pl.multiple_of(ahead[r - first] * SLOTS, SLOTS)
        return late[i, pl.ds(at, slots), :]

    shape = (kinds, kinds)
    to, frm = iota(shape, 0), iota(shape, 1)
    wanted = by_row(route, to % req)
    me = lax.axis_index("grp")
    picked = jnp.zeros((kinds, width), jnp.float32)
    for k in range(n_grp):
        source = lax.rem(me + n_grp - k, n_grp)
        hit = (to // req == frm // req) & (wanted == source * req + frm % req)
        picked = picked + dot(hit.astype(jnp.float32).astype(jnp.bfloat16), tokens[k][...])
    picked_ref[...] = picked
    for copy in slabs:
        copy.wait()

    lane, row = iota((pad, width), 1), iota((pad, width), 0)
    mine = (lane >= row * size) & (lane < (row + 1) * size)
    for r in range(req):
        query = jnp.where(mine, picked[r : r + 1, :], 0.0).astype(jnp.bfloat16)
        here = slice(r * pad, (r + 1) * pad)
        scores[here, :slots] = dot_nt(query, own_rows[0, r])
        scores[here, slots:] = dot_nt(query, sent_part(0, r))
    logit = scores[...] * (size**-0.5) + jnp.concatenate([level[0], level[1]], axis=1)
    top = jnp.max(logit, axis=1, keepdims=True)
    weights = jnp.exp(logit - top).astype(jnp.bfloat16).astype(jnp.float32)
    mass = jnp.sum(weights, axis=1, keepdims=True)

    def spread_out(column, r):
        return jnp.sum(
            jnp.where(mine, column[r * pad : (r + 1) * pad], 0.0), axis=0, keepdims=True
        )

    for r in range(req):
        w = weights[r * pad : (r + 1) * pad].astype(jnp.bfloat16)
        acc = dot(w[:, :slots], own_rows[1, r]) + dot(w[:, slots:], sent_part(1, r))
        acc = jnp.sum(jnp.where(mine, acc, 0.0), axis=0, keepdims=True)
        for p, x in enumerate((top, mass, total[:, :1])):
            stats_ref[p * req + r : p * req + r + 1, :] = spread_out(x, r)
        stats_ref[3 * req + r : 3 * req + r + 1, :] = acc


def attend_part(n_seq, n_grp, heads, lengths, route, out_k, out_v, early, late, level, total, tokens):
    req, rows, width = out_k.shape
    slots, first = rows // 2, early.shape[1]
    hbm = pl.BlockSpec(memory_space=pl.ANY)
    vmem = pl.BlockSpec(memory_space=pltpu.VMEM)
    whole = pltpu.HBM(out_k.shape, out_k.dtype)
    small = pltpu.VMEM((4 * req, width), jnp.float32)
    return pl.pallas_call(
        functools.partial(attend_kernel, n_seq, n_grp, heads, first),
        out_shape=(whole, whole, pltpu.VMEM(late.shape, late.dtype), small, small),
        in_specs=[hbm] * 4 + [vmem] * (4 + n_grp),
        out_specs=(hbm, hbm, vmem, vmem, vmem),
        scratch_shapes=[
            pltpu.SMEM(lengths.shape, jnp.int32),
            pltpu.SMEM(route.shape, jnp.int32),
            pltpu.VMEM((2, req, slots, width), jnp.bfloat16),
            pltpu.VMEM((total.shape[0], rows), jnp.float32),
            pltpu.SemaphoreType.DMA((2,)),
            pltpu.SemaphoreType.DMA((2,)),
        ],
        input_output_aliases={2: 0, 3: 1, 5: 2},
        compiler_params=pltpu.CompilerParams(vmem_limit_bytes=VMEM_LIMIT),
        cost_estimate=LIGHT,
        name="attend",
    )(
        *far(lengths, route, out_k, out_v),
        *near(early, late, level, total),
        *near(*tokens),
    )


def place(n_seq, first, part, out_k, out_v, sem):
    _, sent = half_of("seq", n_seq)
    _, count, rows, _ = part.shape
    return fetch(
        [
            (part.at[i], out.at[pl.ds(first, count), lanes(sent, rows), :])
            for i, out in enumerate((out_k, out_v))
        ],
        sem,
    )


def merge_kernel(count, relative, size, *refs):
    stats, refs = refs[:count], refs[count:]
    picked_ref, weight_ref, log_ref, decay_ref, out_ref = refs
    heads, req, rows = log_ref.shape
    width = picked_ref.shape[1]
    seq = lax.axis_index("seq")
    places = [lax.rem(seq + count - k, count) if relative else jnp.int32(k) for k in range(count)]
    tops, masses, totals, accs = [
        [ref[p * req : (p + 1) * req, :] for ref in stats] for p in range(4)
    ]

    def later(place):
        total = jnp.zeros_like(totals[0])
        for k in range(count):
            total = total + jnp.where(places[k] > place, totals[k], 0.0)
        return total

    tops = [tops[k] + later(places[k]) for k in range(count)]
    top = functools.reduce(jnp.maximum, tops)
    scales = [jnp.exp(t - top) for t in tops]
    mass = sum(s * x for s, x in zip(scales, masses))
    acc = sum(s * x for s, x in zip(scales, accs))
    query, key, value, gate = [picked_ref[p * req : (p + 1) * req, :] for p in range(4)]
    one, two = iota((width, width), 0), iota((width, width), 1)
    same = (one // size == two // size).astype(jnp.float32).astype(jnp.bfloat16)
    own = split_dot(query * key, same) * (size**-0.5)
    past = top + gate
    joint = jnp.maximum(past, own)
    scale, self_weight = jnp.exp(past - joint), jnp.exp(own - joint)
    attended = (scale * acc + self_weight * value) / (scale * mass + self_weight)
    beyond = later(seq)
    for h in range(heads):
        decay_ref[h] = jnp.exp(log_ref[h] + beyond[:, h * size : h * size + 1])
    out_ref[...] = dot(attended.astype(jnp.bfloat16), weight_ref[...])


def merge_part(stats, relative, picked, out_weight, logs, size):
    req = logs.shape[1]
    vmem = pl.BlockSpec(memory_space=pltpu.VMEM)
    return pl.pallas_call(
        functools.partial(merge_kernel, len(stats), relative, size),
        out_shape=(
            jax.ShapeDtypeStruct(logs.shape, jnp.float32),
            jax.ShapeDtypeStruct((req, out_weight.shape[1]), jnp.float32),
        ),
        in_specs=[vmem] * (len(stats) + 3),
        out_specs=(vmem, vmem),
        compiler_params=pltpu.CompilerParams(vmem_limit_bytes=VMEM_LIMIT),
        cost_estimate=MERGE,
        name="merge_and_project",
    )(*near(*stats, picked, out_weight, logs))


def sum_kernel(count, *refs):
    parts, out = refs[:count], refs[-1]
    me = lax.axis_index("head")
    total = jnp.zeros(out.shape, jnp.float32)
    for place in range(count):
        for k in range(count):
            total = total + jnp.where(lax.rem(me + count - k, count) == place, parts[k][...], 0.0)
    out[...] = total.astype(out.dtype)


def sum_part(parts, placed):
    return pl.pallas_call(
        functools.partial(sum_kernel, len(parts)),
        out_shape=pltpu.HBM(parts[0].shape, jnp.bfloat16),
        in_specs=[pl.BlockSpec(memory_space=pltpu.VMEM)] * (len(parts) + 1),
        out_specs=pl.BlockSpec(memory_space=pltpu.VMEM),
        compiler_params=pltpu.CompilerParams(vmem_limit_bytes=VMEM_LIMIT),
        cost_estimate=LIGHT,
        name="sum_heads",
    )(*parts, placed)


def place_kernel(n_seq, first, part, old_k, old_v, out_k, out_v, placed_ref, sem):
    copies = place(n_seq, first, part, out_k, out_v, sem)
    placed_ref[...] = jnp.zeros_like(placed_ref)
    for copy in copies:
        copy.wait()


def place_part(n_seq, first, part, out_k, out_v):
    hbm = pl.BlockSpec(memory_space=pl.ANY)
    vmem = pl.BlockSpec(memory_space=pltpu.VMEM)
    shape = pltpu.HBM(out_k.shape, out_k.dtype)
    return pl.pallas_call(
        functools.partial(place_kernel, n_seq, first),
        out_shape=(shape, shape, pltpu.VMEM((8, LANES), jnp.float32)),
        in_specs=[vmem, hbm, hbm],
        out_specs=(hbm, hbm, vmem),
        scratch_shapes=[pltpu.SemaphoreType.DMA((2,))],
        input_output_aliases={1: 0, 2: 1},
        compiler_params=pltpu.CompilerParams(vmem_limit_bytes=VMEM_LIMIT),
        cost_estimate=LIGHT,
        name="place_received",
    )(*near(part), *far(out_k, out_v))


def place_late_kernel(n_seq, first, part, len_hbm, old_k, old_v, out_k, out_v, lengths, sem_s, sem):
    _, sent = half_of("seq", n_seq)
    (load,) = fetch([(len_hbm, lengths)], sem_s)
    load.wait()
    req, rows, _ = out_k.shape
    slots = rows // 2
    most = slots // SLOTS
    seq = lax.axis_index("seq")
    if n_seq == 2:
        start = (1 - seq) * (4 * slots) + seq * (2 * slots)
    else:
        start = seq * (4 * slots) + sent * (2 * slots)
    ahead, _ = offsets(lengths, first, start, most)
    for phase in ("start", "wait"):
        for j, skip in enumerate(ahead):
            live = live_blocks(lengths, first + j, start, most)
            for blocks in range(1, most + 1):
                size = blocks * SLOTS

                @pl.when(live == blocks)
                def _(j=j, skip=skip, size=size):
                    for i, out in enumerate((out_k, out_v)):
                        source = pl.ds(pl.multiple_of(skip * SLOTS, SLOTS), size)
                        target = pl.ds(pl.multiple_of(sent * slots, SLOTS), size)
                        copy = pltpu.make_async_copy(
                            part.at[i, source, :], out.at[first + j, target, :], sem.at[i, j]
                        )
                        getattr(copy, phase)()


def place_late_part(n_seq, first, part, lengths, out_k, out_v):
    hbm = pl.BlockSpec(memory_space=pl.ANY)
    vmem = pl.BlockSpec(memory_space=pltpu.VMEM)
    shape = pltpu.HBM(out_k.shape, out_k.dtype)
    return pl.pallas_call(
        functools.partial(place_late_kernel, n_seq, first),
        out_shape=(shape, shape),
        in_specs=[vmem, hbm, hbm, hbm],
        out_specs=(hbm, hbm),
        scratch_shapes=[
            pltpu.SMEM(lengths.shape, jnp.int32),
            pltpu.SemaphoreType.DMA((1,)),
            pltpu.SemaphoreType.DMA((2, lengths.shape[0] - first)),
        ],
        input_output_aliases={2: 0, 3: 1},
        compiler_params=pltpu.CompilerParams(vmem_limit_bytes=VMEM_LIMIT),
        cost_estimate=LIGHT,
        name="place_live",
    )(*near(part), *far(lengths, out_k, out_v))


def others(value, axis):
    count = lax.axis_size(axis)
    return [value] + [
        lax.ppermute(value, axis, [(i, (i + k) % count) for i in range(count)])
        for k in range(1, count)
    ]


def swap(value, n_seq):
    return lax.ppermute(value, "seq", [(0, 1), (1, 0)]) if n_seq == 2 else value


def shards(
    keys, values, log_forget, keep, merge_weight, lengths, route, fresh, new_forget, out_weight
):
    req, pos, width = keys.shape
    heads = log_forget.shape[1]
    size = width // heads
    n_seq, n_grp = lax.axis_size("seq"), lax.axis_size("grp")
    early, packed, choice = first_part(
        n_seq,
        FIRST,
        lengths,
        keep,
        merge_weight,
        fresh.reshape(3 * req, width),
        new_forget,
        keys,
        values,
    )
    exchange = functools.partial(swap, n_seq=n_seq)
    first_received = exchange(early)
    tokens = others(packed, "grp")
    out_k, out_v, late, logs, level, total = own_part(
        n_seq,
        FIRST,
        lengths,
        keep,
        merge_weight,
        log_forget.transpose(1, 0, 2),
        keys,
        values,
        packed,
    )
    out_k, out_v, late, stats, picked = attend_part(
        n_seq, n_grp, heads, lengths, route, out_k, out_v, early, late, level, total, tokens
    )

    def finish(rows, early, late, stats, picked, out_weight, logs, lengths, out_k, out_v):
        if n_seq == 2:
            all_stats = others(stats, "seq")
        else:
            gathered = lax.all_gather(stats, "seq")
            all_stats = [gathered[i] for i in range(n_seq)]
        received = exchange(late[:, :rows])
        decay, partial = merge_part(all_stats, n_seq == 2, picked, out_weight, logs, size)
        out_k, out_v, placed = place_part(n_seq, 0, early, out_k, out_v)
        layer_out = sum_part(others(partial, "head"), placed)
        out_k, out_v = place_late_part(n_seq, FIRST, received, lengths, out_k, out_v)
        return decay, layer_out, out_k, out_v

    operands = (first_received, late, stats, picked, out_weight, logs, lengths, out_k, out_v)
    if n_seq == 2:
        step = STEP * SLOTS
        branches = [
            functools.partial(finish, rows) for rows in range(step, late.shape[1] + 1, step)
        ]
        decay, layer_out, out_k, out_v = lax.switch(choice[0], branches, *operands)
    else:
        decay, layer_out, out_k, out_v = finish(late.shape[1], *operands)
    if n_seq != 2:
        out_k, out_v = (
            lax.all_to_all(x, "seq", split_axis=1, concat_axis=1, tiled=True) for x in (out_k, out_v)
        )
    return out_k, out_v, decay.transpose(1, 0, 2), layer_out


def solution(mesh):
    return jax.shard_map(
        shards,
        mesh=mesh,
        in_specs=(
            P("grp", "seq", "head"),
            P("grp", "seq", "head"),
            P("grp", "head", "seq"),
            P("grp", "seq"),
            P("grp", "seq"),
            P("grp"),
            P("grp"),
            P(None, "grp", "head"),
            P("grp", "head"),
            P("head", "seq"),
        ),
        out_specs=(
            P("grp", "seq", "head"),
            P("grp", "seq", "head"),
            P("grp", "head", "seq"),
            P("grp", "seq"),
        ),
        check_vma=False,
    )
```

```python
import functools

import jax
import jax.numpy as jnp
from jax import lax
from jax.experimental import pallas as pl
from jax.experimental.pallas import tpu as pltpu
from jax.sharding import PartitionSpec as P

BLOCK = 64
SLOTS = 32
LANES = 128
BLOCK_LOG = BLOCK.bit_length() - 1
SLOT_LOG = SLOTS.bit_length() - 1
EMPTY_LOG = -10000.0
FIRST = 12
STEP = 2
SURE = 3
VMEM_LIMIT = 16 * 1024 * 1024


LIGHT = pl.CostEstimate(flops=1, bytes_accessed=1, transcendentals=0)
MERGE = pl.CostEstimate(flops=1 << 36, bytes_accessed=1, transcendentals=0)


def dot(a, b):
    return lax.dot_general(a, b, (((1,), (0,)), ((), ())), preferred_element_type=jnp.float32)


def dot_nt(a, b):
    return lax.dot_general(a, b, (((1,), (1,)), ((), ())), preferred_element_type=jnp.float32)


def iota(shape, dim):
    return lax.broadcasted_iota(jnp.int32, shape, dim)


def three(x):
    hi = x.astype(jnp.bfloat16).astype(jnp.float32)
    rest = x - hi
    mid = rest.astype(jnp.bfloat16).astype(jnp.float32)
    return hi, mid, rest - mid


def split_dot(x, ones):
    rows = x.shape[0]
    parts = dot(jnp.concatenate(three(x), axis=0).astype(jnp.bfloat16), ones)
    return parts[:rows] + parts[rows : 2 * rows] + parts[2 * rows :]


def half_of(axis, count):
    own = lax.axis_index(axis) if count == 2 else jnp.int32(0)
    return own, 1 - own


def by_row(ref, row):
    picked = jnp.zeros_like(row)
    for r in range(ref.shape[0]):
        picked = jnp.where(row == r, ref[r], picked)
    return picked


def live_blocks(lengths, r, start, most):
    return jnp.clip((lengths[r] - start) >> BLOCK_LOG, 0, most)


def offsets(lengths, start, most):
    total = jnp.int32(0)
    ahead, live = [], []
    for r in range(lengths.shape[0]):
        ahead.append(total)
        live.append(live_blocks(lengths, r, start, most))
        total = total + live[-1]
    return ahead, live, total


def plan(keep, weight, start, len_ref):
    rows, width = keep.shape
    one, two = iota((width, width), 0), iota((width, width), 1)
    same = (one ^ two) < BLOCK
    upto = (same & (one <= two)).astype(jnp.float32).astype(jnp.bfloat16)
    block = same.astype(jnp.float32).astype(jnp.bfloat16)
    kept = keep == 1
    rank = dot(keep.astype(jnp.float32).astype(jnp.bfloat16), upto) - 1.0
    weighted = jnp.where(kept, 0.0, weight)
    share = (weighted / split_dot(weighted, block)).astype(jnp.bfloat16).astype(jnp.float32)
    lane, row = iota((rows, width), 1), iota((rows, width), 0)
    slot = jnp.where(kept, rank.astype(jnp.int32), SLOTS - 1) + (lane >> BLOCK_LOG) * SLOTS
    slot = jnp.where(start + lane < by_row(len_ref, row), slot, -1)
    return slot, jnp.where(kept, 1.0, share)


def select(slot, factor, r):
    width = slot.shape[1]
    shape = (width // 2, width)
    hit = iota(shape, 0) == slot[r : r + 1, :]
    return jnp.where(hit, jnp.broadcast_to(factor[r : r + 1, :], shape), 0.0).astype(jnp.bfloat16)


def lanes(half, width):
    return pl.ds(pl.multiple_of(half * width, width), width)


def far(*arrays):
    return [pltpu.with_memory_space_constraint(x, pltpu.HBM) for x in arrays]


def near(*arrays):
    return [pltpu.with_memory_space_constraint(x, pltpu.VMEM) for x in arrays]


def fetch(pairs, sem):
    copies = [pltpu.make_async_copy(src, dst, sem.at[i]) for i, (src, dst) in enumerate(pairs)]
    for copy in copies:
        copy.start()
    return copies


def first_kernel(n_seq, len_hbm, keep_hbm, weight_hbm, fresh_hbm, gate_hbm, keys, values, *rest):
    out, packed, size_ref, lengths, keep, weight, fresh, gates, raw, sem_s, sem_r = rest
    _, sent = half_of("seq", n_seq)
    req, width = keep.shape
    most = width // BLOCK
    slots = most * SLOTS
    small = fetch(
        [
            (len_hbm, lengths),
            (keep_hbm.at[:, lanes(sent, width)], keep),
            (weight_hbm.at[:, lanes(sent, width)], weight),
            (fresh_hbm, fresh),
            (gate_hbm, gates),
        ],
        sem_s,
    )

    def slab(i, r):
        source = (keys, values)[i].at[r, lanes(sent, width), :]
        return pltpu.make_async_copy(source, raw.at[i, r], sem_r.at[i, r])

    sure = min(SURE, req)
    for r in range(sure):
        for i in range(2):
            slab(i, r).start()
    out[...] = jnp.zeros_like(out)
    for copy in small:
        copy.wait()
    start = lax.axis_index("seq") * (2 * width) + sent * width
    ahead, live, _ = offsets(lengths, start, most)
    for r in range(sure, req):

        @pl.when(ahead[r] < FIRST)
        def _(r=r):
            for i in range(2):
                slab(i, r).start()

    slot, factor = plan(keep[...], weight[...], start, lengths)
    _, _, total = offsets(lengths, width, most)
    sizes = (req * most - FIRST) // STEP
    size_ref[0] = jnp.clip((total - FIRST - 1) >> (STEP.bit_length() - 1), 0, sizes - 1)

    new, gate = fresh[...].astype(jnp.float32), gates[...].astype(jnp.float32)
    heads = gate.shape[1]
    lane = iota((req, new.shape[1]), 1)
    size = new.shape[1] // heads
    spread = jnp.zeros((req, new.shape[1]), jnp.float32)
    for h in range(heads):
        inside = (lane >= h * size) & (lane < (h + 1) * size)
        spread = jnp.where(inside, gate[:, h : h + 1], spread)
    packed[...] = jnp.concatenate([new, spread], axis=0).astype(jnp.bfloat16)

    def pack(r):
        chosen = select(slot, factor, r)
        for i in range(2):
            slab(i, r).wait()
            rows = dot(chosen, raw[i, r]).astype(jnp.bfloat16)
            if (r + 1) * most <= FIRST:
                at = pl.ds(pl.multiple_of(ahead[r] * SLOTS, SLOTS), slots)
                out[i, at, :] = rows
                continue
            for b in range(most):

                @pl.when((b < live[r]) & (ahead[r] + b < FIRST))
                def _(i=i, b=b, rows=rows):
                    at = pl.ds(pl.multiple_of((ahead[r] + b) * SLOTS, SLOTS), SLOTS)
                    out[i, at, :] = rows[b * SLOTS : (b + 1) * SLOTS]

    for r in range(req):
        if r < sure:
            pack(r)
        else:
            pl.when(ahead[r] < FIRST)(functools.partial(pack, r))


def first_part(n_seq, lengths, keep, weight, fresh, gates, keys, values):
    req, pos, width = keys.shape
    half = pos // 2
    hbm = pl.BlockSpec(memory_space=pl.ANY)
    vmem = pl.BlockSpec(memory_space=pltpu.VMEM)
    return pl.pallas_call(
        functools.partial(first_kernel, n_seq),
        out_shape=(
            pltpu.VMEM((2, FIRST * SLOTS, width), jnp.bfloat16),
            pltpu.VMEM((fresh.shape[0] + req, width), jnp.bfloat16),
            jax.ShapeDtypeStruct((1,), jnp.int32),
        ),
        in_specs=[hbm] * 7,
        out_specs=(vmem, vmem, pl.BlockSpec(memory_space=pltpu.SMEM)),
        scratch_shapes=[
            pltpu.SMEM(lengths.shape, jnp.int32),
            pltpu.VMEM((req, half), jnp.int32),
            pltpu.VMEM((req, half), jnp.float32),
            pltpu.VMEM(fresh.shape, fresh.dtype),
            pltpu.VMEM(gates.shape, gates.dtype),
            pltpu.VMEM((2, req, half, width), jnp.bfloat16),
            pltpu.SemaphoreType.DMA((5,)),
            pltpu.SemaphoreType.DMA((2, req)),
        ],
        compiler_params=pltpu.CompilerParams(vmem_limit_bytes=VMEM_LIMIT),
        cost_estimate=LIGHT,
        name="compact_first_sent",
    )(*far(lengths, keep, weight, fresh, gates, keys, values))


def own_kernel(
    n_seq, len_hbm, keep_hbm, weight_hbm, forget_hbm, keys, values, early, *rest
):
    out_k, out_v, chunk, log_ref, level_ref, total_ref = rest[:6]
    lengths, keep, weight, gates, raw, late, forget, rows, zeros = rest[6:15]
    sem_s, sem_l, sem_r, sem_o, sem_z = rest[15:]
    own, sent = half_of("seq", n_seq)
    seq = lax.axis_index("seq")
    heads, req, pos = forget_hbm.shape
    half = pos // 2
    slots = half // 2
    most = half // BLOCK
    first = FIRST // most
    pad = forget.shape[1] // req
    small = fetch(
        [(len_hbm, lengths), (keep_hbm, keep), (weight_hbm, weight), (forget_hbm, gates)], sem_s
    )
    both = ((0, keys), (1, values))
    late_slabs = fetch(
        [
            (source.at[r, lanes(sent, half), :], late.at[i, r - first])
            for r in range(first, req)
            for i, source in both
        ],
        sem_l,
    )
    slabs = fetch(
        [
            (source.at[r, lanes(own, half), :], raw.at[i, r])
            for r in range(req)
            for i, source in both
        ],
        sem_r,
    )
    zeros[...] = jnp.zeros_like(zeros)
    stores = fetch([(zeros, out.at[:, lanes(sent, slots), :]) for out in (out_k, out_v)], sem_z)
    chunk[:, : FIRST * SLOTS, :] = early[...]
    chunk[:, FIRST * SLOTS :, :] = jnp.zeros(
        (2, chunk.shape[1] - FIRST * SLOTS, chunk.shape[2]), chunk.dtype
    )
    for copy in small:
        copy.wait()
    ahead, alive, _ = offsets(lengths, seq * pos + sent * half, most)

    forget[...] = jnp.zeros_like(forget)
    live = seq * pos + iota((req, pos), 1) < by_row(lengths, iota((req, pos), 0))
    for h in range(heads):
        gate = jnp.where(live, gates[h], 0.0)
        for c in range(pos // LANES):
            forget[c, pl.ds(h, req, stride=pad), :] = gate[:, c * LANES : (c + 1) * LANES]
    flat = jnp.concatenate([forget[c] for c in range(pos // LANES)], axis=1)
    total_ref[...] = jnp.broadcast_to(jnp.sum(flat, axis=1, keepdims=True), total_ref.shape)
    one, two = iota((half, half), 0), iota((half, half), 1)
    after = (((one ^ two) < BLOCK) & (one > two)).astype(jnp.float32).astype(jnp.bfloat16)
    ends = iota((pos, slots), 1) >> SLOT_LOG
    begins = iota((pos, slots), 0) >> BLOCK_LOG
    last = iota((req * pad, slots), 1) & (SLOTS - 1) == SLOTS - 1

    for i, h in enumerate((own, sent)):
        slot, factor = plan(
            keep[:, lanes(h, half)], weight[:, lanes(h, half)], seq * pos + h * half, lengths
        )
        near = half // LANES
        inner = split_dot(
            jnp.concatenate([forget[h * near + c] for c in range(near)], axis=1), after
        )
        beyond = split_dot(
            flat, (begins > ends + h * (half // BLOCK)).astype(jnp.float32).astype(jnp.bfloat16)
        )
        spread = jnp.exp(inner)
        high = spread.astype(jnp.bfloat16).astype(jnp.float32)
        planes = three(inner) + (high, spread - high, jnp.ones_like(inner))
        found = []
        for r in range(req):
            chosen = select(slot, factor, r)
            stack = jnp.concatenate([x[r * pad : (r + 1) * pad] for x in planes], axis=0)
            found.append(dot_nt(stack.astype(jnp.bfloat16), chosen))
            if i == 0:
                for k, out in enumerate((out_k, out_v)):
                    slabs[2 * r + k].wait()
                    rows[k, r] = dot(chosen, raw[k, r]).astype(jnp.bfloat16)
                    stores.append(
                        pltpu.make_async_copy(
                            rows.at[k, r], out.at[r, lanes(own, slots), :], sem_o.at[2 * r + k]
                        )
                    )
                    stores[-1].start()
            elif r >= first:
                for k in range(2):
                    late_slabs[2 * (r - first) + k].wait()

                @pl.when(ahead[r] + alive[r] > FIRST)
                def _(r=r, chosen=chosen):
                    at = pl.ds(pl.multiple_of(ahead[r] * SLOTS, SLOTS), slots)
                    for k in range(2):
                        chunk[k, at, :] = dot(chosen, late[k, r - first]).astype(jnp.bfloat16)
        at = [
            jnp.concatenate([x[p * pad : (p + 1) * pad] for x in found], axis=0) for p in range(6)
        ]
        filled = at[5] > 0.5
        kept = at[0] + at[1] + at[2]
        merged = jnp.log(jnp.where(filled, at[3] + at[4], 1.0))
        level_ref[i] = jnp.where(filled, jnp.where(last, merged, kept) + beyond, EMPTY_LOG)
        for k in range(heads):
            log_ref[k, :, lanes(h, slots)] = level_ref[i, pl.ds(k, req, stride=pad), :]
    for copy in stores:
        copy.wait()


def own_part(n_seq, lengths, keep, weight, forget, keys, values, early):
    req, pos, width = keys.shape
    heads = forget.shape[0]
    half, slots, pad = pos // 2, pos // 4, -(-heads // 8) * 8
    late = req - FIRST // (half // BLOCK)
    hbm = pl.BlockSpec(memory_space=pl.ANY)
    vmem = pl.BlockSpec(memory_space=pltpu.VMEM)
    whole = pltpu.HBM((req, 2 * slots, width), jnp.bfloat16)
    return pl.pallas_call(
        functools.partial(own_kernel, n_seq),
        out_shape=(
            whole,
            whole,
            pltpu.VMEM((2, req * slots, width), jnp.bfloat16),
            pltpu.VMEM((heads, req, 2 * slots), jnp.float32),
            pltpu.VMEM((2, req * pad, slots), jnp.float32),
            pltpu.VMEM((req * pad, LANES), jnp.float32),
        ),
        in_specs=[hbm] * 6 + [vmem],
        out_specs=(hbm, hbm, vmem, vmem, vmem, vmem),
        scratch_shapes=[
            pltpu.SMEM(lengths.shape, jnp.int32),
            pltpu.VMEM(keep.shape, keep.dtype),
            pltpu.VMEM(weight.shape, weight.dtype),
            pltpu.VMEM(forget.shape, forget.dtype),
            pltpu.VMEM((2, req, half, width), jnp.bfloat16),
            pltpu.VMEM((2, late, half, width), jnp.bfloat16),
            pltpu.VMEM((pos // LANES, req * pad, LANES), jnp.float32),
            pltpu.VMEM((2, req, slots, width), jnp.bfloat16),
            pltpu.VMEM((req, slots, width), jnp.bfloat16),
            pltpu.SemaphoreType.DMA((4,)),
            pltpu.SemaphoreType.DMA((2 * late,)),
            pltpu.SemaphoreType.DMA((2 * req,)),
            pltpu.SemaphoreType.DMA((2 * req,)),
            pltpu.SemaphoreType.DMA((2,)),
        ],
        compiler_params=pltpu.CompilerParams(vmem_limit_bytes=VMEM_LIMIT),
        cost_estimate=LIGHT,
        name="compact_own",
    )(*far(lengths, keep, weight, forget, keys, values), *near(early))


def attend_kernel(n_seq, n_grp, heads, *refs):
    len_hbm, route_hbm, out_k, out_v, late, level, total = refs[:7]
    tokens, rest = refs[7 : 7 + n_grp], refs[7 + n_grp :]
    _, _, stats_ref, picked_ref, lengths, route, own_rows, scores, sem_s, sem_r = rest
    own, sent = half_of("seq", n_seq)
    kinds, width = picked_ref.shape
    req = kinds // 4
    size = width // heads
    slots = own_rows.shape[2]
    pad = total.shape[0] // req
    small = fetch([(len_hbm, lengths), (route_hbm, route)], sem_s)
    slabs = fetch(
        [
            (out_k.at[:, lanes(own, slots), :], own_rows.at[0]),
            (out_v.at[:, lanes(own, slots), :], own_rows.at[1]),
        ],
        sem_r,
    )
    for copy in small:
        copy.wait()
    start = lax.axis_index("seq") * (4 * slots) + sent * (2 * slots)
    ahead, _, _ = offsets(lengths, start, slots // SLOTS)

    def sent_part(i, r):
        at = pl.multiple_of(ahead[r] * SLOTS, SLOTS)
        return late[i, pl.ds(at, slots), :]

    shape = (kinds, kinds)
    to, frm = iota(shape, 0), iota(shape, 1)
    wanted = by_row(route, to % req)
    me = lax.axis_index("grp")
    picked = jnp.zeros((kinds, width), jnp.float32)
    for k in range(n_grp):
        source = lax.rem(me + n_grp - k, n_grp)
        hit = (to // req == frm // req) & (wanted == source * req + frm % req)
        picked = picked + dot(hit.astype(jnp.float32).astype(jnp.bfloat16), tokens[k][...])
    picked_ref[...] = picked
    for copy in slabs:
        copy.wait()

    lane, row = iota((pad, width), 1), iota((pad, width), 0)
    mine = (lane >= row * size) & (lane < (row + 1) * size)
    for r in range(req):
        query = jnp.where(mine, picked[r : r + 1, :], 0.0).astype(jnp.bfloat16)
        here = slice(r * pad, (r + 1) * pad)
        scores[here, :slots] = dot_nt(query, own_rows[0, r])
        scores[here, slots:] = dot_nt(query, sent_part(0, r))
    logit = scores[...] * (size**-0.5) + jnp.concatenate([level[0], level[1]], axis=1)
    top = jnp.max(logit, axis=1, keepdims=True)
    weights = jnp.exp(logit - top).astype(jnp.bfloat16).astype(jnp.float32)
    mass = jnp.sum(weights, axis=1, keepdims=True)

    def spread_out(column, r):
        return jnp.sum(
            jnp.where(mine, column[r * pad : (r + 1) * pad], 0.0), axis=0, keepdims=True
        )

    for r in range(req):
        w = weights[r * pad : (r + 1) * pad].astype(jnp.bfloat16)
        acc = dot(w[:, :slots], own_rows[1, r]) + dot(w[:, slots:], sent_part(1, r))
        acc = jnp.sum(jnp.where(mine, acc, 0.0), axis=0, keepdims=True)
        for p, x in enumerate((top, mass, total[:, :1])):
            stats_ref[p * req + r : p * req + r + 1, :] = spread_out(x, r)
        stats_ref[3 * req + r : 3 * req + r + 1, :] = acc


def attend_part(n_seq, n_grp, heads, lengths, route, out_k, out_v, late, level, total, tokens):
    req, rows, width = out_k.shape
    slots = rows // 2
    hbm = pl.BlockSpec(memory_space=pl.ANY)
    vmem = pl.BlockSpec(memory_space=pltpu.VMEM)
    whole = pltpu.HBM(out_k.shape, out_k.dtype)
    small = pltpu.VMEM((4 * req, width), jnp.float32)
    return pl.pallas_call(
        functools.partial(attend_kernel, n_seq, n_grp, heads),
        out_shape=(whole, whole, small, small),
        in_specs=[hbm] * 4 + [vmem] * (3 + n_grp),
        out_specs=(hbm, hbm, vmem, vmem),
        scratch_shapes=[
            pltpu.SMEM(lengths.shape, jnp.int32),
            pltpu.SMEM(route.shape, jnp.int32),
            pltpu.VMEM((2, req, slots, width), jnp.bfloat16),
            pltpu.VMEM((total.shape[0], rows), jnp.float32),
            pltpu.SemaphoreType.DMA((2,)),
            pltpu.SemaphoreType.DMA((2,)),
        ],
        input_output_aliases={2: 0, 3: 1},
        compiler_params=pltpu.CompilerParams(vmem_limit_bytes=VMEM_LIMIT),
        cost_estimate=LIGHT,
        name="attend",
    )(
        *far(lengths, route, out_k, out_v),
        *near(late, level, total),
        *near(*tokens),
    )


def merge_kernel(count, relative, size, *refs):
    stats, refs = refs[:count], refs[count:]
    picked_ref, weight_ref, log_ref, decay_ref, out_ref = refs
    heads, req, rows = log_ref.shape
    width = picked_ref.shape[1]
    seq = lax.axis_index("seq")
    places = [lax.rem(seq + count - k, count) if relative else jnp.int32(k) for k in range(count)]
    tops, masses, totals, accs = [
        [ref[p * req : (p + 1) * req, :] for ref in stats] for p in range(4)
    ]

    def later(place):
        total = jnp.zeros_like(totals[0])
        for k in range(count):
            total = total + jnp.where(places[k] > place, totals[k], 0.0)
        return total

    tops = [tops[k] + later(places[k]) for k in range(count)]
    top = functools.reduce(jnp.maximum, tops)
    scales = [jnp.exp(t - top) for t in tops]
    mass = sum(s * x for s, x in zip(scales, masses))
    acc = sum(s * x for s, x in zip(scales, accs))
    query, key, value, gate = [picked_ref[p * req : (p + 1) * req, :] for p in range(4)]
    one, two = iota((width, width), 0), iota((width, width), 1)
    same = (one // size == two // size).astype(jnp.float32).astype(jnp.bfloat16)
    own = split_dot(query * key, same) * (size**-0.5)
    past = top + gate
    joint = jnp.maximum(past, own)
    scale, self_weight = jnp.exp(past - joint), jnp.exp(own - joint)
    attended = (scale * acc + self_weight * value) / (scale * mass + self_weight)
    beyond = later(seq)
    for h in range(heads):
        decay_ref[h] = jnp.exp(log_ref[h] + beyond[:, h * size : h * size + 1])
    out_ref[...] = dot(attended.astype(jnp.bfloat16), weight_ref[...])


def merge_part(stats, relative, picked, out_weight, logs, size):
    req = logs.shape[1]
    vmem = pl.BlockSpec(memory_space=pltpu.VMEM)
    return pl.pallas_call(
        functools.partial(merge_kernel, len(stats), relative, size),
        out_shape=(
            jax.ShapeDtypeStruct(logs.shape, jnp.float32),
            jax.ShapeDtypeStruct((req, out_weight.shape[1]), jnp.float32),
        ),
        in_specs=[vmem] * (len(stats) + 3),
        out_specs=(vmem, vmem),
        compiler_params=pltpu.CompilerParams(vmem_limit_bytes=VMEM_LIMIT),
        cost_estimate=MERGE,
        name="merge_and_project",
    )(*near(*stats, picked, out_weight, logs))


def sum_kernel(count, *refs):
    parts, out = refs[:count], refs[-1]
    me = lax.axis_index("head")
    total = jnp.zeros(out.shape, jnp.float32)
    for place in range(count):
        for k in range(count):
            total = total + jnp.where(lax.rem(me + count - k, count) == place, parts[k][...], 0.0)
    out[...] = total.astype(out.dtype)


def sum_part(parts, placed):
    return pl.pallas_call(
        functools.partial(sum_kernel, len(parts)),
        out_shape=pltpu.HBM(parts[0].shape, jnp.bfloat16),
        in_specs=[pl.BlockSpec(memory_space=pltpu.VMEM)] * (len(parts) + 1),
        out_specs=pl.BlockSpec(memory_space=pltpu.VMEM),
        compiler_params=pltpu.CompilerParams(vmem_limit_bytes=VMEM_LIMIT),
        cost_estimate=LIGHT,
        name="sum_heads",
    )(*parts, placed)


def place_kernel(n_seq, first, part, len_hbm, old_k, old_v, out_k, out_v, *rest):
    _, sent = half_of("seq", n_seq)
    placed_ref, lengths, sem_s, sem = rest
    (load,) = fetch([(len_hbm, lengths)], sem_s)
    placed_ref[...] = jnp.zeros_like(placed_ref)
    load.wait()
    req, rows, _ = out_k.shape
    slots = rows // 2
    most = slots // SLOTS
    seq = lax.axis_index("seq")
    if n_seq == 2:
        start = (1 - seq) * (4 * slots) + seq * (2 * slots)
    else:
        start = seq * (4 * slots) + sent * (2 * slots)
    ahead, live, _ = offsets(lengths, start, most)
    held = part.shape[1] // SLOTS
    for phase in ("start", "wait"):
        for r in range(req):
            low = jnp.clip(first - ahead[r], 0, live[r])
            high = jnp.clip(first + held - ahead[r], 0, live[r])
            for blocks in range(1, most + 1):

                @pl.when(high - low == blocks)
                def _(r=r, low=low, size=blocks * SLOTS):
                    begin = pl.multiple_of((ahead[r] + low - first) * SLOTS, SLOTS)
                    end = pl.multiple_of(sent * slots + low * SLOTS, SLOTS)
                    for i, out in enumerate((out_k, out_v)):
                        copy = pltpu.make_async_copy(
                            part.at[i, pl.ds(begin, size), :],
                            out.at[r, pl.ds(end, size), :],
                            sem.at[i, r],
                        )
                        getattr(copy, phase)()


def place_part(n_seq, first, part, lengths, out_k, out_v):
    hbm = pl.BlockSpec(memory_space=pl.ANY)
    vmem = pl.BlockSpec(memory_space=pltpu.VMEM)
    shape = pltpu.HBM(out_k.shape, out_k.dtype)
    return pl.pallas_call(
        functools.partial(place_kernel, n_seq, first),
        out_shape=(shape, shape, pltpu.VMEM((8, LANES), jnp.float32)),
        in_specs=[vmem, hbm, hbm, hbm],
        out_specs=(hbm, hbm, vmem),
        scratch_shapes=[
            pltpu.SMEM(lengths.shape, jnp.int32),
            pltpu.SemaphoreType.DMA((1,)),
            pltpu.SemaphoreType.DMA((2, lengths.shape[0])),
        ],
        input_output_aliases={2: 0, 3: 1},
        compiler_params=pltpu.CompilerParams(vmem_limit_bytes=VMEM_LIMIT),
        cost_estimate=LIGHT,
        name="place_received",
    )(*near(part), *far(lengths, out_k, out_v))


def others(value, axis):
    count = lax.axis_size(axis)
    return [value] + [
        lax.ppermute(value, axis, [(i, (i + k) % count) for i in range(count)])
        for k in range(1, count)
    ]


def swap(value, n_seq):
    return lax.ppermute(value, "seq", [(0, 1), (1, 0)]) if n_seq == 2 else value


def shards(
    keys, values, log_forget, keep, merge_weight, lengths, route, fresh, new_forget, out_weight
):
    req, pos, width = keys.shape
    heads = log_forget.shape[1]
    size = width // heads
    n_seq, n_grp = lax.axis_size("seq"), lax.axis_size("grp")
    early, packed, choice = first_part(
        n_seq,
        lengths,
        keep,
        merge_weight,
        fresh.reshape(3 * req, width),
        new_forget,
        keys,
        values,
    )
    exchange = functools.partial(swap, n_seq=n_seq)
    first_received = exchange(early)
    tokens = others(packed, "grp")
    out_k, out_v, late, logs, level, total = own_part(
        n_seq,
        lengths,
        keep,
        merge_weight,
        log_forget.transpose(1, 0, 2),
        keys,
        values,
        early,
    )
    out_k, out_v, stats, picked = attend_part(
        n_seq, n_grp, heads, lengths, route, out_k, out_v, late, level, total, tokens
    )

    sent_first = FIRST * SLOTS
    rest = late.shape[1] - sent_first

    def finish(rows, early, late, stats, picked, out_weight, logs, lengths, out_k, out_v):
        if n_seq == 2:
            all_stats = others(stats, "seq")
        else:
            gathered = lax.all_gather(stats, "seq")
            all_stats = [gathered[i] for i in range(n_seq)]
        received = exchange(late[:, sent_first : sent_first + rows])
        decay, partial = merge_part(all_stats, n_seq == 2, picked, out_weight, logs, size)
        out_k, out_v, placed = place_part(n_seq, 0, early, lengths, out_k, out_v)
        layer_out = sum_part(others(partial, "head"), placed)
        out_k, out_v, _ = place_part(n_seq, FIRST, received, lengths, out_k, out_v)
        return decay, layer_out, out_k, out_v

    operands = (first_received, late, stats, picked, out_weight, logs, lengths, out_k, out_v)
    if n_seq == 2:
        step = STEP * SLOTS
        branches = [
            functools.partial(finish, rows) for rows in range(step, rest + 1, step)
        ]
        decay, layer_out, out_k, out_v = lax.switch(choice[0], branches, *operands)
    else:
        decay, layer_out, out_k, out_v = finish(rest, *operands)
    if n_seq != 2:
        out_k, out_v = (
            lax.all_to_all(x, "seq", split_axis=1, concat_axis=1, tiled=True) for x in (out_k, out_v)
        )
    return out_k, out_v, decay.transpose(1, 0, 2), layer_out


def solution(mesh):
    return jax.shard_map(
        shards,
        mesh=mesh,
        in_specs=(
            P("grp", "seq", "head"),
            P("grp", "seq", "head"),
            P("grp", "head", "seq"),
            P("grp", "seq"),
            P("grp", "seq"),
            P("grp"),
            P("grp"),
            P(None, "grp", "head"),
            P("grp", "head"),
            P("head", "seq"),
        ),
        out_specs=(
            P("grp", "seq", "head"),
            P("grp", "seq", "head"),
            P("grp", "head", "seq"),
            P("grp", "seq"),
        ),
        check_vma=False,
    )
```

```python
import functools

import jax
import jax.numpy as jnp
from jax import lax
from jax.experimental import pallas as pl
from jax.experimental.pallas import tpu as pltpu
from jax.sharding import PartitionSpec as P

BLOCK = 64
SLOTS = 32
LANES = 128
BLOCK_LOG = BLOCK.bit_length() - 1
SLOT_LOG = SLOTS.bit_length() - 1
EMPTY_LOG = -10000.0
FIRST = 10
SIZES = (3, 6, 8, 10, 12, 14, 17)
SURE = 3
VMEM_LIMIT = 16 * 1024 * 1024


LIGHT = pl.CostEstimate(flops=1, bytes_accessed=1, transcendentals=0)
MERGE = pl.CostEstimate(flops=1 << 36, bytes_accessed=1, transcendentals=0)


def dot(a, b):
    return lax.dot_general(a, b, (((1,), (0,)), ((), ())), preferred_element_type=jnp.float32)


def dot_nt(a, b):
    return lax.dot_general(a, b, (((1,), (1,)), ((), ())), preferred_element_type=jnp.float32)


def iota(shape, dim):
    return lax.broadcasted_iota(jnp.int32, shape, dim)


def three(x):
    hi = x.astype(jnp.bfloat16).astype(jnp.float32)
    rest = x - hi
    mid = rest.astype(jnp.bfloat16).astype(jnp.float32)
    return hi, mid, rest - mid


def split_dot(x, ones):
    rows = x.shape[0]
    parts = dot(jnp.concatenate(three(x), axis=0).astype(jnp.bfloat16), ones)
    return parts[:rows] + parts[rows : 2 * rows] + parts[2 * rows :]


def half_of(axis, count):
    own = lax.axis_index(axis) if count == 2 else jnp.int32(0)
    return own, 1 - own


def by_row(ref, row):
    picked = jnp.zeros_like(row)
    for r in range(ref.shape[0]):
        picked = jnp.where(row == r, ref[r], picked)
    return picked


def live_blocks(lengths, r, start, most):
    return jnp.clip((lengths[r] - start) >> BLOCK_LOG, 0, most)


def offsets(lengths, start, most):
    total = jnp.int32(0)
    ahead, live = [], []
    for r in range(lengths.shape[0]):
        ahead.append(total)
        live.append(live_blocks(lengths, r, start, most))
        total = total + live[-1]
    return ahead, live, total


def plan(keep, weight, start, len_ref):
    rows, width = keep.shape
    one, two = iota((width, width), 0), iota((width, width), 1)
    same = (one ^ two) < BLOCK
    upto = (same & (one <= two)).astype(jnp.float32).astype(jnp.bfloat16)
    block = same.astype(jnp.float32).astype(jnp.bfloat16)
    kept = keep == 1
    rank = dot(keep.astype(jnp.float32).astype(jnp.bfloat16), upto) - 1.0
    weighted = jnp.where(kept, 0.0, weight)
    share = (weighted / split_dot(weighted, block)).astype(jnp.bfloat16).astype(jnp.float32)
    lane, row = iota((rows, width), 1), iota((rows, width), 0)
    slot = jnp.where(kept, rank.astype(jnp.int32), SLOTS - 1) + (lane >> BLOCK_LOG) * SLOTS
    slot = jnp.where(start + lane < by_row(len_ref, row), slot, -1)
    return slot, jnp.where(kept, 1.0, share)


def select(slot, factor, r):
    width = slot.shape[1]
    shape = (width // 2, width)
    hit = iota(shape, 0) == slot[r : r + 1, :]
    return jnp.where(hit, jnp.broadcast_to(factor[r : r + 1, :], shape), 0.0).astype(jnp.bfloat16)


def lanes(half, width):
    return pl.ds(pl.multiple_of(half * width, width), width)


def far(*arrays):
    return [pltpu.with_memory_space_constraint(x, pltpu.HBM) for x in arrays]


def near(*arrays):
    return [pltpu.with_memory_space_constraint(x, pltpu.VMEM) for x in arrays]


def fetch(pairs, sem):
    copies = [pltpu.make_async_copy(src, dst, sem.at[i]) for i, (src, dst) in enumerate(pairs)]
    for copy in copies:
        copy.start()
    return copies


def store_blocks(out, i, rows, ahead, live, low, high):
    for b in range(rows.shape[0] // SLOTS):
        number = ahead + b

        @pl.when((b < live) & (number >= low) & (number < high))
        def _(b=b, number=number):
            at = pl.ds(pl.multiple_of((number - low) * SLOTS, SLOTS), SLOTS)
            out[i, at, :] = rows[b * SLOTS : (b + 1) * SLOTS]


def rest_kernel(n_seq, len_hbm, keep_hbm, weight_hbm, keys, values, early, out, *rest):
    lengths, keep, weight, raw, sem_s, sem_r = rest
    _, sent = half_of("seq", n_seq)
    req, width = keep.shape
    most = width // BLOCK
    small = fetch(
        [
            (len_hbm, lengths),
            (keep_hbm.at[:, lanes(sent, width)], keep),
            (weight_hbm.at[:, lanes(sent, width)], weight),
        ],
        sem_s,
    )
    for copy in small:
        copy.wait()
    start = lax.axis_index("seq") * (2 * width) + sent * width
    ahead, live, _ = offsets(lengths, start, most)
    begin = FIRST // most

    def slab(i, r):
        source = (keys, values)[i].at[r, lanes(sent, width), :]
        return pltpu.make_async_copy(source, raw.at[i, r - begin], sem_r.at[i, r - begin])

    needed = [ahead[r] + live[r] > FIRST for r in range(begin, req)]
    for r in range(begin, req):

        @pl.when(needed[r - begin])
        def _(r=r):
            for i in range(2):
                slab(i, r).start()

    slot, factor = plan(keep[...], weight[...], start, lengths)
    for r in range(begin, req):

        @pl.when(needed[r - begin])
        def _(r=r):
            chosen = select(slot, factor, r)
            for i in range(2):
                slab(i, r).wait()
                rows = dot(chosen, raw[i, r - begin]).astype(jnp.bfloat16)
                store_blocks(out, i, rows, ahead[r], live[r], FIRST, req * most)


def rest_part(n_seq, lengths, keep, weight, keys, values, early):
    req, pos, width = keys.shape
    half = pos // 2
    most = half // BLOCK
    late = req - FIRST // most
    hbm = pl.BlockSpec(memory_space=pl.ANY)
    vmem = pl.BlockSpec(memory_space=pltpu.VMEM)
    return pl.pallas_call(
        functools.partial(rest_kernel, n_seq),
        out_shape=pltpu.VMEM((2, (req * most - FIRST) * SLOTS, width), jnp.bfloat16),
        in_specs=[hbm] * 6,
        out_specs=vmem,
        scratch_shapes=[
            pltpu.SMEM(lengths.shape, jnp.int32),
            pltpu.VMEM((req, half), jnp.int32),
            pltpu.VMEM((req, half), jnp.float32),
            pltpu.VMEM((2, late, half, width), jnp.bfloat16),
            pltpu.SemaphoreType.DMA((3,)),
            pltpu.SemaphoreType.DMA((2, late)),
        ],
        compiler_params=pltpu.CompilerParams(vmem_limit_bytes=VMEM_LIMIT),
        cost_estimate=LIGHT,
        name="compact_rest_sent",
    )(*far(lengths, keep, weight, keys, values), early)


def first_kernel(n_seq, len_hbm, keep_hbm, weight_hbm, fresh_hbm, gate_hbm, keys, values, *rest):
    out, packed, size_ref, lengths, keep, weight, fresh, gates, raw, sem_s, sem_r = rest
    _, sent = half_of("seq", n_seq)
    req, width = keep.shape
    most = width // BLOCK
    small = fetch(
        [
            (len_hbm, lengths),
            (keep_hbm.at[:, lanes(sent, width)], keep),
            (weight_hbm.at[:, lanes(sent, width)], weight),
            (fresh_hbm, fresh),
            (gate_hbm, gates),
        ],
        sem_s,
    )

    def slab(i, r):
        source = (keys, values)[i].at[r, lanes(sent, width), :]
        return pltpu.make_async_copy(source, raw.at[i, r], sem_r.at[i, r])

    sure = min(SURE, req)
    for r in range(sure):
        for i in range(2):
            slab(i, r).start()
    for copy in small:
        copy.wait()
    start = lax.axis_index("seq") * (2 * width) + sent * width
    ahead, live, _ = offsets(lengths, start, most)
    for r in range(sure, req):

        @pl.when(ahead[r] < FIRST)
        def _(r=r):
            for i in range(2):
                slab(i, r).start()

    slot, factor = plan(keep[...], weight[...], start, lengths)
    _, _, total = offsets(lengths, width, most)
    choice = jnp.int32(0)
    for size in SIZES:
        choice = choice + (total - FIRST > size).astype(jnp.int32)
    size_ref[0] = choice

    new, gate = fresh[...].astype(jnp.float32), gates[...].astype(jnp.float32)
    heads = gate.shape[1]
    lane = iota((req, new.shape[1]), 1)
    size = new.shape[1] // heads
    spread = jnp.zeros((req, new.shape[1]), jnp.float32)
    for h in range(heads):
        inside = (lane >= h * size) & (lane < (h + 1) * size)
        spread = jnp.where(inside, gate[:, h : h + 1], spread)
    packed[...] = jnp.concatenate([new, spread], axis=0).astype(jnp.bfloat16)

    def pack(r):
        chosen = select(slot, factor, r)
        for i in range(2):
            slab(i, r).wait()
            rows = dot(chosen, raw[i, r]).astype(jnp.bfloat16)
            if (r + 1) * most <= FIRST:
                at = pl.ds(pl.multiple_of(ahead[r] * SLOTS, SLOTS), most * SLOTS)
                out[i, at, :] = rows
            else:
                store_blocks(out, i, rows, ahead[r], live[r], 0, FIRST)

    for r in range(req):
        if r < sure:
            pack(r)
        else:
            pl.when(ahead[r] < FIRST)(functools.partial(pack, r))


def first_part(n_seq, lengths, keep, weight, fresh, gates, keys, values):
    req, pos, width = keys.shape
    half = pos // 2
    hbm = pl.BlockSpec(memory_space=pl.ANY)
    vmem = pl.BlockSpec(memory_space=pltpu.VMEM)
    return pl.pallas_call(
        functools.partial(first_kernel, n_seq),
        out_shape=(
            pltpu.VMEM((2, FIRST * SLOTS, width), jnp.bfloat16),
            pltpu.VMEM((fresh.shape[0] + req, width), jnp.bfloat16),
            jax.ShapeDtypeStruct((1,), jnp.int32),
        ),
        in_specs=[hbm] * 7,
        out_specs=(vmem, vmem, pl.BlockSpec(memory_space=pltpu.SMEM)),
        scratch_shapes=[
            pltpu.SMEM(lengths.shape, jnp.int32),
            pltpu.VMEM((req, half), jnp.int32),
            pltpu.VMEM((req, half), jnp.float32),
            pltpu.VMEM(fresh.shape, fresh.dtype),
            pltpu.VMEM(gates.shape, gates.dtype),
            pltpu.VMEM((2, req, half, width), jnp.bfloat16),
            pltpu.SemaphoreType.DMA((5,)),
            pltpu.SemaphoreType.DMA((2, req)),
        ],
        compiler_params=pltpu.CompilerParams(vmem_limit_bytes=VMEM_LIMIT),
        cost_estimate=LIGHT,
        name="compact_first_sent",
    )(*far(lengths, keep, weight, fresh, gates, keys, values))


def fill_gates(forget, gates, lengths, start):
    heads, req, pos = gates.shape
    pad = forget.shape[1] // req
    forget[...] = jnp.zeros_like(forget)
    live = start + iota((req, pos), 1) < by_row(lengths, iota((req, pos), 0))
    for h in range(heads):
        gate = jnp.where(live, gates[h], 0.0)
        for c in range(pos // LANES):
            forget[c, pl.ds(h, req, stride=pad), :] = gate[:, c * LANES : (c + 1) * LANES]
    return jnp.concatenate([forget[c] for c in range(pos // LANES)], axis=1)


def mask(condition):
    return condition.astype(jnp.float32).astype(jnp.bfloat16)


def own_kernel(n_seq, len_hbm, keep_hbm, weight_hbm, forget_hbm, keys, values, after_ref, *rest):
    out_k, out_v, log_ref, lengths, keep, weight, gates, raw, forget, level, rows = rest[:11]
    zeros, sem_s, sem_r, sem_o, sem_z = rest[11:]
    own, sent = half_of("seq", n_seq)
    seq = lax.axis_index("seq")
    heads, req, pos = forget_hbm.shape
    half = pos // 2
    slots = half // 2
    pad = forget.shape[1] // req
    small = fetch(
        [(len_hbm, lengths), (keep_hbm, keep), (weight_hbm, weight), (forget_hbm, gates)], sem_s
    )
    slabs = fetch(
        [
            (source.at[r, lanes(own, half), :], raw.at[i, r])
            for r in range(req)
            for i, source in enumerate((keys, values))
        ],
        sem_r,
    )
    zeros[...] = jnp.zeros_like(zeros)
    stores = fetch([(zeros, out.at[:, lanes(sent, slots), :]) for out in (out_k, out_v)], sem_z)
    for copy in small:
        copy.wait()

    flat = fill_gates(forget, gates, lengths, seq * pos)
    one, two = iota((half, half), 0), iota((half, half), 1)
    after = mask(((one ^ two) < BLOCK) & (one > two))
    ends = iota((pos, slots), 1) >> SLOT_LOG
    begins = iota((pos, slots), 0) >> BLOCK_LOG
    last = iota((req * pad, slots), 1) & (SLOTS - 1) == SLOTS - 1

    for i, h in enumerate((own, sent)):
        slot, factor = plan(
            keep[:, lanes(h, half)], weight[:, lanes(h, half)], seq * pos + h * half, lengths
        )
        count = half // LANES
        inner = split_dot(
            jnp.concatenate([forget[h * count + c] for c in range(count)], axis=1), after
        )
        beyond = split_dot(flat, mask(begins > ends + h * (half // BLOCK)))
        spread = jnp.exp(inner)
        high = spread.astype(jnp.bfloat16).astype(jnp.float32)
        planes = three(inner) + (high, spread - high, jnp.ones_like(inner))
        found = []
        for r in range(req):
            chosen = select(slot, factor, r)
            stack = jnp.concatenate([x[r * pad : (r + 1) * pad] for x in planes], axis=0)
            found.append(dot_nt(stack.astype(jnp.bfloat16), chosen))
            if i == 0:
                for k, out in enumerate((out_k, out_v)):
                    slabs[2 * r + k].wait()
                    rows[k, r] = dot(chosen, raw[k, r]).astype(jnp.bfloat16)
                    stores.append(
                        pltpu.make_async_copy(
                            rows.at[k, r], out.at[r, lanes(own, slots), :], sem_o.at[2 * r + k]
                        )
                    )
                    stores[-1].start()
        at = [
            jnp.concatenate([x[p * pad : (p + 1) * pad] for x in found], axis=0) for p in range(6)
        ]
        filled = at[5] > 0.5
        kept = at[0] + at[1] + at[2]
        merged = jnp.log(jnp.where(filled, at[3] + at[4], 1.0))
        level[...] = jnp.where(filled, jnp.where(last, merged, kept) + beyond, EMPTY_LOG)
        for k in range(heads):
            log_ref[k, :, lanes(h, slots)] = level[pl.ds(k, req, stride=pad), :]
    for copy in stores:
        copy.wait()


def own_part(n_seq, lengths, keep, weight, forget, keys, values, later):
    req, pos, width = keys.shape
    heads = forget.shape[0]
    half, slots, pad = pos // 2, pos // 4, -(-heads // 8) * 8
    hbm = pl.BlockSpec(memory_space=pl.ANY)
    vmem = pl.BlockSpec(memory_space=pltpu.VMEM)
    whole = pltpu.HBM((req, 2 * slots, width), jnp.bfloat16)
    return pl.pallas_call(
        functools.partial(own_kernel, n_seq),
        out_shape=(whole, whole, pltpu.VMEM((heads, req, 2 * slots), jnp.float32)),
        in_specs=[hbm] * 7,
        out_specs=(hbm, hbm, vmem),
        scratch_shapes=[
            pltpu.SMEM(lengths.shape, jnp.int32),
            pltpu.VMEM(keep.shape, keep.dtype),
            pltpu.VMEM(weight.shape, weight.dtype),
            pltpu.VMEM(forget.shape, forget.dtype),
            pltpu.VMEM((2, req, half, width), jnp.bfloat16),
            pltpu.VMEM((pos // LANES, req * pad, LANES), jnp.float32),
            pltpu.VMEM((req * pad, slots), jnp.float32),
            pltpu.VMEM((2, req, slots, width), jnp.bfloat16),
            pltpu.VMEM((req, slots, width), jnp.bfloat16),
            pltpu.SemaphoreType.DMA((4,)),
            pltpu.SemaphoreType.DMA((2 * req,)),
            pltpu.SemaphoreType.DMA((2 * req,)),
            pltpu.SemaphoreType.DMA((2,)),
        ],
        compiler_params=pltpu.CompilerParams(vmem_limit_bytes=VMEM_LIMIT),
        cost_estimate=LIGHT,
        name="compact_own",
    )(*far(lengths, keep, weight, forget, keys, values), later)


def attend_kernel(n_grp, len_hbm, route_hbm, keep_hbm, weight_hbm, forget_hbm, keys, values, *rest):
    tokens, rest = rest[:n_grp], rest[n_grp:]
    _, stats_ref, picked_ref, lengths, route, keep, weight, gates, raw_k, raw_v = rest[:10]
    forget, scores, sem_s, sem_k, sem_v = rest[10:]
    seq = lax.axis_index("seq")
    heads, req, pos = forget_hbm.shape
    kinds, width = picked_ref.shape
    half = pos // 2
    size = width // heads
    pad = forget.shape[1] // req
    small = fetch(
        [
            (len_hbm, lengths),
            (route_hbm, route),
            (keep_hbm, keep),
            (weight_hbm, weight),
            (forget_hbm, gates),
        ],
        sem_s,
    )
    key_slabs = fetch([(keys.at[r], raw_k.at[r]) for r in range(req)], sem_k)
    value_slabs = fetch([(values.at[r], raw_v.at[r]) for r in range(req)], sem_v)

    for copy in small:
        copy.wait()

    shape = (kinds, kinds)
    to, frm = iota(shape, 0), iota(shape, 1)
    wanted = by_row(route, to % req)
    me = lax.axis_index("grp")
    picked = jnp.zeros((kinds, width), jnp.float32)
    for k in range(n_grp):
        source = lax.rem(me + n_grp - k, n_grp)
        hit = (to // req == frm // req) & (wanted == source * req + frm % req)
        picked = picked + dot(mask(hit), tokens[k][...])
    picked_ref[...] = picked

    flat = fill_gates(forget, gates, lengths, seq * pos)
    total = jnp.sum(flat, axis=1, keepdims=True)
    one, two = iota((pos, pos), 0), iota((pos, pos), 1)
    to_end = split_dot(flat, mask(one > two))
    one, two = iota((half, half), 0), iota((half, half), 1)
    same = (one ^ two) < BLOCK
    after, block = mask(same & (one > two)), mask(same)

    def by_halves(x, ones):
        parts = [split_dot(x[:, i * half : (i + 1) * half], ones) for i in range(2)]
        return jnp.concatenate(parts, axis=1)

    inner = by_halves(flat, after)

    keeps = keep[...] == 1
    weighted = jnp.where(keeps, 0.0, weight[...])
    share = (weighted / by_halves(weighted, block)).astype(jnp.bfloat16).astype(jnp.float32)
    lane, row = iota((req, pos), 1), iota((req, pos), 0)
    live = (seq * pos + lane < by_row(lengths, row)).astype(jnp.float32)
    kept = jnp.where(keeps, live, 0.0)

    def all_heads(x):
        rows = [jnp.broadcast_to(x[r : r + 1, :], (pad, pos)) for r in range(req)]
        return jnp.concatenate(rows, axis=0)

    share, live, kept = all_heads(share), all_heads(live) > 0, all_heads(kept) > 0
    merged = (to_end - inner) + jnp.log(by_halves(share * jnp.exp(inner), block))

    lane, row = iota((pad, width), 1), iota((pad, width), 0)
    mine = (lane >= row * size) & (lane < (row + 1) * size)
    for r in range(req):
        query = jnp.where(mine, picked[r : r + 1, :], 0.0).astype(jnp.bfloat16)
        key_slabs[r].wait()
        scores[r * pad : (r + 1) * pad, :] = dot_nt(query, raw_k[r])
    score = scores[...] * (size**-0.5)
    own_logit = jnp.where(kept, score + to_end, EMPTY_LOG)
    merged_logit = jnp.where(live, by_halves(share * score, block) + merged, EMPTY_LOG)
    top = jnp.max(jnp.maximum(own_logit, merged_logit), axis=1, keepdims=True)

    def weights(logit, there):
        weight = jnp.where(there, jnp.exp(logit - top), 0.0)
        return weight.astype(jnp.bfloat16).astype(jnp.float32)

    own_weight, merged_weight = weights(own_logit, kept), weights(merged_logit, live)
    once = iota((req * pad, pos), 1) & (BLOCK - 1) == 0
    mass = jnp.sum(own_weight + jnp.where(once, merged_weight, 0.0), axis=1, keepdims=True)
    factor = (own_weight + share * merged_weight).astype(jnp.bfloat16)

    def spread_out(column, r):
        return jnp.sum(
            jnp.where(mine, column[r * pad : (r + 1) * pad], 0.0), axis=0, keepdims=True
        )

    for r in range(req):
        value_slabs[r].wait()
        acc = dot(factor[r * pad : (r + 1) * pad], raw_v[r])
        acc = jnp.sum(jnp.where(mine, acc, 0.0), axis=0, keepdims=True)
        for p, x in enumerate((top, mass, total)):
            stats_ref[p * req + r : p * req + r + 1, :] = spread_out(x, r)
        stats_ref[3 * req + r : 3 * req + r + 1, :] = acc


def attend_part(n_grp, lengths, route, keep, weight, forget, keys, values, tokens, late):
    req, pos, width = keys.shape
    heads = forget.shape[0]
    pad = -(-heads // 8) * 8
    hbm = pl.BlockSpec(memory_space=pl.ANY)
    vmem = pl.BlockSpec(memory_space=pltpu.VMEM)
    small = pltpu.VMEM((4 * req, width), jnp.float32)
    return pl.pallas_call(
        functools.partial(attend_kernel, n_grp),
        out_shape=(small, small),
        in_specs=[hbm] * 7 + [vmem] * n_grp + [hbm],
        out_specs=(vmem, vmem),
        scratch_shapes=[
            pltpu.SMEM(lengths.shape, jnp.int32),
            pltpu.SMEM(route.shape, jnp.int32),
            pltpu.VMEM(keep.shape, keep.dtype),
            pltpu.VMEM(weight.shape, weight.dtype),
            pltpu.VMEM(forget.shape, forget.dtype),
            pltpu.VMEM(keys.shape, keys.dtype),
            pltpu.VMEM(values.shape, values.dtype),
            pltpu.VMEM((pos // LANES, req * pad, LANES), jnp.float32),
            pltpu.VMEM((req * pad, pos), jnp.float32),
            pltpu.SemaphoreType.DMA((5,)),
            pltpu.SemaphoreType.DMA((req,)),
            pltpu.SemaphoreType.DMA((req,)),
        ],
        compiler_params=pltpu.CompilerParams(vmem_limit_bytes=VMEM_LIMIT),
        cost_estimate=LIGHT,
        name="attend",
    )(*far(lengths, route, keep, weight, forget, keys, values), *near(*tokens), late)


def merge_kernel(count, relative, size, *refs):
    stats, refs = refs[:count], refs[count:]
    picked_ref, weight_ref, later_ref, out_ref = refs
    req, width = later_ref.shape
    seq = lax.axis_index("seq")
    places = [lax.rem(seq + count - k, count) if relative else jnp.int32(k) for k in range(count)]
    tops, masses, totals, accs = [
        [ref[p * req : (p + 1) * req, :] for ref in stats] for p in range(4)
    ]

    def later(place):
        total = jnp.zeros_like(totals[0])
        for k in range(count):
            total = total + jnp.where(places[k] > place, totals[k], 0.0)
        return total

    tops = [tops[k] + later(places[k]) for k in range(count)]
    top = functools.reduce(jnp.maximum, tops)
    scales = [jnp.exp(t - top) for t in tops]
    mass = sum(s * x for s, x in zip(scales, masses))
    acc = sum(s * x for s, x in zip(scales, accs))
    query, key, value, gate = [picked_ref[p * req : (p + 1) * req, :] for p in range(4)]
    one, two = iota((width, width), 0), iota((width, width), 1)
    same = (one // size == two // size).astype(jnp.float32).astype(jnp.bfloat16)
    own = split_dot(query * key, same) * (size**-0.5)
    past = top + gate
    joint = jnp.maximum(past, own)
    scale, self_weight = jnp.exp(past - joint), jnp.exp(own - joint)
    attended = (scale * acc + self_weight * value) / (scale * mass + self_weight)
    later_ref[...] = later(seq)
    out_ref[...] = dot(attended.astype(jnp.bfloat16), weight_ref[...])


def merge_part(stats, relative, picked, out_weight, size):
    req, width = stats[0].shape[0] // 4, stats[0].shape[1]
    vmem = pl.BlockSpec(memory_space=pltpu.VMEM)
    return pl.pallas_call(
        functools.partial(merge_kernel, len(stats), relative, size),
        out_shape=(
            pltpu.VMEM((req, width), jnp.float32),
            pltpu.VMEM((req, out_weight.shape[1]), jnp.float32),
        ),
        in_specs=[vmem] * (len(stats) + 2),
        out_specs=(vmem, vmem),
        compiler_params=pltpu.CompilerParams(vmem_limit_bytes=VMEM_LIMIT),
        cost_estimate=MERGE,
        name="merge_and_project",
    )(*near(*stats, picked, out_weight))


def sum_kernel(count, size, *refs):
    parts, (later_ref, log_ref, _, out, decay_ref) = refs[:count], refs[count:]
    me = lax.axis_index("head")
    total = jnp.zeros(out.shape, jnp.float32)
    for place in range(count):
        for k in range(count):
            total = total + jnp.where(lax.rem(me + count - k, count) == place, parts[k][...], 0.0)
    out[...] = total.astype(out.dtype)
    for h in range(log_ref.shape[0]):
        decay_ref[h] = jnp.exp(log_ref[h] + later_ref[:, h * size : h * size + 1])


def sum_part(parts, later, logs, placed, size):
    vmem = pl.BlockSpec(memory_space=pltpu.VMEM)
    return pl.pallas_call(
        functools.partial(sum_kernel, len(parts), size),
        out_shape=(
            pltpu.HBM(parts[0].shape, jnp.bfloat16),
            pltpu.HBM(logs.shape, jnp.float32),
        ),
        in_specs=[vmem] * (len(parts) + 3),
        out_specs=(vmem, vmem),
        compiler_params=pltpu.CompilerParams(vmem_limit_bytes=VMEM_LIMIT),
        cost_estimate=LIGHT,
        name="sum_heads_and_decay",
    )(*parts, later, logs, placed)


def place_kernel(n_seq, first, part, len_hbm, old_k, old_v, out_k, out_v, *rest):
    _, sent = half_of("seq", n_seq)
    placed_ref, lengths, sem_s, sem = rest
    (load,) = fetch([(len_hbm, lengths)], sem_s)
    placed_ref[...] = jnp.zeros_like(placed_ref)
    load.wait()
    req, rows, _ = out_k.shape
    slots = rows // 2
    most = slots // SLOTS
    seq = lax.axis_index("seq")
    if n_seq == 2:
        start = (1 - seq) * (4 * slots) + seq * (2 * slots)
    else:
        start = seq * (4 * slots) + sent * (2 * slots)
    ahead, live, _ = offsets(lengths, start, most)
    held = part.shape[1] // SLOTS
    for phase in ("start", "wait"):
        for r in range(req):
            low = jnp.clip(first - ahead[r], 0, live[r])
            high = jnp.clip(first + held - ahead[r], 0, live[r])
            for blocks in range(1, most + 1):

                @pl.when(high - low == blocks)
                def _(r=r, low=low, size=blocks * SLOTS):
                    begin = pl.multiple_of((ahead[r] + low - first) * SLOTS, SLOTS)
                    end = pl.multiple_of(sent * slots + low * SLOTS, SLOTS)
                    for i, out in enumerate((out_k, out_v)):
                        copy = pltpu.make_async_copy(
                            part.at[i, pl.ds(begin, size), :],
                            out.at[r, pl.ds(end, size), :],
                            sem.at[i, r],
                        )
                        getattr(copy, phase)()


def place_part(n_seq, first, part, lengths, out_k, out_v):
    hbm = pl.BlockSpec(memory_space=pl.ANY)
    vmem = pl.BlockSpec(memory_space=pltpu.VMEM)
    shape = pltpu.HBM(out_k.shape, out_k.dtype)
    return pl.pallas_call(
        functools.partial(place_kernel, n_seq, first),
        out_shape=(shape, shape, pltpu.VMEM((8, LANES), jnp.float32)),
        in_specs=[vmem, hbm, hbm, hbm],
        out_specs=(hbm, hbm, vmem),
        scratch_shapes=[
            pltpu.SMEM(lengths.shape, jnp.int32),
            pltpu.SemaphoreType.DMA((1,)),
            pltpu.SemaphoreType.DMA((2, lengths.shape[0])),
        ],
        input_output_aliases={2: 0, 3: 1},
        compiler_params=pltpu.CompilerParams(vmem_limit_bytes=VMEM_LIMIT),
        cost_estimate=LIGHT,
        name="place_received",
    )(*near(part), *far(lengths, out_k, out_v))


def others(value, axis):
    count = lax.axis_size(axis)
    return [value] + [
        lax.ppermute(value, axis, [(i, (i + k) % count) for i in range(count)])
        for k in range(1, count)
    ]


def swap(value, n_seq):
    return lax.ppermute(value, "seq", [(0, 1), (1, 0)]) if n_seq == 2 else value


def shards(
    keys, values, log_forget, keep, merge_weight, lengths, route, fresh, new_forget, out_weight
):
    req, pos, width = keys.shape
    heads = log_forget.shape[1]
    size = width // heads
    n_seq, n_grp = lax.axis_size("seq"), lax.axis_size("grp")
    early, packed, choice = first_part(
        n_seq,
        lengths,
        keep,
        merge_weight,
        fresh.reshape(3 * req, width),
        new_forget,
        keys,
        values,
    )
    exchange = functools.partial(swap, n_seq=n_seq)
    first_received = exchange(early)
    tokens = others(packed, "grp")
    late = rest_part(n_seq, lengths, keep, merge_weight, keys, values, early)
    forget = log_forget.transpose(1, 0, 2)
    stats, picked = attend_part(
        n_grp, lengths, route, keep, merge_weight, forget, keys, values, tokens, late
    )

    def finish(rows, early, late, stats, picked, out_weight, *cache):
        if n_seq == 2:
            all_stats = others(stats, "seq")
        else:
            gathered = lax.all_gather(stats, "seq")
            all_stats = [gathered[i] for i in range(n_seq)]
        received = exchange(late[:, :rows])
        later, partial = merge_part(all_stats, n_seq == 2, picked, out_weight, size)
        out_k, out_v, logs = own_part(n_seq, *cache, later)
        out_k, out_v, placed = place_part(n_seq, 0, early, lengths, out_k, out_v)
        layer_out, decay = sum_part(others(partial, "head"), later, logs, placed, size)
        out_k, out_v, _ = place_part(n_seq, FIRST, received, lengths, out_k, out_v)
        return decay, layer_out, out_k, out_v

    cache = (lengths, keep, merge_weight, forget, keys, values)
    operands = (first_received, late, stats, picked, out_weight) + cache
    if n_seq == 2:
        branches = [
            functools.partial(finish, size * SLOTS)
            for size in SIZES + (late.shape[1] // SLOTS,)
        ]
        decay, layer_out, out_k, out_v = lax.switch(choice[0], branches, *operands)
    else:
        decay, layer_out, out_k, out_v = finish(late.shape[1], *operands)
    if n_seq != 2:
        out_k, out_v = (
            lax.all_to_all(x, "seq", split_axis=1, concat_axis=1, tiled=True) for x in (out_k, out_v)
        )
    return out_k, out_v, decay.transpose(1, 0, 2), layer_out


def solution(mesh):
    return jax.shard_map(
        shards,
        mesh=mesh,
        in_specs=(
            P("grp", "seq", "head"),
            P("grp", "seq", "head"),
            P("grp", "head", "seq"),
            P("grp", "seq"),
            P("grp", "seq"),
            P("grp"),
            P("grp"),
            P(None, "grp", "head"),
            P("grp", "head"),
            P("head", "seq"),
        ),
        out_specs=(
            P("grp", "seq", "head"),
            P("grp", "seq", "head"),
            P("grp", "head", "seq"),
            P("grp", "seq"),
        ),
        check_vma=False,
    )
```

```python
import functools

import jax
import jax.numpy as jnp
from jax import lax
from jax.experimental import pallas as pl
from jax.experimental.pallas import tpu as pltpu
from jax.sharding import PartitionSpec as P

BLOCK = 64
SLOTS = 32
LANES = 128
BLOCK_LOG = BLOCK.bit_length() - 1
SLOT_LOG = SLOTS.bit_length() - 1
EMPTY_LOG = -10000.0
FIRST = 11
SECOND = 4
SIZES = (1, 3, 5, 7, 9, 12)
SURE = 3
VMEM_LIMIT = 16 * 1024 * 1024


LIGHT = pl.CostEstimate(flops=1, bytes_accessed=1, transcendentals=0)
MERGE = pl.CostEstimate(flops=1 << 36, bytes_accessed=1, transcendentals=0)


def dot(a, b):
    return lax.dot_general(a, b, (((1,), (0,)), ((), ())), preferred_element_type=jnp.float32)


def dot_nt(a, b):
    return lax.dot_general(a, b, (((1,), (1,)), ((), ())), preferred_element_type=jnp.float32)


def iota(shape, dim):
    return lax.broadcasted_iota(jnp.int32, shape, dim)


def three(x):
    hi = x.astype(jnp.bfloat16).astype(jnp.float32)
    rest = x - hi
    mid = rest.astype(jnp.bfloat16).astype(jnp.float32)
    return hi, mid, rest - mid


def split_dot(x, ones):
    rows = x.shape[0]
    parts = dot(jnp.concatenate(three(x), axis=0).astype(jnp.bfloat16), ones)
    return parts[:rows] + parts[rows : 2 * rows] + parts[2 * rows :]


def half_of(axis, count):
    own = lax.axis_index(axis) if count == 2 else jnp.int32(0)
    return own, 1 - own


def by_row(ref, row):
    picked = jnp.zeros_like(row)
    for r in range(ref.shape[0]):
        picked = jnp.where(row == r, ref[r], picked)
    return picked


def live_blocks(lengths, r, start, most):
    return jnp.clip((lengths[r] - start) >> BLOCK_LOG, 0, most)


def offsets(lengths, start, most):
    total = jnp.int32(0)
    ahead, live = [], []
    for r in range(lengths.shape[0]):
        ahead.append(total)
        live.append(live_blocks(lengths, r, start, most))
        total = total + live[-1]
    return ahead, live, total


def plan(keep, weight, start, len_ref):
    rows, width = keep.shape
    one, two = iota((width, width), 0), iota((width, width), 1)
    same = (one ^ two) < BLOCK
    upto = (same & (one <= two)).astype(jnp.float32).astype(jnp.bfloat16)
    block = same.astype(jnp.float32).astype(jnp.bfloat16)
    kept = keep == 1
    rank = dot(keep.astype(jnp.float32).astype(jnp.bfloat16), upto) - 1.0
    weighted = jnp.where(kept, 0.0, weight)
    share = (weighted / split_dot(weighted, block)).astype(jnp.bfloat16).astype(jnp.float32)
    lane, row = iota((rows, width), 1), iota((rows, width), 0)
    slot = jnp.where(kept, rank.astype(jnp.int32), SLOTS - 1) + (lane >> BLOCK_LOG) * SLOTS
    slot = jnp.where(start + lane < by_row(len_ref, row), slot, -1)
    return slot, jnp.where(kept, 1.0, share)


def select(slot, factor, r):
    width = slot.shape[1]
    shape = (width // 2, width)
    hit = iota(shape, 0) == slot[r : r + 1, :]
    return jnp.where(hit, jnp.broadcast_to(factor[r : r + 1, :], shape), 0.0).astype(jnp.bfloat16)


def lanes(half, width):
    return pl.ds(pl.multiple_of(half * width, width), width)


def far(*arrays):
    return [pltpu.with_memory_space_constraint(x, pltpu.HBM) for x in arrays]


def near(*arrays):
    return [pltpu.with_memory_space_constraint(x, pltpu.VMEM) for x in arrays]


def fetch(pairs, sem):
    copies = [pltpu.make_async_copy(src, dst, sem.at[i]) for i, (src, dst) in enumerate(pairs)]
    for copy in copies:
        copy.start()
    return copies


def first_kernel(n_seq, len_hbm, keep_hbm, weight_hbm, fresh_hbm, gate_hbm, keys, values, *rest):
    out, packed, size_ref, lengths, keep, weight, fresh, gates, raw, sem_s, sem_r = rest
    _, sent = half_of("seq", n_seq)
    req, width = keep.shape
    most = width // BLOCK
    slots = most * SLOTS
    small = fetch(
        [
            (len_hbm, lengths),
            (keep_hbm.at[:, lanes(sent, width)], keep),
            (weight_hbm.at[:, lanes(sent, width)], weight),
            (fresh_hbm, fresh),
            (gate_hbm, gates),
        ],
        sem_s,
    )

    def slab(i, r):
        source = (keys, values)[i].at[r, lanes(sent, width), :]
        return pltpu.make_async_copy(source, raw.at[i, r], sem_r.at[i, r])

    sure = min(SURE, req)
    for r in range(sure):
        for i in range(2):
            slab(i, r).start()
    out[...] = jnp.zeros_like(out)
    for copy in small:
        copy.wait()
    start = lax.axis_index("seq") * (2 * width) + sent * width
    ahead, live, _ = offsets(lengths, start, most)
    for r in range(sure, req):

        @pl.when(ahead[r] < FIRST)
        def _(r=r):
            for i in range(2):
                slab(i, r).start()

    slot, factor = plan(keep[...], weight[...], start, lengths)
    _, _, total = offsets(lengths, width, most)
    choice = jnp.int32(0)
    for size in SIZES:
        choice = choice + (total - FIRST - SECOND > size).astype(jnp.int32)
    size_ref[0] = choice

    new, gate = fresh[...].astype(jnp.float32), gates[...].astype(jnp.float32)
    heads = gate.shape[1]
    lane = iota((req, new.shape[1]), 1)
    size = new.shape[1] // heads
    spread = jnp.zeros((req, new.shape[1]), jnp.float32)
    for h in range(heads):
        inside = (lane >= h * size) & (lane < (h + 1) * size)
        spread = jnp.where(inside, gate[:, h : h + 1], spread)
    packed[...] = jnp.concatenate([new, spread], axis=0).astype(jnp.bfloat16)

    def pack(r):
        chosen = select(slot, factor, r)
        for i in range(2):
            slab(i, r).wait()
            rows = dot(chosen, raw[i, r]).astype(jnp.bfloat16)
            if (r + 1) * most <= FIRST:
                at = pl.ds(pl.multiple_of(ahead[r] * SLOTS, SLOTS), slots)
                out[i, at, :] = rows
                continue
            for b in range(most):

                @pl.when((b < live[r]) & (ahead[r] + b < FIRST))
                def _(i=i, b=b, rows=rows):
                    at = pl.ds(pl.multiple_of((ahead[r] + b) * SLOTS, SLOTS), SLOTS)
                    out[i, at, :] = rows[b * SLOTS : (b + 1) * SLOTS]

    for r in range(req):
        if r < sure:
            pack(r)
        else:
            pl.when(ahead[r] < FIRST)(functools.partial(pack, r))


def first_part(n_seq, lengths, keep, weight, fresh, gates, keys, values):
    req, pos, width = keys.shape
    half = pos // 2
    hbm = pl.BlockSpec(memory_space=pl.ANY)
    vmem = pl.BlockSpec(memory_space=pltpu.VMEM)
    return pl.pallas_call(
        functools.partial(first_kernel, n_seq),
        out_shape=(
            pltpu.VMEM((2, FIRST * SLOTS, width), jnp.bfloat16),
            pltpu.VMEM((fresh.shape[0] + req, width), jnp.bfloat16),
            jax.ShapeDtypeStruct((1,), jnp.int32),
        ),
        in_specs=[hbm] * 7,
        out_specs=(vmem, vmem, pl.BlockSpec(memory_space=pltpu.SMEM)),
        scratch_shapes=[
            pltpu.SMEM(lengths.shape, jnp.int32),
            pltpu.VMEM((req, half), jnp.int32),
            pltpu.VMEM((req, half), jnp.float32),
            pltpu.VMEM(fresh.shape, fresh.dtype),
            pltpu.VMEM(gates.shape, gates.dtype),
            pltpu.VMEM((2, req, half, width), jnp.bfloat16),
            pltpu.SemaphoreType.DMA((5,)),
            pltpu.SemaphoreType.DMA((2, req)),
        ],
        compiler_params=pltpu.CompilerParams(vmem_limit_bytes=VMEM_LIMIT),
        cost_estimate=LIGHT,
        name="compact_first_sent",
    )(*far(lengths, keep, weight, fresh, gates, keys, values))


def own_kernel(
    n_seq, len_ref, keep, weight, gates, keys, values, early, *rest
):
    out_k, out_v, chunk, log_ref, level_ref, total_ref = rest[:6]
    lengths, raw, late, forget, rows, zeros, sem_s, sem_l, sem_r, sem_o, sem_z = rest[6:]
    own, sent = half_of("seq", n_seq)
    seq = lax.axis_index("seq")
    heads, req, pos = gates.shape
    half = pos // 2
    slots = half // 2
    most = half // BLOCK
    first = FIRST // most
    pad = forget.shape[1] // req
    small = fetch([(len_ref, lengths)], sem_s)
    both = ((0, keys), (1, values))
    late_slabs = fetch(
        [
            (source.at[r, lanes(sent, half), :], late.at[i, r - first])
            for r in range(first, req)
            for i, source in both
        ],
        sem_l,
    )
    slabs = fetch(
        [
            (source.at[r, lanes(own, half), :], raw.at[i, r])
            for r in range(req)
            for i, source in both
        ],
        sem_r,
    )
    zeros[...] = jnp.zeros_like(zeros)
    stores = fetch([(zeros, out.at[:, lanes(sent, slots), :]) for out in (out_k, out_v)], sem_z)
    chunk[:, : FIRST * SLOTS, :] = early[...]
    chunk[:, FIRST * SLOTS :, :] = jnp.zeros(
        (2, chunk.shape[1] - FIRST * SLOTS, chunk.shape[2]), chunk.dtype
    )
    for copy in small:
        copy.wait()
    ahead, alive, _ = offsets(lengths, seq * pos + sent * half, most)

    forget[...] = jnp.zeros_like(forget)
    live = seq * pos + iota((req, pos), 1) < by_row(lengths, iota((req, pos), 0))
    for h in range(heads):
        gate = jnp.where(live, gates[h], 0.0)
        for c in range(pos // LANES):
            forget[c, pl.ds(h, req, stride=pad), :] = gate[:, c * LANES : (c + 1) * LANES]
    flat = jnp.concatenate([forget[c] for c in range(pos // LANES)], axis=1)
    total_ref[...] = jnp.broadcast_to(jnp.sum(flat, axis=1, keepdims=True), total_ref.shape)
    one, two = iota((half, half), 0), iota((half, half), 1)
    after = (((one ^ two) < BLOCK) & (one > two)).astype(jnp.float32).astype(jnp.bfloat16)
    ends = iota((pos, slots), 1) >> SLOT_LOG
    begins = iota((pos, slots), 0) >> BLOCK_LOG
    last = iota((req * pad, slots), 1) & (SLOTS - 1) == SLOTS - 1

    for i, h in enumerate((own, sent)):
        slot, factor = plan(
            keep[:, lanes(h, half)], weight[:, lanes(h, half)], seq * pos + h * half, lengths
        )
        near = half // LANES
        inner = split_dot(
            jnp.concatenate([forget[h * near + c] for c in range(near)], axis=1), after
        )
        beyond = split_dot(
            flat, (begins > ends + h * (half // BLOCK)).astype(jnp.float32).astype(jnp.bfloat16)
        )
        spread = jnp.exp(inner)
        high = spread.astype(jnp.bfloat16).astype(jnp.float32)
        planes = three(inner) + (high, spread - high, jnp.ones_like(inner))
        found = []
        for r in range(req):
            chosen = select(slot, factor, r)
            stack = jnp.concatenate([x[r * pad : (r + 1) * pad] for x in planes], axis=0)
            found.append(dot_nt(stack.astype(jnp.bfloat16), chosen))
            if i == 0:
                for k, out in enumerate((out_k, out_v)):
                    slabs[2 * r + k].wait()
                    rows[k, r] = dot(chosen, raw[k, r]).astype(jnp.bfloat16)
                    stores.append(
                        pltpu.make_async_copy(
                            rows.at[k, r], out.at[r, lanes(own, slots), :], sem_o.at[2 * r + k]
                        )
                    )
                    stores[-1].start()
            elif r >= first:
                for k in range(2):
                    late_slabs[2 * (r - first) + k].wait()

                @pl.when(ahead[r] + alive[r] > FIRST)
                def _(r=r, chosen=chosen):
                    at = pl.ds(pl.multiple_of(ahead[r] * SLOTS, SLOTS), slots)
                    for k in range(2):
                        chunk[k, at, :] = dot(chosen, late[k, r - first]).astype(jnp.bfloat16)
        at = [
            jnp.concatenate([x[p * pad : (p + 1) * pad] for x in found], axis=0) for p in range(6)
        ]
        filled = at[5] > 0.5
        kept = at[0] + at[1] + at[2]
        merged = jnp.log(jnp.where(filled, at[3] + at[4], 1.0))
        level_ref[i] = jnp.where(filled, jnp.where(last, merged, kept) + beyond, EMPTY_LOG)
        for k in range(heads):
            log_ref[k, :, lanes(h, slots)] = level_ref[i, pl.ds(k, req, stride=pad), :]
    for copy in stores:
        copy.wait()


def own_part(n_seq, lengths, keep, weight, forget, keys, values, early):
    req, pos, width = keys.shape
    heads = forget.shape[0]
    half, slots, pad = pos // 2, pos // 4, -(-heads // 8) * 8
    late = req - FIRST // (half // BLOCK)
    hbm = pl.BlockSpec(memory_space=pl.ANY)
    vmem = pl.BlockSpec(memory_space=pltpu.VMEM)
    whole = pltpu.HBM((req, 2 * slots, width), jnp.bfloat16)
    return pl.pallas_call(
        functools.partial(own_kernel, n_seq),
        out_shape=(
            whole,
            whole,
            pltpu.VMEM((2, req * slots, width), jnp.bfloat16),
            pltpu.VMEM((heads, req, 2 * slots), jnp.float32),
            pltpu.VMEM((2, req * pad, slots), jnp.float32),
            pltpu.VMEM((req * pad, LANES), jnp.float32),
        ),
        in_specs=[vmem] * 4 + [hbm] * 2 + [vmem],
        out_specs=(hbm, hbm, vmem, vmem, vmem, vmem),
        scratch_shapes=[
            pltpu.SMEM(lengths.shape, jnp.int32),
            pltpu.VMEM((2, req, half, width), jnp.bfloat16),
            pltpu.VMEM((2, late, half, width), jnp.bfloat16),
            pltpu.VMEM((pos // LANES, req * pad, LANES), jnp.float32),
            pltpu.VMEM((2, req, slots, width), jnp.bfloat16),
            pltpu.VMEM((req, slots, width), jnp.bfloat16),
            pltpu.SemaphoreType.DMA((1,)),
            pltpu.SemaphoreType.DMA((2 * late,)),
            pltpu.SemaphoreType.DMA((2 * req,)),
            pltpu.SemaphoreType.DMA((2 * req,)),
            pltpu.SemaphoreType.DMA((2,)),
        ],
        compiler_params=pltpu.CompilerParams(vmem_limit_bytes=VMEM_LIMIT),
        cost_estimate=LIGHT,
        name="compact_own",
    )(*near(lengths, keep, weight, forget), *far(keys, values), *near(early))


def attend_kernel(n_seq, n_grp, heads, *refs):
    len_hbm, route_hbm, out_k, out_v, late, level, total = refs[:7]
    tokens, rest = refs[7 : 7 + n_grp], refs[7 + n_grp :]
    _, _, stats_ref, picked_ref, lengths, route, own_rows, scores, sem_s, sem_r = rest
    own, sent = half_of("seq", n_seq)
    kinds, width = picked_ref.shape
    req = kinds // 4
    size = width // heads
    slots = own_rows.shape[2]
    pad = total.shape[0] // req
    small = fetch([(len_hbm, lengths), (route_hbm, route)], sem_s)
    slabs = fetch(
        [
            (out_k.at[:, lanes(own, slots), :], own_rows.at[0]),
            (out_v.at[:, lanes(own, slots), :], own_rows.at[1]),
        ],
        sem_r,
    )
    for copy in small:
        copy.wait()
    start = lax.axis_index("seq") * (4 * slots) + sent * (2 * slots)
    ahead, _, _ = offsets(lengths, start, slots // SLOTS)

    def sent_part(i, r):
        at = pl.multiple_of(ahead[r] * SLOTS, SLOTS)
        return late[i, pl.ds(at, slots), :]

    shape = (kinds, kinds)
    to, frm = iota(shape, 0), iota(shape, 1)
    wanted = by_row(route, to % req)
    me = lax.axis_index("grp")
    picked = jnp.zeros((kinds, width), jnp.float32)
    for k in range(n_grp):
        source = lax.rem(me + n_grp - k, n_grp)
        hit = (to // req == frm // req) & (wanted == source * req + frm % req)
        picked = picked + dot(hit.astype(jnp.float32).astype(jnp.bfloat16), tokens[k][...])
    picked_ref[...] = picked
    for copy in slabs:
        copy.wait()

    lane, row = iota((pad, width), 1), iota((pad, width), 0)
    mine = (lane >= row * size) & (lane < (row + 1) * size)
    for r in range(req):
        query = jnp.where(mine, picked[r : r + 1, :], 0.0).astype(jnp.bfloat16)
        here = slice(r * pad, (r + 1) * pad)
        scores[here, :slots] = dot_nt(query, own_rows[0, r])
        scores[here, slots:] = dot_nt(query, sent_part(0, r))
    logit = scores[...] * (size**-0.5) + jnp.concatenate([level[0], level[1]], axis=1)
    top = jnp.max(logit, axis=1, keepdims=True)
    weights = jnp.exp(logit - top).astype(jnp.bfloat16).astype(jnp.float32)
    mass = jnp.sum(weights, axis=1, keepdims=True)

    def spread_out(column, r):
        return jnp.sum(
            jnp.where(mine, column[r * pad : (r + 1) * pad], 0.0), axis=0, keepdims=True
        )

    for r in range(req):
        w = weights[r * pad : (r + 1) * pad].astype(jnp.bfloat16)
        acc = dot(w[:, :slots], own_rows[1, r]) + dot(w[:, slots:], sent_part(1, r))
        acc = jnp.sum(jnp.where(mine, acc, 0.0), axis=0, keepdims=True)
        for p, x in enumerate((top, mass, total[:, :1])):
            stats_ref[p * req + r : p * req + r + 1, :] = spread_out(x, r)
        stats_ref[3 * req + r : 3 * req + r + 1, :] = acc


def attend_part(n_seq, n_grp, heads, lengths, route, out_k, out_v, late, level, total, tokens):
    req, rows, width = out_k.shape
    slots = rows // 2
    hbm = pl.BlockSpec(memory_space=pl.ANY)
    vmem = pl.BlockSpec(memory_space=pltpu.VMEM)
    whole = pltpu.HBM(out_k.shape, out_k.dtype)
    small = pltpu.VMEM((4 * req, width), jnp.float32)
    return pl.pallas_call(
        functools.partial(attend_kernel, n_seq, n_grp, heads),
        out_shape=(whole, whole, small, small),
        in_specs=[vmem] * 2 + [hbm] * 2 + [vmem] * (3 + n_grp),
        out_specs=(hbm, hbm, vmem, vmem),
        scratch_shapes=[
            pltpu.SMEM(lengths.shape, jnp.int32),
            pltpu.SMEM(route.shape, jnp.int32),
            pltpu.VMEM((2, req, slots, width), jnp.bfloat16),
            pltpu.VMEM((total.shape[0], rows), jnp.float32),
            pltpu.SemaphoreType.DMA((2,)),
            pltpu.SemaphoreType.DMA((2,)),
        ],
        input_output_aliases={2: 0, 3: 1},
        compiler_params=pltpu.CompilerParams(vmem_limit_bytes=VMEM_LIMIT),
        cost_estimate=LIGHT,
        name="attend",
    )(
        *near(lengths, route),
        *far(out_k, out_v),
        *near(late, level, total),
        *near(*tokens),
    )


def merge_kernel(count, relative, size, *refs):
    stats, refs = refs[:count], refs[count:]
    picked_ref, weight_ref, log_ref, _, decay_ref, out_ref = refs
    heads, req, rows = log_ref.shape
    width = picked_ref.shape[1]
    seq = lax.axis_index("seq")
    places = [lax.rem(seq + count - k, count) if relative else jnp.int32(k) for k in range(count)]
    tops, masses, totals, accs = [
        [ref[p * req : (p + 1) * req, :] for ref in stats] for p in range(4)
    ]

    def later(place):
        total = jnp.zeros_like(totals[0])
        for k in range(count):
            total = total + jnp.where(places[k] > place, totals[k], 0.0)
        return total

    tops = [tops[k] + later(places[k]) for k in range(count)]
    top = functools.reduce(jnp.maximum, tops)
    scales = [jnp.exp(t - top) for t in tops]
    mass = sum(s * x for s, x in zip(scales, masses))
    acc = sum(s * x for s, x in zip(scales, accs))
    query, key, value, gate = [picked_ref[p * req : (p + 1) * req, :] for p in range(4)]
    one, two = iota((width, width), 0), iota((width, width), 1)
    same = (one // size == two // size).astype(jnp.float32).astype(jnp.bfloat16)
    own = split_dot(query * key, same) * (size**-0.5)
    past = top + gate
    joint = jnp.maximum(past, own)
    scale, self_weight = jnp.exp(past - joint), jnp.exp(own - joint)
    attended = (scale * acc + self_weight * value) / (scale * mass + self_weight)
    beyond = later(seq)
    for h in range(heads):
        decay_ref[h] = jnp.exp(log_ref[h] + beyond[:, h * size : h * size + 1])
    out_ref[...] = dot(attended.astype(jnp.bfloat16), weight_ref[...])


def merge_part(stats, relative, picked, out_weight, logs, second, size):
    req = logs.shape[1]
    vmem = pl.BlockSpec(memory_space=pltpu.VMEM)
    return pl.pallas_call(
        functools.partial(merge_kernel, len(stats), relative, size),
        out_shape=(
            jax.ShapeDtypeStruct(logs.shape, jnp.float32),
            jax.ShapeDtypeStruct((req, out_weight.shape[1]), jnp.float32),
        ),
        in_specs=[vmem] * (len(stats) + 3) + [pl.BlockSpec(memory_space=pl.ANY)],
        out_specs=(vmem, vmem),
        compiler_params=pltpu.CompilerParams(vmem_limit_bytes=VMEM_LIMIT),
        cost_estimate=MERGE,
        name="merge_and_project",
    )(*near(*stats, picked, out_weight, logs), second)


def sum_kernel(count, *refs):
    parts, out = refs[:count], refs[-1]
    me = lax.axis_index("head")
    total = jnp.zeros(out.shape, jnp.float32)
    for place in range(count):
        for k in range(count):
            total = total + jnp.where(lax.rem(me + count - k, count) == place, parts[k][...], 0.0)
    out[...] = total.astype(out.dtype)


def sum_part(parts, placed):
    return pl.pallas_call(
        functools.partial(sum_kernel, len(parts)),
        out_shape=pltpu.HBM(parts[0].shape, jnp.bfloat16),
        in_specs=[pl.BlockSpec(memory_space=pltpu.VMEM)] * (len(parts) + 1),
        out_specs=pl.BlockSpec(memory_space=pltpu.VMEM),
        compiler_params=pltpu.CompilerParams(vmem_limit_bytes=VMEM_LIMIT),
        cost_estimate=LIGHT,
        name="sum_heads",
    )(*parts, placed)


def place_kernel(n_seq, first, count, *refs):
    parts, refs = refs[:count], refs[count:]
    len_ref, _, _, out_k, out_v, placed_ref, lengths, sem_s, sem = refs
    _, sent = half_of("seq", n_seq)
    (load,) = fetch([(len_ref, lengths)], sem_s)
    placed_ref[...] = jnp.zeros_like(placed_ref)
    load.wait()
    req, rows, _ = out_k.shape
    slots = rows // 2
    most = slots // SLOTS
    seq = lax.axis_index("seq")
    if n_seq == 2:
        start = (1 - seq) * (4 * slots) + seq * (2 * slots)
    else:
        start = seq * (4 * slots) + sent * (2 * slots)
    ahead, live, _ = offsets(lengths, start, most)
    for phase in ("start", "wait"):
        begin = first
        for p, part in enumerate(parts):
            held = part.shape[1] // SLOTS
            for r in range(req):
                if begin >= (r + 1) * most:
                    continue
                low = jnp.clip(begin - ahead[r], 0, live[r])
                high = jnp.clip(begin + held - ahead[r], 0, live[r])
                for blocks in range(1, min(most, held) + 1):

                    @pl.when(high - low == blocks)
                    def _(p=p, part=part, begin=begin, r=r, low=low, size=blocks * SLOTS):
                        src = pl.multiple_of((ahead[r] + low - begin) * SLOTS, SLOTS)
                        dst = pl.multiple_of(sent * slots + low * SLOTS, SLOTS)
                        for i, out in enumerate((out_k, out_v)):
                            copy = pltpu.make_async_copy(
                                part.at[i, pl.ds(src, size), :],
                                out.at[r, pl.ds(dst, size), :],
                                sem.at[p, i, r],
                            )
                            getattr(copy, phase)()

            begin += held


def place_part(n_seq, first, parts, lengths, out_k, out_v):
    hbm = pl.BlockSpec(memory_space=pl.ANY)
    vmem = pl.BlockSpec(memory_space=pltpu.VMEM)
    shape = pltpu.HBM(out_k.shape, out_k.dtype)
    count = len(parts)
    return pl.pallas_call(
        functools.partial(place_kernel, n_seq, first, count),
        out_shape=(shape, shape, pltpu.VMEM((8, LANES), jnp.float32)),
        in_specs=[vmem] * (count + 1) + [hbm, hbm],
        out_specs=(hbm, hbm, vmem),
        scratch_shapes=[
            pltpu.SMEM(lengths.shape, jnp.int32),
            pltpu.SemaphoreType.DMA((1,)),
            pltpu.SemaphoreType.DMA((count, 2, lengths.shape[0])),
        ],
        input_output_aliases={count + 1: 0, count + 2: 1},
        compiler_params=pltpu.CompilerParams(vmem_limit_bytes=VMEM_LIMIT),
        cost_estimate=LIGHT,
        name="place_received",
    )(*near(*parts, lengths), *far(out_k, out_v))


def others(value, axis):
    count = lax.axis_size(axis)
    return [value] + [
        lax.ppermute(value, axis, [(i, (i + k) % count) for i in range(count)])
        for k in range(1, count)
    ]


def swap(value, n_seq):
    return lax.ppermute(value, "seq", [(0, 1), (1, 0)]) if n_seq == 2 else value


def shards(
    keys, values, log_forget, keep, merge_weight, lengths, route, fresh, new_forget, out_weight
):
    req, pos, width = keys.shape
    heads = log_forget.shape[1]
    size = width // heads
    n_seq, n_grp = lax.axis_size("seq"), lax.axis_size("grp")
    early, packed, choice = first_part(
        n_seq,
        lengths,
        keep,
        merge_weight,
        fresh.reshape(3 * req, width),
        new_forget,
        keys,
        values,
    )
    exchange = functools.partial(swap, n_seq=n_seq)
    first_received = exchange(early)
    tokens = others(packed, "grp")
    out_k, out_v, late, logs, level, total = own_part(
        n_seq,
        lengths,
        keep,
        merge_weight,
        log_forget.transpose(1, 0, 2),
        keys,
        values,
        early,
    )
    begin, end = FIRST * SLOTS, (FIRST + SECOND) * SLOTS
    rest = late.shape[1] - end

    def finish(rows, early, late, logs, level, total, tokens, out_weight, lengths, route, *outs):
        second = exchange(late[:, begin:end])
        out_k, out_v, stats, picked = attend_part(
            n_seq, n_grp, heads, lengths, route, *outs, late, level, total, tokens
        )
        if n_seq == 2:
            all_stats = others(stats, "seq")
        else:
            gathered = lax.all_gather(stats, "seq")
            all_stats = [gathered[i] for i in range(n_seq)]
        third = exchange(late[:, end : end + rows])
        decay, partial = merge_part(
            all_stats, n_seq == 2, picked, out_weight, logs, second, size
        )
        out_k, out_v, placed = place_part(n_seq, 0, (early, second), lengths, out_k, out_v)
        layer_out = sum_part(others(partial, "head"), placed)
        out_k, out_v, _ = place_part(n_seq, FIRST + SECOND, (third,), lengths, out_k, out_v)
        return decay, layer_out, out_k, out_v

    operands = (first_received, late, logs, level, total, tokens, out_weight, lengths, route)
    operands += (out_k, out_v)
    if n_seq == 2:
        branches = [
            functools.partial(finish, blocks * SLOTS) for blocks in SIZES + (rest // SLOTS,)
        ]
        decay, layer_out, out_k, out_v = lax.switch(choice[0], branches, *operands)
    else:
        decay, layer_out, out_k, out_v = finish(rest, *operands)
    if n_seq != 2:
        out_k, out_v = (
            lax.all_to_all(x, "seq", split_axis=1, concat_axis=1, tiled=True) for x in (out_k, out_v)
        )
    return out_k, out_v, decay.transpose(1, 0, 2), layer_out


def solution(mesh):
    return jax.shard_map(
        shards,
        mesh=mesh,
        in_specs=(
            P("grp", "seq", "head"),
            P("grp", "seq", "head"),
            P("grp", "head", "seq"),
            P("grp", "seq"),
            P("grp", "seq"),
            P("grp"),
            P("grp"),
            P(None, "grp", "head"),
            P("grp", "head"),
            P("head", "seq"),
        ),
        out_specs=(
            P("grp", "seq", "head"),
            P("grp", "seq", "head"),
            P("grp", "head", "seq"),
            P("grp", "seq"),
        ),
        check_vma=False,
    )
```

```python
import functools

import jax
import jax.numpy as jnp
from jax import lax
from jax.experimental import pallas as pl
from jax.experimental.pallas import tpu as pltpu
from jax.sharding import PartitionSpec as P

BLOCK = 64
SLOTS = 32
LANES = 128
BLOCK_LOG = BLOCK.bit_length() - 1
SLOT_LOG = SLOTS.bit_length() - 1
EMPTY_LOG = -10000.0
FIRST = 9
SECOND = 4
SIZES = (2, 4, 6, 8, 10, 12, 14)
SURE = 3
EAGER = 5
VMEM_LIMIT = 16 * 1024 * 1024


LIGHT = pl.CostEstimate(flops=1, bytes_accessed=1, transcendentals=0)
MERGE = pl.CostEstimate(flops=1 << 36, bytes_accessed=1, transcendentals=0)


def dot(a, b):
    return lax.dot_general(a, b, (((1,), (0,)), ((), ())), preferred_element_type=jnp.float32)


def dot_nt(a, b):
    return lax.dot_general(a, b, (((1,), (1,)), ((), ())), preferred_element_type=jnp.float32)


def iota(shape, dim):
    return lax.broadcasted_iota(jnp.int32, shape, dim)


def three(x):
    hi = x.astype(jnp.bfloat16).astype(jnp.float32)
    rest = x - hi
    mid = rest.astype(jnp.bfloat16).astype(jnp.float32)
    return hi, mid, rest - mid


def split_dot(x, ones):
    rows = x.shape[0]
    parts = dot(jnp.concatenate(three(x), axis=0).astype(jnp.bfloat16), ones)
    return parts[:rows] + parts[rows : 2 * rows] + parts[2 * rows :]


def half_of(axis, count):
    own = lax.axis_index(axis) if count == 2 else jnp.int32(0)
    return own, 1 - own


def by_row(ref, row):
    picked = jnp.zeros_like(row)
    for r in range(ref.shape[0]):
        picked = jnp.where(row == r, ref[r], picked)
    return picked


def live_blocks(lengths, r, start, most):
    return jnp.clip((lengths[r] - start) >> BLOCK_LOG, 0, most)


def offsets(lengths, start, most):
    total = jnp.int32(0)
    ahead, live = [], []
    for r in range(lengths.shape[0]):
        ahead.append(total)
        live.append(live_blocks(lengths, r, start, most))
        total = total + live[-1]
    return ahead, live, total


def plan(keep, weight, start, len_ref):
    rows, width = keep.shape
    one, two = iota((width, width), 0), iota((width, width), 1)
    same = (one ^ two) < BLOCK
    upto = (same & (one <= two)).astype(jnp.float32).astype(jnp.bfloat16)
    block = same.astype(jnp.float32).astype(jnp.bfloat16)
    kept = keep == 1
    rank = dot(keep.astype(jnp.float32).astype(jnp.bfloat16), upto) - 1.0
    weighted = jnp.where(kept, 0.0, weight)
    share = (weighted / split_dot(weighted, block)).astype(jnp.bfloat16).astype(jnp.float32)
    lane, row = iota((rows, width), 1), iota((rows, width), 0)
    slot = jnp.where(kept, rank.astype(jnp.int32), SLOTS - 1) + (lane >> BLOCK_LOG) * SLOTS
    slot = jnp.where(start + lane < by_row(len_ref, row), slot, -1)
    return slot, jnp.where(kept, 1.0, share)


def select(slot, factor, r):
    width = slot.shape[1]
    shape = (width // 2, width)
    hit = iota(shape, 0) == slot[r : r + 1, :]
    return jnp.where(hit, jnp.broadcast_to(factor[r : r + 1, :], shape), 0.0).astype(jnp.bfloat16)


def lanes(half, width):
    return pl.ds(pl.multiple_of(half * width, width), width)


def far(*arrays):
    return [pltpu.with_memory_space_constraint(x, pltpu.HBM) for x in arrays]


def near(*arrays):
    return [pltpu.with_memory_space_constraint(x, pltpu.VMEM) for x in arrays]


def fetch(pairs, sem):
    copies = [pltpu.make_async_copy(src, dst, sem.at[i]) for i, (src, dst) in enumerate(pairs)]
    for copy in copies:
        copy.start()
    return copies


def first_kernel(n_seq, len_hbm, keep_hbm, weight_hbm, fresh_hbm, gate_hbm, keys, values, *rest):
    out, packed, size_ref, lengths, keep, weight, fresh, gates, raw, row_buf, sem_s, sem_r = rest
    _, sent = half_of("seq", n_seq)
    req, width = keep.shape
    most = width // BLOCK
    small = fetch(
        [
            (len_hbm, lengths),
            (keep_hbm.at[:, lanes(sent, width)], keep),
            (weight_hbm.at[:, lanes(sent, width)], weight),
            (fresh_hbm, fresh),
            (gate_hbm, gates),
        ],
        sem_s,
    )

    def slab(i, r):
        source = (keys, values)[i].at[r, lanes(sent, width), :]
        return pltpu.make_async_copy(source, raw.at[i, r], sem_r.at[i, r])

    eager = min(EAGER, req)
    for r in range(eager):
        for i in range(2):
            slab(i, r).start()
    row_buf[...] = jnp.zeros_like(row_buf)
    for copy in small:
        copy.wait()
    start = lax.axis_index("seq") * (2 * width) + sent * width
    ahead, live, _ = offsets(lengths, start, most)
    needed = [(ahead[r] < FIRST) & (live[r] > 0) for r in range(req)]
    for r in range(eager, req):

        @pl.when(needed[r])
        def _(r=r):
            for i in range(2):
                slab(i, r).start()

    slot, factor = plan(keep[...], weight[...], start, lengths)
    _, _, total = offsets(lengths, width, most)
    choice = jnp.int32(0)
    for size in SIZES:
        choice = choice + (total - FIRST - SECOND > size).astype(jnp.int32)
    size_ref[0] = choice

    new, gate = fresh[...].astype(jnp.float32), gates[...].astype(jnp.float32)
    heads = gate.shape[1]
    lane = iota((req, new.shape[1]), 1)
    size = new.shape[1] // heads
    spread = jnp.zeros((req, new.shape[1]), jnp.float32)
    for h in range(heads):
        inside = (lane >= h * size) & (lane < (h + 1) * size)
        spread = jnp.where(inside, gate[:, h : h + 1], spread)
    packed[...] = jnp.concatenate([new, spread], axis=0).astype(jnp.bfloat16)

    def pack(r):
        chosen = select(slot, factor, r)
        at = pl.ds(pl.multiple_of(ahead[r] * SLOTS, SLOTS), most * SLOTS)
        for i in range(2):
            if r >= eager:
                slab(i, r).wait()
            row_buf[i, at, :] = dot(chosen, raw[i, r]).astype(jnp.bfloat16)

    for r in range(req):
        if r < eager:
            for i in range(2):
                slab(i, r).wait()
        if r < SURE:
            pack(r)
        else:
            pl.when(needed[r])(functools.partial(pack, r))
    out[...] = row_buf[:, : FIRST * SLOTS, :]


def first_part(n_seq, lengths, keep, weight, fresh, gates, keys, values):
    req, pos, width = keys.shape
    half = pos // 2
    hbm = pl.BlockSpec(memory_space=pl.ANY)
    vmem = pl.BlockSpec(memory_space=pltpu.VMEM)
    return pl.pallas_call(
        functools.partial(first_kernel, n_seq),
        out_shape=(
            pltpu.VMEM((2, FIRST * SLOTS, width), jnp.bfloat16),
            pltpu.VMEM((fresh.shape[0] + req, width), jnp.bfloat16),
            jax.ShapeDtypeStruct((1,), jnp.int32),
        ),
        in_specs=[hbm] * 7,
        out_specs=(vmem, vmem, pl.BlockSpec(memory_space=pltpu.SMEM)),
        scratch_shapes=[
            pltpu.SMEM(lengths.shape, jnp.int32),
            pltpu.VMEM((req, half), jnp.int32),
            pltpu.VMEM((req, half), jnp.float32),
            pltpu.VMEM(fresh.shape, fresh.dtype),
            pltpu.VMEM(gates.shape, gates.dtype),
            pltpu.VMEM((2, req, half, width), jnp.bfloat16),
            pltpu.VMEM((2, (FIRST - 1) * SLOTS + half // 2, width), jnp.bfloat16),
            pltpu.SemaphoreType.DMA((5,)),
            pltpu.SemaphoreType.DMA((2, req)),
        ],
        compiler_params=pltpu.CompilerParams(vmem_limit_bytes=VMEM_LIMIT),
        cost_estimate=LIGHT,
        name="compact_first_sent",
    )(*far(lengths, keep, weight, fresh, gates, keys, values))


def own_kernel(
    n_seq, len_ref, keep, weight, gates, keys, values, early, *rest
):
    out_k, out_v, chunk, log_ref, level_ref, total_ref = rest[:6]
    lengths, raw, late, forget, rows, zeros, sem_s, sem_l, sem_r, sem_o, sem_z = rest[6:]
    own, sent = half_of("seq", n_seq)
    seq = lax.axis_index("seq")
    heads, req, pos = gates.shape
    half = pos // 2
    slots = half // 2
    most = half // BLOCK
    first = FIRST // most
    pad = forget.shape[1] // req
    small = fetch([(len_ref, lengths)], sem_s)
    both = ((0, keys), (1, values))
    late_slabs = fetch(
        [
            (source.at[r, lanes(sent, half), :], late.at[i, r - first])
            for r in range(first, req)
            for i, source in both
        ],
        sem_l,
    )
    slabs = fetch(
        [
            (source.at[r, lanes(own, half), :], raw.at[i, r])
            for r in range(req)
            for i, source in both
        ],
        sem_r,
    )
    zeros[...] = jnp.zeros_like(zeros)
    stores = fetch([(zeros, out.at[:, lanes(sent, slots), :]) for out in (out_k, out_v)], sem_z)
    chunk[:, : FIRST * SLOTS, :] = early[...]
    chunk[:, FIRST * SLOTS :, :] = jnp.zeros(
        (2, chunk.shape[1] - FIRST * SLOTS, chunk.shape[2]), chunk.dtype
    )
    for copy in small:
        copy.wait()
    ahead, alive, _ = offsets(lengths, seq * pos + sent * half, most)

    forget[...] = jnp.zeros_like(forget)
    live = seq * pos + iota((req, pos), 1) < by_row(lengths, iota((req, pos), 0))
    for h in range(heads):
        gate = jnp.where(live, gates[h], 0.0)
        for c in range(pos // LANES):
            forget[c, pl.ds(h, req, stride=pad), :] = gate[:, c * LANES : (c + 1) * LANES]
    flat = jnp.concatenate([forget[c] for c in range(pos // LANES)], axis=1)
    total_ref[...] = jnp.broadcast_to(jnp.sum(flat, axis=1, keepdims=True), total_ref.shape)
    one, two = iota((half, half), 0), iota((half, half), 1)
    after = (((one ^ two) < BLOCK) & (one > two)).astype(jnp.float32).astype(jnp.bfloat16)
    ends = iota((pos, slots), 1) >> SLOT_LOG
    begins = iota((pos, slots), 0) >> BLOCK_LOG
    last = iota((req * pad, slots), 1) & (SLOTS - 1) == SLOTS - 1

    for i, h in enumerate((own, sent)):
        slot, factor = plan(
            keep[:, lanes(h, half)], weight[:, lanes(h, half)], seq * pos + h * half, lengths
        )
        near = half // LANES
        inner = split_dot(
            jnp.concatenate([forget[h * near + c] for c in range(near)], axis=1), after
        )
        beyond = split_dot(
            flat, (begins > ends + h * (half // BLOCK)).astype(jnp.float32).astype(jnp.bfloat16)
        )
        spread = jnp.exp(inner)
        high = spread.astype(jnp.bfloat16).astype(jnp.float32)
        planes = three(inner) + (high, spread - high, jnp.ones_like(inner))
        found = []
        for r in range(req):
            chosen = select(slot, factor, r)
            stack = jnp.concatenate([x[r * pad : (r + 1) * pad] for x in planes], axis=0)
            found.append(dot_nt(stack.astype(jnp.bfloat16), chosen))
            if i == 0:
                for k, out in enumerate((out_k, out_v)):
                    slabs[2 * r + k].wait()
                    rows[k, r] = dot(chosen, raw[k, r]).astype(jnp.bfloat16)
                    stores.append(
                        pltpu.make_async_copy(
                            rows.at[k, r], out.at[r, lanes(own, slots), :], sem_o.at[2 * r + k]
                        )
                    )
                    stores[-1].start()
            elif r >= first:
                for k in range(2):
                    late_slabs[2 * (r - first) + k].wait()

                @pl.when((ahead[r] + alive[r] > FIRST) & (alive[r] > 0))
                def _(r=r, chosen=chosen):
                    at = pl.ds(pl.multiple_of(ahead[r] * SLOTS, SLOTS), slots)
                    for k in range(2):
                        chunk[k, at, :] = dot(chosen, late[k, r - first]).astype(jnp.bfloat16)
        at = [
            jnp.concatenate([x[p * pad : (p + 1) * pad] for x in found], axis=0) for p in range(6)
        ]
        filled = at[5] > 0.5
        kept = at[0] + at[1] + at[2]
        merged = jnp.log(jnp.where(filled, at[3] + at[4], 1.0))
        level_ref[i] = jnp.where(filled, jnp.where(last, merged, kept) + beyond, EMPTY_LOG)
        for k in range(heads):
            log_ref[k, :, lanes(h, slots)] = level_ref[i, pl.ds(k, req, stride=pad), :]
    for copy in stores:
        copy.wait()


def own_part(n_seq, lengths, keep, weight, forget, keys, values, early):
    req, pos, width = keys.shape
    heads = forget.shape[0]
    half, slots, pad = pos // 2, pos // 4, -(-heads // 8) * 8
    late = req - FIRST // (half // BLOCK)
    hbm = pl.BlockSpec(memory_space=pl.ANY)
    vmem = pl.BlockSpec(memory_space=pltpu.VMEM)
    whole = pltpu.HBM((req, 2 * slots, width), jnp.bfloat16)
    return pl.pallas_call(
        functools.partial(own_kernel, n_seq),
        out_shape=(
            whole,
            whole,
            pltpu.VMEM((2, req * slots, width), jnp.bfloat16),
            pltpu.VMEM((heads, req, 2 * slots), jnp.float32),
            pltpu.VMEM((2, req * pad, slots), jnp.float32),
            pltpu.VMEM((req * pad, LANES), jnp.float32),
        ),
        in_specs=[vmem] * 4 + [hbm] * 2 + [vmem],
        out_specs=(hbm, hbm, vmem, vmem, vmem, vmem),
        scratch_shapes=[
            pltpu.SMEM(lengths.shape, jnp.int32),
            pltpu.VMEM((2, req, half, width), jnp.bfloat16),
            pltpu.VMEM((2, late, half, width), jnp.bfloat16),
            pltpu.VMEM((pos // LANES, req * pad, LANES), jnp.float32),
            pltpu.VMEM((2, req, slots, width), jnp.bfloat16),
            pltpu.VMEM((req, slots, width), jnp.bfloat16),
            pltpu.SemaphoreType.DMA((1,)),
            pltpu.SemaphoreType.DMA((2 * late,)),
            pltpu.SemaphoreType.DMA((2 * req,)),
            pltpu.SemaphoreType.DMA((2 * req,)),
            pltpu.SemaphoreType.DMA((2,)),
        ],
        compiler_params=pltpu.CompilerParams(vmem_limit_bytes=VMEM_LIMIT),
        cost_estimate=LIGHT,
        name="compact_own",
    )(*near(lengths, keep, weight, forget), *far(keys, values), *near(early))


def attend_kernel(n_seq, n_grp, heads, *refs):
    len_hbm, route_hbm, out_k, out_v, late, level, total = refs[:7]
    tokens, rest = refs[7 : 7 + n_grp], refs[7 + n_grp :]
    _, _, stats_ref, picked_ref, lengths, route, own_rows, scores, sem_s, sem_r = rest
    own, sent = half_of("seq", n_seq)
    kinds, width = picked_ref.shape
    req = kinds // 4
    size = width // heads
    slots = own_rows.shape[2]
    pad = total.shape[0] // req
    small = fetch([(len_hbm, lengths), (route_hbm, route)], sem_s)
    slabs = fetch(
        [
            (out_k.at[:, lanes(own, slots), :], own_rows.at[0]),
            (out_v.at[:, lanes(own, slots), :], own_rows.at[1]),
        ],
        sem_r,
    )
    for copy in small:
        copy.wait()
    start = lax.axis_index("seq") * (4 * slots) + sent * (2 * slots)
    ahead, _, _ = offsets(lengths, start, slots // SLOTS)

    def sent_part(i, r):
        at = pl.multiple_of(ahead[r] * SLOTS, SLOTS)
        return late[i, pl.ds(at, slots), :]

    shape = (kinds, kinds)
    to, frm = iota(shape, 0), iota(shape, 1)
    wanted = by_row(route, to % req)
    me = lax.axis_index("grp")
    picked = jnp.zeros((kinds, width), jnp.float32)
    for k in range(n_grp):
        source = lax.rem(me + n_grp - k, n_grp)
        hit = (to // req == frm // req) & (wanted == source * req + frm % req)
        picked = picked + dot(hit.astype(jnp.float32).astype(jnp.bfloat16), tokens[k][...])
    picked_ref[...] = picked
    for copy in slabs:
        copy.wait()

    lane, row = iota((pad, width), 1), iota((pad, width), 0)
    mine = (lane >= row * size) & (lane < (row + 1) * size)
    for r in range(req):
        query = jnp.where(mine, picked[r : r + 1, :], 0.0).astype(jnp.bfloat16)
        here = slice(r * pad, (r + 1) * pad)
        scores[here, :slots] = dot_nt(query, own_rows[0, r])
        scores[here, slots:] = dot_nt(query, sent_part(0, r))
    logit = scores[...] * (size**-0.5) + jnp.concatenate([level[0], level[1]], axis=1)
    top = jnp.max(logit, axis=1, keepdims=True)
    weights = jnp.exp(logit - top).astype(jnp.bfloat16).astype(jnp.float32)
    mass = jnp.sum(weights, axis=1, keepdims=True)

    def spread_out(column, r):
        return jnp.sum(
            jnp.where(mine, column[r * pad : (r + 1) * pad], 0.0), axis=0, keepdims=True
        )

    for r in range(req):
        w = weights[r * pad : (r + 1) * pad].astype(jnp.bfloat16)
        acc = dot(w[:, :slots], own_rows[1, r]) + dot(w[:, slots:], sent_part(1, r))
        acc = jnp.sum(jnp.where(mine, acc, 0.0), axis=0, keepdims=True)
        for p, x in enumerate((top, mass, total[:, :1])):
            stats_ref[p * req + r : p * req + r + 1, :] = spread_out(x, r)
        stats_ref[3 * req + r : 3 * req + r + 1, :] = acc


def attend_part(n_seq, n_grp, heads, lengths, route, out_k, out_v, late, level, total, tokens):
    req, rows, width = out_k.shape
    slots = rows // 2
    hbm = pl.BlockSpec(memory_space=pl.ANY)
    vmem = pl.BlockSpec(memory_space=pltpu.VMEM)
    whole = pltpu.HBM(out_k.shape, out_k.dtype)
    small = pltpu.VMEM((4 * req, width), jnp.float32)
    return pl.pallas_call(
        functools.partial(attend_kernel, n_seq, n_grp, heads),
        out_shape=(whole, whole, small, small),
        in_specs=[vmem] * 2 + [hbm] * 2 + [vmem] * (3 + n_grp),
        out_specs=(hbm, hbm, vmem, vmem),
        scratch_shapes=[
            pltpu.SMEM(lengths.shape, jnp.int32),
            pltpu.SMEM(route.shape, jnp.int32),
            pltpu.VMEM((2, req, slots, width), jnp.bfloat16),
            pltpu.VMEM((total.shape[0], rows), jnp.float32),
            pltpu.SemaphoreType.DMA((2,)),
            pltpu.SemaphoreType.DMA((2,)),
        ],
        input_output_aliases={2: 0, 3: 1},
        compiler_params=pltpu.CompilerParams(vmem_limit_bytes=VMEM_LIMIT),
        cost_estimate=LIGHT,
        name="attend",
    )(
        *near(lengths, route),
        *far(out_k, out_v),
        *near(late, level, total),
        *near(*tokens),
    )


def merge_kernel(count, relative, size, *refs):
    stats, refs = refs[:count], refs[count:]
    picked_ref, weight_ref, _, later_ref, out_ref = refs
    req, width = later_ref.shape
    seq = lax.axis_index("seq")
    places = [lax.rem(seq + count - k, count) if relative else jnp.int32(k) for k in range(count)]
    tops, masses, totals, accs = [
        [ref[p * req : (p + 1) * req, :] for ref in stats] for p in range(4)
    ]

    def later(place):
        total = jnp.zeros_like(totals[0])
        for k in range(count):
            total = total + jnp.where(places[k] > place, totals[k], 0.0)
        return total

    tops = [tops[k] + later(places[k]) for k in range(count)]
    top = functools.reduce(jnp.maximum, tops)
    scales = [jnp.exp(t - top) for t in tops]
    mass = sum(s * x for s, x in zip(scales, masses))
    acc = sum(s * x for s, x in zip(scales, accs))
    query, key, value, gate = [picked_ref[p * req : (p + 1) * req, :] for p in range(4)]
    one, two = iota((width, width), 0), iota((width, width), 1)
    same = (one // size == two // size).astype(jnp.float32).astype(jnp.bfloat16)
    own = split_dot(query * key, same) * (size**-0.5)
    past = top + gate
    joint = jnp.maximum(past, own)
    scale, self_weight = jnp.exp(past - joint), jnp.exp(own - joint)
    attended = (scale * acc + self_weight * value) / (scale * mass + self_weight)
    later_ref[...] = later(seq)
    out_ref[...] = dot(attended.astype(jnp.bfloat16), weight_ref[...])


def merge_part(stats, relative, picked, out_weight, second, size):
    req, width = stats[0].shape[0] // 4, stats[0].shape[1]
    vmem = pl.BlockSpec(memory_space=pltpu.VMEM)
    return pl.pallas_call(
        functools.partial(merge_kernel, len(stats), relative, size),
        out_shape=(
            pltpu.VMEM((req, width), jnp.float32),
            pltpu.VMEM((req, out_weight.shape[1]), jnp.float32),
        ),
        in_specs=[vmem] * (len(stats) + 2) + [pl.BlockSpec(memory_space=pl.ANY)],
        out_specs=(vmem, vmem),
        compiler_params=pltpu.CompilerParams(vmem_limit_bytes=VMEM_LIMIT),
        cost_estimate=MERGE,
        name="merge_and_project",
    )(*near(*stats, picked, out_weight), second)


def sum_kernel(count, size, *refs):
    parts, (later_ref, log_ref, _, out, decay_ref) = refs[:count], refs[count:]
    me = lax.axis_index("head")
    total = jnp.zeros(out.shape, jnp.float32)
    for place in range(count):
        for k in range(count):
            total = total + jnp.where(lax.rem(me + count - k, count) == place, parts[k][...], 0.0)
    out[...] = total.astype(out.dtype)
    for h in range(log_ref.shape[0]):
        decay_ref[h] = jnp.exp(log_ref[h] + later_ref[:, h * size : h * size + 1])


def sum_part(parts, later, logs, placed, size):
    vmem = pl.BlockSpec(memory_space=pltpu.VMEM)
    return pl.pallas_call(
        functools.partial(sum_kernel, len(parts), size),
        out_shape=(
            pltpu.HBM(parts[0].shape, jnp.bfloat16),
            pltpu.HBM(logs.shape, jnp.float32),
        ),
        in_specs=[vmem] * (len(parts) + 3),
        out_specs=(vmem, vmem),
        compiler_params=pltpu.CompilerParams(vmem_limit_bytes=VMEM_LIMIT),
        cost_estimate=LIGHT,
        name="sum_heads_and_decay",
    )(*parts, later, logs, placed)


def place_kernel(n_seq, first, count, *refs):
    parts, refs = refs[:count], refs[count:]
    len_ref, _, _, out_k, out_v, placed_ref, lengths, sem_s, sem = refs
    _, sent = half_of("seq", n_seq)
    (load,) = fetch([(len_ref, lengths)], sem_s)
    placed_ref[...] = jnp.zeros_like(placed_ref)
    load.wait()
    req, rows, _ = out_k.shape
    slots = rows // 2
    most = slots // SLOTS
    seq = lax.axis_index("seq")
    if n_seq == 2:
        start = (1 - seq) * (4 * slots) + seq * (2 * slots)
    else:
        start = seq * (4 * slots) + sent * (2 * slots)
    ahead, live, _ = offsets(lengths, start, most)
    for phase in ("start", "wait"):
        begin = first
        for p, part in enumerate(parts):
            held = part.shape[1] // SLOTS
            for r in range(req):
                if begin >= (r + 1) * most:
                    continue
                low = jnp.clip(begin - ahead[r], 0, live[r])
                high = jnp.clip(begin + held - ahead[r], 0, live[r])
                for blocks in range(1, min(most, held) + 1):

                    @pl.when(high - low == blocks)
                    def _(p=p, part=part, begin=begin, r=r, low=low, size=blocks * SLOTS):
                        src = pl.multiple_of((ahead[r] + low - begin) * SLOTS, SLOTS)
                        dst = pl.multiple_of(sent * slots + low * SLOTS, SLOTS)
                        for i, out in enumerate((out_k, out_v)):
                            copy = pltpu.make_async_copy(
                                part.at[i, pl.ds(src, size), :],
                                out.at[r, pl.ds(dst, size), :],
                                sem.at[p, i, r],
                            )
                            getattr(copy, phase)()

            begin += held


def place_part(n_seq, first, parts, lengths, out_k, out_v):
    hbm = pl.BlockSpec(memory_space=pl.ANY)
    vmem = pl.BlockSpec(memory_space=pltpu.VMEM)
    shape = pltpu.HBM(out_k.shape, out_k.dtype)
    count = len(parts)
    return pl.pallas_call(
        functools.partial(place_kernel, n_seq, first, count),
        out_shape=(shape, shape, pltpu.VMEM((8, LANES), jnp.float32)),
        in_specs=[vmem] * (count + 1) + [hbm, hbm],
        out_specs=(hbm, hbm, vmem),
        scratch_shapes=[
            pltpu.SMEM(lengths.shape, jnp.int32),
            pltpu.SemaphoreType.DMA((1,)),
            pltpu.SemaphoreType.DMA((count, 2, lengths.shape[0])),
        ],
        input_output_aliases={count + 1: 0, count + 2: 1},
        compiler_params=pltpu.CompilerParams(vmem_limit_bytes=VMEM_LIMIT),
        cost_estimate=LIGHT,
        name="place_received",
    )(*near(*parts, lengths), *far(out_k, out_v))


def others(value, axis):
    count = lax.axis_size(axis)
    return [value] + [
        lax.ppermute(value, axis, [(i, (i + k) % count) for i in range(count)])
        for k in range(1, count)
    ]


def swap(value, n_seq):
    return lax.ppermute(value, "seq", [(0, 1), (1, 0)]) if n_seq == 2 else value


def shards(
    keys, values, log_forget, keep, merge_weight, lengths, route, fresh, new_forget, out_weight
):
    req, pos, width = keys.shape
    heads = log_forget.shape[1]
    size = width // heads
    n_seq, n_grp = lax.axis_size("seq"), lax.axis_size("grp")
    early, packed, choice = first_part(
        n_seq,
        lengths,
        keep,
        merge_weight,
        fresh.reshape(3 * req, width),
        new_forget,
        keys,
        values,
    )
    exchange = functools.partial(swap, n_seq=n_seq)
    first_received = exchange(early)
    tokens = others(packed, "grp")
    out_k, out_v, late, logs, level, total = own_part(
        n_seq,
        lengths,
        keep,
        merge_weight,
        log_forget.transpose(1, 0, 2),
        keys,
        values,
        early,
    )
    begin, end = FIRST * SLOTS, (FIRST + SECOND) * SLOTS
    rest = late.shape[1] - end

    def finish(rows, early, late, logs, level, total, tokens, out_weight, lengths, route, *outs):
        second = exchange(late[:, begin:end])
        out_k, out_v, stats, picked = attend_part(
            n_seq, n_grp, heads, lengths, route, *outs, late, level, total, tokens
        )
        if n_seq == 2:
            all_stats = others(stats, "seq")
        else:
            gathered = lax.all_gather(stats, "seq")
            all_stats = [gathered[i] for i in range(n_seq)]
        third = exchange(late[:, end : end + rows])
        later, partial = merge_part(all_stats, n_seq == 2, picked, out_weight, second, size)
        out_k, out_v, placed = place_part(n_seq, 0, (early, second), lengths, out_k, out_v)
        layer_out, decay = sum_part(others(partial, "head"), later, logs, placed, size)
        out_k, out_v, _ = place_part(n_seq, FIRST + SECOND, (third,), lengths, out_k, out_v)
        return decay, layer_out, out_k, out_v

    operands = (first_received, late, logs, level, total, tokens, out_weight, lengths, route)
    operands += (out_k, out_v)
    if n_seq == 2:
        branches = [
            functools.partial(finish, blocks * SLOTS) for blocks in SIZES + (rest // SLOTS,)
        ]
        decay, layer_out, out_k, out_v = lax.switch(choice[0], branches, *operands)
    else:
        decay, layer_out, out_k, out_v = finish(rest, *operands)
    if n_seq != 2:
        out_k, out_v = (
            lax.all_to_all(x, "seq", split_axis=1, concat_axis=1, tiled=True) for x in (out_k, out_v)
        )
    return out_k, out_v, decay.transpose(1, 0, 2), layer_out


def solution(mesh):
    return jax.shard_map(
        shards,
        mesh=mesh,
        in_specs=(
            P("grp", "seq", "head"),
            P("grp", "seq", "head"),
            P("grp", "head", "seq"),
            P("grp", "seq"),
            P("grp", "seq"),
            P("grp"),
            P("grp"),
            P(None, "grp", "head"),
            P("grp", "head"),
            P("head", "seq"),
        ),
        out_specs=(
            P("grp", "seq", "head"),
            P("grp", "seq", "head"),
            P("grp", "head", "seq"),
            P("grp", "seq"),
        ),
        check_vma=False,
    )
```

```python
import functools

import jax
import jax.numpy as jnp
from jax import lax
from jax.experimental import pallas as pl
from jax.experimental.pallas import tpu as pltpu
from jax.sharding import PartitionSpec as P

BLOCK = 64
SLOTS = 32
LANES = 128
BLOCK_LOG = BLOCK.bit_length() - 1
SLOT_LOG = SLOTS.bit_length() - 1
EMPTY_LOG = -10000.0
FIRST = 9
SECOND = 4
SIZES = (4, 7, 9, 11, 12, 13, 15, 17)
SURE = 3
EAGER = 5
VMEM_LIMIT = 16 * 1024 * 1024


LIGHT = pl.CostEstimate(flops=1, bytes_accessed=1, transcendentals=0)
MERGE = pl.CostEstimate(flops=1 << 36, bytes_accessed=1, transcendentals=0)


def dot(a, b):
    return lax.dot_general(a, b, (((1,), (0,)), ((), ())), preferred_element_type=jnp.float32)


def dot_nt(a, b):
    return lax.dot_general(a, b, (((1,), (1,)), ((), ())), preferred_element_type=jnp.float32)


def iota(shape, dim):
    return lax.broadcasted_iota(jnp.int32, shape, dim)


def three(x):
    hi = x.astype(jnp.bfloat16).astype(jnp.float32)
    rest = x - hi
    mid = rest.astype(jnp.bfloat16).astype(jnp.float32)
    return hi, mid, rest - mid


def split_dot(x, ones):
    rows = x.shape[0]
    parts = dot(jnp.concatenate(three(x), axis=0).astype(jnp.bfloat16), ones)
    return parts[:rows] + parts[rows : 2 * rows] + parts[2 * rows :]


def half_of(axis, count):
    own = lax.axis_index(axis) if count == 2 else jnp.int32(0)
    return own, 1 - own


def by_row(ref, row):
    picked = jnp.zeros_like(row)
    for r in range(ref.shape[0]):
        picked = jnp.where(row == r, ref[r], picked)
    return picked


def live_blocks(lengths, r, start, most):
    return jnp.clip((lengths[r] - start) >> BLOCK_LOG, 0, most)


def offsets(lengths, start, most):
    total = jnp.int32(0)
    ahead, live = [], []
    for r in range(lengths.shape[0]):
        ahead.append(total)
        live.append(live_blocks(lengths, r, start, most))
        total = total + live[-1]
    return ahead, live, total


def mask(condition):
    return condition.astype(jnp.float32).astype(jnp.bfloat16)


def block_masks(width):
    one, two = iota((width, width), 0), iota((width, width), 1)
    same = (one ^ two) < BLOCK
    return mask(same & (one <= two)), mask(same), mask(same & (one > two))


def plan(keep, weight, start, len_ref, upto, block):
    rows, width = keep.shape
    kept = keep == 1
    rank = dot(keep.astype(jnp.float32).astype(jnp.bfloat16), upto) - 1.0
    weighted = jnp.where(kept, 0.0, weight)
    share = (weighted / split_dot(weighted, block)).astype(jnp.bfloat16).astype(jnp.float32)
    lane, row = iota((rows, width), 1), iota((rows, width), 0)
    slot = jnp.where(kept, rank.astype(jnp.int32), SLOTS - 1) + (lane >> BLOCK_LOG) * SLOTS
    slot = jnp.where(start + lane < by_row(len_ref, row), slot, -1)
    return slot, jnp.where(kept, 1.0, share)


def select(slot, factor, r):
    width = slot.shape[1]
    shape = (width // 2, width)
    hit = iota(shape, 0) == slot[r : r + 1, :]
    return jnp.where(hit, jnp.broadcast_to(factor[r : r + 1, :], shape), 0.0).astype(jnp.bfloat16)


def lanes(half, width):
    return pl.ds(pl.multiple_of(half * width, width), width)


def far(*arrays):
    return [pltpu.with_memory_space_constraint(x, pltpu.HBM) for x in arrays]


def near(*arrays):
    return [pltpu.with_memory_space_constraint(x, pltpu.VMEM) for x in arrays]


def fetch(pairs, sem):
    copies = [pltpu.make_async_copy(src, dst, sem.at[i]) for i, (src, dst) in enumerate(pairs)]
    for copy in copies:
        copy.start()
    return copies


def first_kernel(n_seq, len_hbm, keep_hbm, weight_hbm, fresh_hbm, gate_hbm, keys, values, *rest):
    out, packed, size_ref, lengths, keep, weight, fresh, gates, raw, row_buf, sem_s, sem_r = rest
    _, sent = half_of("seq", n_seq)
    req, width = keep.shape
    most = width // BLOCK
    small = fetch(
        [
            (len_hbm, lengths),
            (keep_hbm.at[:, lanes(sent, width)], keep),
            (weight_hbm.at[:, lanes(sent, width)], weight),
            (fresh_hbm, fresh),
            (gate_hbm, gates),
        ],
        sem_s,
    )

    def slab(i, r):
        source = (keys, values)[i].at[r, lanes(sent, width), :]
        return pltpu.make_async_copy(source, raw.at[i, r], sem_r.at[i, r])

    eager = min(EAGER, req)
    for r in range(eager):
        for i in range(2):
            slab(i, r).start()
    row_buf[...] = jnp.zeros_like(row_buf)
    upto, block, _ = block_masks(width)
    for copy in small:
        copy.wait()
    start = lax.axis_index("seq") * (2 * width) + sent * width
    ahead, live, _ = offsets(lengths, start, most)
    needed = [(ahead[r] < FIRST) & (live[r] > 0) for r in range(req)]
    for r in range(eager, req):

        @pl.when(needed[r])
        def _(r=r):
            for i in range(2):
                slab(i, r).start()

    slot, factor = plan(keep[...], weight[...], start, lengths, upto, block)
    _, _, total = offsets(lengths, width, most)
    choice = jnp.int32(0)
    for size in SIZES:
        choice = choice + (total - FIRST - SECOND > size).astype(jnp.int32)
    size_ref[0] = choice

    new, gate = fresh[...].astype(jnp.float32), gates[...].astype(jnp.float32)
    heads = gate.shape[1]
    lane = iota((req, new.shape[1]), 1)
    size = new.shape[1] // heads
    spread = jnp.zeros((req, new.shape[1]), jnp.float32)
    for h in range(heads):
        inside = (lane >= h * size) & (lane < (h + 1) * size)
        spread = jnp.where(inside, gate[:, h : h + 1], spread)
    packed[...] = jnp.concatenate([new, spread], axis=0).astype(jnp.bfloat16)

    def pack(r):
        chosen = select(slot, factor, r)
        at = pl.ds(pl.multiple_of(ahead[r] * SLOTS, SLOTS), most * SLOTS)
        for i in range(2):
            if r >= eager:
                slab(i, r).wait()
            row_buf[i, at, :] = dot(chosen, raw[i, r]).astype(jnp.bfloat16)

    for r in range(req):
        if r < eager:
            for i in range(2):
                slab(i, r).wait()
        if r < SURE:
            pack(r)
        else:
            pl.when(needed[r])(functools.partial(pack, r))
    out[...] = row_buf[:, : FIRST * SLOTS, :]


def first_part(n_seq, lengths, keep, weight, fresh, gates, keys, values):
    req, pos, width = keys.shape
    half = pos // 2
    hbm = pl.BlockSpec(memory_space=pl.ANY)
    vmem = pl.BlockSpec(memory_space=pltpu.VMEM)
    return pl.pallas_call(
        functools.partial(first_kernel, n_seq),
        out_shape=(
            pltpu.VMEM((2, FIRST * SLOTS, width), jnp.bfloat16),
            pltpu.VMEM((fresh.shape[0] + req, width), jnp.bfloat16),
            jax.ShapeDtypeStruct((1,), jnp.int32),
        ),
        in_specs=[hbm] * 7,
        out_specs=(vmem, vmem, pl.BlockSpec(memory_space=pltpu.SMEM)),
        scratch_shapes=[
            pltpu.SMEM(lengths.shape, jnp.int32),
            pltpu.VMEM((req, half), jnp.int32),
            pltpu.VMEM((req, half), jnp.float32),
            pltpu.VMEM(fresh.shape, fresh.dtype),
            pltpu.VMEM(gates.shape, gates.dtype),
            pltpu.VMEM((2, req, half, width), jnp.bfloat16),
            pltpu.VMEM((2, (FIRST - 1) * SLOTS + half // 2, width), jnp.bfloat16),
            pltpu.SemaphoreType.DMA((5,)),
            pltpu.SemaphoreType.DMA((2, req)),
        ],
        compiler_params=pltpu.CompilerParams(vmem_limit_bytes=VMEM_LIMIT),
        cost_estimate=LIGHT,
        name="compact_first_sent",
    )(*far(lengths, keep, weight, fresh, gates, keys, values))


def own_kernel(
    n_seq, len_ref, keep, weight, gates, keys, values, early, *rest
):
    out_k, out_v, chunk, log_ref, level_ref, total_ref = rest[:6]
    lengths, raw, late, forget, rows, zeros, sem_s, sem_l, sem_r, sem_o, sem_z = rest[6:]
    own, sent = half_of("seq", n_seq)
    seq = lax.axis_index("seq")
    heads, req, pos = gates.shape
    half = pos // 2
    slots = half // 2
    most = half // BLOCK
    first = FIRST // most
    pad = forget.shape[1] // req
    small = fetch([(len_ref, lengths)], sem_s)
    both = ((0, keys), (1, values))
    late_slabs = fetch(
        [
            (source.at[r, lanes(sent, half), :], late.at[i, r - first])
            for r in range(first, req)
            for i, source in both
        ],
        sem_l,
    )
    slabs = fetch(
        [
            (source.at[r, lanes(own, half), :], raw.at[i, r])
            for r in range(req)
            for i, source in both
        ],
        sem_r,
    )
    zeros[...] = jnp.zeros_like(zeros)
    stores = fetch([(zeros, out.at[:, lanes(sent, slots), :]) for out in (out_k, out_v)], sem_z)
    chunk[:, : FIRST * SLOTS, :] = early[...]
    chunk[:, FIRST * SLOTS :, :] = jnp.zeros(
        (2, chunk.shape[1] - FIRST * SLOTS, chunk.shape[2]), chunk.dtype
    )
    upto, block, after = block_masks(half)
    for copy in small:
        copy.wait()
    ahead, alive, _ = offsets(lengths, seq * pos + sent * half, most)

    forget[...] = jnp.zeros_like(forget)
    live = seq * pos + iota((req, pos), 1) < by_row(lengths, iota((req, pos), 0))
    for h in range(heads):
        gate = jnp.where(live, gates[h], 0.0)
        for c in range(pos // LANES):
            forget[c, pl.ds(h, req, stride=pad), :] = gate[:, c * LANES : (c + 1) * LANES]
    flat = jnp.concatenate([forget[c] for c in range(pos // LANES)], axis=1)
    total_ref[...] = jnp.broadcast_to(jnp.sum(flat, axis=1, keepdims=True), total_ref.shape)
    ends = iota((pos, slots), 1) >> SLOT_LOG
    begins = iota((pos, slots), 0) >> BLOCK_LOG
    last = iota((req * pad, slots), 1) & (SLOTS - 1) == SLOTS - 1

    for i, h in enumerate((own, sent)):
        slot, factor = plan(
            keep[:, lanes(h, half)],
            weight[:, lanes(h, half)],
            seq * pos + h * half,
            lengths,
            upto,
            block,
        )
        near = half // LANES
        inner = split_dot(
            jnp.concatenate([forget[h * near + c] for c in range(near)], axis=1), after
        )
        beyond = split_dot(
            flat, (begins > ends + h * (half // BLOCK)).astype(jnp.float32).astype(jnp.bfloat16)
        )
        spread = jnp.exp(inner)
        high = spread.astype(jnp.bfloat16).astype(jnp.float32)
        planes = three(inner) + (high, spread - high, jnp.ones_like(inner))
        found = []
        for r in range(req):
            chosen = select(slot, factor, r)
            stack = jnp.concatenate([x[r * pad : (r + 1) * pad] for x in planes], axis=0)
            found.append(dot_nt(stack.astype(jnp.bfloat16), chosen))
            if i == 0:
                for k, out in enumerate((out_k, out_v)):
                    slabs[2 * r + k].wait()
                    rows[k, r] = dot(chosen, raw[k, r]).astype(jnp.bfloat16)
                    stores.append(
                        pltpu.make_async_copy(
                            rows.at[k, r], out.at[r, lanes(own, slots), :], sem_o.at[2 * r + k]
                        )
                    )
                    stores[-1].start()
            elif r >= first:
                for k in range(2):
                    late_slabs[2 * (r - first) + k].wait()

                @pl.when((ahead[r] + alive[r] > FIRST) & (alive[r] > 0))
                def _(r=r, chosen=chosen):
                    at = pl.ds(pl.multiple_of(ahead[r] * SLOTS, SLOTS), slots)
                    for k in range(2):
                        chunk[k, at, :] = dot(chosen, late[k, r - first]).astype(jnp.bfloat16)
        at = [
            jnp.concatenate([x[p * pad : (p + 1) * pad] for x in found], axis=0) for p in range(6)
        ]
        filled = at[5] > 0.5
        kept = at[0] + at[1] + at[2]
        merged = jnp.log(jnp.where(filled, at[3] + at[4], 1.0))
        level_ref[i] = jnp.where(filled, jnp.where(last, merged, kept) + beyond, EMPTY_LOG)
        for k in range(heads):
            log_ref[k, :, lanes(h, slots)] = level_ref[i, pl.ds(k, req, stride=pad), :]
    for copy in stores:
        copy.wait()


def own_part(n_seq, lengths, keep, weight, forget, keys, values, early):
    req, pos, width = keys.shape
    heads = forget.shape[0]
    half, slots, pad = pos // 2, pos // 4, -(-heads // 8) * 8
    late = req - FIRST // (half // BLOCK)
    hbm = pl.BlockSpec(memory_space=pl.ANY)
    vmem = pl.BlockSpec(memory_space=pltpu.VMEM)
    whole = pltpu.HBM((req, 2 * slots, width), jnp.bfloat16)
    return pl.pallas_call(
        functools.partial(own_kernel, n_seq),
        out_shape=(
            whole,
            whole,
            pltpu.VMEM((2, req * slots, width), jnp.bfloat16),
            pltpu.VMEM((heads, req, 2 * slots), jnp.float32),
            pltpu.VMEM((2, req * pad, slots), jnp.float32),
            pltpu.VMEM((req * pad, LANES), jnp.float32),
        ),
        in_specs=[vmem] * 4 + [hbm] * 2 + [vmem],
        out_specs=(hbm, hbm, vmem, vmem, vmem, vmem),
        scratch_shapes=[
            pltpu.SMEM(lengths.shape, jnp.int32),
            pltpu.VMEM((2, req, half, width), jnp.bfloat16),
            pltpu.VMEM((2, late, half, width), jnp.bfloat16),
            pltpu.VMEM((pos // LANES, req * pad, LANES), jnp.float32),
            pltpu.VMEM((2, req, slots, width), jnp.bfloat16),
            pltpu.VMEM((req, slots, width), jnp.bfloat16),
            pltpu.SemaphoreType.DMA((1,)),
            pltpu.SemaphoreType.DMA((2 * late,)),
            pltpu.SemaphoreType.DMA((2 * req,)),
            pltpu.SemaphoreType.DMA((2 * req,)),
            pltpu.SemaphoreType.DMA((2,)),
        ],
        compiler_params=pltpu.CompilerParams(vmem_limit_bytes=VMEM_LIMIT),
        cost_estimate=LIGHT,
        name="compact_own",
    )(*near(lengths, keep, weight, forget), *far(keys, values), *near(early))


def attend_kernel(n_seq, n_grp, heads, *refs):
    len_hbm, route_hbm, out_k, out_v, late, level, total = refs[:7]
    tokens, rest = refs[7 : 7 + n_grp], refs[7 + n_grp :]
    _, _, stats_ref, picked_ref, lengths, route, own_rows, scores, sem_s, sem_r = rest
    own, sent = half_of("seq", n_seq)
    kinds, width = picked_ref.shape
    req = kinds // 4
    size = width // heads
    slots = own_rows.shape[2]
    pad = total.shape[0] // req
    small = fetch([(len_hbm, lengths), (route_hbm, route)], sem_s)
    slabs = fetch(
        [
            (out_k.at[:, lanes(own, slots), :], own_rows.at[0]),
            (out_v.at[:, lanes(own, slots), :], own_rows.at[1]),
        ],
        sem_r,
    )
    for copy in small:
        copy.wait()
    start = lax.axis_index("seq") * (4 * slots) + sent * (2 * slots)
    ahead, _, _ = offsets(lengths, start, slots // SLOTS)

    def sent_part(i, r):
        at = pl.multiple_of(ahead[r] * SLOTS, SLOTS)
        return late[i, pl.ds(at, slots), :]

    shape = (kinds, kinds)
    to, frm = iota(shape, 0), iota(shape, 1)
    wanted = by_row(route, to % req)
    me = lax.axis_index("grp")
    picked = jnp.zeros((kinds, width), jnp.float32)
    for k in range(n_grp):
        source = lax.rem(me + n_grp - k, n_grp)
        hit = (to // req == frm // req) & (wanted == source * req + frm % req)
        picked = picked + dot(hit.astype(jnp.float32).astype(jnp.bfloat16), tokens[k][...])
    picked_ref[...] = picked
    for copy in slabs:
        copy.wait()

    lane, row = iota((pad, width), 1), iota((pad, width), 0)
    mine = (lane >= row * size) & (lane < (row + 1) * size)
    for r in range(req):
        query = jnp.where(mine, picked[r : r + 1, :], 0.0).astype(jnp.bfloat16)
        here = slice(r * pad, (r + 1) * pad)
        scores[here, :slots] = dot_nt(query, own_rows[0, r])
        scores[here, slots:] = dot_nt(query, sent_part(0, r))
    logit = scores[...] * (size**-0.5) + jnp.concatenate([level[0], level[1]], axis=1)
    top = jnp.max(logit, axis=1, keepdims=True)
    weights = jnp.exp(logit - top).astype(jnp.bfloat16).astype(jnp.float32)
    mass = jnp.sum(weights, axis=1, keepdims=True)

    def spread_out(column, r):
        return jnp.sum(
            jnp.where(mine, column[r * pad : (r + 1) * pad], 0.0), axis=0, keepdims=True
        )

    for r in range(req):
        w = weights[r * pad : (r + 1) * pad].astype(jnp.bfloat16)
        acc = dot(w[:, :slots], own_rows[1, r]) + dot(w[:, slots:], sent_part(1, r))
        acc = jnp.sum(jnp.where(mine, acc, 0.0), axis=0, keepdims=True)
        for p, x in enumerate((top, mass, total[:, :1])):
            stats_ref[p * req + r : p * req + r + 1, :] = spread_out(x, r)
        stats_ref[3 * req + r : 3 * req + r + 1, :] = acc


def attend_part(n_seq, n_grp, heads, lengths, route, out_k, out_v, late, level, total, tokens):
    req, rows, width = out_k.shape
    slots = rows // 2
    hbm = pl.BlockSpec(memory_space=pl.ANY)
    vmem = pl.BlockSpec(memory_space=pltpu.VMEM)
    whole = pltpu.HBM(out_k.shape, out_k.dtype)
    small = pltpu.VMEM((4 * req, width), jnp.float32)
    return pl.pallas_call(
        functools.partial(attend_kernel, n_seq, n_grp, heads),
        out_shape=(whole, whole, small, small),
        in_specs=[vmem] * 2 + [hbm] * 2 + [vmem] * (3 + n_grp),
        out_specs=(hbm, hbm, vmem, vmem),
        scratch_shapes=[
            pltpu.SMEM(lengths.shape, jnp.int32),
            pltpu.SMEM(route.shape, jnp.int32),
            pltpu.VMEM((2, req, slots, width), jnp.bfloat16),
            pltpu.VMEM((total.shape[0], rows), jnp.float32),
            pltpu.SemaphoreType.DMA((2,)),
            pltpu.SemaphoreType.DMA((2,)),
        ],
        input_output_aliases={2: 0, 3: 1},
        compiler_params=pltpu.CompilerParams(vmem_limit_bytes=VMEM_LIMIT),
        cost_estimate=LIGHT,
        name="attend",
    )(
        *near(lengths, route),
        *far(out_k, out_v),
        *near(late, level, total),
        *near(*tokens),
    )


def merge_kernel(count, relative, size, *refs):
    stats, refs = refs[:count], refs[count:]
    picked_ref, weight_ref, _, later_ref, out_ref = refs
    req, width = later_ref.shape
    seq = lax.axis_index("seq")
    places = [lax.rem(seq + count - k, count) if relative else jnp.int32(k) for k in range(count)]
    tops, masses, totals, accs = [
        [ref[p * req : (p + 1) * req, :] for ref in stats] for p in range(4)
    ]

    def later(place):
        total = jnp.zeros_like(totals[0])
        for k in range(count):
            total = total + jnp.where(places[k] > place, totals[k], 0.0)
        return total

    tops = [tops[k] + later(places[k]) for k in range(count)]
    top = functools.reduce(jnp.maximum, tops)
    scales = [jnp.exp(t - top) for t in tops]
    mass = sum(s * x for s, x in zip(scales, masses))
    acc = sum(s * x for s, x in zip(scales, accs))
    query, key, value, gate = [picked_ref[p * req : (p + 1) * req, :] for p in range(4)]
    one, two = iota((width, width), 0), iota((width, width), 1)
    same = (one // size == two // size).astype(jnp.float32).astype(jnp.bfloat16)
    own = split_dot(query * key, same) * (size**-0.5)
    past = top + gate
    joint = jnp.maximum(past, own)
    scale, self_weight = jnp.exp(past - joint), jnp.exp(own - joint)
    attended = (scale * acc + self_weight * value) / (scale * mass + self_weight)
    later_ref[...] = later(seq)
    out_ref[...] = dot(attended.astype(jnp.bfloat16), weight_ref[...])


def merge_part(stats, relative, picked, out_weight, second, size):
    req, width = stats[0].shape[0] // 4, stats[0].shape[1]
    vmem = pl.BlockSpec(memory_space=pltpu.VMEM)
    return pl.pallas_call(
        functools.partial(merge_kernel, len(stats), relative, size),
        out_shape=(
            pltpu.VMEM((req, width), jnp.float32),
            pltpu.VMEM((req, out_weight.shape[1]), jnp.float32),
        ),
        in_specs=[vmem] * (len(stats) + 2) + [pl.BlockSpec(memory_space=pl.ANY)],
        out_specs=(vmem, vmem),
        compiler_params=pltpu.CompilerParams(vmem_limit_bytes=VMEM_LIMIT),
        cost_estimate=MERGE,
        name="merge_and_project",
    )(*near(*stats, picked, out_weight), second)


def sum_kernel(count, size, *refs):
    parts, (later_ref, log_ref, _, out, decay_ref) = refs[:count], refs[count:]
    me = lax.axis_index("head")
    total = jnp.zeros(out.shape, jnp.float32)
    for place in range(count):
        for k in range(count):
            total = total + jnp.where(lax.rem(me + count - k, count) == place, parts[k][...], 0.0)
    out[...] = total.astype(out.dtype)
    for h in range(log_ref.shape[0]):
        decay_ref[h] = jnp.exp(log_ref[h] + later_ref[:, h * size : h * size + 1])


def sum_part(parts, later, logs, placed, size):
    vmem = pl.BlockSpec(memory_space=pltpu.VMEM)
    return pl.pallas_call(
        functools.partial(sum_kernel, len(parts), size),
        out_shape=(
            pltpu.HBM(parts[0].shape, jnp.bfloat16),
            pltpu.HBM(logs.shape, jnp.float32),
        ),
        in_specs=[vmem] * (len(parts) + 3),
        out_specs=(vmem, vmem),
        compiler_params=pltpu.CompilerParams(vmem_limit_bytes=VMEM_LIMIT),
        cost_estimate=LIGHT,
        name="sum_heads_and_decay",
    )(*parts, later, logs, placed)


def place_kernel(n_seq, first, count, *refs):
    parts, refs = refs[:count], refs[count:]
    len_ref, _, _, out_k, out_v, placed_ref, lengths, sem_s, sem = refs
    _, sent = half_of("seq", n_seq)
    (load,) = fetch([(len_ref, lengths)], sem_s)
    placed_ref[...] = jnp.zeros_like(placed_ref)
    load.wait()
    req, rows, _ = out_k.shape
    slots = rows // 2
    most = slots // SLOTS
    seq = lax.axis_index("seq")
    if n_seq == 2:
        start = (1 - seq) * (4 * slots) + seq * (2 * slots)
    else:
        start = seq * (4 * slots) + sent * (2 * slots)
    ahead, live, _ = offsets(lengths, start, most)
    for phase in ("start", "wait"):
        begin = first
        for p, part in enumerate(parts):
            held = part.shape[1] // SLOTS
            for r in range(req):
                if begin >= (r + 1) * most:
                    continue
                low = jnp.clip(begin - ahead[r], 0, live[r])
                high = jnp.clip(begin + held - ahead[r], 0, live[r])
                size = pl.multiple_of((high - low) * SLOTS, SLOTS)

                @pl.when(high > low)
                def _(p=p, part=part, begin=begin, r=r, low=low, size=size):
                    src = pl.multiple_of((ahead[r] + low - begin) * SLOTS, SLOTS)
                    dst = pl.multiple_of(sent * slots + low * SLOTS, SLOTS)
                    for i, out in enumerate((out_k, out_v)):
                        copy = pltpu.make_async_copy(
                            part.at[i, pl.ds(src, size), :],
                            out.at[r, pl.ds(dst, size), :],
                            sem.at[p, i, r],
                        )
                        getattr(copy, phase)()

            begin += held


def place_part(n_seq, first, parts, lengths, out_k, out_v):
    hbm = pl.BlockSpec(memory_space=pl.ANY)
    vmem = pl.BlockSpec(memory_space=pltpu.VMEM)
    shape = pltpu.HBM(out_k.shape, out_k.dtype)
    count = len(parts)
    return pl.pallas_call(
        functools.partial(place_kernel, n_seq, first, count),
        out_shape=(shape, shape, pltpu.VMEM((8, LANES), jnp.float32)),
        in_specs=[vmem] * (count + 1) + [hbm, hbm],
        out_specs=(hbm, hbm, vmem),
        scratch_shapes=[
            pltpu.SMEM(lengths.shape, jnp.int32),
            pltpu.SemaphoreType.DMA((1,)),
            pltpu.SemaphoreType.DMA((count, 2, lengths.shape[0])),
        ],
        input_output_aliases={count + 1: 0, count + 2: 1},
        compiler_params=pltpu.CompilerParams(vmem_limit_bytes=VMEM_LIMIT),
        cost_estimate=LIGHT,
        name="place_received",
    )(*near(*parts, lengths), *far(out_k, out_v))


def others(value, axis):
    count = lax.axis_size(axis)
    return [value] + [
        lax.ppermute(value, axis, [(i, (i + k) % count) for i in range(count)])
        for k in range(1, count)
    ]


def swap(value, n_seq):
    return lax.ppermute(value, "seq", [(0, 1), (1, 0)]) if n_seq == 2 else value


def shards(
    keys, values, log_forget, keep, merge_weight, lengths, route, fresh, new_forget, out_weight
):
    req, pos, width = keys.shape
    heads = log_forget.shape[1]
    size = width // heads
    n_seq, n_grp = lax.axis_size("seq"), lax.axis_size("grp")
    early, packed, choice = first_part(
        n_seq,
        lengths,
        keep,
        merge_weight,
        fresh.reshape(3 * req, width),
        new_forget,
        keys,
        values,
    )
    exchange = functools.partial(swap, n_seq=n_seq)
    first_received = exchange(early)
    tokens = others(packed, "grp")
    out_k, out_v, late, logs, level, total = own_part(
        n_seq,
        lengths,
        keep,
        merge_weight,
        log_forget.transpose(1, 0, 2),
        keys,
        values,
        early,
    )
    begin, end = FIRST * SLOTS, (FIRST + SECOND) * SLOTS
    rest = late.shape[1] - end

    def finish(rows, early, late, logs, level, total, tokens, out_weight, lengths, route, *outs):
        second = exchange(late[:, begin:end])
        out_k, out_v, stats, picked = attend_part(
            n_seq, n_grp, heads, lengths, route, *outs, late, level, total, tokens
        )
        if n_seq == 2:
            all_stats = others(stats, "seq")
        else:
            gathered = lax.all_gather(stats, "seq")
            all_stats = [gathered[i] for i in range(n_seq)]
        third = exchange(late[:, end : end + rows])
        later, partial = merge_part(all_stats, n_seq == 2, picked, out_weight, second, size)
        out_k, out_v, placed = place_part(n_seq, 0, (early, second), lengths, out_k, out_v)
        layer_out, decay = sum_part(others(partial, "head"), later, logs, placed, size)
        out_k, out_v, _ = place_part(n_seq, FIRST + SECOND, (third,), lengths, out_k, out_v)
        return decay, layer_out, out_k, out_v

    operands = (first_received, late, logs, level, total, tokens, out_weight, lengths, route)
    operands += (out_k, out_v)
    if n_seq == 2:
        branches = [
            functools.partial(finish, blocks * SLOTS) for blocks in SIZES + (rest // SLOTS,)
        ]
        decay, layer_out, out_k, out_v = lax.switch(choice[0], branches, *operands)
    else:
        decay, layer_out, out_k, out_v = finish(rest, *operands)
    if n_seq != 2:
        out_k, out_v = (
            lax.all_to_all(x, "seq", split_axis=1, concat_axis=1, tiled=True) for x in (out_k, out_v)
        )
    return out_k, out_v, decay.transpose(1, 0, 2), layer_out


def solution(mesh):
    return jax.shard_map(
        shards,
        mesh=mesh,
        in_specs=(
            P("grp", "seq", "head"),
            P("grp", "seq", "head"),
            P("grp", "head", "seq"),
            P("grp", "seq"),
            P("grp", "seq"),
            P("grp"),
            P("grp"),
            P(None, "grp", "head"),
            P("grp", "head"),
            P("head", "seq"),
        ),
        out_specs=(
            P("grp", "seq", "head"),
            P("grp", "seq", "head"),
            P("grp", "head", "seq"),
            P("grp", "seq"),
        ),
        check_vma=False,
    )
```

```python
import functools

import jax
import jax.numpy as jnp
from jax import lax
from jax.experimental import pallas as pl
from jax.experimental.pallas import tpu as pltpu
from jax.sharding import PartitionSpec as P

BLOCK = 64
SLOTS = 32
LANES = 128
BLOCK_LOG = BLOCK.bit_length() - 1
SLOT_LOG = SLOTS.bit_length() - 1
EMPTY_LOG = -10000.0
FIRST = 8
SECOND = 3
SIZES = (6, 9, 11, 13, 14, 15, 17, 19)
LAST = 4
SURE = 2
EAGER = 5
VMEM_LIMIT = 16 * 1024 * 1024


LIGHT = pl.CostEstimate(flops=1, bytes_accessed=1, transcendentals=0)
MERGE = pl.CostEstimate(flops=1 << 36, bytes_accessed=1, transcendentals=0)


def dot(a, b):
    return lax.dot_general(a, b, (((1,), (0,)), ((), ())), preferred_element_type=jnp.float32)


def dot_nt(a, b):
    return lax.dot_general(a, b, (((1,), (1,)), ((), ())), preferred_element_type=jnp.float32)


def iota(shape, dim):
    return lax.broadcasted_iota(jnp.int32, shape, dim)


def three(x):
    hi = x.astype(jnp.bfloat16).astype(jnp.float32)
    rest = x - hi
    mid = rest.astype(jnp.bfloat16).astype(jnp.float32)
    return hi, mid, rest - mid


def split_dot(x, ones):
    rows = x.shape[0]
    parts = dot(jnp.concatenate(three(x), axis=0).astype(jnp.bfloat16), ones)
    return parts[:rows] + parts[rows : 2 * rows] + parts[2 * rows :]


def half_of(axis, count):
    own = lax.axis_index(axis) if count == 2 else jnp.int32(0)
    return own, 1 - own


def by_row(ref, row):
    picked = jnp.zeros_like(row)
    for r in range(ref.shape[0]):
        picked = jnp.where(row == r, ref[r], picked)
    return picked


def live_blocks(lengths, r, start, most):
    return jnp.clip((lengths[r] - start) >> BLOCK_LOG, 0, most)


def offsets(lengths, start, most):
    total = jnp.int32(0)
    ahead, live = [], []
    for r in range(lengths.shape[0]):
        ahead.append(total)
        live.append(live_blocks(lengths, r, start, most))
        total = total + live[-1]
    return ahead, live, total


def mask(condition):
    return condition.astype(jnp.float32).astype(jnp.bfloat16)


def block_masks(width):
    one, two = iota((width, width), 0), iota((width, width), 1)
    same = (one ^ two) < BLOCK
    return mask(same & (one <= two)), mask(same), mask(same & (one > two))


def plan(keep, weight, start, len_ref, upto, block):
    rows, width = keep.shape
    kept = keep == 1
    rank = dot(keep.astype(jnp.float32).astype(jnp.bfloat16), upto) - 1.0
    weighted = jnp.where(kept, 0.0, weight)
    share = (weighted / split_dot(weighted, block)).astype(jnp.bfloat16).astype(jnp.float32)
    lane, row = iota((rows, width), 1), iota((rows, width), 0)
    slot = jnp.where(kept, rank.astype(jnp.int32), SLOTS - 1) + (lane >> BLOCK_LOG) * SLOTS
    slot = jnp.where(start + lane < by_row(len_ref, row), slot, -1)
    return slot, jnp.where(kept, 1.0, share)


def select(slot, factor, r):
    width = slot.shape[1]
    shape = (width // 2, width)
    hit = iota(shape, 0) == slot[r : r + 1, :]
    return jnp.where(hit, jnp.broadcast_to(factor[r : r + 1, :], shape), 0.0).astype(jnp.bfloat16)


def lanes(half, width):
    return pl.ds(pl.multiple_of(half * width, width), width)


def far(*arrays):
    return [pltpu.with_memory_space_constraint(x, pltpu.HBM) for x in arrays]


def near(*arrays):
    return [pltpu.with_memory_space_constraint(x, pltpu.VMEM) for x in arrays]


def fetch(pairs, sem):
    copies = [pltpu.make_async_copy(src, dst, sem.at[i]) for i, (src, dst) in enumerate(pairs)]
    for copy in copies:
        copy.start()
    return copies


def first_kernel(n_seq, len_hbm, keep_hbm, weight_hbm, fresh_hbm, gate_hbm, keys, values, *rest):
    out, packed, size_ref, lengths, keep, weight, fresh, gates, raw, row_buf, sem_s, sem_r = rest
    _, sent = half_of("seq", n_seq)
    req, width = keep.shape
    most = width // BLOCK
    small = fetch(
        [
            (len_hbm, lengths),
            (keep_hbm.at[:, lanes(sent, width)], keep),
            (weight_hbm.at[:, lanes(sent, width)], weight),
            (fresh_hbm, fresh),
            (gate_hbm, gates),
        ],
        sem_s,
    )

    channels = keys.shape[2]

    def slab(i, r):
        source = (keys, values)[i].at[r, lanes(sent, width), :]
        target = raw.at[r, :, pl.ds(i * channels, channels)]
        return pltpu.make_async_copy(source, target, sem_r.at[i, r])

    eager = min(EAGER, req)
    for r in range(eager):
        for i in range(2):
            slab(i, r).start()
    row_buf[...] = jnp.zeros_like(row_buf)
    upto, block, _ = block_masks(width)
    for copy in small:
        copy.wait()
    start = lax.axis_index("seq") * (2 * width) + sent * width
    ahead, live, _ = offsets(lengths, start, most)
    needed = [(ahead[r] < FIRST) & (live[r] > 0) for r in range(req)]
    for r in range(eager, req):

        @pl.when(needed[r])
        def _(r=r):
            for i in range(2):
                slab(i, r).start()

    slot, factor = plan(keep[...], weight[...], start, lengths, upto, block)
    _, _, total = offsets(lengths, width, most)
    choice = jnp.int32(0)
    for size in SIZES:
        choice = choice + (total - FIRST - SECOND > size).astype(jnp.int32)
    size_ref[0] = choice

    new, gate = fresh[...].astype(jnp.float32), gates[...].astype(jnp.float32)
    heads = gate.shape[1]
    lane = iota((req, new.shape[1]), 1)
    size = new.shape[1] // heads
    spread = jnp.zeros((req, new.shape[1]), jnp.float32)
    for h in range(heads):
        inside = (lane >= h * size) & (lane < (h + 1) * size)
        spread = jnp.where(inside, gate[:, h : h + 1], spread)
    packed[...] = jnp.concatenate([new, spread], axis=0).astype(jnp.bfloat16)

    def pack(r):
        chosen = select(slot, factor, r)
        at = pl.ds(pl.multiple_of(ahead[r] * SLOTS, SLOTS), most * SLOTS)
        if r >= eager:
            for i in range(2):
                slab(i, r).wait()
        rows = dot(chosen, raw[r]).astype(jnp.bfloat16)
        for i in range(2):
            row_buf[i, at, :] = rows[:, i * channels : (i + 1) * channels]

    for r in range(req):
        if r < eager:
            for i in range(2):
                slab(i, r).wait()
        if r < SURE:
            pack(r)
        else:
            pl.when(needed[r])(functools.partial(pack, r))
    out[...] = row_buf[:, : FIRST * SLOTS, :]


def first_part(n_seq, lengths, keep, weight, fresh, gates, keys, values):
    req, pos, width = keys.shape
    half = pos // 2
    hbm = pl.BlockSpec(memory_space=pl.ANY)
    vmem = pl.BlockSpec(memory_space=pltpu.VMEM)
    return pl.pallas_call(
        functools.partial(first_kernel, n_seq),
        out_shape=(
            pltpu.VMEM((2, FIRST * SLOTS, width), jnp.bfloat16),
            pltpu.VMEM((fresh.shape[0] + req, width), jnp.bfloat16),
            jax.ShapeDtypeStruct((1,), jnp.int32),
        ),
        in_specs=[hbm] * 7,
        out_specs=(vmem, vmem, pl.BlockSpec(memory_space=pltpu.SMEM)),
        scratch_shapes=[
            pltpu.SMEM(lengths.shape, jnp.int32),
            pltpu.VMEM((req, half), jnp.int32),
            pltpu.VMEM((req, half), jnp.float32),
            pltpu.VMEM(fresh.shape, fresh.dtype),
            pltpu.VMEM(gates.shape, gates.dtype),
            pltpu.VMEM((req, half, 2 * width), jnp.bfloat16),
            pltpu.VMEM((2, (FIRST - 1) * SLOTS + half // 2, width), jnp.bfloat16),
            pltpu.SemaphoreType.DMA((5,)),
            pltpu.SemaphoreType.DMA((2, req)),
        ],
        compiler_params=pltpu.CompilerParams(vmem_limit_bytes=VMEM_LIMIT),
        cost_estimate=LIGHT,
        name="compact_first_sent",
    )(*far(lengths, keep, weight, fresh, gates, keys, values))


def own_kernel(
    n_seq, len_ref, keep, weight, gates, keys, values, early, *rest
):
    out_k, out_v, chunk, rows, log_ref, level_ref, total_ref = rest[:7]
    lengths, raw, late, forget, zeros, sem_s, sem_l, sem_r, sem_o, sem_z = rest[7:]
    own, sent = half_of("seq", n_seq)
    seq = lax.axis_index("seq")
    heads, req, pos = gates.shape
    half = pos // 2
    slots = half // 2
    most = half // BLOCK
    first = FIRST // most
    pad = forget.shape[1] // req
    small = fetch([(len_ref, lengths)], sem_s)
    both = ((0, keys), (1, values))
    channels = keys.shape[2]

    def part(i):
        return pl.ds(i * channels, channels)

    late_slabs = fetch(
        [
            (source.at[r, lanes(sent, half), :], late.at[r - first, :, part(i)])
            for r in range(first, req)
            for i, source in both
        ],
        sem_l,
    )
    slabs = fetch(
        [
            (source.at[r, lanes(own, half), :], raw.at[r, :, part(i)])
            for r in range(req)
            for i, source in both
        ],
        sem_r,
    )
    zeros[...] = jnp.zeros_like(zeros)
    stores = fetch([(zeros, out.at[:, lanes(sent, slots), :]) for out in (out_k, out_v)], sem_z)
    chunk[:, : FIRST * SLOTS, :] = early[...]
    chunk[:, FIRST * SLOTS :, :] = jnp.zeros(
        (2, chunk.shape[1] - FIRST * SLOTS, chunk.shape[2]), chunk.dtype
    )
    upto, block, after = block_masks(half)
    for copy in small:
        copy.wait()
    ahead, alive, _ = offsets(lengths, seq * pos + sent * half, most)

    forget[...] = jnp.zeros_like(forget)
    live = seq * pos + iota((req, pos), 1) < by_row(lengths, iota((req, pos), 0))
    for h in range(heads):
        gate = jnp.where(live, gates[h], 0.0)
        for c in range(pos // LANES):
            forget[c, pl.ds(h, req, stride=pad), :] = gate[:, c * LANES : (c + 1) * LANES]
    flat = jnp.concatenate([forget[c] for c in range(pos // LANES)], axis=1)
    total_ref[...] = jnp.broadcast_to(jnp.sum(flat, axis=1, keepdims=True), total_ref.shape)
    ends = iota((pos, slots), 1) >> SLOT_LOG
    begins = iota((pos, slots), 0) >> BLOCK_LOG
    last = iota((req * pad, slots), 1) & (SLOTS - 1) == SLOTS - 1

    for i, h in enumerate((own, sent)):
        slot, factor = plan(
            keep[:, lanes(h, half)],
            weight[:, lanes(h, half)],
            seq * pos + h * half,
            lengths,
            upto,
            block,
        )
        near = half // LANES
        inner = split_dot(
            jnp.concatenate([forget[h * near + c] for c in range(near)], axis=1), after
        )
        beyond = split_dot(
            flat, (begins > ends + h * (half // BLOCK)).astype(jnp.float32).astype(jnp.bfloat16)
        )
        spread = jnp.exp(inner)
        high = spread.astype(jnp.bfloat16).astype(jnp.float32)
        planes = three(inner) + (high, spread - high, jnp.ones_like(inner))
        found = []
        for r in range(req):
            chosen = select(slot, factor, r)
            stack = jnp.concatenate([x[r * pad : (r + 1) * pad] for x in planes], axis=0)
            found.append(dot_nt(stack.astype(jnp.bfloat16), chosen))
            if i == 0:
                for k in range(2):
                    slabs[2 * r + k].wait()
                made = dot(chosen, raw[r]).astype(jnp.bfloat16)
                for k, out in enumerate((out_k, out_v)):
                    rows[k, r] = made[:, k * channels : (k + 1) * channels]
                    stores.append(
                        pltpu.make_async_copy(
                            rows.at[k, r], out.at[r, lanes(own, slots), :], sem_o.at[2 * r + k]
                        )
                    )
                    stores[-1].start()
            elif r >= first:
                for k in range(2):
                    late_slabs[2 * (r - first) + k].wait()

                @pl.when((ahead[r] + alive[r] > FIRST) & (alive[r] > 0))
                def _(r=r, chosen=chosen):
                    at = pl.ds(pl.multiple_of(ahead[r] * SLOTS, SLOTS), slots)
                    made = dot(chosen, late[r - first]).astype(jnp.bfloat16)
                    for k in range(2):
                        chunk[k, at, :] = made[:, k * channels : (k + 1) * channels]
        at = [
            jnp.concatenate([x[p * pad : (p + 1) * pad] for x in found], axis=0) for p in range(6)
        ]
        filled = at[5] > 0.5
        kept = at[0] + at[1] + at[2]
        merged = jnp.log(jnp.where(filled, at[3] + at[4], 1.0))
        level_ref[i] = jnp.where(filled, jnp.where(last, merged, kept) + beyond, EMPTY_LOG)
        for k in range(heads):
            log_ref[k, :, lanes(h, slots)] = level_ref[i, pl.ds(k, req, stride=pad), :]
    for copy in stores:
        copy.wait()


def own_part(n_seq, lengths, keep, weight, forget, keys, values, early):
    req, pos, width = keys.shape
    heads = forget.shape[0]
    half, slots, pad = pos // 2, pos // 4, -(-heads // 8) * 8
    late = req - FIRST // (half // BLOCK)
    hbm = pl.BlockSpec(memory_space=pl.ANY)
    vmem = pl.BlockSpec(memory_space=pltpu.VMEM)
    whole = pltpu.HBM((req, 2 * slots, width), jnp.bfloat16)
    return pl.pallas_call(
        functools.partial(own_kernel, n_seq),
        out_shape=(
            whole,
            whole,
            pltpu.VMEM((2, req * slots, width), jnp.bfloat16),
            pltpu.VMEM((2, req, slots, width), jnp.bfloat16),
            pltpu.VMEM((heads, req, 2 * slots), jnp.float32),
            pltpu.VMEM((2, req * pad, slots), jnp.float32),
            pltpu.VMEM((req * pad, LANES), jnp.float32),
        ),
        in_specs=[vmem] * 4 + [hbm] * 2 + [vmem],
        out_specs=(hbm, hbm, vmem, vmem, vmem, vmem, vmem),
        scratch_shapes=[
            pltpu.SMEM(lengths.shape, jnp.int32),
            pltpu.VMEM((req, half, 2 * width), jnp.bfloat16),
            pltpu.VMEM((late, half, 2 * width), jnp.bfloat16),
            pltpu.VMEM((pos // LANES, req * pad, LANES), jnp.float32),
            pltpu.VMEM((req, slots, width), jnp.bfloat16),
            pltpu.SemaphoreType.DMA((1,)),
            pltpu.SemaphoreType.DMA((2 * late,)),
            pltpu.SemaphoreType.DMA((2 * req,)),
            pltpu.SemaphoreType.DMA((2 * req,)),
            pltpu.SemaphoreType.DMA((2,)),
        ],
        compiler_params=pltpu.CompilerParams(vmem_limit_bytes=VMEM_LIMIT),
        cost_estimate=LIGHT,
        name="compact_own",
    )(*near(lengths, keep, weight, forget), *far(keys, values), *near(early))


def attend_kernel(n_seq, n_grp, heads, *refs):
    len_hbm, route_hbm, own_rows, late, level, total = refs[:6]
    tokens, rest = refs[6 : 6 + n_grp], refs[6 + n_grp :]
    stats_ref, picked_ref, lengths, route, scores, sem_s = rest
    _, sent = half_of("seq", n_seq)
    kinds, width = picked_ref.shape
    req = kinds // 4
    size = width // heads
    slots = own_rows.shape[2]
    pad = total.shape[0] // req
    small = fetch([(len_hbm, lengths), (route_hbm, route)], sem_s)
    for copy in small:
        copy.wait()
    start = lax.axis_index("seq") * (4 * slots) + sent * (2 * slots)
    ahead, _, _ = offsets(lengths, start, slots // SLOTS)

    def sent_part(i, r):
        at = pl.multiple_of(ahead[r] * SLOTS, SLOTS)
        return late[i, pl.ds(at, slots), :]

    shape = (kinds, kinds)
    to, frm = iota(shape, 0), iota(shape, 1)
    wanted = by_row(route, to % req)
    me = lax.axis_index("grp")
    picked = jnp.zeros((kinds, width), jnp.float32)
    for k in range(n_grp):
        source = lax.rem(me + n_grp - k, n_grp)
        hit = (to // req == frm // req) & (wanted == source * req + frm % req)
        picked = picked + dot(hit.astype(jnp.float32).astype(jnp.bfloat16), tokens[k][...])
    picked_ref[...] = picked

    lane, row = iota((pad, width), 1), iota((pad, width), 0)
    mine = (lane >= row * size) & (lane < (row + 1) * size)
    for r in range(req):
        query = jnp.where(mine, picked[r : r + 1, :], 0.0).astype(jnp.bfloat16)
        here = slice(r * pad, (r + 1) * pad)
        scores[here, :slots] = dot_nt(query, own_rows[0, r])
        scores[here, slots:] = dot_nt(query, sent_part(0, r))
    logit = scores[...] * (size**-0.5) + jnp.concatenate([level[0], level[1]], axis=1)
    top = jnp.max(logit, axis=1, keepdims=True)
    weights = jnp.exp(logit - top).astype(jnp.bfloat16).astype(jnp.float32)
    mass = jnp.sum(weights, axis=1, keepdims=True)

    def spread_out(column, r):
        return jnp.sum(
            jnp.where(mine, column[r * pad : (r + 1) * pad], 0.0), axis=0, keepdims=True
        )

    for r in range(req):
        w = weights[r * pad : (r + 1) * pad].astype(jnp.bfloat16)
        acc = dot(w[:, :slots], own_rows[1, r]) + dot(w[:, slots:], sent_part(1, r))
        acc = jnp.sum(jnp.where(mine, acc, 0.0), axis=0, keepdims=True)
        for p, x in enumerate((top, mass, total[:, :1])):
            stats_ref[p * req + r : p * req + r + 1, :] = spread_out(x, r)
        stats_ref[3 * req + r : 3 * req + r + 1, :] = acc


def attend_part(n_seq, n_grp, heads, lengths, route, own_rows, late, level, total, tokens):
    _, req, slots, width = own_rows.shape
    vmem = pl.BlockSpec(memory_space=pltpu.VMEM)
    small = pltpu.VMEM((4 * req, width), jnp.float32)
    return pl.pallas_call(
        functools.partial(attend_kernel, n_seq, n_grp, heads),
        out_shape=(small, small),
        in_specs=[vmem] * (6 + n_grp),
        out_specs=(vmem, vmem),
        scratch_shapes=[
            pltpu.SMEM(lengths.shape, jnp.int32),
            pltpu.SMEM(route.shape, jnp.int32),
            pltpu.VMEM((total.shape[0], 2 * slots), jnp.float32),
            pltpu.SemaphoreType.DMA((2,)),
        ],
        compiler_params=pltpu.CompilerParams(vmem_limit_bytes=VMEM_LIMIT),
        cost_estimate=LIGHT,
        name="attend",
    )(*near(lengths, route, own_rows, late, level, total), *near(*tokens))


def merge_kernel(count, relative, size, *refs):
    stats, refs = refs[:count], refs[count:]
    picked_ref, weight_ref, _, later_ref, out_ref = refs
    req, width = later_ref.shape
    seq = lax.axis_index("seq")
    places = [lax.rem(seq + count - k, count) if relative else jnp.int32(k) for k in range(count)]
    tops, masses, totals, accs = [
        [ref[p * req : (p + 1) * req, :] for ref in stats] for p in range(4)
    ]

    def later(place):
        total = jnp.zeros_like(totals[0])
        for k in range(count):
            total = total + jnp.where(places[k] > place, totals[k], 0.0)
        return total

    tops = [tops[k] + later(places[k]) for k in range(count)]
    top = functools.reduce(jnp.maximum, tops)
    scales = [jnp.exp(t - top) for t in tops]
    mass = sum(s * x for s, x in zip(scales, masses))
    acc = sum(s * x for s, x in zip(scales, accs))
    query, key, value, gate = [picked_ref[p * req : (p + 1) * req, :] for p in range(4)]
    one, two = iota((width, width), 0), iota((width, width), 1)
    same = (one // size == two // size).astype(jnp.float32).astype(jnp.bfloat16)
    own = split_dot(query * key, same) * (size**-0.5)
    past = top + gate
    joint = jnp.maximum(past, own)
    scale, self_weight = jnp.exp(past - joint), jnp.exp(own - joint)
    attended = (scale * acc + self_weight * value) / (scale * mass + self_weight)
    later_ref[...] = later(seq)
    out_ref[...] = dot(attended.astype(jnp.bfloat16), weight_ref[...])


def merge_part(stats, relative, picked, out_weight, second, size):
    req, width = stats[0].shape[0] // 4, stats[0].shape[1]
    vmem = pl.BlockSpec(memory_space=pltpu.VMEM)
    return pl.pallas_call(
        functools.partial(merge_kernel, len(stats), relative, size),
        out_shape=(
            pltpu.VMEM((req, width), jnp.float32),
            pltpu.VMEM((req, out_weight.shape[1]), jnp.float32),
        ),
        in_specs=[vmem] * (len(stats) + 2) + [pl.BlockSpec(memory_space=pl.ANY)],
        out_specs=(vmem, vmem),
        compiler_params=pltpu.CompilerParams(vmem_limit_bytes=VMEM_LIMIT),
        cost_estimate=MERGE,
        name="merge_and_project",
    )(*near(*stats, picked, out_weight), second)


def sum_kernel(count, size, *refs):
    parts, (later_ref, log_ref, _, out, decay_ref) = refs[:count], refs[count:]
    me = lax.axis_index("head")
    total = jnp.zeros(out.shape, jnp.float32)
    for place in range(count):
        for k in range(count):
            total = total + jnp.where(lax.rem(me + count - k, count) == place, parts[k][...], 0.0)
    out[...] = total.astype(out.dtype)
    for h in range(log_ref.shape[0]):
        decay_ref[h] = jnp.exp(log_ref[h] + later_ref[:, h * size : h * size + 1])


def sum_part(parts, later, logs, placed, size):
    vmem = pl.BlockSpec(memory_space=pltpu.VMEM)
    return pl.pallas_call(
        functools.partial(sum_kernel, len(parts), size),
        out_shape=(
            pltpu.HBM(parts[0].shape, jnp.bfloat16),
            pltpu.HBM(logs.shape, jnp.float32),
        ),
        in_specs=[vmem] * (len(parts) + 3),
        out_specs=(vmem, vmem),
        compiler_params=pltpu.CompilerParams(vmem_limit_bytes=VMEM_LIMIT),
        cost_estimate=LIGHT,
        name="sum_heads_and_decay",
    )(*parts, later, logs, placed)


def place_kernel(n_seq, first, count, *refs):
    parts, refs = refs[:count], refs[count:]
    len_ref, _, _, out_k, out_v, placed_ref, lengths, sem_s, sem = refs
    _, sent = half_of("seq", n_seq)
    (load,) = fetch([(len_ref, lengths)], sem_s)
    placed_ref[...] = jnp.zeros_like(placed_ref)
    load.wait()
    req, rows, _ = out_k.shape
    slots = rows // 2
    most = slots // SLOTS
    seq = lax.axis_index("seq")
    if n_seq == 2:
        start = (1 - seq) * (4 * slots) + seq * (2 * slots)
    else:
        start = seq * (4 * slots) + sent * (2 * slots)
    ahead, live, _ = offsets(lengths, start, most)
    for phase in ("start", "wait"):
        begin = first
        for p, part in enumerate(parts):
            held = part.shape[1] // SLOTS
            for r in range(req):
                if begin >= (r + 1) * most:
                    continue
                low = jnp.clip(begin - ahead[r], 0, live[r])
                high = jnp.clip(begin + held - ahead[r], 0, live[r])
                size = pl.multiple_of((high - low) * SLOTS, SLOTS)

                @pl.when(high > low)
                def _(p=p, part=part, begin=begin, r=r, low=low, size=size):
                    src = pl.multiple_of((ahead[r] + low - begin) * SLOTS, SLOTS)
                    dst = pl.multiple_of(sent * slots + low * SLOTS, SLOTS)
                    for i, out in enumerate((out_k, out_v)):
                        copy = pltpu.make_async_copy(
                            part.at[i, pl.ds(src, size), :],
                            out.at[r, pl.ds(dst, size), :],
                            sem.at[p, i, r],
                        )
                        getattr(copy, phase)()

            begin += held


def place_part(n_seq, first, parts, lengths, out_k, out_v):
    hbm = pl.BlockSpec(memory_space=pl.ANY)
    vmem = pl.BlockSpec(memory_space=pltpu.VMEM)
    shape = pltpu.HBM(out_k.shape, out_k.dtype)
    count = len(parts)
    return pl.pallas_call(
        functools.partial(place_kernel, n_seq, first, count),
        out_shape=(shape, shape, pltpu.VMEM((8, LANES), jnp.float32)),
        in_specs=[vmem] * (count + 1) + [hbm, hbm],
        out_specs=(hbm, hbm, vmem),
        scratch_shapes=[
            pltpu.SMEM(lengths.shape, jnp.int32),
            pltpu.SemaphoreType.DMA((1,)),
            pltpu.SemaphoreType.DMA((count, 2, lengths.shape[0])),
        ],
        input_output_aliases={count + 1: 0, count + 2: 1},
        compiler_params=pltpu.CompilerParams(vmem_limit_bytes=VMEM_LIMIT),
        cost_estimate=LIGHT,
        name="place_received",
    )(*near(*parts, lengths), *far(out_k, out_v))


def others(value, axis):
    count = lax.axis_size(axis)
    return [value] + [
        lax.ppermute(value, axis, [(i, (i + k) % count) for i in range(count)])
        for k in range(1, count)
    ]


def swap(value, n_seq):
    return lax.ppermute(value, "seq", [(0, 1), (1, 0)]) if n_seq == 2 else value


def shards(
    keys, values, log_forget, keep, merge_weight, lengths, route, fresh, new_forget, out_weight
):
    req, pos, width = keys.shape
    heads = log_forget.shape[1]
    size = width // heads
    n_seq, n_grp = lax.axis_size("seq"), lax.axis_size("grp")
    early, packed, choice = first_part(
        n_seq,
        lengths,
        keep,
        merge_weight,
        fresh.reshape(3 * req, width),
        new_forget,
        keys,
        values,
    )
    exchange = functools.partial(swap, n_seq=n_seq)
    first_received = exchange(early)
    tokens = others(packed, "grp")
    out_k, out_v, late, own_rows, logs, level, total = own_part(
        n_seq,
        lengths,
        keep,
        merge_weight,
        log_forget.transpose(1, 0, 2),
        keys,
        values,
        early,
    )
    begin, end = FIRST * SLOTS, (FIRST + SECOND) * SLOTS
    rest = late.shape[1] - end

    def finish(rows, early, late, own_rows, logs, level, total, tokens, *others_in):
        out_weight, lengths, route, out_k, out_v = others_in
        second = exchange(late[:, begin:end])
        stats, picked = attend_part(
            n_seq, n_grp, heads, lengths, route, own_rows, late, level, total, tokens
        )
        if n_seq == 2:
            all_stats = others(stats, "seq")
        else:
            gathered = lax.all_gather(stats, "seq")
            all_stats = [gathered[i] for i in range(n_seq)]
        ends = [end, end + rows]
        if rows > 2 * LAST * SLOTS:
            ends.insert(1, end + rows - LAST * SLOTS)
        third = [exchange(late[:, low:high]) for low, high in zip(ends, ends[1:])]
        later, partial = merge_part(all_stats, n_seq == 2, picked, out_weight, second, size)
        out_k, out_v, placed = place_part(n_seq, 0, (early, second), lengths, out_k, out_v)
        layer_out, decay = sum_part(others(partial, "head"), later, logs, placed, size)
        for low, part in zip(ends, third):
            out_k, out_v, _ = place_part(n_seq, low // SLOTS, (part,), lengths, out_k, out_v)
        return decay, layer_out, out_k, out_v

    operands = (first_received, late, own_rows, logs, level, total, tokens)
    operands += (out_weight, lengths, route, out_k, out_v)
    if n_seq == 2:
        branches = [
            functools.partial(finish, blocks * SLOTS) for blocks in SIZES + (rest // SLOTS,)
        ]
        decay, layer_out, out_k, out_v = lax.switch(choice[0], branches, *operands)
    else:
        decay, layer_out, out_k, out_v = finish(rest, *operands)
    if n_seq != 2:
        out_k, out_v = (
            lax.all_to_all(x, "seq", split_axis=1, concat_axis=1, tiled=True) for x in (out_k, out_v)
        )
    return out_k, out_v, decay.transpose(1, 0, 2), layer_out


def solution(mesh):
    return jax.shard_map(
        shards,
        mesh=mesh,
        in_specs=(
            P("grp", "seq", "head"),
            P("grp", "seq", "head"),
            P("grp", "head", "seq"),
            P("grp", "seq"),
            P("grp", "seq"),
            P("grp"),
            P("grp"),
            P(None, "grp", "head"),
            P("grp", "head"),
            P("head", "seq"),
        ),
        out_specs=(
            P("grp", "seq", "head"),
            P("grp", "seq", "head"),
            P("grp", "head", "seq"),
            P("grp", "seq"),
        ),
        check_vma=False,
    )
```

```python
import functools

import jax
import jax.numpy as jnp
from jax import lax
from jax.experimental import pallas as pl
from jax.experimental.pallas import tpu as pltpu
from jax.sharding import PartitionSpec as P

BLOCK = 64
SLOTS = 32
LANES = 128
BLOCK_LOG = BLOCK.bit_length() - 1
SLOT_LOG = SLOTS.bit_length() - 1
EMPTY_LOG = -10000.0
FIRST = 8
SECOND = 3
SIZES = (6, 9, 11, 13, 14, 15, 17, 19)
LAST = 4
SURE = 2
EAGER = 5
VMEM_LIMIT = 16 * 1024 * 1024


LIGHT = pl.CostEstimate(flops=1, bytes_accessed=1, transcendentals=0)
MERGE = pl.CostEstimate(flops=1 << 36, bytes_accessed=1, transcendentals=0)


def dot(a, b):
    return lax.dot_general(a, b, (((1,), (0,)), ((), ())), preferred_element_type=jnp.float32)


def dot_nt(a, b):
    return lax.dot_general(a, b, (((1,), (1,)), ((), ())), preferred_element_type=jnp.float32)


def iota(shape, dim):
    return lax.broadcasted_iota(jnp.int32, shape, dim)


def three(x):
    hi = x.astype(jnp.bfloat16).astype(jnp.float32)
    rest = x - hi
    mid = rest.astype(jnp.bfloat16).astype(jnp.float32)
    return hi, mid, rest - mid


def split_dot(x, ones):
    rows = x.shape[0]
    parts = dot(jnp.concatenate(three(x), axis=0).astype(jnp.bfloat16), ones)
    return parts[:rows] + parts[rows : 2 * rows] + parts[2 * rows :]


def half_of(axis, count):
    own = lax.axis_index(axis) if count == 2 else jnp.int32(0)
    return own, 1 - own


def by_row(ref, row):
    picked = jnp.zeros_like(row)
    for r in range(ref.shape[0]):
        picked = jnp.where(row == r, ref[r], picked)
    return picked


def live_blocks(lengths, r, start, most):
    return jnp.clip((lengths[r] - start) >> BLOCK_LOG, 0, most)


def offsets(lengths, start, most):
    total = jnp.int32(0)
    ahead, live = [], []
    for r in range(lengths.shape[0]):
        ahead.append(total)
        live.append(live_blocks(lengths, r, start, most))
        total = total + live[-1]
    return ahead, live, total


def mask(condition):
    return condition.astype(jnp.float32).astype(jnp.bfloat16)


def block_masks(width):
    one, two = iota((width, width), 0), iota((width, width), 1)
    same = (one ^ two) < BLOCK
    return mask(same & (one <= two)), mask(same), mask(same & (one > two))


def plan(keep, weight, start, len_ref, upto, block):
    rows, width = keep.shape
    kept = keep == 1
    rank = dot(keep.astype(jnp.float32).astype(jnp.bfloat16), upto) - 1.0
    weighted = jnp.where(kept, 0.0, weight)
    share = (weighted / split_dot(weighted, block)).astype(jnp.bfloat16).astype(jnp.float32)
    lane, row = iota((rows, width), 1), iota((rows, width), 0)
    slot = jnp.where(kept, rank.astype(jnp.int32), SLOTS - 1) + (lane >> BLOCK_LOG) * SLOTS
    slot = jnp.where(start + lane < by_row(len_ref, row), slot, -1)
    return slot, jnp.where(kept, 1.0, share)


def select(slot, factor, r):
    width = slot.shape[1]
    shape = (width // 2, width)
    hit = iota(shape, 0) == slot[r : r + 1, :]
    return jnp.where(hit, jnp.broadcast_to(factor[r : r + 1, :], shape), 0.0).astype(jnp.bfloat16)


def lanes(half, width):
    return pl.ds(pl.multiple_of(half * width, width), width)


def far(*arrays):
    return [pltpu.with_memory_space_constraint(x, pltpu.HBM) for x in arrays]


def near(*arrays):
    return [pltpu.with_memory_space_constraint(x, pltpu.VMEM) for x in arrays]


def fetch(pairs, sem):
    copies = [pltpu.make_async_copy(src, dst, sem.at[i]) for i, (src, dst) in enumerate(pairs)]
    for copy in copies:
        copy.start()
    return copies


def first_kernel(n_seq, len_hbm, keep_hbm, weight_hbm, fresh_hbm, gate_hbm, keys, values, *rest):
    out, packed, size_ref, lengths, keep, weight, fresh, gates, raw, row_buf, sem_s, sem_r = rest
    _, sent = half_of("seq", n_seq)
    req, width = keep.shape
    most = width // BLOCK
    small = fetch(
        [
            (len_hbm, lengths),
            (keep_hbm.at[:, lanes(sent, width)], keep),
            (weight_hbm.at[:, lanes(sent, width)], weight),
            (fresh_hbm, fresh),
            (gate_hbm, gates),
        ],
        sem_s,
    )

    channels = keys.shape[2]

    def slab(i, r):
        source = (keys, values)[i].at[r, lanes(sent, width), :]
        target = raw.at[r, :, pl.ds(i * channels, channels)]
        return pltpu.make_async_copy(source, target, sem_r.at[i, r])

    eager = min(EAGER, req)
    for r in range(eager):
        for i in range(2):
            slab(i, r).start()
    row_buf[...] = jnp.zeros_like(row_buf)
    upto, block, _ = block_masks(width)
    for copy in small:
        copy.wait()
    start = lax.axis_index("seq") * (2 * width) + sent * width
    ahead, live, _ = offsets(lengths, start, most)
    needed = [(ahead[r] < FIRST) & (live[r] > 0) for r in range(req)]
    for r in range(eager, req):

        @pl.when(needed[r])
        def _(r=r):
            for i in range(2):
                slab(i, r).start()

    slot, factor = plan(keep[...], weight[...], start, lengths, upto, block)
    _, _, total = offsets(lengths, width, most)
    choice = jnp.int32(0)
    for size in SIZES:
        choice = choice + (total - FIRST - SECOND > size).astype(jnp.int32)
    size_ref[0] = choice

    new, gate = fresh[...].astype(jnp.float32), gates[...].astype(jnp.float32)
    heads = gate.shape[1]
    lane = iota((req, new.shape[1]), 1)
    size = new.shape[1] // heads
    spread = jnp.zeros((req, new.shape[1]), jnp.float32)
    for h in range(heads):
        inside = (lane >= h * size) & (lane < (h + 1) * size)
        spread = jnp.where(inside, gate[:, h : h + 1], spread)
    packed[...] = jnp.concatenate([new, spread], axis=0).astype(jnp.bfloat16)

    def pack(r):
        chosen = select(slot, factor, r)
        at = pl.ds(pl.multiple_of(ahead[r] * SLOTS, SLOTS), most * SLOTS)
        if r >= eager:
            for i in range(2):
                slab(i, r).wait()
        rows = dot(chosen, raw[r]).astype(jnp.bfloat16)
        for i in range(2):
            row_buf[i, at, :] = rows[:, i * channels : (i + 1) * channels]

    for r in range(req):
        if r < eager:
            for i in range(2):
                slab(i, r).wait()
        if r < SURE:
            pack(r)
        else:
            pl.when(needed[r])(functools.partial(pack, r))
    out[...] = row_buf[:, : FIRST * SLOTS, :]


def first_part(n_seq, lengths, keep, weight, fresh, gates, keys, values):
    req, pos, width = keys.shape
    half = pos // 2
    hbm = pl.BlockSpec(memory_space=pl.ANY)
    smem = pl.BlockSpec(memory_space=pltpu.SMEM)
    vmem = pl.BlockSpec(memory_space=pltpu.VMEM)
    return pl.pallas_call(
        functools.partial(first_kernel, n_seq),
        out_shape=(
            pltpu.VMEM((2, FIRST * SLOTS, width), jnp.bfloat16),
            pltpu.VMEM((fresh.shape[0] + req, width), jnp.bfloat16),
            jax.ShapeDtypeStruct((1,), jnp.int32),
            pltpu.SMEM(lengths.shape, jnp.int32),
        ),
        in_specs=[hbm] * 7,
        out_specs=(vmem, vmem, smem, smem),
        scratch_shapes=[
            pltpu.VMEM((req, half), jnp.int32),
            pltpu.VMEM((req, half), jnp.float32),
            pltpu.VMEM(fresh.shape, fresh.dtype),
            pltpu.VMEM(gates.shape, gates.dtype),
            pltpu.VMEM((req, half, 2 * width), jnp.bfloat16),
            pltpu.VMEM((2, (FIRST - 1) * SLOTS + half // 2, width), jnp.bfloat16),
            pltpu.SemaphoreType.DMA((5,)),
            pltpu.SemaphoreType.DMA((2, req)),
        ],
        compiler_params=pltpu.CompilerParams(vmem_limit_bytes=VMEM_LIMIT),
        cost_estimate=LIGHT,
        name="compact_first_sent",
    )(*far(lengths, keep, weight, fresh, gates, keys, values))


def own_kernel(
    n_seq, lengths, keep, weight, gates, keys, values, early, *rest
):
    out_k, out_v, chunk, rows, log_ref, level_ref, total_ref = rest[:7]
    raw, late, forget, zeros, sem_l, sem_r, sem_o, sem_z = rest[7:]
    own, sent = half_of("seq", n_seq)
    seq = lax.axis_index("seq")
    heads, req, pos = gates.shape
    half = pos // 2
    slots = half // 2
    most = half // BLOCK
    first = FIRST // most
    pad = forget.shape[1] // req
    both = ((0, keys), (1, values))
    channels = keys.shape[2]

    def part(i):
        return pl.ds(i * channels, channels)

    late_slabs = fetch(
        [
            (source.at[r, lanes(sent, half), :], late.at[r - first, :, part(i)])
            for r in range(first, req)
            for i, source in both
        ],
        sem_l,
    )
    slabs = fetch(
        [
            (source.at[r, lanes(own, half), :], raw.at[r, :, part(i)])
            for r in range(req)
            for i, source in both
        ],
        sem_r,
    )
    zeros[...] = jnp.zeros_like(zeros)
    stores = fetch([(zeros, out.at[:, lanes(sent, slots), :]) for out in (out_k, out_v)], sem_z)
    chunk[:, : FIRST * SLOTS, :] = early[...]
    chunk[:, FIRST * SLOTS :, :] = jnp.zeros(
        (2, chunk.shape[1] - FIRST * SLOTS, chunk.shape[2]), chunk.dtype
    )
    upto, block, after = block_masks(half)
    ahead, alive, _ = offsets(lengths, seq * pos + sent * half, most)

    forget[...] = jnp.zeros_like(forget)
    live = seq * pos + iota((req, pos), 1) < by_row(lengths, iota((req, pos), 0))
    for h in range(heads):
        gate = jnp.where(live, gates[h], 0.0)
        for c in range(pos // LANES):
            forget[c, pl.ds(h, req, stride=pad), :] = gate[:, c * LANES : (c + 1) * LANES]
    flat = jnp.concatenate([forget[c] for c in range(pos // LANES)], axis=1)
    total_ref[...] = jnp.broadcast_to(jnp.sum(flat, axis=1, keepdims=True), total_ref.shape)
    ends = iota((pos, slots), 1) >> SLOT_LOG
    begins = iota((pos, slots), 0) >> BLOCK_LOG
    last = iota((req * pad, slots), 1) & (SLOTS - 1) == SLOTS - 1

    for i, h in enumerate((own, sent)):
        slot, factor = plan(
            keep[:, lanes(h, half)],
            weight[:, lanes(h, half)],
            seq * pos + h * half,
            lengths,
            upto,
            block,
        )
        near = half // LANES
        inner = split_dot(
            jnp.concatenate([forget[h * near + c] for c in range(near)], axis=1), after
        )
        beyond = split_dot(
            flat, (begins > ends + h * (half // BLOCK)).astype(jnp.float32).astype(jnp.bfloat16)
        )
        spread = jnp.exp(inner)
        high = spread.astype(jnp.bfloat16).astype(jnp.float32)
        planes = three(inner) + (high, spread - high, jnp.ones_like(inner))
        found = []
        for r in range(req):
            chosen = select(slot, factor, r)
            stack = jnp.concatenate([x[r * pad : (r + 1) * pad] for x in planes], axis=0)
            found.append(dot_nt(stack.astype(jnp.bfloat16), chosen))
            if i == 0:
                for k in range(2):
                    slabs[2 * r + k].wait()
                made = dot(chosen, raw[r]).astype(jnp.bfloat16)
                for k, out in enumerate((out_k, out_v)):
                    rows[k, r] = made[:, k * channels : (k + 1) * channels]
                    stores.append(
                        pltpu.make_async_copy(
                            rows.at[k, r], out.at[r, lanes(own, slots), :], sem_o.at[2 * r + k]
                        )
                    )
                    stores[-1].start()
            elif r >= first:
                for k in range(2):
                    late_slabs[2 * (r - first) + k].wait()

                @pl.when((ahead[r] + alive[r] > FIRST) & (alive[r] > 0))
                def _(r=r, chosen=chosen):
                    at = pl.ds(pl.multiple_of(ahead[r] * SLOTS, SLOTS), slots)
                    made = dot(chosen, late[r - first]).astype(jnp.bfloat16)
                    for k in range(2):
                        chunk[k, at, :] = made[:, k * channels : (k + 1) * channels]
        at = [
            jnp.concatenate([x[p * pad : (p + 1) * pad] for x in found], axis=0) for p in range(6)
        ]
        filled = at[5] > 0.5
        kept = at[0] + at[1] + at[2]
        merged = jnp.log(jnp.where(filled, at[3] + at[4], 1.0))
        level_ref[i] = jnp.where(filled, jnp.where(last, merged, kept) + beyond, EMPTY_LOG)
        for k in range(heads):
            log_ref[k, :, lanes(h, slots)] = level_ref[i, pl.ds(k, req, stride=pad), :]
    for copy in stores:
        copy.wait()


def own_part(n_seq, lengths, keep, weight, forget, keys, values, early):
    req, pos, width = keys.shape
    heads = forget.shape[0]
    half, slots, pad = pos // 2, pos // 4, -(-heads // 8) * 8
    late = req - FIRST // (half // BLOCK)
    hbm = pl.BlockSpec(memory_space=pl.ANY)
    vmem = pl.BlockSpec(memory_space=pltpu.VMEM)
    whole = pltpu.HBM((req, 2 * slots, width), jnp.bfloat16)
    return pl.pallas_call(
        functools.partial(own_kernel, n_seq),
        out_shape=(
            whole,
            whole,
            pltpu.VMEM((2, req * slots, width), jnp.bfloat16),
            pltpu.VMEM((2, req, slots, width), jnp.bfloat16),
            pltpu.VMEM((heads, req, 2 * slots), jnp.float32),
            pltpu.VMEM((2, req * pad, slots), jnp.float32),
            pltpu.VMEM((req * pad, LANES), jnp.float32),
        ),
        in_specs=[pl.BlockSpec(memory_space=pltpu.SMEM)] + [vmem] * 3 + [hbm] * 2 + [vmem],
        out_specs=(hbm, hbm, vmem, vmem, vmem, vmem, vmem),
        scratch_shapes=[
            pltpu.VMEM((req, half, 2 * width), jnp.bfloat16),
            pltpu.VMEM((late, half, 2 * width), jnp.bfloat16),
            pltpu.VMEM((pos // LANES, req * pad, LANES), jnp.float32),
            pltpu.VMEM((req, slots, width), jnp.bfloat16),
            pltpu.SemaphoreType.DMA((2 * late,)),
            pltpu.SemaphoreType.DMA((2 * req,)),
            pltpu.SemaphoreType.DMA((2 * req,)),
            pltpu.SemaphoreType.DMA((2,)),
        ],
        compiler_params=pltpu.CompilerParams(vmem_limit_bytes=VMEM_LIMIT),
        cost_estimate=LIGHT,
        name="compact_own",
    )(lengths, *near(keep, weight, forget), *far(keys, values), *near(early))


def attend_kernel(n_seq, n_grp, heads, *refs):
    lengths, route_hbm, own_rows, late, level, total = refs[:6]
    tokens, rest = refs[6 : 6 + n_grp], refs[6 + n_grp :]
    stats_ref, picked_ref, route, scores, sem_s = rest
    _, sent = half_of("seq", n_seq)
    kinds, width = picked_ref.shape
    req = kinds // 4
    size = width // heads
    slots = own_rows.shape[2]
    pad = total.shape[0] // req
    small = fetch([(route_hbm, route)], sem_s)
    for copy in small:
        copy.wait()
    start = lax.axis_index("seq") * (4 * slots) + sent * (2 * slots)
    ahead, _, _ = offsets(lengths, start, slots // SLOTS)

    def sent_part(i, r):
        at = pl.multiple_of(ahead[r] * SLOTS, SLOTS)
        return late[i, pl.ds(at, slots), :]

    shape = (kinds, kinds)
    to, frm = iota(shape, 0), iota(shape, 1)
    wanted = by_row(route, to % req)
    me = lax.axis_index("grp")
    picked = jnp.zeros((kinds, width), jnp.float32)
    for k in range(n_grp):
        source = lax.rem(me + n_grp - k, n_grp)
        hit = (to // req == frm // req) & (wanted == source * req + frm % req)
        picked = picked + dot(hit.astype(jnp.float32).astype(jnp.bfloat16), tokens[k][...])
    picked_ref[...] = picked

    lane, row = iota((pad, width), 1), iota((pad, width), 0)
    mine = (lane >= row * size) & (lane < (row + 1) * size)
    for r in range(req):
        query = jnp.where(mine, picked[r : r + 1, :], 0.0).astype(jnp.bfloat16)
        here = slice(r * pad, (r + 1) * pad)
        scores[here, :slots] = dot_nt(query, own_rows[0, r])
        scores[here, slots:] = dot_nt(query, sent_part(0, r))
    logit = scores[...] * (size**-0.5) + jnp.concatenate([level[0], level[1]], axis=1)
    top = jnp.max(logit, axis=1, keepdims=True)
    weights = jnp.exp(logit - top).astype(jnp.bfloat16).astype(jnp.float32)
    mass = jnp.sum(weights, axis=1, keepdims=True)

    def spread_out(column, r):
        return jnp.sum(
            jnp.where(mine, column[r * pad : (r + 1) * pad], 0.0), axis=0, keepdims=True
        )

    for r in range(req):
        w = weights[r * pad : (r + 1) * pad].astype(jnp.bfloat16)
        acc = dot(w[:, :slots], own_rows[1, r]) + dot(w[:, slots:], sent_part(1, r))
        acc = jnp.sum(jnp.where(mine, acc, 0.0), axis=0, keepdims=True)
        for p, x in enumerate((top, mass, total[:, :1])):
            stats_ref[p * req + r : p * req + r + 1, :] = spread_out(x, r)
        stats_ref[3 * req + r : 3 * req + r + 1, :] = acc


def attend_part(n_seq, n_grp, heads, lengths, route, own_rows, late, level, total, tokens):
    _, req, slots, width = own_rows.shape
    vmem = pl.BlockSpec(memory_space=pltpu.VMEM)
    small = pltpu.VMEM((4 * req, width), jnp.float32)
    return pl.pallas_call(
        functools.partial(attend_kernel, n_seq, n_grp, heads),
        out_shape=(small, small),
        in_specs=[pl.BlockSpec(memory_space=pltpu.SMEM)] + [vmem] * (5 + n_grp),
        out_specs=(vmem, vmem),
        scratch_shapes=[
            pltpu.SMEM(route.shape, jnp.int32),
            pltpu.VMEM((total.shape[0], 2 * slots), jnp.float32),
            pltpu.SemaphoreType.DMA((1,)),
        ],
        compiler_params=pltpu.CompilerParams(vmem_limit_bytes=VMEM_LIMIT),
        cost_estimate=LIGHT,
        name="attend",
    )(lengths, *near(route, own_rows, late, level, total), *near(*tokens))


def merge_kernel(count, relative, size, *refs):
    stats, refs = refs[:count], refs[count:]
    picked_ref, weight_ref, _, later_ref, out_ref = refs
    req, width = later_ref.shape
    seq = lax.axis_index("seq")
    places = [lax.rem(seq + count - k, count) if relative else jnp.int32(k) for k in range(count)]
    tops, masses, totals, accs = [
        [ref[p * req : (p + 1) * req, :] for ref in stats] for p in range(4)
    ]

    def later(place):
        total = jnp.zeros_like(totals[0])
        for k in range(count):
            total = total + jnp.where(places[k] > place, totals[k], 0.0)
        return total

    tops = [tops[k] + later(places[k]) for k in range(count)]
    top = functools.reduce(jnp.maximum, tops)
    scales = [jnp.exp(t - top) for t in tops]
    mass = sum(s * x for s, x in zip(scales, masses))
    acc = sum(s * x for s, x in zip(scales, accs))
    query, key, value, gate = [picked_ref[p * req : (p + 1) * req, :] for p in range(4)]
    one, two = iota((width, width), 0), iota((width, width), 1)
    same = (one // size == two // size).astype(jnp.float32).astype(jnp.bfloat16)
    own = split_dot(query * key, same) * (size**-0.5)
    past = top + gate
    joint = jnp.maximum(past, own)
    scale, self_weight = jnp.exp(past - joint), jnp.exp(own - joint)
    attended = (scale * acc + self_weight * value) / (scale * mass + self_weight)
    later_ref[...] = later(seq)
    out_ref[...] = dot(attended.astype(jnp.bfloat16), weight_ref[...])


def merge_part(stats, relative, picked, out_weight, second, size):
    req, width = stats[0].shape[0] // 4, stats[0].shape[1]
    vmem = pl.BlockSpec(memory_space=pltpu.VMEM)
    return pl.pallas_call(
        functools.partial(merge_kernel, len(stats), relative, size),
        out_shape=(
            pltpu.VMEM((req, width), jnp.float32),
            pltpu.VMEM((req, out_weight.shape[1]), jnp.float32),
        ),
        in_specs=[vmem] * (len(stats) + 2) + [pl.BlockSpec(memory_space=pl.ANY)],
        out_specs=(vmem, vmem),
        compiler_params=pltpu.CompilerParams(vmem_limit_bytes=VMEM_LIMIT),
        cost_estimate=MERGE,
        name="merge_and_project",
    )(*near(*stats, picked, out_weight), second)


def sum_kernel(count, size, *refs):
    parts, (later_ref, log_ref, _, out, decay_ref) = refs[:count], refs[count:]
    me = lax.axis_index("head")
    total = jnp.zeros(out.shape, jnp.float32)
    for place in range(count):
        for k in range(count):
            total = total + jnp.where(lax.rem(me + count - k, count) == place, parts[k][...], 0.0)
    out[...] = total.astype(out.dtype)
    for h in range(log_ref.shape[0]):
        decay_ref[h] = jnp.exp(log_ref[h] + later_ref[:, h * size : h * size + 1])


def sum_part(parts, later, logs, placed, size):
    vmem = pl.BlockSpec(memory_space=pltpu.VMEM)
    return pl.pallas_call(
        functools.partial(sum_kernel, len(parts), size),
        out_shape=(
            pltpu.HBM(parts[0].shape, jnp.bfloat16),
            pltpu.HBM(logs.shape, jnp.float32),
        ),
        in_specs=[vmem] * (len(parts) + 3),
        out_specs=(vmem, vmem),
        compiler_params=pltpu.CompilerParams(vmem_limit_bytes=VMEM_LIMIT),
        cost_estimate=LIGHT,
        name="sum_heads_and_decay",
    )(*parts, later, logs, placed)


def place_kernel(n_seq, first, count, marked, *refs):
    parts, refs = refs[:count], refs[count:]
    lengths, _, _, out_k, out_v, *placed_ref, sem = refs
    _, sent = half_of("seq", n_seq)
    if marked:
        placed_ref[0][...] = jnp.zeros_like(placed_ref[0])
    req, rows, _ = out_k.shape
    slots = rows // 2
    most = slots // SLOTS
    seq = lax.axis_index("seq")
    if n_seq == 2:
        start = (1 - seq) * (4 * slots) + seq * (2 * slots)
    else:
        start = seq * (4 * slots) + sent * (2 * slots)
    ahead, live, _ = offsets(lengths, start, most)
    for phase in ("start", "wait"):
        begin = first
        for p, part in enumerate(parts):
            held = part.shape[1] // SLOTS
            for r in range(req):
                if begin >= (r + 1) * most:
                    continue
                low = jnp.clip(begin - ahead[r], 0, live[r])
                high = jnp.clip(begin + held - ahead[r], 0, live[r])
                size = pl.multiple_of((high - low) * SLOTS, SLOTS)

                @pl.when(high > low)
                def _(p=p, part=part, begin=begin, r=r, low=low, size=size):
                    src = pl.multiple_of((ahead[r] + low - begin) * SLOTS, SLOTS)
                    dst = pl.multiple_of(sent * slots + low * SLOTS, SLOTS)
                    for i, out in enumerate((out_k, out_v)):
                        copy = pltpu.make_async_copy(
                            part.at[i, pl.ds(src, size), :],
                            out.at[r, pl.ds(dst, size), :],
                            sem.at[p, i, r],
                        )
                        getattr(copy, phase)()

            begin += held


def place_part(n_seq, first, parts, lengths, out_k, out_v, marked=False):
    hbm = pl.BlockSpec(memory_space=pl.ANY)
    smem = pl.BlockSpec(memory_space=pltpu.SMEM)
    vmem = pl.BlockSpec(memory_space=pltpu.VMEM)
    shape = pltpu.HBM(out_k.shape, out_k.dtype)
    count = len(parts)
    return pl.pallas_call(
        functools.partial(place_kernel, n_seq, first, count, marked),
        out_shape=(shape, shape) + (pltpu.VMEM((8, LANES), jnp.float32),) * marked,
        in_specs=[vmem] * count + [smem, hbm, hbm],
        out_specs=(hbm, hbm) + (vmem,) * marked,
        scratch_shapes=[
            pltpu.SemaphoreType.DMA((count, 2, lengths.shape[0])),
        ],
        input_output_aliases={count + 1: 0, count + 2: 1},
        compiler_params=pltpu.CompilerParams(vmem_limit_bytes=VMEM_LIMIT),
        cost_estimate=LIGHT,
        name="place_received",
    )(*near(*parts), lengths, *far(out_k, out_v))


def others(value, axis):
    count = lax.axis_size(axis)
    return [value] + [
        lax.ppermute(value, axis, [(i, (i + k) % count) for i in range(count)])
        for k in range(1, count)
    ]


def swap(value, n_seq):
    return lax.ppermute(value, "seq", [(0, 1), (1, 0)]) if n_seq == 2 else value


def shards(
    keys, values, log_forget, keep, merge_weight, lengths, route, fresh, new_forget, out_weight
):
    req, pos, width = keys.shape
    heads = log_forget.shape[1]
    size = width // heads
    n_seq, n_grp = lax.axis_size("seq"), lax.axis_size("grp")
    early, packed, choice, held_lengths = first_part(
        n_seq,
        lengths,
        keep,
        merge_weight,
        fresh.reshape(3 * req, width),
        new_forget,
        keys,
        values,
    )
    exchange = functools.partial(swap, n_seq=n_seq)
    first_received = exchange(early)
    tokens = others(packed, "grp")
    out_k, out_v, late, own_rows, logs, level, total = own_part(
        n_seq,
        held_lengths,
        keep,
        merge_weight,
        log_forget.transpose(1, 0, 2),
        keys,
        values,
        early,
    )
    begin, end = FIRST * SLOTS, (FIRST + SECOND) * SLOTS
    rest = late.shape[1] - end

    def finish(rows, early, late, own_rows, logs, level, total, tokens, *others_in):
        out_weight, lengths, route, out_k, out_v = others_in
        second = exchange(late[:, begin:end])
        stats, picked = attend_part(
            n_seq, n_grp, heads, lengths, route, own_rows, late, level, total, tokens
        )
        if n_seq == 2:
            all_stats = others(stats, "seq")
        else:
            gathered = lax.all_gather(stats, "seq")
            all_stats = [gathered[i] for i in range(n_seq)]
        ends = [end, end + rows]
        if rows > 3 * LAST * SLOTS:
            ends.insert(1, end + rows - LAST * SLOTS)
        third = [exchange(late[:, low:high]) for low, high in zip(ends, ends[1:])]
        later, partial = merge_part(all_stats, n_seq == 2, picked, out_weight, second, size)
        out_k, out_v, placed = place_part(
            n_seq, 0, (early, second), lengths, out_k, out_v, marked=True
        )
        layer_out, decay = sum_part(others(partial, "head"), later, logs, placed, size)
        for low, part in zip(ends, third):
            out_k, out_v = place_part(n_seq, low // SLOTS, (part,), lengths, out_k, out_v)
        return decay, layer_out, out_k, out_v

    operands = (first_received, late, own_rows, logs, level, total, tokens)
    operands += (out_weight, held_lengths, route, out_k, out_v)
    if n_seq == 2:
        branches = [
            functools.partial(finish, blocks * SLOTS) for blocks in SIZES + (rest // SLOTS,)
        ]
        decay, layer_out, out_k, out_v = lax.switch(choice[0], branches, *operands)
    else:
        decay, layer_out, out_k, out_v = finish(rest, *operands)
    if n_seq != 2:
        out_k, out_v = (
            lax.all_to_all(x, "seq", split_axis=1, concat_axis=1, tiled=True) for x in (out_k, out_v)
        )
    return out_k, out_v, decay.transpose(1, 0, 2), layer_out


def solution(mesh):
    return jax.shard_map(
        shards,
        mesh=mesh,
        in_specs=(
            P("grp", "seq", "head"),
            P("grp", "seq", "head"),
            P("grp", "head", "seq"),
            P("grp", "seq"),
            P("grp", "seq"),
            P("grp"),
            P("grp"),
            P(None, "grp", "head"),
            P("grp", "head"),
            P("head", "seq"),
        ),
        out_specs=(
            P("grp", "seq", "head"),
            P("grp", "seq", "head"),
            P("grp", "head", "seq"),
            P("grp", "seq"),
        ),
        check_vma=False,
    )
```

```python
import functools

import jax
import jax.numpy as jnp
from jax import lax
from jax.experimental import pallas as pl
from jax.experimental.pallas import tpu as pltpu
from jax.sharding import PartitionSpec as P

BLOCK = 64
SLOTS = 32
LANES = 128
BLOCK_LOG = BLOCK.bit_length() - 1
SLOT_LOG = SLOTS.bit_length() - 1
EMPTY_LOG = -10000.0
FIRST = 8
SECOND = 3
SIZES = (7, 9, 11, 12, 13, 14, 15, 16, 17, 19)
LAST = 4
SURE = 2
EAGER = 5
VMEM_LIMIT = 16 * 1024 * 1024


LIGHT = pl.CostEstimate(flops=1, bytes_accessed=1, transcendentals=0)
MERGE = pl.CostEstimate(flops=1 << 36, bytes_accessed=1, transcendentals=0)


def dot(a, b):
    return lax.dot_general(a, b, (((1,), (0,)), ((), ())), preferred_element_type=jnp.float32)


def dot_nt(a, b):
    return lax.dot_general(a, b, (((1,), (1,)), ((), ())), preferred_element_type=jnp.float32)


def iota(shape, dim):
    return lax.broadcasted_iota(jnp.int32, shape, dim)


def three(x):
    hi = x.astype(jnp.bfloat16).astype(jnp.float32)
    rest = x - hi
    mid = rest.astype(jnp.bfloat16).astype(jnp.float32)
    return hi, mid, rest - mid


def split_dot(x, ones):
    rows = x.shape[0]
    parts = dot(jnp.concatenate(three(x), axis=0).astype(jnp.bfloat16), ones)
    return parts[:rows] + parts[rows : 2 * rows] + parts[2 * rows :]


def half_of(axis, count):
    own = lax.axis_index(axis) if count == 2 else jnp.int32(0)
    return own, 1 - own


def by_row(ref, row):
    picked = jnp.zeros_like(row)
    for r in range(ref.shape[0]):
        picked = jnp.where(row == r, ref[r], picked)
    return picked


def live_blocks(lengths, r, start, most):
    return jnp.clip((lengths[r] - start) >> BLOCK_LOG, 0, most)


def offsets(lengths, start, most):
    total = jnp.int32(0)
    ahead, live = [], []
    for r in range(lengths.shape[0]):
        ahead.append(total)
        live.append(live_blocks(lengths, r, start, most))
        total = total + live[-1]
    return ahead, live, total


def mask(condition):
    return condition.astype(jnp.float32).astype(jnp.bfloat16)


def block_masks(width):
    one, two = iota((width, width), 0), iota((width, width), 1)
    same = (one ^ two) < BLOCK
    return mask(same & (one <= two)), mask(same), mask(same & (one > two))


def plan(keep, weight, start, len_ref, upto, block):
    rows, width = keep.shape
    kept = keep == 1
    rank = dot(keep.astype(jnp.float32).astype(jnp.bfloat16), upto) - 1.0
    weighted = jnp.where(kept, 0.0, weight)
    share = (weighted / split_dot(weighted, block)).astype(jnp.bfloat16).astype(jnp.float32)
    lane, row = iota((rows, width), 1), iota((rows, width), 0)
    slot = jnp.where(kept, rank.astype(jnp.int32), SLOTS - 1) + (lane >> BLOCK_LOG) * SLOTS
    slot = jnp.where(start + lane < by_row(len_ref, row), slot, -1)
    return slot, jnp.where(kept, 1.0, share)


def select(slot, factor, r):
    width = slot.shape[1]
    shape = (width // 2, width)
    hit = iota(shape, 0) == slot[r : r + 1, :]
    return jnp.where(hit, jnp.broadcast_to(factor[r : r + 1, :], shape), 0.0).astype(jnp.bfloat16)


def lanes(half, width):
    return pl.ds(pl.multiple_of(half * width, width), width)


def far(*arrays):
    return [pltpu.with_memory_space_constraint(x, pltpu.HBM) for x in arrays]


def near(*arrays):
    return [pltpu.with_memory_space_constraint(x, pltpu.VMEM) for x in arrays]


def fetch(pairs, sem):
    copies = [pltpu.make_async_copy(src, dst, sem.at[i]) for i, (src, dst) in enumerate(pairs)]
    for copy in copies:
        copy.start()
    return copies


def first_kernel(
    n_seq, len_hbm, route_hbm, keep_hbm, weight_hbm, fresh_hbm, gate_hbm, keys, values, *rest
):
    out, packed, size_ref, lengths, route, keep, weight, fresh, gates, raw, row_buf = rest[:11]
    sem_s, sem_r = rest[11:]
    _, sent = half_of("seq", n_seq)
    req, width = keep.shape
    most = width // BLOCK
    small = fetch(
        [
            (len_hbm, lengths),
            (keep_hbm.at[:, lanes(sent, width)], keep),
            (weight_hbm.at[:, lanes(sent, width)], weight),
            (fresh_hbm, fresh),
            (gate_hbm, gates),
            (route_hbm, route),
        ],
        sem_s,
    )

    channels = keys.shape[2]

    def slab(i, r):
        source = (keys, values)[i].at[r, lanes(sent, width), :]
        target = raw.at[r, :, pl.ds(i * channels, channels)]
        return pltpu.make_async_copy(source, target, sem_r.at[i, r])

    eager = min(EAGER, req)
    for r in range(eager):
        for i in range(2):
            slab(i, r).start()
    row_buf[...] = jnp.zeros_like(row_buf)
    upto, block, _ = block_masks(width)
    for copy in small:
        copy.wait()
    start = lax.axis_index("seq") * (2 * width) + sent * width
    ahead, live, _ = offsets(lengths, start, most)
    needed = [(ahead[r] < FIRST) & (live[r] > 0) for r in range(req)]
    for r in range(eager, req):

        @pl.when(needed[r])
        def _(r=r):
            for i in range(2):
                slab(i, r).start()

    slot, factor = plan(keep[...], weight[...], start, lengths, upto, block)
    _, _, total = offsets(lengths, width, most)
    choice = jnp.int32(0)
    for size in SIZES:
        choice = choice + (total - FIRST - SECOND > size).astype(jnp.int32)
    size_ref[0] = choice

    new, gate = fresh[...].astype(jnp.float32), gates[...].astype(jnp.float32)
    heads = gate.shape[1]
    lane = iota((req, new.shape[1]), 1)
    size = new.shape[1] // heads
    spread = jnp.zeros((req, new.shape[1]), jnp.float32)
    for h in range(heads):
        inside = (lane >= h * size) & (lane < (h + 1) * size)
        spread = jnp.where(inside, gate[:, h : h + 1], spread)
    packed[...] = jnp.concatenate([new, spread], axis=0).astype(jnp.bfloat16)

    def pack(r):
        chosen = select(slot, factor, r)
        at = pl.ds(pl.multiple_of(ahead[r] * SLOTS, SLOTS), most * SLOTS)
        if r >= eager:
            for i in range(2):
                slab(i, r).wait()
        rows = dot(chosen, raw[r]).astype(jnp.bfloat16)
        for i in range(2):
            row_buf[i, at, :] = rows[:, i * channels : (i + 1) * channels]

    for r in range(req):
        if r < eager:
            for i in range(2):
                slab(i, r).wait()
        if r < SURE:
            pack(r)
        else:
            pl.when(needed[r])(functools.partial(pack, r))
    out[...] = row_buf[:, : FIRST * SLOTS, :]


def first_part(n_seq, lengths, route, keep, weight, fresh, gates, keys, values):
    req, pos, width = keys.shape
    half = pos // 2
    hbm = pl.BlockSpec(memory_space=pl.ANY)
    smem = pl.BlockSpec(memory_space=pltpu.SMEM)
    vmem = pl.BlockSpec(memory_space=pltpu.VMEM)
    return pl.pallas_call(
        functools.partial(first_kernel, n_seq),
        out_shape=(
            pltpu.VMEM((2, FIRST * SLOTS, width), jnp.bfloat16),
            pltpu.VMEM((fresh.shape[0] + req, width), jnp.bfloat16),
            jax.ShapeDtypeStruct((1,), jnp.int32),
            pltpu.SMEM(lengths.shape, jnp.int32),
            pltpu.SMEM(route.shape, jnp.int32),
        ),
        in_specs=[hbm] * 8,
        out_specs=(vmem, vmem, smem, smem, smem),
        scratch_shapes=[
            pltpu.VMEM((req, half), jnp.int32),
            pltpu.VMEM((req, half), jnp.float32),
            pltpu.VMEM(fresh.shape, fresh.dtype),
            pltpu.VMEM(gates.shape, gates.dtype),
            pltpu.VMEM((req, half, 2 * width), jnp.bfloat16),
            pltpu.VMEM((2, (FIRST - 1) * SLOTS + half // 2, width), jnp.bfloat16),
            pltpu.SemaphoreType.DMA((6,)),
            pltpu.SemaphoreType.DMA((2, req)),
        ],
        compiler_params=pltpu.CompilerParams(vmem_limit_bytes=VMEM_LIMIT),
        cost_estimate=LIGHT,
        name="compact_first_sent",
    )(*far(lengths, route, keep, weight, fresh, gates, keys, values))


def own_kernel(
    n_seq, lengths, keep, weight, gates, keys, values, early, *rest
):
    out_k, out_v, chunk, rows, log_ref, level_ref, total_ref = rest[:7]
    raw, late, forget, zeros, sem_l, sem_r, sem_o, sem_z = rest[7:]
    own, sent = half_of("seq", n_seq)
    seq = lax.axis_index("seq")
    heads, req, pos = gates.shape
    half = pos // 2
    slots = half // 2
    most = half // BLOCK
    first = FIRST // most
    pad = forget.shape[1] // req
    both = ((0, keys), (1, values))
    channels = keys.shape[2]

    def part(i):
        return pl.ds(i * channels, channels)

    late_slabs = fetch(
        [
            (source.at[r, lanes(sent, half), :], late.at[r - first, :, part(i)])
            for r in range(first, req)
            for i, source in both
        ],
        sem_l,
    )
    slabs = fetch(
        [
            (source.at[r, lanes(own, half), :], raw.at[r, :, part(i)])
            for r in range(req)
            for i, source in both
        ],
        sem_r,
    )
    zeros[...] = jnp.zeros_like(zeros)
    stores = fetch([(zeros, out.at[:, lanes(sent, slots), :]) for out in (out_k, out_v)], sem_z)
    chunk[:, : FIRST * SLOTS, :] = early[...]
    chunk[:, FIRST * SLOTS :, :] = jnp.zeros(
        (2, chunk.shape[1] - FIRST * SLOTS, chunk.shape[2]), chunk.dtype
    )
    upto, block, after = block_masks(half)
    ahead, alive, _ = offsets(lengths, seq * pos + sent * half, most)

    forget[...] = jnp.zeros_like(forget)
    live = seq * pos + iota((req, pos), 1) < by_row(lengths, iota((req, pos), 0))
    for h in range(heads):
        gate = jnp.where(live, gates[h], 0.0)
        for c in range(pos // LANES):
            forget[c, pl.ds(h, req, stride=pad), :] = gate[:, c * LANES : (c + 1) * LANES]
    flat = jnp.concatenate([forget[c] for c in range(pos // LANES)], axis=1)
    total_ref[...] = jnp.broadcast_to(jnp.sum(flat, axis=1, keepdims=True), total_ref.shape)
    ends = iota((pos, slots), 1) >> SLOT_LOG
    begins = iota((pos, slots), 0) >> BLOCK_LOG
    last = iota((req * pad, slots), 1) & (SLOTS - 1) == SLOTS - 1

    for i, h in enumerate((own, sent)):
        slot, factor = plan(
            keep[:, lanes(h, half)],
            weight[:, lanes(h, half)],
            seq * pos + h * half,
            lengths,
            upto,
            block,
        )
        near = half // LANES
        inner = split_dot(
            jnp.concatenate([forget[h * near + c] for c in range(near)], axis=1), after
        )
        beyond = split_dot(
            flat, (begins > ends + h * (half // BLOCK)).astype(jnp.float32).astype(jnp.bfloat16)
        )
        spread = jnp.exp(inner)
        high = spread.astype(jnp.bfloat16).astype(jnp.float32)
        planes = three(inner) + (high, spread - high, jnp.ones_like(inner))
        found = []
        for r in range(req):
            chosen = select(slot, factor, r)
            stack = jnp.concatenate([x[r * pad : (r + 1) * pad] for x in planes], axis=0)
            found.append(dot_nt(stack.astype(jnp.bfloat16), chosen))
            if i == 0:
                for k in range(2):
                    slabs[2 * r + k].wait()
                made = dot(chosen, raw[r]).astype(jnp.bfloat16)
                for k, out in enumerate((out_k, out_v)):
                    rows[k, r] = made[:, k * channels : (k + 1) * channels]
                    stores.append(
                        pltpu.make_async_copy(
                            rows.at[k, r], out.at[r, lanes(own, slots), :], sem_o.at[2 * r + k]
                        )
                    )
                    stores[-1].start()
            elif r >= first:
                for k in range(2):
                    late_slabs[2 * (r - first) + k].wait()

                @pl.when((ahead[r] + alive[r] > FIRST) & (alive[r] > 0))
                def _(r=r, chosen=chosen):
                    at = pl.ds(pl.multiple_of(ahead[r] * SLOTS, SLOTS), slots)
                    made = dot(chosen, late[r - first]).astype(jnp.bfloat16)
                    for k in range(2):
                        chunk[k, at, :] = made[:, k * channels : (k + 1) * channels]
        at = [
            jnp.concatenate([x[p * pad : (p + 1) * pad] for x in found], axis=0) for p in range(6)
        ]
        filled = at[5] > 0.5
        kept = at[0] + at[1] + at[2]
        merged = jnp.log(jnp.where(filled, at[3] + at[4], 1.0))
        level_ref[i] = jnp.where(filled, jnp.where(last, merged, kept) + beyond, EMPTY_LOG)
        for k in range(heads):
            log_ref[k, :, lanes(h, slots)] = level_ref[i, pl.ds(k, req, stride=pad), :]
    for copy in stores:
        copy.wait()


def own_part(n_seq, lengths, keep, weight, forget, keys, values, early):
    req, pos, width = keys.shape
    heads = forget.shape[0]
    half, slots, pad = pos // 2, pos // 4, -(-heads // 8) * 8
    late = req - FIRST // (half // BLOCK)
    hbm = pl.BlockSpec(memory_space=pl.ANY)
    vmem = pl.BlockSpec(memory_space=pltpu.VMEM)
    whole = pltpu.HBM((req, 2 * slots, width), jnp.bfloat16)
    return pl.pallas_call(
        functools.partial(own_kernel, n_seq),
        out_shape=(
            whole,
            whole,
            pltpu.VMEM((2, req * slots, width), jnp.bfloat16),
            pltpu.VMEM((2, req, slots, width), jnp.bfloat16),
            pltpu.VMEM((heads, req, 2 * slots), jnp.float32),
            pltpu.VMEM((2, req * pad, slots), jnp.float32),
            pltpu.VMEM((req * pad, LANES), jnp.float32),
        ),
        in_specs=[pl.BlockSpec(memory_space=pltpu.SMEM)] + [vmem] * 3 + [hbm] * 2 + [vmem],
        out_specs=(hbm, hbm, vmem, vmem, vmem, vmem, vmem),
        scratch_shapes=[
            pltpu.VMEM((req, half, 2 * width), jnp.bfloat16),
            pltpu.VMEM((late, half, 2 * width), jnp.bfloat16),
            pltpu.VMEM((pos // LANES, req * pad, LANES), jnp.float32),
            pltpu.VMEM((req, slots, width), jnp.bfloat16),
            pltpu.SemaphoreType.DMA((2 * late,)),
            pltpu.SemaphoreType.DMA((2 * req,)),
            pltpu.SemaphoreType.DMA((2 * req,)),
            pltpu.SemaphoreType.DMA((2,)),
        ],
        compiler_params=pltpu.CompilerParams(vmem_limit_bytes=VMEM_LIMIT),
        cost_estimate=LIGHT,
        name="compact_own",
    )(lengths, *near(keep, weight, forget), *far(keys, values), *near(early))


def attend_kernel(n_seq, n_grp, heads, *refs):
    lengths, route, own_rows, late, level, total = refs[:6]
    tokens, rest = refs[6 : 6 + n_grp], refs[6 + n_grp :]
    stats_ref, picked_ref, scores = rest
    _, sent = half_of("seq", n_seq)
    kinds, width = picked_ref.shape
    req = kinds // 4
    size = width // heads
    slots = own_rows.shape[2]
    pad = total.shape[0] // req
    start = lax.axis_index("seq") * (4 * slots) + sent * (2 * slots)
    ahead, _, _ = offsets(lengths, start, slots // SLOTS)

    def sent_part(i, r):
        at = pl.multiple_of(ahead[r] * SLOTS, SLOTS)
        return late[i, pl.ds(at, slots), :]

    shape = (kinds, kinds)
    to, frm = iota(shape, 0), iota(shape, 1)
    wanted = by_row(route, to % req)
    me = lax.axis_index("grp")
    picked = jnp.zeros((kinds, width), jnp.float32)
    for k in range(n_grp):
        source = lax.rem(me + n_grp - k, n_grp)
        hit = (to // req == frm // req) & (wanted == source * req + frm % req)
        picked = picked + dot(hit.astype(jnp.float32).astype(jnp.bfloat16), tokens[k][...])
    picked_ref[...] = picked

    lane, row = iota((pad, width), 1), iota((pad, width), 0)
    mine = (lane >= row * size) & (lane < (row + 1) * size)
    for r in range(req):
        query = jnp.where(mine, picked[r : r + 1, :], 0.0).astype(jnp.bfloat16)
        here = slice(r * pad, (r + 1) * pad)
        scores[here, :slots] = dot_nt(query, own_rows[0, r])
        scores[here, slots:] = dot_nt(query, sent_part(0, r))
    logit = scores[...] * (size**-0.5) + jnp.concatenate([level[0], level[1]], axis=1)
    top = jnp.max(logit, axis=1, keepdims=True)
    weights = jnp.exp(logit - top).astype(jnp.bfloat16).astype(jnp.float32)
    mass = jnp.sum(weights, axis=1, keepdims=True)

    def spread_out(column, r):
        return jnp.sum(
            jnp.where(mine, column[r * pad : (r + 1) * pad], 0.0), axis=0, keepdims=True
        )

    for r in range(req):
        w = weights[r * pad : (r + 1) * pad].astype(jnp.bfloat16)
        acc = dot(w[:, :slots], own_rows[1, r]) + dot(w[:, slots:], sent_part(1, r))
        acc = jnp.sum(jnp.where(mine, acc, 0.0), axis=0, keepdims=True)
        for p, x in enumerate((top, mass, total[:, :1])):
            stats_ref[p * req + r : p * req + r + 1, :] = spread_out(x, r)
        stats_ref[3 * req + r : 3 * req + r + 1, :] = acc


def attend_part(n_seq, n_grp, heads, lengths, route, own_rows, late, level, total, tokens):
    _, req, slots, width = own_rows.shape
    vmem = pl.BlockSpec(memory_space=pltpu.VMEM)
    small = pltpu.VMEM((4 * req, width), jnp.float32)
    return pl.pallas_call(
        functools.partial(attend_kernel, n_seq, n_grp, heads),
        out_shape=(small, small),
        in_specs=[pl.BlockSpec(memory_space=pltpu.SMEM)] * 2 + [vmem] * (4 + n_grp),
        out_specs=(vmem, vmem),
        scratch_shapes=[
            pltpu.VMEM((total.shape[0], 2 * slots), jnp.float32),
        ],
        compiler_params=pltpu.CompilerParams(vmem_limit_bytes=VMEM_LIMIT),
        cost_estimate=LIGHT,
        name="attend",
    )(lengths, route, *near(own_rows, late, level, total), *near(*tokens))


def merge_kernel(count, relative, size, *refs):
    stats, refs = refs[:count], refs[count:]
    picked_ref, weight_ref, _, later_ref, out_ref = refs
    req, width = later_ref.shape
    seq = lax.axis_index("seq")
    places = [lax.rem(seq + count - k, count) if relative else jnp.int32(k) for k in range(count)]
    tops, masses, totals, accs = [
        [ref[p * req : (p + 1) * req, :] for ref in stats] for p in range(4)
    ]

    def later(place):
        total = jnp.zeros_like(totals[0])
        for k in range(count):
            total = total + jnp.where(places[k] > place, totals[k], 0.0)
        return total

    tops = [tops[k] + later(places[k]) for k in range(count)]
    top = functools.reduce(jnp.maximum, tops)
    scales = [jnp.exp(t - top) for t in tops]
    mass = sum(s * x for s, x in zip(scales, masses))
    acc = sum(s * x for s, x in zip(scales, accs))
    query, key, value, gate = [picked_ref[p * req : (p + 1) * req, :] for p in range(4)]
    one, two = iota((width, width), 0), iota((width, width), 1)
    same = (one // size == two // size).astype(jnp.float32).astype(jnp.bfloat16)
    own = split_dot(query * key, same) * (size**-0.5)
    past = top + gate
    joint = jnp.maximum(past, own)
    scale, self_weight = jnp.exp(past - joint), jnp.exp(own - joint)
    attended = (scale * acc + self_weight * value) / (scale * mass + self_weight)
    later_ref[...] = later(seq)
    out_ref[...] = dot(attended.astype(jnp.bfloat16), weight_ref[...])


def merge_part(stats, relative, picked, out_weight, second, size):
    req, width = stats[0].shape[0] // 4, stats[0].shape[1]
    vmem = pl.BlockSpec(memory_space=pltpu.VMEM)
    return pl.pallas_call(
        functools.partial(merge_kernel, len(stats), relative, size),
        out_shape=(
            pltpu.VMEM((req, width), jnp.float32),
            pltpu.VMEM((req, out_weight.shape[1]), jnp.float32),
        ),
        in_specs=[vmem] * (len(stats) + 2) + [pl.BlockSpec(memory_space=pl.ANY)],
        out_specs=(vmem, vmem),
        compiler_params=pltpu.CompilerParams(vmem_limit_bytes=VMEM_LIMIT),
        cost_estimate=MERGE,
        name="merge_and_project",
    )(*near(*stats, picked, out_weight), second)


def sum_kernel(count, size, *refs):
    parts, (later_ref, log_ref, _, out, decay_ref) = refs[:count], refs[count:]
    me = lax.axis_index("head")
    total = jnp.zeros(out.shape, jnp.float32)
    for place in range(count):
        for k in range(count):
            total = total + jnp.where(lax.rem(me + count - k, count) == place, parts[k][...], 0.0)
    out[...] = total.astype(out.dtype)
    for h in range(log_ref.shape[0]):
        decay_ref[h] = jnp.exp(log_ref[h] + later_ref[:, h * size : h * size + 1])


def sum_part(parts, later, logs, placed, size):
    vmem = pl.BlockSpec(memory_space=pltpu.VMEM)
    return pl.pallas_call(
        functools.partial(sum_kernel, len(parts), size),
        out_shape=(
            pltpu.HBM(parts[0].shape, jnp.bfloat16),
            pltpu.HBM(logs.shape, jnp.float32),
        ),
        in_specs=[vmem] * (len(parts) + 3),
        out_specs=(vmem, vmem),
        compiler_params=pltpu.CompilerParams(vmem_limit_bytes=VMEM_LIMIT),
        cost_estimate=LIGHT,
        name="sum_heads_and_decay",
    )(*parts, later, logs, placed)


def place_kernel(n_seq, first, count, marked, *refs):
    parts, refs = refs[:count], refs[count:]
    lengths, _, _, out_k, out_v, *placed_ref, sem = refs
    _, sent = half_of("seq", n_seq)
    if marked:
        placed_ref[0][...] = jnp.zeros_like(placed_ref[0])
    req, rows, _ = out_k.shape
    slots = rows // 2
    most = slots // SLOTS
    seq = lax.axis_index("seq")
    if n_seq == 2:
        start = (1 - seq) * (4 * slots) + seq * (2 * slots)
    else:
        start = seq * (4 * slots) + sent * (2 * slots)
    ahead, live, _ = offsets(lengths, start, most)
    for phase in ("start", "wait"):
        begin = first
        for p, part in enumerate(parts):
            held = part.shape[1] // SLOTS
            for r in range(req):
                if begin >= (r + 1) * most:
                    continue
                low = jnp.clip(begin - ahead[r], 0, live[r])
                high = jnp.clip(begin + held - ahead[r], 0, live[r])
                size = pl.multiple_of((high - low) * SLOTS, SLOTS)

                @pl.when(high > low)
                def _(p=p, part=part, begin=begin, r=r, low=low, size=size):
                    src = pl.multiple_of((ahead[r] + low - begin) * SLOTS, SLOTS)
                    dst = pl.multiple_of(sent * slots + low * SLOTS, SLOTS)
                    for i, out in enumerate((out_k, out_v)):
                        copy = pltpu.make_async_copy(
                            part.at[i, pl.ds(src, size), :],
                            out.at[r, pl.ds(dst, size), :],
                            sem.at[p, i, r],
                        )
                        getattr(copy, phase)()

            begin += held


def place_part(n_seq, first, parts, lengths, out_k, out_v, marked=False):
    hbm = pl.BlockSpec(memory_space=pl.ANY)
    smem = pl.BlockSpec(memory_space=pltpu.SMEM)
    vmem = pl.BlockSpec(memory_space=pltpu.VMEM)
    shape = pltpu.HBM(out_k.shape, out_k.dtype)
    count = len(parts)
    return pl.pallas_call(
        functools.partial(place_kernel, n_seq, first, count, marked),
        out_shape=(shape, shape) + (pltpu.VMEM((8, LANES), jnp.float32),) * marked,
        in_specs=[vmem] * count + [smem, hbm, hbm],
        out_specs=(hbm, hbm) + (vmem,) * marked,
        scratch_shapes=[
            pltpu.SemaphoreType.DMA((count, 2, lengths.shape[0])),
        ],
        input_output_aliases={count + 1: 0, count + 2: 1},
        compiler_params=pltpu.CompilerParams(vmem_limit_bytes=VMEM_LIMIT),
        cost_estimate=LIGHT,
        name="place_received",
    )(*near(*parts), lengths, *far(out_k, out_v))


def others(value, axis):
    count = lax.axis_size(axis)
    return [value] + [
        lax.ppermute(value, axis, [(i, (i + k) % count) for i in range(count)])
        for k in range(1, count)
    ]


def swap(value, n_seq):
    return lax.ppermute(value, "seq", [(0, 1), (1, 0)]) if n_seq == 2 else value


def shards(
    keys, values, log_forget, keep, merge_weight, lengths, route, fresh, new_forget, out_weight
):
    req, pos, width = keys.shape
    heads = log_forget.shape[1]
    size = width // heads
    n_seq, n_grp = lax.axis_size("seq"), lax.axis_size("grp")
    early, packed, choice, held_lengths, held_route = first_part(
        n_seq,
        lengths,
        route,
        keep,
        merge_weight,
        fresh.reshape(3 * req, width),
        new_forget,
        keys,
        values,
    )
    exchange = functools.partial(swap, n_seq=n_seq)
    first_received = exchange(early)
    tokens = others(packed, "grp")
    out_k, out_v, late, own_rows, logs, level, total = own_part(
        n_seq,
        held_lengths,
        keep,
        merge_weight,
        log_forget.transpose(1, 0, 2),
        keys,
        values,
        early,
    )
    begin, end = FIRST * SLOTS, (FIRST + SECOND) * SLOTS
    rest = late.shape[1] - end

    def finish(rows, early, late, own_rows, logs, level, total, tokens, *others_in):
        out_weight, lengths, route, out_k, out_v = others_in
        second = exchange(late[:, begin:end])
        stats, picked = attend_part(
            n_seq, n_grp, heads, lengths, route, own_rows, late, level, total, tokens
        )
        if n_seq == 2:
            all_stats = others(stats, "seq")
        else:
            gathered = lax.all_gather(stats, "seq")
            all_stats = [gathered[i] for i in range(n_seq)]
        ends = [end, end + rows]
        if rows > 3 * LAST * SLOTS:
            ends.insert(1, end + rows - LAST * SLOTS)
        third = [exchange(late[:, low:high]) for low, high in zip(ends, ends[1:])]
        later, partial = merge_part(all_stats, n_seq == 2, picked, out_weight, second, size)
        out_k, out_v, placed = place_part(
            n_seq, 0, (early, second), lengths, out_k, out_v, marked=True
        )
        layer_out, decay = sum_part(others(partial, "head"), later, logs, placed, size)
        for low, part in zip(ends, third):
            out_k, out_v = place_part(n_seq, low // SLOTS, (part,), lengths, out_k, out_v)
        return decay, layer_out, out_k, out_v

    operands = (first_received, late, own_rows, logs, level, total, tokens)
    operands += (out_weight, held_lengths, held_route, out_k, out_v)
    if n_seq == 2:
        branches = [
            functools.partial(finish, blocks * SLOTS) for blocks in SIZES + (rest // SLOTS,)
        ]
        decay, layer_out, out_k, out_v = lax.switch(choice[0], branches, *operands)
    else:
        decay, layer_out, out_k, out_v = finish(rest, *operands)
    if n_seq != 2:
        out_k, out_v = (
            lax.all_to_all(x, "seq", split_axis=1, concat_axis=1, tiled=True) for x in (out_k, out_v)
        )
    return out_k, out_v, decay.transpose(1, 0, 2), layer_out


def solution(mesh):
    return jax.shard_map(
        shards,
        mesh=mesh,
        in_specs=(
            P("grp", "seq", "head"),
            P("grp", "seq", "head"),
            P("grp", "head", "seq"),
            P("grp", "seq"),
            P("grp", "seq"),
            P("grp"),
            P("grp"),
            P(None, "grp", "head"),
            P("grp", "head"),
            P("head", "seq"),
        ),
        out_specs=(
            P("grp", "seq", "head"),
            P("grp", "seq", "head"),
            P("grp", "head", "seq"),
            P("grp", "seq"),
        ),
        check_vma=False,
    )
```

```python
import functools

import jax
import jax.numpy as jnp
from jax import lax
from jax.experimental import pallas as pl
from jax.experimental.pallas import tpu as pltpu
from jax.sharding import PartitionSpec as P

BLOCK = 64
SLOTS = 32
LANES = 128
BLOCK_LOG = BLOCK.bit_length() - 1
SLOT_LOG = SLOTS.bit_length() - 1
EMPTY_LOG = -10000.0
FIRST = 8
SECOND = 3
SIZES = (5, 7, 8, 9, 10, 11, 12, 13, 14, 15, 16, 17, 18, 19, 20)
LAST = 4
SURE = 2
EAGER = 4
VMEM_LIMIT = 16 * 1024 * 1024


LIGHT = pl.CostEstimate(flops=1, bytes_accessed=1, transcendentals=0)
MERGE = pl.CostEstimate(flops=1 << 36, bytes_accessed=1, transcendentals=0)


def dot(a, b):
    return lax.dot_general(a, b, (((1,), (0,)), ((), ())), preferred_element_type=jnp.float32)


def dot_nt(a, b):
    return lax.dot_general(a, b, (((1,), (1,)), ((), ())), preferred_element_type=jnp.float32)


def iota(shape, dim):
    return lax.broadcasted_iota(jnp.int32, shape, dim)


def three(x):
    hi = x.astype(jnp.bfloat16).astype(jnp.float32)
    rest = x - hi
    mid = rest.astype(jnp.bfloat16).astype(jnp.float32)
    return hi, mid, rest - mid


def split_dot(x, ones):
    rows = x.shape[0]
    parts = dot(jnp.concatenate(three(x), axis=0).astype(jnp.bfloat16), ones)
    return parts[:rows] + parts[rows : 2 * rows] + parts[2 * rows :]


def half_of(axis, count):
    own = lax.axis_index(axis) if count == 2 else jnp.int32(0)
    return own, 1 - own


def by_row(ref, row):
    picked = jnp.zeros_like(row)
    for r in range(ref.shape[0]):
        picked = jnp.where(row == r, ref[r], picked)
    return picked


def live_blocks(lengths, r, start, most):
    return jnp.clip((lengths[r] - start) >> BLOCK_LOG, 0, most)


def offsets(lengths, start, most):
    total = jnp.int32(0)
    ahead, live = [], []
    for r in range(lengths.shape[0]):
        ahead.append(total)
        live.append(live_blocks(lengths, r, start, most))
        total = total + live[-1]
    return ahead, live, total


def mask(condition):
    return condition.astype(jnp.float32).astype(jnp.bfloat16)


def block_masks(width):
    one, two = iota((width, width), 0), iota((width, width), 1)
    same = (one ^ two) < BLOCK
    return mask(same & (one <= two)), mask(same), mask(same & (one > two))


def plan(keep, weight, start, len_ref, upto, block):
    rows, width = keep.shape
    kept = keep == 1
    rank = dot(keep.astype(jnp.float32).astype(jnp.bfloat16), upto) - 1.0
    weighted = jnp.where(kept, 0.0, weight)
    share = (weighted / split_dot(weighted, block)).astype(jnp.bfloat16).astype(jnp.float32)
    lane, row = iota((rows, width), 1), iota((rows, width), 0)
    slot = jnp.where(kept, rank.astype(jnp.int32), SLOTS - 1) + (lane >> BLOCK_LOG) * SLOTS
    slot = jnp.where(start + lane < by_row(len_ref, row), slot, -1)
    return slot, jnp.where(kept, 1.0, share)


def select(slot, factor, r):
    width = slot.shape[1]
    shape = (width // 2, width)
    hit = iota(shape, 0) == slot[r : r + 1, :]
    return jnp.where(hit, jnp.broadcast_to(factor[r : r + 1, :], shape), 0.0).astype(jnp.bfloat16)


def lanes(half, width):
    return pl.ds(pl.multiple_of(half * width, width), width)


def far(*arrays):
    return [pltpu.with_memory_space_constraint(x, pltpu.HBM) for x in arrays]


def near(*arrays):
    return [pltpu.with_memory_space_constraint(x, pltpu.VMEM) for x in arrays]


def fetch(pairs, sem):
    copies = [pltpu.make_async_copy(src, dst, sem.at[i]) for i, (src, dst) in enumerate(pairs)]
    for copy in copies:
        copy.start()
    return copies


def first_kernel(
    n_seq, len_hbm, route_hbm, keep_hbm, weight_hbm, fresh_hbm, gate_hbm, keys, values, *rest
):
    out, packed, size_ref, lengths, route, keep, weight, fresh, gates, raw, row_buf = rest[:11]
    sem_s, sem_t, sem_r = rest[11:]
    _, sent = half_of("seq", n_seq)
    req, width = keep.shape
    most = width // BLOCK
    small = fetch(
        [
            (len_hbm, lengths),
            (keep_hbm.at[:, lanes(sent, width)], keep),
            (weight_hbm.at[:, lanes(sent, width)], weight),
        ],
        sem_s,
    )

    channels = keys.shape[2]

    def slab(i, r):
        source = (keys, values)[i].at[r, lanes(sent, width), :]
        target = raw.at[r, :, pl.ds(i * channels, channels)]
        return pltpu.make_async_copy(source, target, sem_r.at[i, r])

    eager = min(EAGER, req)
    for r in range(eager):
        for i in range(2):
            slab(i, r).start()
    tokens = fetch([(fresh_hbm, fresh), (gate_hbm, gates), (route_hbm, route)], sem_t)
    row_buf[...] = jnp.zeros_like(row_buf)
    upto, block, _ = block_masks(width)
    for copy in small:
        copy.wait()
    start = lax.axis_index("seq") * (2 * width) + sent * width
    ahead, live, _ = offsets(lengths, start, most)
    needed = [(ahead[r] < FIRST) & (live[r] > 0) for r in range(req)]
    for r in range(eager, req):

        @pl.when(needed[r])
        def _(r=r):
            for i in range(2):
                slab(i, r).start()

    slot, factor = plan(keep[...], weight[...], start, lengths, upto, block)
    _, _, total = offsets(lengths, width, most)
    choice = jnp.int32(0)
    for size in SIZES:
        choice = choice + (total - FIRST - SECOND > size).astype(jnp.int32)
    size_ref[0] = choice

    def pack(r):
        chosen = select(slot, factor, r)
        at = pl.ds(pl.multiple_of(ahead[r] * SLOTS, SLOTS), most * SLOTS)
        if r >= eager:
            for i in range(2):
                slab(i, r).wait()
        rows = dot(chosen, raw[r]).astype(jnp.bfloat16)
        for i in range(2):
            row_buf[i, at, :] = rows[:, i * channels : (i + 1) * channels]

    for r in range(req):
        if r < eager:
            for i in range(2):
                slab(i, r).wait()
        if r < SURE:
            pack(r)
        else:
            pl.when(needed[r])(functools.partial(pack, r))

    for copy in tokens:
        copy.wait()
    new, gate = fresh[...].astype(jnp.float32), gates[...].astype(jnp.float32)
    heads = gate.shape[1]
    lane = iota((req, new.shape[1]), 1)
    size = new.shape[1] // heads
    spread = jnp.zeros((req, new.shape[1]), jnp.float32)
    for h in range(heads):
        inside = (lane >= h * size) & (lane < (h + 1) * size)
        spread = jnp.where(inside, gate[:, h : h + 1], spread)
    packed[...] = jnp.concatenate([new, spread], axis=0).astype(jnp.bfloat16)

    out[...] = row_buf[:, : FIRST * SLOTS, :]


def first_part(n_seq, lengths, route, keep, weight, fresh, gates, keys, values):
    req, pos, width = keys.shape
    half = pos // 2
    hbm = pl.BlockSpec(memory_space=pl.ANY)
    smem = pl.BlockSpec(memory_space=pltpu.SMEM)
    vmem = pl.BlockSpec(memory_space=pltpu.VMEM)
    return pl.pallas_call(
        functools.partial(first_kernel, n_seq),
        out_shape=(
            pltpu.VMEM((2, FIRST * SLOTS, width), jnp.bfloat16),
            pltpu.VMEM((fresh.shape[0] + req, width), jnp.bfloat16),
            jax.ShapeDtypeStruct((1,), jnp.int32),
            pltpu.SMEM(lengths.shape, jnp.int32),
            pltpu.SMEM(route.shape, jnp.int32),
        ),
        in_specs=[hbm] * 8,
        out_specs=(vmem, vmem, smem, smem, smem),
        scratch_shapes=[
            pltpu.VMEM((req, half), jnp.int32),
            pltpu.VMEM((req, half), jnp.float32),
            pltpu.VMEM(fresh.shape, fresh.dtype),
            pltpu.VMEM(gates.shape, gates.dtype),
            pltpu.VMEM((req, half, 2 * width), jnp.bfloat16),
            pltpu.VMEM((2, (FIRST - 1) * SLOTS + half // 2, width), jnp.bfloat16),
            pltpu.SemaphoreType.DMA((3,)),
            pltpu.SemaphoreType.DMA((3,)),
            pltpu.SemaphoreType.DMA((2, req)),
        ],
        compiler_params=pltpu.CompilerParams(vmem_limit_bytes=VMEM_LIMIT),
        cost_estimate=LIGHT,
        name="compact_first_sent",
    )(*far(lengths, route, keep, weight, fresh, gates, keys, values))


def own_kernel(
    n_seq, lengths, keep, weight, gates, keys, values, early, *rest
):
    out_k, out_v, chunk, rows, log_ref, level_ref, total_ref = rest[:7]
    raw, late, forget, zeros, sem_l, sem_r, sem_o, sem_z = rest[7:]
    own, sent = half_of("seq", n_seq)
    seq = lax.axis_index("seq")
    heads, req, pos = gates.shape
    half = pos // 2
    slots = half // 2
    most = half // BLOCK
    first = FIRST // most
    pad = forget.shape[1] // req
    both = ((0, keys), (1, values))
    channels = keys.shape[2]

    def part(i):
        return pl.ds(i * channels, channels)

    late_slabs = fetch(
        [
            (source.at[r, lanes(sent, half), :], late.at[r - first, :, part(i)])
            for r in range(first, req)
            for i, source in both
        ],
        sem_l,
    )
    slabs = fetch(
        [
            (source.at[r, lanes(own, half), :], raw.at[r, :, part(i)])
            for r in range(req)
            for i, source in both
        ],
        sem_r,
    )
    zeros[...] = jnp.zeros_like(zeros)
    stores = fetch([(zeros, out.at[:, lanes(sent, slots), :]) for out in (out_k, out_v)], sem_z)
    chunk[:, : FIRST * SLOTS, :] = early[...]
    chunk[:, FIRST * SLOTS :, :] = jnp.zeros(
        (2, chunk.shape[1] - FIRST * SLOTS, chunk.shape[2]), chunk.dtype
    )
    upto, block, after = block_masks(half)
    ahead, alive, _ = offsets(lengths, seq * pos + sent * half, most)

    forget[...] = jnp.zeros_like(forget)
    live = seq * pos + iota((req, pos), 1) < by_row(lengths, iota((req, pos), 0))
    for h in range(heads):
        gate = jnp.where(live, gates[h], 0.0)
        for c in range(pos // LANES):
            forget[c, pl.ds(h, req, stride=pad), :] = gate[:, c * LANES : (c + 1) * LANES]
    flat = jnp.concatenate([forget[c] for c in range(pos // LANES)], axis=1)
    total_ref[...] = jnp.broadcast_to(jnp.sum(flat, axis=1, keepdims=True), total_ref.shape)
    ends = iota((pos, slots), 1) >> SLOT_LOG
    begins = iota((pos, slots), 0) >> BLOCK_LOG
    last = iota((req * pad, slots), 1) & (SLOTS - 1) == SLOTS - 1

    for i, h in enumerate((own, sent)):
        slot, factor = plan(
            keep[:, lanes(h, half)],
            weight[:, lanes(h, half)],
            seq * pos + h * half,
            lengths,
            upto,
            block,
        )
        near = half // LANES
        inner = split_dot(
            jnp.concatenate([forget[h * near + c] for c in range(near)], axis=1), after
        )
        beyond = split_dot(
            flat, (begins > ends + h * (half // BLOCK)).astype(jnp.float32).astype(jnp.bfloat16)
        )
        spread = jnp.exp(inner)
        high = spread.astype(jnp.bfloat16).astype(jnp.float32)
        planes = three(inner) + (high, spread - high, jnp.ones_like(inner))
        found = []
        for r in range(req):
            chosen = select(slot, factor, r)
            stack = jnp.concatenate([x[r * pad : (r + 1) * pad] for x in planes], axis=0)
            found.append(dot_nt(stack.astype(jnp.bfloat16), chosen))
            if i == 0:
                for k in range(2):
                    slabs[2 * r + k].wait()
                made = dot(chosen, raw[r]).astype(jnp.bfloat16)
                for k, out in enumerate((out_k, out_v)):
                    rows[k, r] = made[:, k * channels : (k + 1) * channels]
                    stores.append(
                        pltpu.make_async_copy(
                            rows.at[k, r], out.at[r, lanes(own, slots), :], sem_o.at[2 * r + k]
                        )
                    )
                    stores[-1].start()
            elif r >= first:
                for k in range(2):
                    late_slabs[2 * (r - first) + k].wait()

                @pl.when((ahead[r] + alive[r] > FIRST) & (alive[r] > 0))
                def _(r=r, chosen=chosen):
                    at = pl.ds(pl.multiple_of(ahead[r] * SLOTS, SLOTS), slots)
                    made = dot(chosen, late[r - first]).astype(jnp.bfloat16)
                    for k in range(2):
                        chunk[k, at, :] = made[:, k * channels : (k + 1) * channels]
        at = [
            jnp.concatenate([x[p * pad : (p + 1) * pad] for x in found], axis=0) for p in range(6)
        ]
        filled = at[5] > 0.5
        kept = at[0] + at[1] + at[2]
        merged = jnp.log(jnp.where(filled, at[3] + at[4], 1.0))
        level_ref[i] = jnp.where(filled, jnp.where(last, merged, kept) + beyond, EMPTY_LOG)
        for k in range(heads):
            log_ref[k, :, lanes(h, slots)] = level_ref[i, pl.ds(k, req, stride=pad), :]
    for copy in stores:
        copy.wait()


def own_part(n_seq, lengths, keep, weight, forget, keys, values, early):
    req, pos, width = keys.shape
    heads = forget.shape[0]
    half, slots, pad = pos // 2, pos // 4, -(-heads // 8) * 8
    late = req - FIRST // (half // BLOCK)
    hbm = pl.BlockSpec(memory_space=pl.ANY)
    vmem = pl.BlockSpec(memory_space=pltpu.VMEM)
    whole = pltpu.HBM((req, 2 * slots, width), jnp.bfloat16)
    return pl.pallas_call(
        functools.partial(own_kernel, n_seq),
        out_shape=(
            whole,
            whole,
            pltpu.VMEM((2, req * slots, width), jnp.bfloat16),
            pltpu.VMEM((2, req, slots, width), jnp.bfloat16),
            pltpu.VMEM((heads, req, 2 * slots), jnp.float32),
            pltpu.VMEM((2, req * pad, slots), jnp.float32),
            pltpu.VMEM((req * pad, LANES), jnp.float32),
        ),
        in_specs=[pl.BlockSpec(memory_space=pltpu.SMEM)] + [vmem] * 3 + [hbm] * 2 + [vmem],
        out_specs=(hbm, hbm, vmem, vmem, vmem, vmem, vmem),
        scratch_shapes=[
            pltpu.VMEM((req, half, 2 * width), jnp.bfloat16),
            pltpu.VMEM((late, half, 2 * width), jnp.bfloat16),
            pltpu.VMEM((pos // LANES, req * pad, LANES), jnp.float32),
            pltpu.VMEM((req, slots, width), jnp.bfloat16),
            pltpu.SemaphoreType.DMA((2 * late,)),
            pltpu.SemaphoreType.DMA((2 * req,)),
            pltpu.SemaphoreType.DMA((2 * req,)),
            pltpu.SemaphoreType.DMA((2,)),
        ],
        compiler_params=pltpu.CompilerParams(vmem_limit_bytes=VMEM_LIMIT),
        cost_estimate=LIGHT,
        name="compact_own",
    )(lengths, *near(keep, weight, forget), *far(keys, values), *near(early))


def attend_kernel(n_seq, n_grp, heads, *refs):
    lengths, route, own_rows, late, level, total = refs[:6]
    tokens, rest = refs[6 : 6 + n_grp], refs[6 + n_grp :]
    stats_ref, picked_ref, scores = rest
    _, sent = half_of("seq", n_seq)
    kinds, width = picked_ref.shape
    req = kinds // 4
    size = width // heads
    slots = own_rows.shape[2]
    pad = total.shape[0] // req
    start = lax.axis_index("seq") * (4 * slots) + sent * (2 * slots)
    ahead, _, _ = offsets(lengths, start, slots // SLOTS)

    def sent_part(i, r):
        at = pl.multiple_of(ahead[r] * SLOTS, SLOTS)
        return late[i, pl.ds(at, slots), :]

    shape = (kinds, kinds)
    to, frm = iota(shape, 0), iota(shape, 1)
    wanted = by_row(route, to % req)
    me = lax.axis_index("grp")
    picked = jnp.zeros((kinds, width), jnp.float32)
    for k in range(n_grp):
        source = lax.rem(me + n_grp - k, n_grp)
        hit = (to // req == frm // req) & (wanted == source * req + frm % req)
        picked = picked + dot(hit.astype(jnp.float32).astype(jnp.bfloat16), tokens[k][...])
    picked_ref[...] = picked

    lane, row = iota((pad, width), 1), iota((pad, width), 0)
    mine = (lane >= row * size) & (lane < (row + 1) * size)
    for r in range(req):
        query = jnp.where(mine, picked[r : r + 1, :], 0.0).astype(jnp.bfloat16)
        here = slice(r * pad, (r + 1) * pad)
        scores[here, :slots] = dot_nt(query, own_rows[0, r])
        scores[here, slots:] = dot_nt(query, sent_part(0, r))
    logit = scores[...] * (size**-0.5) + jnp.concatenate([level[0], level[1]], axis=1)
    top = jnp.max(logit, axis=1, keepdims=True)
    weights = jnp.exp(logit - top).astype(jnp.bfloat16).astype(jnp.float32)
    mass = jnp.sum(weights, axis=1, keepdims=True)

    def spread_out(column, r):
        return jnp.sum(
            jnp.where(mine, column[r * pad : (r + 1) * pad], 0.0), axis=0, keepdims=True
        )

    for r in range(req):
        w = weights[r * pad : (r + 1) * pad].astype(jnp.bfloat16)
        acc = dot(w[:, :slots], own_rows[1, r]) + dot(w[:, slots:], sent_part(1, r))
        acc = jnp.sum(jnp.where(mine, acc, 0.0), axis=0, keepdims=True)
        for p, x in enumerate((top, mass, total[:, :1])):
            stats_ref[p * req + r : p * req + r + 1, :] = spread_out(x, r)
        stats_ref[3 * req + r : 3 * req + r + 1, :] = acc


def attend_part(n_seq, n_grp, heads, lengths, route, own_rows, late, level, total, tokens):
    _, req, slots, width = own_rows.shape
    vmem = pl.BlockSpec(memory_space=pltpu.VMEM)
    small = pltpu.VMEM((4 * req, width), jnp.float32)
    return pl.pallas_call(
        functools.partial(attend_kernel, n_seq, n_grp, heads),
        out_shape=(small, small),
        in_specs=[pl.BlockSpec(memory_space=pltpu.SMEM)] * 2 + [vmem] * (4 + n_grp),
        out_specs=(vmem, vmem),
        scratch_shapes=[
            pltpu.VMEM((total.shape[0], 2 * slots), jnp.float32),
        ],
        compiler_params=pltpu.CompilerParams(vmem_limit_bytes=VMEM_LIMIT),
        cost_estimate=LIGHT,
        name="attend",
    )(lengths, route, *near(own_rows, late, level, total), *near(*tokens))


def merge_kernel(count, relative, size, *refs):
    stats, refs = refs[:count], refs[count:]
    picked_ref, weight_ref, _, later_ref, out_ref = refs
    req, width = later_ref.shape
    seq = lax.axis_index("seq")
    places = [lax.rem(seq + count - k, count) if relative else jnp.int32(k) for k in range(count)]
    tops, masses, totals, accs = [
        [ref[p * req : (p + 1) * req, :] for ref in stats] for p in range(4)
    ]

    def later(place):
        total = jnp.zeros_like(totals[0])
        for k in range(count):
            total = total + jnp.where(places[k] > place, totals[k], 0.0)
        return total

    tops = [tops[k] + later(places[k]) for k in range(count)]
    top = functools.reduce(jnp.maximum, tops)
    scales = [jnp.exp(t - top) for t in tops]
    mass = sum(s * x for s, x in zip(scales, masses))
    acc = sum(s * x for s, x in zip(scales, accs))
    query, key, value, gate = [picked_ref[p * req : (p + 1) * req, :] for p in range(4)]
    one, two = iota((width, width), 0), iota((width, width), 1)
    same = (one // size == two // size).astype(jnp.float32).astype(jnp.bfloat16)
    own = split_dot(query * key, same) * (size**-0.5)
    past = top + gate
    joint = jnp.maximum(past, own)
    scale, self_weight = jnp.exp(past - joint), jnp.exp(own - joint)
    attended = (scale * acc + self_weight * value) / (scale * mass + self_weight)
    later_ref[...] = later(seq)
    out_ref[...] = dot(attended.astype(jnp.bfloat16), weight_ref[...])


def merge_part(stats, relative, picked, out_weight, second, size):
    req, width = stats[0].shape[0] // 4, stats[0].shape[1]
    vmem = pl.BlockSpec(memory_space=pltpu.VMEM)
    return pl.pallas_call(
        functools.partial(merge_kernel, len(stats), relative, size),
        out_shape=(
            pltpu.VMEM((req, width), jnp.float32),
            pltpu.VMEM((req, out_weight.shape[1]), jnp.float32),
        ),
        in_specs=[vmem] * (len(stats) + 2) + [pl.BlockSpec(memory_space=pl.ANY)],
        out_specs=(vmem, vmem),
        compiler_params=pltpu.CompilerParams(vmem_limit_bytes=VMEM_LIMIT),
        cost_estimate=MERGE,
        name="merge_and_project",
    )(*near(*stats, picked, out_weight), second)


def sum_kernel(count, size, *refs):
    parts, (later_ref, log_ref, _, out, decay_ref) = refs[:count], refs[count:]
    me = lax.axis_index("head")
    total = jnp.zeros(out.shape, jnp.float32)
    for place in range(count):
        for k in range(count):
            total = total + jnp.where(lax.rem(me + count - k, count) == place, parts[k][...], 0.0)
    out[...] = total.astype(out.dtype)
    for h in range(log_ref.shape[0]):
        decay_ref[h] = jnp.exp(log_ref[h] + later_ref[:, h * size : h * size + 1])


def sum_part(parts, later, logs, placed, size):
    vmem = pl.BlockSpec(memory_space=pltpu.VMEM)
    return pl.pallas_call(
        functools.partial(sum_kernel, len(parts), size),
        out_shape=(
            pltpu.HBM(parts[0].shape, jnp.bfloat16),
            pltpu.HBM(logs.shape, jnp.float32),
        ),
        in_specs=[vmem] * (len(parts) + 3),
        out_specs=(vmem, vmem),
        compiler_params=pltpu.CompilerParams(vmem_limit_bytes=VMEM_LIMIT),
        cost_estimate=LIGHT,
        name="sum_heads_and_decay",
    )(*parts, later, logs, placed)


def place_kernel(n_seq, first, count, marked, *refs):
    parts, refs = refs[:count], refs[count:]
    lengths, _, _, out_k, out_v, *placed_ref, sem = refs
    _, sent = half_of("seq", n_seq)
    if marked:
        placed_ref[0][...] = jnp.zeros_like(placed_ref[0])
    req, rows, _ = out_k.shape
    slots = rows // 2
    most = slots // SLOTS
    seq = lax.axis_index("seq")
    if n_seq == 2:
        start = (1 - seq) * (4 * slots) + seq * (2 * slots)
    else:
        start = seq * (4 * slots) + sent * (2 * slots)
    ahead, live, _ = offsets(lengths, start, most)
    for phase in ("start", "wait"):
        begin = first
        for p, part in enumerate(parts):
            held = part.shape[1] // SLOTS
            for r in range(req):
                if begin >= (r + 1) * most:
                    continue
                low = jnp.clip(begin - ahead[r], 0, live[r])
                high = jnp.clip(begin + held - ahead[r], 0, live[r])
                size = pl.multiple_of((high - low) * SLOTS, SLOTS)

                @pl.when(high > low)
                def _(p=p, part=part, begin=begin, r=r, low=low, size=size):
                    src = pl.multiple_of((ahead[r] + low - begin) * SLOTS, SLOTS)
                    dst = pl.multiple_of(sent * slots + low * SLOTS, SLOTS)
                    for i, out in enumerate((out_k, out_v)):
                        copy = pltpu.make_async_copy(
                            part.at[i, pl.ds(src, size), :],
                            out.at[r, pl.ds(dst, size), :],
                            sem.at[p, i, r],
                        )
                        getattr(copy, phase)()

            begin += held


def place_part(n_seq, first, parts, lengths, out_k, out_v, marked=False):
    hbm = pl.BlockSpec(memory_space=pl.ANY)
    smem = pl.BlockSpec(memory_space=pltpu.SMEM)
    vmem = pl.BlockSpec(memory_space=pltpu.VMEM)
    shape = pltpu.HBM(out_k.shape, out_k.dtype)
    count = len(parts)
    return pl.pallas_call(
        functools.partial(place_kernel, n_seq, first, count, marked),
        out_shape=(shape, shape) + (pltpu.VMEM((8, LANES), jnp.float32),) * marked,
        in_specs=[vmem] * count + [smem, hbm, hbm],
        out_specs=(hbm, hbm) + (vmem,) * marked,
        scratch_shapes=[
            pltpu.SemaphoreType.DMA((count, 2, lengths.shape[0])),
        ],
        input_output_aliases={count + 1: 0, count + 2: 1},
        compiler_params=pltpu.CompilerParams(vmem_limit_bytes=VMEM_LIMIT),
        cost_estimate=LIGHT,
        name="place_received",
    )(*near(*parts), lengths, *far(out_k, out_v))


def others(value, axis):
    count = lax.axis_size(axis)
    return [value] + [
        lax.ppermute(value, axis, [(i, (i + k) % count) for i in range(count)])
        for k in range(1, count)
    ]


def swap(value, n_seq):
    return lax.ppermute(value, "seq", [(0, 1), (1, 0)]) if n_seq == 2 else value


def shards(
    keys, values, log_forget, keep, merge_weight, lengths, route, fresh, new_forget, out_weight
):
    req, pos, width = keys.shape
    heads = log_forget.shape[1]
    size = width // heads
    n_seq, n_grp = lax.axis_size("seq"), lax.axis_size("grp")
    early, packed, choice, held_lengths, held_route = first_part(
        n_seq,
        lengths,
        route,
        keep,
        merge_weight,
        fresh.reshape(3 * req, width),
        new_forget,
        keys,
        values,
    )
    exchange = functools.partial(swap, n_seq=n_seq)
    first_received = exchange(early)
    tokens = others(packed, "grp")
    out_k, out_v, late, own_rows, logs, level, total = own_part(
        n_seq,
        held_lengths,
        keep,
        merge_weight,
        log_forget.transpose(1, 0, 2),
        keys,
        values,
        early,
    )
    begin, end = FIRST * SLOTS, (FIRST + SECOND) * SLOTS
    rest = late.shape[1] - end

    def finish(rows, early, late, own_rows, logs, level, total, tokens, *others_in):
        out_weight, lengths, route, out_k, out_v = others_in
        second = exchange(late[:, begin:end])
        stats, picked = attend_part(
            n_seq, n_grp, heads, lengths, route, own_rows, late, level, total, tokens
        )
        if n_seq == 2:
            all_stats = others(stats, "seq")
        else:
            gathered = lax.all_gather(stats, "seq")
            all_stats = [gathered[i] for i in range(n_seq)]
        ends = [end, end + rows]
        if rows > 3 * LAST * SLOTS:
            ends.insert(1, end + rows - LAST * SLOTS)
        third = [exchange(late[:, low:high]) for low, high in zip(ends, ends[1:])]
        later, partial = merge_part(all_stats, n_seq == 2, picked, out_weight, second, size)
        out_k, out_v, placed = place_part(
            n_seq, 0, (early, second), lengths, out_k, out_v, marked=True
        )
        layer_out, decay = sum_part(others(partial, "head"), later, logs, placed, size)
        for low, part in zip(ends, third):
            out_k, out_v = place_part(n_seq, low // SLOTS, (part,), lengths, out_k, out_v)
        return decay, layer_out, out_k, out_v

    operands = (first_received, late, own_rows, logs, level, total, tokens)
    operands += (out_weight, held_lengths, held_route, out_k, out_v)
    if n_seq == 2:
        branches = [
            functools.partial(finish, blocks * SLOTS) for blocks in SIZES + (rest // SLOTS,)
        ]
        decay, layer_out, out_k, out_v = lax.switch(choice[0], branches, *operands)
    else:
        decay, layer_out, out_k, out_v = finish(rest, *operands)
    if n_seq != 2:
        out_k, out_v = (
            lax.all_to_all(x, "seq", split_axis=1, concat_axis=1, tiled=True) for x in (out_k, out_v)
        )
    return out_k, out_v, decay.transpose(1, 0, 2), layer_out


def solution(mesh):
    return jax.shard_map(
        shards,
        mesh=mesh,
        in_specs=(
            P("grp", "seq", "head"),
            P("grp", "seq", "head"),
            P("grp", "head", "seq"),
            P("grp", "seq"),
            P("grp", "seq"),
            P("grp"),
            P("grp"),
            P(None, "grp", "head"),
            P("grp", "head"),
            P("head", "seq"),
        ),
        out_specs=(
            P("grp", "seq", "head"),
            P("grp", "seq", "head"),
            P("grp", "head", "seq"),
            P("grp", "seq"),
        ),
        check_vma=False,
    )
```

```python
import functools

import jax
import jax.numpy as jnp
from jax import lax
from jax.experimental import pallas as pl
from jax.experimental.pallas import tpu as pltpu
from jax.sharding import PartitionSpec as P

BLOCK = 64
SLOTS = 32
LANES = 128
BLOCK_LOG = BLOCK.bit_length() - 1
SLOT_LOG = SLOTS.bit_length() - 1
EMPTY_LOG = -10000.0
FIRST = 8
SECOND = 3
SIZES = (7, 9, 11, 13, 14, 15, 17, 19)
LAST = 4
SURE = 2
EAGER = 5
VMEM_LIMIT = 16 * 1024 * 1024


LIGHT = pl.CostEstimate(flops=1, bytes_accessed=1, transcendentals=0)
MERGE = pl.CostEstimate(flops=1 << 36, bytes_accessed=1, transcendentals=0)


def dot(a, b):
    return lax.dot_general(a, b, (((1,), (0,)), ((), ())), preferred_element_type=jnp.float32)


def dot_nt(a, b):
    return lax.dot_general(a, b, (((1,), (1,)), ((), ())), preferred_element_type=jnp.float32)


def iota(shape, dim):
    return lax.broadcasted_iota(jnp.int32, shape, dim)


def three(x):
    hi = x.astype(jnp.bfloat16).astype(jnp.float32)
    rest = x - hi
    mid = rest.astype(jnp.bfloat16).astype(jnp.float32)
    return hi, mid, rest - mid


def split_dot(x, ones):
    rows = x.shape[0]
    parts = dot(jnp.concatenate(three(x), axis=0).astype(jnp.bfloat16), ones)
    return parts[:rows] + parts[rows : 2 * rows] + parts[2 * rows :]


def half_of(axis, count):
    own = lax.axis_index(axis) if count == 2 else jnp.int32(0)
    return own, 1 - own


def by_row(ref, row):
    picked = jnp.zeros_like(row)
    for r in range(ref.shape[0]):
        picked = jnp.where(row == r, ref[r], picked)
    return picked


def live_blocks(lengths, r, start, most):
    return jnp.clip((lengths[r] - start) >> BLOCK_LOG, 0, most)


def offsets(lengths, start, most):
    total = jnp.int32(0)
    ahead, live = [], []
    for r in range(lengths.shape[0]):
        ahead.append(total)
        live.append(live_blocks(lengths, r, start, most))
        total = total + live[-1]
    return ahead, live, total


def mask(condition):
    return condition.astype(jnp.float32).astype(jnp.bfloat16)


def block_masks(width):
    one, two = iota((width, width), 0), iota((width, width), 1)
    same = (one ^ two) < BLOCK
    return mask(same & (one <= two)), mask(same), mask(same & (one > two))


def plan(keep, weight, start, len_ref, upto, block):
    rows, width = keep.shape
    kept = keep == 1
    rank = dot(keep.astype(jnp.float32).astype(jnp.bfloat16), upto) - 1.0
    weighted = jnp.where(kept, 0.0, weight)
    share = (weighted / split_dot(weighted, block)).astype(jnp.bfloat16).astype(jnp.float32)
    lane, row = iota((rows, width), 1), iota((rows, width), 0)
    slot = jnp.where(kept, rank.astype(jnp.int32), SLOTS - 1) + (lane >> BLOCK_LOG) * SLOTS
    slot = jnp.where(start + lane < by_row(len_ref, row), slot, -1)
    return slot, jnp.where(kept, 1.0, share)


def select(slot, factor, r):
    width = slot.shape[1]
    shape = (width // 2, width)
    hit = iota(shape, 0) == slot[r : r + 1, :]
    return jnp.where(hit, jnp.broadcast_to(factor[r : r + 1, :], shape), 0.0).astype(jnp.bfloat16)


def lanes(half, width):
    return pl.ds(pl.multiple_of(half * width, width), width)


def far(*arrays):
    return [pltpu.with_memory_space_constraint(x, pltpu.HBM) for x in arrays]


def near(*arrays):
    return [pltpu.with_memory_space_constraint(x, pltpu.VMEM) for x in arrays]


def fetch(pairs, sem):
    copies = [pltpu.make_async_copy(src, dst, sem.at[i]) for i, (src, dst) in enumerate(pairs)]
    for copy in copies:
        copy.start()
    return copies


def first_kernel(
    n_seq, len_hbm, route_hbm, keep_hbm, weight_hbm, fresh_hbm, gate_hbm, keys, values, *rest
):
    out, packed, size_ref, lengths, route, keep, weight, fresh, gates, raw, row_buf = rest[:11]
    sem_s, sem_r = rest[11:]
    _, sent = half_of("seq", n_seq)
    req, width = keep.shape
    most = width // BLOCK
    small = fetch(
        [
            (len_hbm, lengths),
            (keep_hbm.at[:, lanes(sent, width)], keep),
            (weight_hbm.at[:, lanes(sent, width)], weight),
            (fresh_hbm, fresh),
            (gate_hbm, gates),
            (route_hbm, route),
        ],
        sem_s,
    )

    channels = keys.shape[2]

    def slab(i, r):
        source = (keys, values)[i].at[r, lanes(sent, width), :]
        target = raw.at[r, :, pl.ds(i * channels, channels)]
        return pltpu.make_async_copy(source, target, sem_r.at[i, r])

    eager = min(EAGER, req)
    for r in range(eager):
        for i in range(2):
            slab(i, r).start()
    row_buf[...] = jnp.zeros_like(row_buf)
    upto, block, _ = block_masks(width)
    for copy in small:
        copy.wait()
    start = lax.axis_index("seq") * (2 * width) + sent * width
    ahead, live, _ = offsets(lengths, start, most)
    needed = [(ahead[r] < FIRST) & (live[r] > 0) for r in range(req)]
    for r in range(eager, req):

        @pl.when(needed[r])
        def _(r=r):
            for i in range(2):
                slab(i, r).start()

    slot, factor = plan(keep[...], weight[...], start, lengths, upto, block)
    _, _, total = offsets(lengths, width, most)
    choice = jnp.int32(0)
    for size in SIZES:
        choice = choice + (total - FIRST - SECOND > size).astype(jnp.int32)
    size_ref[0] = choice

    new, gate = fresh[...].astype(jnp.float32), gates[...].astype(jnp.float32)
    heads = gate.shape[1]
    lane = iota((req, new.shape[1]), 1)
    size = new.shape[1] // heads
    spread = jnp.zeros((req, new.shape[1]), jnp.float32)
    for h in range(heads):
        inside = (lane >= h * size) & (lane < (h + 1) * size)
        spread = jnp.where(inside, gate[:, h : h + 1], spread)
    packed[...] = jnp.concatenate([new, spread], axis=0).astype(jnp.bfloat16)

    def pack(r):
        chosen = select(slot, factor, r)
        at = pl.ds(pl.multiple_of(ahead[r] * SLOTS, SLOTS), most * SLOTS)
        if r >= eager:
            for i in range(2):
                slab(i, r).wait()
        rows = dot(chosen, raw[r]).astype(jnp.bfloat16)
        for i in range(2):
            row_buf[i, at, :] = rows[:, i * channels : (i + 1) * channels]

    for r in range(req):
        if r < eager:
            for i in range(2):
                slab(i, r).wait()
        if r < SURE:
            pack(r)
        else:
            pl.when(needed[r])(functools.partial(pack, r))
    out[...] = row_buf[:, : FIRST * SLOTS, :]


def first_part(n_seq, lengths, route, keep, weight, fresh, gates, keys, values):
    req, pos, width = keys.shape
    half = pos // 2
    hbm = pl.BlockSpec(memory_space=pl.ANY)
    smem = pl.BlockSpec(memory_space=pltpu.SMEM)
    vmem = pl.BlockSpec(memory_space=pltpu.VMEM)
    return pl.pallas_call(
        functools.partial(first_kernel, n_seq),
        out_shape=(
            pltpu.VMEM((2, FIRST * SLOTS, width), jnp.bfloat16),
            pltpu.VMEM((fresh.shape[0] + req, width), jnp.bfloat16),
            jax.ShapeDtypeStruct((1,), jnp.int32),
            pltpu.SMEM(lengths.shape, jnp.int32),
            pltpu.SMEM(route.shape, jnp.int32),
        ),
        in_specs=[hbm] * 8,
        out_specs=(vmem, vmem, smem, smem, smem),
        scratch_shapes=[
            pltpu.VMEM((req, half), jnp.int32),
            pltpu.VMEM((req, half), jnp.float32),
            pltpu.VMEM(fresh.shape, fresh.dtype),
            pltpu.VMEM(gates.shape, gates.dtype),
            pltpu.VMEM((req, half, 2 * width), jnp.bfloat16),
            pltpu.VMEM((2, (FIRST - 1) * SLOTS + half // 2, width), jnp.bfloat16),
            pltpu.SemaphoreType.DMA((6,)),
            pltpu.SemaphoreType.DMA((2, req)),
        ],
        compiler_params=pltpu.CompilerParams(vmem_limit_bytes=VMEM_LIMIT),
        cost_estimate=LIGHT,
        name="compact_first_sent",
    )(*far(lengths, route, keep, weight, fresh, gates, keys, values))


def own_kernel(
    n_seq, lengths, keep, weight, gates, keys, values, early, *rest
):
    out_k, out_v, chunk, rows, log_ref, level_ref, total_ref = rest[:7]
    raw, late, forget, zeros, sem_l, sem_r, sem_o, sem_z = rest[7:]
    own, sent = half_of("seq", n_seq)
    seq = lax.axis_index("seq")
    heads, req, pos = gates.shape
    half = pos // 2
    slots = half // 2
    most = half // BLOCK
    first = FIRST // most
    pad = forget.shape[1] // req
    both = ((0, keys), (1, values))
    channels = keys.shape[2]

    def part(i):
        return pl.ds(i * channels, channels)

    late_slabs = fetch(
        [
            (source.at[r, lanes(sent, half), :], late.at[r - first, :, part(i)])
            for r in range(first, req)
            for i, source in both
        ],
        sem_l,
    )
    slabs = fetch(
        [
            (source.at[r, lanes(own, half), :], raw.at[r, :, part(i)])
            for r in range(req)
            for i, source in both
        ],
        sem_r,
    )
    zeros[...] = jnp.zeros_like(zeros)
    stores = fetch([(zeros, out.at[:, lanes(sent, slots), :]) for out in (out_k, out_v)], sem_z)
    chunk[:, : FIRST * SLOTS, :] = early[...]
    chunk[:, FIRST * SLOTS :, :] = jnp.zeros(
        (2, chunk.shape[1] - FIRST * SLOTS, chunk.shape[2]), chunk.dtype
    )
    upto, block, after = block_masks(half)
    ahead, alive, _ = offsets(lengths, seq * pos + sent * half, most)

    forget[...] = jnp.zeros_like(forget)
    live = seq * pos + iota((req, pos), 1) < by_row(lengths, iota((req, pos), 0))
    for h in range(heads):
        gate = jnp.where(live, gates[h], 0.0)
        for c in range(pos // LANES):
            forget[c, pl.ds(h, req, stride=pad), :] = gate[:, c * LANES : (c + 1) * LANES]
    flat = jnp.concatenate([forget[c] for c in range(pos // LANES)], axis=1)
    total_ref[...] = jnp.broadcast_to(jnp.sum(flat, axis=1, keepdims=True), total_ref.shape)
    ends = iota((pos, slots), 1) >> SLOT_LOG
    begins = iota((pos, slots), 0) >> BLOCK_LOG
    last = iota((req * pad, slots), 1) & (SLOTS - 1) == SLOTS - 1

    for i, h in enumerate((own, sent)):
        slot, factor = plan(
            keep[:, lanes(h, half)],
            weight[:, lanes(h, half)],
            seq * pos + h * half,
            lengths,
            upto,
            block,
        )
        near = half // LANES
        inner = split_dot(
            jnp.concatenate([forget[h * near + c] for c in range(near)], axis=1), after
        )
        beyond = split_dot(
            flat, (begins > ends + h * (half // BLOCK)).astype(jnp.float32).astype(jnp.bfloat16)
        )
        spread = jnp.exp(inner)
        high = spread.astype(jnp.bfloat16).astype(jnp.float32)
        planes = three(inner) + (high, spread - high, jnp.ones_like(inner))
        found = []
        for r in range(req):
            chosen = select(slot, factor, r)
            stack = jnp.concatenate([x[r * pad : (r + 1) * pad] for x in planes], axis=0)
            found.append(dot_nt(stack.astype(jnp.bfloat16), chosen))
            if i == 0:
                for k in range(2):
                    slabs[2 * r + k].wait()
                made = dot(chosen, raw[r]).astype(jnp.bfloat16)
                for k, out in enumerate((out_k, out_v)):
                    rows[k, r] = made[:, k * channels : (k + 1) * channels]
                    stores.append(
                        pltpu.make_async_copy(
                            rows.at[k, r], out.at[r, lanes(own, slots), :], sem_o.at[2 * r + k]
                        )
                    )
                    stores[-1].start()
            elif r >= first:
                for k in range(2):
                    late_slabs[2 * (r - first) + k].wait()

                @pl.when((ahead[r] + alive[r] > FIRST) & (alive[r] > 0))
                def _(r=r, chosen=chosen):
                    at = pl.ds(pl.multiple_of(ahead[r] * SLOTS, SLOTS), slots)
                    made = dot(chosen, late[r - first]).astype(jnp.bfloat16)
                    for k in range(2):
                        chunk[k, at, :] = made[:, k * channels : (k + 1) * channels]
        at = [
            jnp.concatenate([x[p * pad : (p + 1) * pad] for x in found], axis=0) for p in range(6)
        ]
        filled = at[5] > 0.5
        kept = at[0] + at[1] + at[2]
        merged = jnp.log(jnp.where(filled, at[3] + at[4], 1.0))
        level_ref[i] = jnp.where(filled, jnp.where(last, merged, kept) + beyond, EMPTY_LOG)
        for k in range(heads):
            log_ref[k, :, lanes(h, slots)] = level_ref[i, pl.ds(k, req, stride=pad), :]
    for copy in stores:
        copy.wait()


def own_part(n_seq, lengths, keep, weight, forget, keys, values, early):
    req, pos, width = keys.shape
    heads = forget.shape[0]
    half, slots, pad = pos // 2, pos // 4, -(-heads // 8) * 8
    late = req - FIRST // (half // BLOCK)
    hbm = pl.BlockSpec(memory_space=pl.ANY)
    vmem = pl.BlockSpec(memory_space=pltpu.VMEM)
    whole = pltpu.HBM((req, 2 * slots, width), jnp.bfloat16)
    return pl.pallas_call(
        functools.partial(own_kernel, n_seq),
        out_shape=(
            whole,
            whole,
            pltpu.VMEM((2, req * slots, width), jnp.bfloat16),
            pltpu.VMEM((2, req, slots, width), jnp.bfloat16),
            pltpu.VMEM((heads, req, 2 * slots), jnp.float32),
            pltpu.VMEM((2, req * pad, slots), jnp.float32),
            pltpu.VMEM((req * pad, LANES), jnp.float32),
        ),
        in_specs=[pl.BlockSpec(memory_space=pltpu.SMEM)] + [vmem] * 3 + [hbm] * 2 + [vmem],
        out_specs=(hbm, hbm, vmem, vmem, vmem, vmem, vmem),
        scratch_shapes=[
            pltpu.VMEM((req, half, 2 * width), jnp.bfloat16),
            pltpu.VMEM((late, half, 2 * width), jnp.bfloat16),
            pltpu.VMEM((pos // LANES, req * pad, LANES), jnp.float32),
            pltpu.VMEM((req, slots, width), jnp.bfloat16),
            pltpu.SemaphoreType.DMA((2 * late,)),
            pltpu.SemaphoreType.DMA((2 * req,)),
            pltpu.SemaphoreType.DMA((2 * req,)),
            pltpu.SemaphoreType.DMA((2,)),
        ],
        compiler_params=pltpu.CompilerParams(vmem_limit_bytes=VMEM_LIMIT),
        cost_estimate=LIGHT,
        name="compact_own",
    )(lengths, *near(keep, weight, forget), *far(keys, values), *near(early))


def attend_kernel(n_seq, n_grp, heads, *refs):
    lengths, route, own_rows, late, level, total = refs[:6]
    tokens, rest = refs[6 : 6 + n_grp], refs[6 + n_grp :]
    stats_ref, picked_ref, scores = rest
    _, sent = half_of("seq", n_seq)
    kinds, width = picked_ref.shape
    req = kinds // 4
    size = width // heads
    slots = own_rows.shape[2]
    pad = total.shape[0] // req
    start = lax.axis_index("seq") * (4 * slots) + sent * (2 * slots)
    ahead, _, _ = offsets(lengths, start, slots // SLOTS)

    def sent_part(i, r):
        at = pl.multiple_of(ahead[r] * SLOTS, SLOTS)
        return late[i, pl.ds(at, slots), :]

    shape = (kinds, kinds)
    to, frm = iota(shape, 0), iota(shape, 1)
    wanted = by_row(route, to % req)
    me = lax.axis_index("grp")
    picked = jnp.zeros((kinds, width), jnp.float32)
    for k in range(n_grp):
        source = lax.rem(me + n_grp - k, n_grp)
        hit = (to // req == frm // req) & (wanted == source * req + frm % req)
        picked = picked + dot(hit.astype(jnp.float32).astype(jnp.bfloat16), tokens[k][...])
    picked_ref[...] = picked

    lane, row = iota((pad, width), 1), iota((pad, width), 0)
    mine = (lane >= row * size) & (lane < (row + 1) * size)
    for r in range(req):
        query = jnp.where(mine, picked[r : r + 1, :], 0.0).astype(jnp.bfloat16)
        here = slice(r * pad, (r + 1) * pad)
        scores[here, :slots] = dot_nt(query, own_rows[0, r])
        scores[here, slots:] = dot_nt(query, sent_part(0, r))
    logit = scores[...] * (size**-0.5) + jnp.concatenate([level[0], level[1]], axis=1)
    top = jnp.max(logit, axis=1, keepdims=True)
    weights = jnp.exp(logit - top).astype(jnp.bfloat16).astype(jnp.float32)
    mass = jnp.sum(weights, axis=1, keepdims=True)

    def spread_out(column, r):
        return jnp.sum(
            jnp.where(mine, column[r * pad : (r + 1) * pad], 0.0), axis=0, keepdims=True
        )

    for r in range(req):
        w = weights[r * pad : (r + 1) * pad].astype(jnp.bfloat16)
        acc = dot(w[:, :slots], own_rows[1, r]) + dot(w[:, slots:], sent_part(1, r))
        acc = jnp.sum(jnp.where(mine, acc, 0.0), axis=0, keepdims=True)
        for p, x in enumerate((top, mass, total[:, :1])):
            stats_ref[p * req + r : p * req + r + 1, :] = spread_out(x, r)
        stats_ref[3 * req + r : 3 * req + r + 1, :] = acc


def attend_part(n_seq, n_grp, heads, lengths, route, own_rows, late, level, total, tokens):
    _, req, slots, width = own_rows.shape
    vmem = pl.BlockSpec(memory_space=pltpu.VMEM)
    small = pltpu.VMEM((4 * req, width), jnp.float32)
    return pl.pallas_call(
        functools.partial(attend_kernel, n_seq, n_grp, heads),
        out_shape=(small, small),
        in_specs=[pl.BlockSpec(memory_space=pltpu.SMEM)] * 2 + [vmem] * (4 + n_grp),
        out_specs=(vmem, vmem),
        scratch_shapes=[
            pltpu.VMEM((total.shape[0], 2 * slots), jnp.float32),
        ],
        compiler_params=pltpu.CompilerParams(vmem_limit_bytes=VMEM_LIMIT),
        cost_estimate=LIGHT,
        name="attend",
    )(lengths, route, *near(own_rows, late, level, total), *near(*tokens))


def merge_kernel(count, relative, size, *refs):
    stats, refs = refs[:count], refs[count:]
    picked_ref, weight_ref, _, later_ref, out_ref = refs
    req, width = later_ref.shape
    seq = lax.axis_index("seq")
    places = [lax.rem(seq + count - k, count) if relative else jnp.int32(k) for k in range(count)]
    tops, masses, totals, accs = [
        [ref[p * req : (p + 1) * req, :] for ref in stats] for p in range(4)
    ]

    def later(place):
        total = jnp.zeros_like(totals[0])
        for k in range(count):
            total = total + jnp.where(places[k] > place, totals[k], 0.0)
        return total

    tops = [tops[k] + later(places[k]) for k in range(count)]
    top = functools.reduce(jnp.maximum, tops)
    scales = [jnp.exp(t - top) for t in tops]
    mass = sum(s * x for s, x in zip(scales, masses))
    acc = sum(s * x for s, x in zip(scales, accs))
    query, key, value, gate = [picked_ref[p * req : (p + 1) * req, :] for p in range(4)]
    one, two = iota((width, width), 0), iota((width, width), 1)
    same = (one // size == two // size).astype(jnp.float32).astype(jnp.bfloat16)
    own = split_dot(query * key, same) * (size**-0.5)
    past = top + gate
    joint = jnp.maximum(past, own)
    scale, self_weight = jnp.exp(past - joint), jnp.exp(own - joint)
    attended = (scale * acc + self_weight * value) / (scale * mass + self_weight)
    later_ref[...] = later(seq)
    out_ref[...] = dot(attended.astype(jnp.bfloat16), weight_ref[...])


def merge_part(stats, relative, picked, out_weight, second, size):
    req, width = stats[0].shape[0] // 4, stats[0].shape[1]
    vmem = pl.BlockSpec(memory_space=pltpu.VMEM)
    return pl.pallas_call(
        functools.partial(merge_kernel, len(stats), relative, size),
        out_shape=(
            pltpu.VMEM((req, width), jnp.float32),
            pltpu.VMEM((req, out_weight.shape[1]), jnp.float32),
        ),
        in_specs=[vmem] * (len(stats) + 2) + [pl.BlockSpec(memory_space=pl.ANY)],
        out_specs=(vmem, vmem),
        compiler_params=pltpu.CompilerParams(vmem_limit_bytes=VMEM_LIMIT),
        cost_estimate=MERGE,
        name="merge_and_project",
    )(*near(*stats, picked, out_weight), second)


def sum_kernel(count, size, *refs):
    parts, (later_ref, log_ref, _, out, decay_ref) = refs[:count], refs[count:]
    me = lax.axis_index("head")
    total = jnp.zeros(out.shape, jnp.float32)
    for place in range(count):
        for k in range(count):
            total = total + jnp.where(lax.rem(me + count - k, count) == place, parts[k][...], 0.0)
    out[...] = total.astype(out.dtype)
    for h in range(log_ref.shape[0]):
        decay_ref[h] = jnp.exp(log_ref[h] + later_ref[:, h * size : h * size + 1])


def sum_part(parts, later, logs, placed, size):
    vmem = pl.BlockSpec(memory_space=pltpu.VMEM)
    return pl.pallas_call(
        functools.partial(sum_kernel, len(parts), size),
        out_shape=(
            pltpu.HBM(parts[0].shape, jnp.bfloat16),
            pltpu.HBM(logs.shape, jnp.float32),
        ),
        in_specs=[vmem] * (len(parts) + 3),
        out_specs=(vmem, vmem),
        compiler_params=pltpu.CompilerParams(vmem_limit_bytes=VMEM_LIMIT),
        cost_estimate=LIGHT,
        name="sum_heads_and_decay",
    )(*parts, later, logs, placed)


def place_kernel(n_seq, first, count, marked, *refs):
    parts, refs = refs[:count], refs[count:]
    lengths, _, _, out_k, out_v, *placed_ref, sem = refs
    _, sent = half_of("seq", n_seq)
    if marked:
        placed_ref[0][...] = jnp.zeros_like(placed_ref[0])
    req, rows, _ = out_k.shape
    slots = rows // 2
    most = slots // SLOTS
    seq = lax.axis_index("seq")
    if n_seq == 2:
        start = (1 - seq) * (4 * slots) + seq * (2 * slots)
    else:
        start = seq * (4 * slots) + sent * (2 * slots)
    ahead, live, _ = offsets(lengths, start, most)
    for phase in ("start", "wait"):
        begin = first
        for p, part in enumerate(parts):
            held = part.shape[1] // SLOTS
            for r in range(req):
                if begin >= (r + 1) * most:
                    continue
                low = jnp.clip(begin - ahead[r], 0, live[r])
                high = jnp.clip(begin + held - ahead[r], 0, live[r])
                size = pl.multiple_of((high - low) * SLOTS, SLOTS)

                @pl.when(high > low)
                def _(p=p, part=part, begin=begin, r=r, low=low, size=size):
                    src = pl.multiple_of((ahead[r] + low - begin) * SLOTS, SLOTS)
                    dst = pl.multiple_of(sent * slots + low * SLOTS, SLOTS)
                    for i, out in enumerate((out_k, out_v)):
                        copy = pltpu.make_async_copy(
                            part.at[i, pl.ds(src, size), :],
                            out.at[r, pl.ds(dst, size), :],
                            sem.at[p, i, r],
                        )
                        getattr(copy, phase)()

            begin += held


def place_part(n_seq, first, parts, lengths, out_k, out_v, marked=False):
    hbm = pl.BlockSpec(memory_space=pl.ANY)
    smem = pl.BlockSpec(memory_space=pltpu.SMEM)
    vmem = pl.BlockSpec(memory_space=pltpu.VMEM)
    shape = pltpu.HBM(out_k.shape, out_k.dtype)
    count = len(parts)
    return pl.pallas_call(
        functools.partial(place_kernel, n_seq, first, count, marked),
        out_shape=(shape, shape) + (pltpu.VMEM((8, LANES), jnp.float32),) * marked,
        in_specs=[vmem] * count + [smem, hbm, hbm],
        out_specs=(hbm, hbm) + (vmem,) * marked,
        scratch_shapes=[
            pltpu.SemaphoreType.DMA((count, 2, lengths.shape[0])),
        ],
        input_output_aliases={count + 1: 0, count + 2: 1},
        compiler_params=pltpu.CompilerParams(vmem_limit_bytes=VMEM_LIMIT),
        cost_estimate=LIGHT,
        name="place_received",
    )(*near(*parts), lengths, *far(out_k, out_v))


def others(value, axis):
    count = lax.axis_size(axis)
    return [value] + [
        lax.ppermute(value, axis, [(i, (i + k) % count) for i in range(count)])
        for k in range(1, count)
    ]


def swap(value, n_seq):
    return lax.ppermute(value, "seq", [(0, 1), (1, 0)]) if n_seq == 2 else value


def shards(
    keys, values, log_forget, keep, merge_weight, lengths, route, fresh, new_forget, out_weight
):
    req, pos, width = keys.shape
    heads = log_forget.shape[1]
    size = width // heads
    n_seq, n_grp = lax.axis_size("seq"), lax.axis_size("grp")
    early, packed, choice, held_lengths, held_route = first_part(
        n_seq,
        lengths,
        route,
        keep,
        merge_weight,
        fresh.reshape(3 * req, width),
        new_forget,
        keys,
        values,
    )
    exchange = functools.partial(swap, n_seq=n_seq)
    first_received = exchange(early)
    tokens = others(packed, "grp")
    out_k, out_v, late, own_rows, logs, level, total = own_part(
        n_seq,
        held_lengths,
        keep,
        merge_weight,
        log_forget.transpose(1, 0, 2),
        keys,
        values,
        early,
    )
    begin, end = FIRST * SLOTS, (FIRST + SECOND) * SLOTS
    rest = late.shape[1] - end

    def finish(rows, early, late, own_rows, logs, level, total, tokens, *others_in):
        out_weight, lengths, route, out_k, out_v = others_in
        second = exchange(late[:, begin:end])
        stats, picked = attend_part(
            n_seq, n_grp, heads, lengths, route, own_rows, late, level, total, tokens
        )
        if n_seq == 2:
            all_stats = others(stats, "seq")
        else:
            gathered = lax.all_gather(stats, "seq")
            all_stats = [gathered[i] for i in range(n_seq)]
        ends = [end, end + rows]
        if rows > 3 * LAST * SLOTS:
            ends.insert(1, end + rows - LAST * SLOTS)
        third = [exchange(late[:, low:high]) for low, high in zip(ends, ends[1:])]
        later, partial = merge_part(all_stats, n_seq == 2, picked, out_weight, second, size)
        out_k, out_v, placed = place_part(
            n_seq, 0, (early, second), lengths, out_k, out_v, marked=True
        )
        layer_out, decay = sum_part(others(partial, "head"), later, logs, placed, size)
        for low, part in zip(ends, third):
            out_k, out_v = place_part(n_seq, low // SLOTS, (part,), lengths, out_k, out_v)
        return decay, layer_out, out_k, out_v

    operands = (first_received, late, own_rows, logs, level, total, tokens)
    operands += (out_weight, held_lengths, held_route, out_k, out_v)
    if n_seq == 2:
        branches = [
            functools.partial(finish, blocks * SLOTS) for blocks in SIZES + (rest // SLOTS,)
        ]
        decay, layer_out, out_k, out_v = lax.switch(choice[0], branches, *operands)
    else:
        decay, layer_out, out_k, out_v = finish(rest, *operands)
    if n_seq != 2:
        out_k, out_v = (
            lax.all_to_all(x, "seq", split_axis=1, concat_axis=1, tiled=True) for x in (out_k, out_v)
        )
    return out_k, out_v, decay.transpose(1, 0, 2), layer_out


def solution(mesh):
    return jax.shard_map(
        shards,
        mesh=mesh,
        in_specs=(
            P("grp", "seq", "head"),
            P("grp", "seq", "head"),
            P("grp", "head", "seq"),
            P("grp", "seq"),
            P("grp", "seq"),
            P("grp"),
            P("grp"),
            P(None, "grp", "head"),
            P("grp", "head"),
            P("head", "seq"),
        ),
        out_specs=(
            P("grp", "seq", "head"),
            P("grp", "seq", "head"),
            P("grp", "head", "seq"),
            P("grp", "seq"),
        ),
        check_vma=False,
    )
```

```python
import functools

import jax
import jax.numpy as jnp
from jax import lax
from jax.experimental import pallas as pl
from jax.experimental.pallas import tpu as pltpu
from jax.sharding import PartitionSpec as P

BLOCK = 64
SLOTS = 32
LANES = 128
BLOCK_LOG = BLOCK.bit_length() - 1
SLOT_LOG = SLOTS.bit_length() - 1
EMPTY_LOG = -10000.0
FIRST = 8
SECOND = 3
SIZES = (7, 9, 11, 13, 14, 15, 17, 19)
LAST = 4
SURE = 2
EAGER = 5
VMEM_LIMIT = 16 * 1024 * 1024


LIGHT = pl.CostEstimate(flops=1, bytes_accessed=1, transcendentals=0)
MERGE = pl.CostEstimate(flops=1 << 36, bytes_accessed=1, transcendentals=0)


def dot(a, b):
    return lax.dot_general(a, b, (((1,), (0,)), ((), ())), preferred_element_type=jnp.float32)


def dot_nt(a, b):
    return lax.dot_general(a, b, (((1,), (1,)), ((), ())), preferred_element_type=jnp.float32)


def iota(shape, dim):
    return lax.broadcasted_iota(jnp.int32, shape, dim)


def three(x):
    hi = x.astype(jnp.bfloat16).astype(jnp.float32)
    rest = x - hi
    mid = rest.astype(jnp.bfloat16).astype(jnp.float32)
    return hi, mid, rest - mid


def split_dot(x, ones):
    rows = x.shape[0]
    parts = dot(jnp.concatenate(three(x), axis=0).astype(jnp.bfloat16), ones)
    return parts[:rows] + parts[rows : 2 * rows] + parts[2 * rows :]


def half_of(axis, count):
    own = lax.axis_index(axis) if count == 2 else jnp.int32(0)
    return own, 1 - own


def by_row(ref, row):
    picked = jnp.zeros_like(row)
    for r in range(ref.shape[0]):
        picked = jnp.where(row == r, ref[r], picked)
    return picked


def live_blocks(lengths, r, start, most):
    return jnp.clip((lengths[r] - start) >> BLOCK_LOG, 0, most)


def offsets(lengths, start, most):
    total = jnp.int32(0)
    ahead, live = [], []
    for r in range(lengths.shape[0]):
        ahead.append(total)
        live.append(live_blocks(lengths, r, start, most))
        total = total + live[-1]
    return ahead, live, total


def mask(condition):
    return condition.astype(jnp.float32).astype(jnp.bfloat16)


def block_masks(width):
    one, two = iota((width, width), 0), iota((width, width), 1)
    same = (one ^ two) < BLOCK
    return mask(same & (one <= two)), mask(same), mask(same & (one > two))


def plan(keep, weight, start, len_ref, upto, block):
    rows, width = keep.shape
    kept = keep == 1
    rank = dot(keep.astype(jnp.float32).astype(jnp.bfloat16), upto) - 1.0
    weighted = jnp.where(kept, 0.0, weight)
    share = (weighted / split_dot(weighted, block)).astype(jnp.bfloat16).astype(jnp.float32)
    lane, row = iota((rows, width), 1), iota((rows, width), 0)
    slot = jnp.where(kept, rank.astype(jnp.int32), SLOTS - 1) + (lane >> BLOCK_LOG) * SLOTS
    slot = jnp.where(start + lane < by_row(len_ref, row), slot, -1)
    return slot, jnp.where(kept, 1.0, share)


def select(slot, factor, r):
    width = slot.shape[1]
    shape = (width // 2, width)
    hit = iota(shape, 0) == slot[r : r + 1, :]
    return jnp.where(hit, jnp.broadcast_to(factor[r : r + 1, :], shape), 0.0).astype(jnp.bfloat16)


def lanes(half, width):
    return pl.ds(pl.multiple_of(half * width, width), width)


def far(*arrays):
    return [pltpu.with_memory_space_constraint(x, pltpu.HBM) for x in arrays]


def near(*arrays):
    return [pltpu.with_memory_space_constraint(x, pltpu.VMEM) for x in arrays]


def fetch(pairs, sem):
    copies = [pltpu.make_async_copy(src, dst, sem.at[i]) for i, (src, dst) in enumerate(pairs)]
    for copy in copies:
        copy.start()
    return copies


def first_kernel(
    n_seq, len_hbm, route_hbm, keep_hbm, weight_hbm, fresh_hbm, gate_hbm, keys, values, *rest
):
    out, packed, size_ref, lengths, route, keep, weight, fresh, gates, raw, row_buf = rest[:11]
    sem_s, sem_r = rest[11:]
    _, sent = half_of("seq", n_seq)
    req, width = keep.shape
    most = width // BLOCK
    small = fetch(
        [
            (len_hbm, lengths),
            (keep_hbm.at[:, lanes(sent, width)], keep),
            (weight_hbm.at[:, lanes(sent, width)], weight),
            (fresh_hbm, fresh),
            (gate_hbm, gates),
            (route_hbm, route),
        ],
        sem_s,
    )

    channels = keys.shape[2]

    def slab(i, r):
        source = (keys, values)[i].at[r, lanes(sent, width), :]
        target = raw.at[r, :, pl.ds(i * channels, channels)]
        return pltpu.make_async_copy(source, target, sem_r.at[i, r])

    eager = min(EAGER, req)
    for r in range(eager):
        for i in range(2):
            slab(i, r).start()
    row_buf[...] = jnp.zeros_like(row_buf)
    upto, block, _ = block_masks(width)
    for copy in small:
        copy.wait()
    start = lax.axis_index("seq") * (2 * width) + sent * width
    ahead, live, _ = offsets(lengths, start, most)
    needed = [(ahead[r] < FIRST) & (live[r] > 0) for r in range(req)]
    for r in range(eager, req):

        @pl.when(needed[r])
        def _(r=r):
            for i in range(2):
                slab(i, r).start()

    slot, factor = plan(keep[...], weight[...], start, lengths, upto, block)
    _, _, total = offsets(lengths, width, most)
    choice = jnp.int32(0)
    for size in SIZES:
        choice = choice + (total - FIRST - SECOND > size).astype(jnp.int32)
    size_ref[0] = choice

    new, gate = fresh[...].astype(jnp.float32), gates[...].astype(jnp.float32)
    heads = gate.shape[1]
    lane = iota((req, new.shape[1]), 1)
    size = new.shape[1] // heads
    spread = jnp.zeros((req, new.shape[1]), jnp.float32)
    for h in range(heads):
        inside = (lane >= h * size) & (lane < (h + 1) * size)
        spread = jnp.where(inside, gate[:, h : h + 1], spread)
    packed[...] = jnp.concatenate([new, spread], axis=0).astype(jnp.bfloat16)

    def pack(r):
        chosen = select(slot, factor, r)
        at = pl.ds(pl.multiple_of(ahead[r] * SLOTS, SLOTS), most * SLOTS)
        if r >= eager:
            for i in range(2):
                slab(i, r).wait()
        rows = dot(chosen, raw[r]).astype(jnp.bfloat16)
        for i in range(2):
            row_buf[i, at, :] = rows[:, i * channels : (i + 1) * channels]

    for r in range(req):
        if r < eager:
            for i in range(2):
                slab(i, r).wait()
        if r < SURE:
            pack(r)
        else:
            pl.when(needed[r])(functools.partial(pack, r))
    out[...] = row_buf[:, : FIRST * SLOTS, :]


def first_part(n_seq, lengths, route, keep, weight, fresh, gates, keys, values):
    req, pos, width = keys.shape
    half = pos // 2
    hbm = pl.BlockSpec(memory_space=pl.ANY)
    smem = pl.BlockSpec(memory_space=pltpu.SMEM)
    vmem = pl.BlockSpec(memory_space=pltpu.VMEM)
    return pl.pallas_call(
        functools.partial(first_kernel, n_seq),
        out_shape=(
            pltpu.VMEM((2, FIRST * SLOTS, width), jnp.bfloat16),
            pltpu.VMEM((fresh.shape[0] + req, width), jnp.bfloat16),
            jax.ShapeDtypeStruct((1,), jnp.int32),
            pltpu.SMEM(lengths.shape, jnp.int32),
            pltpu.SMEM(route.shape, jnp.int32),
        ),
        in_specs=[hbm] * 8,
        out_specs=(vmem, vmem, smem, smem, smem),
        scratch_shapes=[
            pltpu.VMEM((req, half), jnp.int32),
            pltpu.VMEM((req, half), jnp.float32),
            pltpu.VMEM(fresh.shape, fresh.dtype),
            pltpu.VMEM(gates.shape, gates.dtype),
            pltpu.VMEM((req, half, 2 * width), jnp.bfloat16),
            pltpu.VMEM((2, (FIRST - 1) * SLOTS + half // 2, width), jnp.bfloat16),
            pltpu.SemaphoreType.DMA((6,)),
            pltpu.SemaphoreType.DMA((2, req)),
        ],
        compiler_params=pltpu.CompilerParams(vmem_limit_bytes=VMEM_LIMIT),
        cost_estimate=LIGHT,
        name="compact_first_sent",
    )(*far(lengths, route, keep, weight, fresh, gates, keys, values))


def own_kernel(
    n_seq, lengths, keep, weight, gates, keys, values, early, *rest
):
    out_k, out_v, chunk, second, rows, log_ref, level_ref, total_ref = rest[:8]
    raw, late, forget, zeros, sem_l, sem_r, sem_o, sem_z = rest[8:]
    own, sent = half_of("seq", n_seq)
    seq = lax.axis_index("seq")
    heads, req, pos = gates.shape
    half = pos // 2
    slots = half // 2
    most = half // BLOCK
    first = FIRST // most
    pad = forget.shape[1] // req
    both = ((0, keys), (1, values))
    channels = keys.shape[2]

    def part(i):
        return pl.ds(i * channels, channels)

    late_slabs = fetch(
        [
            (source.at[r, lanes(sent, half), :], late.at[r - first, :, part(i)])
            for r in range(first, req)
            for i, source in both
        ],
        sem_l,
    )
    slabs = fetch(
        [
            (source.at[r, lanes(own, half), :], raw.at[r, :, part(i)])
            for r in range(req)
            for i, source in both
        ],
        sem_r,
    )
    zeros[...] = jnp.zeros_like(zeros)
    stores = fetch([(zeros, out.at[:, lanes(sent, slots), :]) for out in (out_k, out_v)], sem_z)
    chunk[:, : FIRST * SLOTS, :] = early[...]
    chunk[:, FIRST * SLOTS :, :] = jnp.zeros(
        (2, chunk.shape[1] - FIRST * SLOTS, chunk.shape[2]), chunk.dtype
    )
    upto, block, after = block_masks(half)
    ahead, alive, _ = offsets(lengths, seq * pos + sent * half, most)

    forget[...] = jnp.zeros_like(forget)
    live = seq * pos + iota((req, pos), 1) < by_row(lengths, iota((req, pos), 0))
    for h in range(heads):
        gate = jnp.where(live, gates[h], 0.0)
        for c in range(pos // LANES):
            forget[c, pl.ds(h, req, stride=pad), :] = gate[:, c * LANES : (c + 1) * LANES]
    flat = jnp.concatenate([forget[c] for c in range(pos // LANES)], axis=1)
    total_ref[...] = jnp.broadcast_to(jnp.sum(flat, axis=1, keepdims=True), total_ref.shape)
    ends = iota((pos, slots), 1) >> SLOT_LOG
    begins = iota((pos, slots), 0) >> BLOCK_LOG
    last = iota((req * pad, slots), 1) & (SLOTS - 1) == SLOTS - 1

    for i, h in enumerate((own, sent)):
        slot, factor = plan(
            keep[:, lanes(h, half)],
            weight[:, lanes(h, half)],
            seq * pos + h * half,
            lengths,
            upto,
            block,
        )
        near = half // LANES
        inner = split_dot(
            jnp.concatenate([forget[h * near + c] for c in range(near)], axis=1), after
        )
        beyond = split_dot(
            flat, (begins > ends + h * (half // BLOCK)).astype(jnp.float32).astype(jnp.bfloat16)
        )
        spread = jnp.exp(inner)
        high = spread.astype(jnp.bfloat16).astype(jnp.float32)
        planes = three(inner) + (high, spread - high, jnp.ones_like(inner))
        found = []
        for r in range(req):
            chosen = select(slot, factor, r)
            stack = jnp.concatenate([x[r * pad : (r + 1) * pad] for x in planes], axis=0)
            found.append(dot_nt(stack.astype(jnp.bfloat16), chosen))
            if i == 0:
                for k in range(2):
                    slabs[2 * r + k].wait()
                made = dot(chosen, raw[r]).astype(jnp.bfloat16)
                for k, out in enumerate((out_k, out_v)):
                    rows[k, r] = made[:, k * channels : (k + 1) * channels]
                    stores.append(
                        pltpu.make_async_copy(
                            rows.at[k, r], out.at[r, lanes(own, slots), :], sem_o.at[2 * r + k]
                        )
                    )
                    stores[-1].start()
            elif r >= first:
                for k in range(2):
                    late_slabs[2 * (r - first) + k].wait()

                @pl.when((ahead[r] + alive[r] > FIRST) & (alive[r] > 0))
                def _(r=r, chosen=chosen):
                    at = pl.ds(pl.multiple_of(ahead[r] * SLOTS, SLOTS), slots)
                    made = dot(chosen, late[r - first]).astype(jnp.bfloat16)
                    for k in range(2):
                        chunk[k, at, :] = made[:, k * channels : (k + 1) * channels]
        at = [
            jnp.concatenate([x[p * pad : (p + 1) * pad] for x in found], axis=0) for p in range(6)
        ]
        filled = at[5] > 0.5
        kept = at[0] + at[1] + at[2]
        merged = jnp.log(jnp.where(filled, at[3] + at[4], 1.0))
        level_ref[i] = jnp.where(filled, jnp.where(last, merged, kept) + beyond, EMPTY_LOG)
        for k in range(heads):
            log_ref[k, :, lanes(h, slots)] = level_ref[i, pl.ds(k, req, stride=pad), :]
    second[...] = chunk[:, FIRST * SLOTS : (FIRST + SECOND) * SLOTS, :]
    for copy in stores:
        copy.wait()


def own_part(n_seq, lengths, keep, weight, forget, keys, values, early):
    req, pos, width = keys.shape
    heads = forget.shape[0]
    half, slots, pad = pos // 2, pos // 4, -(-heads // 8) * 8
    late = req - FIRST // (half // BLOCK)
    hbm = pl.BlockSpec(memory_space=pl.ANY)
    vmem = pl.BlockSpec(memory_space=pltpu.VMEM)
    whole = pltpu.HBM((req, 2 * slots, width), jnp.bfloat16)
    return pl.pallas_call(
        functools.partial(own_kernel, n_seq),
        out_shape=(
            whole,
            whole,
            pltpu.VMEM((2, req * slots, width), jnp.bfloat16),
            pltpu.VMEM((2, SECOND * SLOTS, width), jnp.bfloat16),
            pltpu.VMEM((2, req, slots, width), jnp.bfloat16),
            pltpu.VMEM((heads, req, 2 * slots), jnp.float32),
            pltpu.VMEM((2, req * pad, slots), jnp.float32),
            pltpu.VMEM((req * pad, LANES), jnp.float32),
        ),
        in_specs=[pl.BlockSpec(memory_space=pltpu.SMEM)] + [vmem] * 3 + [hbm] * 2 + [vmem],
        out_specs=(hbm, hbm, vmem, vmem, vmem, vmem, vmem, vmem),
        scratch_shapes=[
            pltpu.VMEM((req, half, 2 * width), jnp.bfloat16),
            pltpu.VMEM((late, half, 2 * width), jnp.bfloat16),
            pltpu.VMEM((pos // LANES, req * pad, LANES), jnp.float32),
            pltpu.VMEM((req, slots, width), jnp.bfloat16),
            pltpu.SemaphoreType.DMA((2 * late,)),
            pltpu.SemaphoreType.DMA((2 * req,)),
            pltpu.SemaphoreType.DMA((2 * req,)),
            pltpu.SemaphoreType.DMA((2,)),
        ],
        compiler_params=pltpu.CompilerParams(vmem_limit_bytes=VMEM_LIMIT),
        cost_estimate=LIGHT,
        name="compact_own",
    )(lengths, *near(keep, weight, forget), *far(keys, values), *near(early))


def attend_kernel(n_seq, n_grp, heads, *refs):
    lengths, route, own_rows, late, level, total = refs[:6]
    tokens, rest = refs[6 : 6 + n_grp], refs[6 + n_grp :]
    stats_ref, picked_ref, scores = rest
    _, sent = half_of("seq", n_seq)
    kinds, width = picked_ref.shape
    req = kinds // 4
    size = width // heads
    slots = own_rows.shape[2]
    pad = total.shape[0] // req
    start = lax.axis_index("seq") * (4 * slots) + sent * (2 * slots)
    ahead, _, _ = offsets(lengths, start, slots // SLOTS)

    def sent_part(i, r):
        at = pl.multiple_of(ahead[r] * SLOTS, SLOTS)
        return late[i, pl.ds(at, slots), :]

    shape = (kinds, kinds)
    to, frm = iota(shape, 0), iota(shape, 1)
    wanted = by_row(route, to % req)
    me = lax.axis_index("grp")
    picked = jnp.zeros((kinds, width), jnp.float32)
    for k in range(n_grp):
        source = lax.rem(me + n_grp - k, n_grp)
        hit = (to // req == frm // req) & (wanted == source * req + frm % req)
        picked = picked + dot(hit.astype(jnp.float32).astype(jnp.bfloat16), tokens[k][...])
    picked_ref[...] = picked

    lane, row = iota((pad, width), 1), iota((pad, width), 0)
    mine = (lane >= row * size) & (lane < (row + 1) * size)
    for r in range(req):
        query = jnp.where(mine, picked[r : r + 1, :], 0.0).astype(jnp.bfloat16)
        here = slice(r * pad, (r + 1) * pad)
        scores[here, :slots] = dot_nt(query, own_rows[0, r])
        scores[here, slots:] = dot_nt(query, sent_part(0, r))
    logit = scores[...] * (size**-0.5) + jnp.concatenate([level[0], level[1]], axis=1)
    top = jnp.max(logit, axis=1, keepdims=True)
    weights = jnp.exp(logit - top).astype(jnp.bfloat16).astype(jnp.float32)
    mass = jnp.sum(weights, axis=1, keepdims=True)

    def spread_out(column, r):
        return jnp.sum(
            jnp.where(mine, column[r * pad : (r + 1) * pad], 0.0), axis=0, keepdims=True
        )

    for r in range(req):
        w = weights[r * pad : (r + 1) * pad].astype(jnp.bfloat16)
        acc = dot(w[:, :slots], own_rows[1, r]) + dot(w[:, slots:], sent_part(1, r))
        acc = jnp.sum(jnp.where(mine, acc, 0.0), axis=0, keepdims=True)
        for p, x in enumerate((top, mass, total[:, :1])):
            stats_ref[p * req + r : p * req + r + 1, :] = spread_out(x, r)
        stats_ref[3 * req + r : 3 * req + r + 1, :] = acc


def attend_part(n_seq, n_grp, heads, lengths, route, own_rows, late, level, total, tokens):
    _, req, slots, width = own_rows.shape
    vmem = pl.BlockSpec(memory_space=pltpu.VMEM)
    small = pltpu.VMEM((4 * req, width), jnp.float32)
    return pl.pallas_call(
        functools.partial(attend_kernel, n_seq, n_grp, heads),
        out_shape=(small, small),
        in_specs=[pl.BlockSpec(memory_space=pltpu.SMEM)] * 2 + [vmem] * (4 + n_grp),
        out_specs=(vmem, vmem),
        scratch_shapes=[
            pltpu.VMEM((total.shape[0], 2 * slots), jnp.float32),
        ],
        compiler_params=pltpu.CompilerParams(vmem_limit_bytes=VMEM_LIMIT),
        cost_estimate=LIGHT,
        name="attend",
    )(lengths, route, *near(own_rows, late, level, total), *near(*tokens))


def merge_kernel(count, relative, size, *refs):
    stats, refs = refs[:count], refs[count:]
    picked_ref, weight_ref, _, later_ref, out_ref = refs
    req, width = later_ref.shape
    seq = lax.axis_index("seq")
    places = [lax.rem(seq + count - k, count) if relative else jnp.int32(k) for k in range(count)]
    tops, masses, totals, accs = [
        [ref[p * req : (p + 1) * req, :] for ref in stats] for p in range(4)
    ]

    def later(place):
        total = jnp.zeros_like(totals[0])
        for k in range(count):
            total = total + jnp.where(places[k] > place, totals[k], 0.0)
        return total

    tops = [tops[k] + later(places[k]) for k in range(count)]
    top = functools.reduce(jnp.maximum, tops)
    scales = [jnp.exp(t - top) for t in tops]
    mass = sum(s * x for s, x in zip(scales, masses))
    acc = sum(s * x for s, x in zip(scales, accs))
    query, key, value, gate = [picked_ref[p * req : (p + 1) * req, :] for p in range(4)]
    one, two = iota((width, width), 0), iota((width, width), 1)
    same = (one // size == two // size).astype(jnp.float32).astype(jnp.bfloat16)
    own = split_dot(query * key, same) * (size**-0.5)
    past = top + gate
    joint = jnp.maximum(past, own)
    scale, self_weight = jnp.exp(past - joint), jnp.exp(own - joint)
    attended = (scale * acc + self_weight * value) / (scale * mass + self_weight)
    later_ref[...] = later(seq)
    out_ref[...] = dot(attended.astype(jnp.bfloat16), weight_ref[...])


def merge_part(stats, relative, picked, out_weight, second, size):
    req, width = stats[0].shape[0] // 4, stats[0].shape[1]
    vmem = pl.BlockSpec(memory_space=pltpu.VMEM)
    return pl.pallas_call(
        functools.partial(merge_kernel, len(stats), relative, size),
        out_shape=(
            pltpu.VMEM((req, width), jnp.float32),
            pltpu.VMEM((req, out_weight.shape[1]), jnp.float32),
        ),
        in_specs=[vmem] * (len(stats) + 2) + [pl.BlockSpec(memory_space=pl.ANY)],
        out_specs=(vmem, vmem),
        compiler_params=pltpu.CompilerParams(vmem_limit_bytes=VMEM_LIMIT),
        cost_estimate=MERGE,
        name="merge_and_project",
    )(*near(*stats, picked, out_weight), second)


def sum_kernel(count, size, *refs):
    parts, (later_ref, log_ref, _, out, decay_ref) = refs[:count], refs[count:]
    me = lax.axis_index("head")
    total = jnp.zeros(out.shape, jnp.float32)
    for place in range(count):
        for k in range(count):
            total = total + jnp.where(lax.rem(me + count - k, count) == place, parts[k][...], 0.0)
    out[...] = total.astype(out.dtype)
    for h in range(log_ref.shape[0]):
        decay_ref[h] = jnp.exp(log_ref[h] + later_ref[:, h * size : h * size + 1])


def sum_part(parts, later, logs, placed, size):
    vmem = pl.BlockSpec(memory_space=pltpu.VMEM)
    return pl.pallas_call(
        functools.partial(sum_kernel, len(parts), size),
        out_shape=(
            pltpu.HBM(parts[0].shape, jnp.bfloat16),
            pltpu.HBM(logs.shape, jnp.float32),
        ),
        in_specs=[vmem] * (len(parts) + 3),
        out_specs=(vmem, vmem),
        compiler_params=pltpu.CompilerParams(vmem_limit_bytes=VMEM_LIMIT),
        cost_estimate=LIGHT,
        name="sum_heads_and_decay",
    )(*parts, later, logs, placed)


def place_kernel(n_seq, first, count, marked, *refs):
    parts, refs = refs[:count], refs[count:]
    lengths, _, _, out_k, out_v, *placed_ref, sem = refs
    _, sent = half_of("seq", n_seq)
    if marked:
        placed_ref[0][...] = jnp.zeros_like(placed_ref[0])
    req, rows, _ = out_k.shape
    slots = rows // 2
    most = slots // SLOTS
    seq = lax.axis_index("seq")
    if n_seq == 2:
        start = (1 - seq) * (4 * slots) + seq * (2 * slots)
    else:
        start = seq * (4 * slots) + sent * (2 * slots)
    ahead, live, _ = offsets(lengths, start, most)
    for phase in ("start", "wait"):
        begin = first
        for p, part in enumerate(parts):
            held = part.shape[1] // SLOTS
            for r in range(req):
                if begin >= (r + 1) * most:
                    continue
                low = jnp.clip(begin - ahead[r], 0, live[r])
                high = jnp.clip(begin + held - ahead[r], 0, live[r])
                size = pl.multiple_of((high - low) * SLOTS, SLOTS)

                @pl.when(high > low)
                def _(p=p, part=part, begin=begin, r=r, low=low, size=size):
                    src = pl.multiple_of((ahead[r] + low - begin) * SLOTS, SLOTS)
                    dst = pl.multiple_of(sent * slots + low * SLOTS, SLOTS)
                    for i, out in enumerate((out_k, out_v)):
                        copy = pltpu.make_async_copy(
                            part.at[i, pl.ds(src, size), :],
                            out.at[r, pl.ds(dst, size), :],
                            sem.at[p, i, r],
                        )
                        getattr(copy, phase)()

            begin += held


def place_part(n_seq, first, parts, lengths, out_k, out_v, marked=False):
    hbm = pl.BlockSpec(memory_space=pl.ANY)
    smem = pl.BlockSpec(memory_space=pltpu.SMEM)
    vmem = pl.BlockSpec(memory_space=pltpu.VMEM)
    shape = pltpu.HBM(out_k.shape, out_k.dtype)
    count = len(parts)
    return pl.pallas_call(
        functools.partial(place_kernel, n_seq, first, count, marked),
        out_shape=(shape, shape) + (pltpu.VMEM((8, LANES), jnp.float32),) * marked,
        in_specs=[vmem] * count + [smem, hbm, hbm],
        out_specs=(hbm, hbm) + (vmem,) * marked,
        scratch_shapes=[
            pltpu.SemaphoreType.DMA((count, 2, lengths.shape[0])),
        ],
        input_output_aliases={count + 1: 0, count + 2: 1},
        compiler_params=pltpu.CompilerParams(vmem_limit_bytes=VMEM_LIMIT),
        cost_estimate=LIGHT,
        name="place_received",
    )(*near(*parts), lengths, *far(out_k, out_v))


def others(value, axis):
    count = lax.axis_size(axis)
    return [value] + [
        lax.ppermute(value, axis, [(i, (i + k) % count) for i in range(count)])
        for k in range(1, count)
    ]


def swap(value, n_seq):
    return lax.ppermute(value, "seq", [(0, 1), (1, 0)]) if n_seq == 2 else value


def shards(
    keys, values, log_forget, keep, merge_weight, lengths, route, fresh, new_forget, out_weight
):
    req, pos, width = keys.shape
    heads = log_forget.shape[1]
    size = width // heads
    n_seq, n_grp = lax.axis_size("seq"), lax.axis_size("grp")
    early, packed, choice, held_lengths, held_route = first_part(
        n_seq,
        lengths,
        route,
        keep,
        merge_weight,
        fresh.reshape(3 * req, width),
        new_forget,
        keys,
        values,
    )
    exchange = functools.partial(swap, n_seq=n_seq)
    first_received = exchange(early)
    tokens = others(packed, "grp")
    out_k, out_v, late, next_rows, own_rows, logs, level, total = own_part(
        n_seq,
        held_lengths,
        keep,
        merge_weight,
        log_forget.transpose(1, 0, 2),
        keys,
        values,
        early,
    )
    end = (FIRST + SECOND) * SLOTS
    rest = late.shape[1] - end

    def finish(rows, early, next_rows, late, own_rows, logs, level, total, tokens, *others_in):
        out_weight, lengths, route, out_k, out_v = others_in
        second = exchange(next_rows)
        stats, picked = attend_part(
            n_seq, n_grp, heads, lengths, route, own_rows, late, level, total, tokens
        )
        if n_seq == 2:
            all_stats = others(stats, "seq")
        else:
            gathered = lax.all_gather(stats, "seq")
            all_stats = [gathered[i] for i in range(n_seq)]
        ends = [end, end + rows]
        if rows > 3 * LAST * SLOTS:
            ends.insert(1, end + rows - LAST * SLOTS)
        third = [exchange(late[:, low:high]) for low, high in zip(ends, ends[1:])]
        later, partial = merge_part(all_stats, n_seq == 2, picked, out_weight, second, size)
        out_k, out_v, placed = place_part(
            n_seq, 0, (early, second), lengths, out_k, out_v, marked=True
        )
        layer_out, decay = sum_part(others(partial, "head"), later, logs, placed, size)
        for low, part in zip(ends, third):
            out_k, out_v = place_part(n_seq, low // SLOTS, (part,), lengths, out_k, out_v)
        return decay, layer_out, out_k, out_v

    operands = (first_received, next_rows, late, own_rows, logs, level, total, tokens)
    operands += (out_weight, held_lengths, held_route, out_k, out_v)
    if n_seq == 2:
        branches = [
            functools.partial(finish, blocks * SLOTS) for blocks in SIZES + (rest // SLOTS,)
        ]
        decay, layer_out, out_k, out_v = lax.switch(choice[0], branches, *operands)
    else:
        decay, layer_out, out_k, out_v = finish(rest, *operands)
    if n_seq != 2:
        out_k, out_v = (
            lax.all_to_all(x, "seq", split_axis=1, concat_axis=1, tiled=True) for x in (out_k, out_v)
        )
    return out_k, out_v, decay.transpose(1, 0, 2), layer_out


def solution(mesh):
    return jax.shard_map(
        shards,
        mesh=mesh,
        in_specs=(
            P("grp", "seq", "head"),
            P("grp", "seq", "head"),
            P("grp", "head", "seq"),
            P("grp", "seq"),
            P("grp", "seq"),
            P("grp"),
            P("grp"),
            P(None, "grp", "head"),
            P("grp", "head"),
            P("head", "seq"),
        ),
        out_specs=(
            P("grp", "seq", "head"),
            P("grp", "seq", "head"),
            P("grp", "head", "seq"),
            P("grp", "seq"),
        ),
        check_vma=False,
    )
```

```python
import functools

import jax
import jax.numpy as jnp
from jax import lax
from jax.experimental import pallas as pl
from jax.experimental.pallas import tpu as pltpu
from jax.sharding import PartitionSpec as P

BLOCK = 64
SLOTS = 32
LANES = 128
BLOCK_LOG = BLOCK.bit_length() - 1
SLOT_LOG = SLOTS.bit_length() - 1
EMPTY_LOG = -10000.0
FIRST = 8
SECOND = 3
SIZES = (8, 10, 12, 13, 14, 15, 16, 17, 19)
LAST = 4
SURE = 2
EAGER = 5
VMEM_LIMIT = 16 * 1024 * 1024


LIGHT = pl.CostEstimate(flops=1, bytes_accessed=1, transcendentals=0)
MERGE = pl.CostEstimate(flops=1 << 36, bytes_accessed=1, transcendentals=0)


def dot(a, b):
    return lax.dot_general(a, b, (((1,), (0,)), ((), ())), preferred_element_type=jnp.float32)


def dot_nt(a, b):
    return lax.dot_general(a, b, (((1,), (1,)), ((), ())), preferred_element_type=jnp.float32)


def iota(shape, dim):
    return lax.broadcasted_iota(jnp.int32, shape, dim)


def three(x):
    hi = x.astype(jnp.bfloat16).astype(jnp.float32)
    rest = x - hi
    mid = rest.astype(jnp.bfloat16).astype(jnp.float32)
    return hi, mid, rest - mid


def split_dot(x, ones):
    rows = x.shape[0]
    parts = dot(jnp.concatenate(three(x), axis=0).astype(jnp.bfloat16), ones)
    return parts[:rows] + parts[rows : 2 * rows] + parts[2 * rows :]


def half_of(axis, count):
    own = lax.axis_index(axis) if count == 2 else jnp.int32(0)
    return own, 1 - own


def by_row(ref, row):
    picked = jnp.zeros_like(row)
    for r in range(ref.shape[0]):
        picked = jnp.where(row == r, ref[r], picked)
    return picked


def live_blocks(lengths, r, start, most):
    return jnp.clip((lengths[r] - start) >> BLOCK_LOG, 0, most)


def offsets(lengths, start, most):
    total = jnp.int32(0)
    ahead, live = [], []
    for r in range(lengths.shape[0]):
        ahead.append(total)
        live.append(live_blocks(lengths, r, start, most))
        total = total + live[-1]
    return ahead, live, total


def mask(condition):
    return condition.astype(jnp.float32).astype(jnp.bfloat16)


def block_masks(width):
    one, two = iota((width, width), 0), iota((width, width), 1)
    same = (one ^ two) < BLOCK
    return mask(same & (one <= two)), mask(same), mask(same & (one > two))


def plan(keep, weight, start, len_ref, upto, block):
    rows, width = keep.shape
    kept = keep == 1
    rank = dot(keep.astype(jnp.float32).astype(jnp.bfloat16), upto) - 1.0
    weighted = jnp.where(kept, 0.0, weight)
    share = (weighted / split_dot(weighted, block)).astype(jnp.bfloat16).astype(jnp.float32)
    lane, row = iota((rows, width), 1), iota((rows, width), 0)
    slot = jnp.where(kept, rank.astype(jnp.int32), SLOTS - 1) + (lane >> BLOCK_LOG) * SLOTS
    slot = jnp.where(start + lane < by_row(len_ref, row), slot, -1)
    return slot, jnp.where(kept, 1.0, share)


def select(slot, factor, r):
    width = slot.shape[1]
    shape = (width // 2, width)
    hit = iota(shape, 0) == slot[r : r + 1, :]
    return jnp.where(hit, jnp.broadcast_to(factor[r : r + 1, :], shape), 0.0).astype(jnp.bfloat16)


def lanes(half, width):
    return pl.ds(pl.multiple_of(half * width, width), width)


def far(*arrays):
    return [pltpu.with_memory_space_constraint(x, pltpu.HBM) for x in arrays]


def near(*arrays):
    return [pltpu.with_memory_space_constraint(x, pltpu.VMEM) for x in arrays]


def fetch(pairs, sem):
    copies = [pltpu.make_async_copy(src, dst, sem.at[i]) for i, (src, dst) in enumerate(pairs)]
    for copy in copies:
        copy.start()
    return copies


def first_kernel(
    n_seq, len_hbm, route_hbm, keep_hbm, weight_hbm, fresh_hbm, gate_hbm, keys, values, *rest
):
    out, packed, size_ref, lengths, route, keep, weight, fresh, gates, raw, row_buf = rest[:11]
    sem_s, sem_r = rest[11:]
    _, sent = half_of("seq", n_seq)
    req, width = keep.shape
    most = width // BLOCK
    small = fetch(
        [
            (len_hbm, lengths),
            (keep_hbm.at[:, lanes(sent, width)], keep),
            (weight_hbm.at[:, lanes(sent, width)], weight),
            (fresh_hbm, fresh),
            (gate_hbm, gates),
            (route_hbm, route),
        ],
        sem_s,
    )

    channels = keys.shape[2]

    def slab(i, r):
        source = (keys, values)[i].at[r, lanes(sent, width), :]
        target = raw.at[r, :, pl.ds(i * channels, channels)]
        return pltpu.make_async_copy(source, target, sem_r.at[i, r])

    eager = min(EAGER, req)
    for r in range(eager):
        for i in range(2):
            slab(i, r).start()
    row_buf[...] = jnp.zeros_like(row_buf)
    upto, block, _ = block_masks(width)
    for copy in small:
        copy.wait()
    start = lax.axis_index("seq") * (2 * width) + sent * width
    ahead, live, _ = offsets(lengths, start, most)
    needed = [(ahead[r] < FIRST) & (live[r] > 0) for r in range(req)]
    for r in range(eager, req):

        @pl.when(needed[r])
        def _(r=r):
            for i in range(2):
                slab(i, r).start()

    slot, factor = plan(keep[...], weight[...], start, lengths, upto, block)
    _, _, total = offsets(lengths, width, most)
    choice = jnp.int32(0)
    for size in SIZES:
        choice = choice + (total - FIRST - SECOND > size).astype(jnp.int32)
    size_ref[0] = choice

    new, gate = fresh[...].astype(jnp.float32), gates[...].astype(jnp.float32)
    heads = gate.shape[1]
    lane = iota((req, new.shape[1]), 1)
    size = new.shape[1] // heads
    spread = jnp.zeros((req, new.shape[1]), jnp.float32)
    for h in range(heads):
        inside = (lane >= h * size) & (lane < (h + 1) * size)
        spread = jnp.where(inside, gate[:, h : h + 1], spread)
    packed[...] = jnp.concatenate([new, spread], axis=0).astype(jnp.bfloat16)

    def pack(r):
        chosen = select(slot, factor, r)
        at = pl.ds(pl.multiple_of(ahead[r] * SLOTS, SLOTS), most * SLOTS)
        if r >= eager:
            for i in range(2):
                slab(i, r).wait()
        rows = dot(chosen, raw[r]).astype(jnp.bfloat16)
        for i in range(2):
            row_buf[i, at, :] = rows[:, i * channels : (i + 1) * channels]

    for r in range(req):
        if r < eager:
            for i in range(2):
                slab(i, r).wait()
        if r < SURE:
            pack(r)
        else:
            pl.when(needed[r])(functools.partial(pack, r))
    out[...] = row_buf[:, : FIRST * SLOTS, :]


def first_part(n_seq, lengths, route, keep, weight, fresh, gates, keys, values):
    req, pos, width = keys.shape
    half = pos // 2
    hbm = pl.BlockSpec(memory_space=pl.ANY)
    smem = pl.BlockSpec(memory_space=pltpu.SMEM)
    vmem = pl.BlockSpec(memory_space=pltpu.VMEM)
    return pl.pallas_call(
        functools.partial(first_kernel, n_seq),
        out_shape=(
            pltpu.VMEM((2, FIRST * SLOTS, width), jnp.bfloat16),
            pltpu.VMEM((fresh.shape[0] + req, width), jnp.bfloat16),
            jax.ShapeDtypeStruct((1,), jnp.int32),
            pltpu.SMEM(lengths.shape, jnp.int32),
            pltpu.SMEM(route.shape, jnp.int32),
        ),
        in_specs=[hbm] * 8,
        out_specs=(vmem, vmem, smem, smem, smem),
        scratch_shapes=[
            pltpu.VMEM((req, half), jnp.int32),
            pltpu.VMEM((req, half), jnp.float32),
            pltpu.VMEM(fresh.shape, fresh.dtype),
            pltpu.VMEM(gates.shape, gates.dtype),
            pltpu.VMEM((req, half, 2 * width), jnp.bfloat16),
            pltpu.VMEM((2, (FIRST - 1) * SLOTS + half // 2, width), jnp.bfloat16),
            pltpu.SemaphoreType.DMA((6,)),
            pltpu.SemaphoreType.DMA((2, req)),
        ],
        compiler_params=pltpu.CompilerParams(vmem_limit_bytes=VMEM_LIMIT),
        cost_estimate=LIGHT,
        name="compact_first_sent",
    )(*far(lengths, route, keep, weight, fresh, gates, keys, values))


def own_kernel(
    n_seq, lengths, keep, weight, gates, keys, values, early, *rest
):
    out_k, out_v, chunk, second, rows, log_ref, level_ref, total_ref = rest[:8]
    raw, late, forget, zeros, sem_l, sem_r, sem_o, sem_z = rest[8:]
    own, sent = half_of("seq", n_seq)
    seq = lax.axis_index("seq")
    heads, req, pos = gates.shape
    half = pos // 2
    slots = half // 2
    most = half // BLOCK
    first = FIRST // most
    pad = forget.shape[1] // req
    both = ((0, keys), (1, values))
    channels = keys.shape[2]

    def part(i):
        return pl.ds(i * channels, channels)

    late_slabs = fetch(
        [
            (source.at[r, lanes(sent, half), :], late.at[r - first, :, part(i)])
            for r in range(first, req)
            for i, source in both
        ],
        sem_l,
    )
    slabs = fetch(
        [
            (source.at[r, lanes(own, half), :], raw.at[r, :, part(i)])
            for r in range(req)
            for i, source in both
        ],
        sem_r,
    )
    zeros[...] = jnp.zeros_like(zeros)
    stores = fetch([(zeros, out.at[:, lanes(sent, slots), :]) for out in (out_k, out_v)], sem_z)
    chunk[:, : FIRST * SLOTS, :] = early[...]
    chunk[:, FIRST * SLOTS :, :] = jnp.zeros(
        (2, chunk.shape[1] - FIRST * SLOTS, chunk.shape[2]), chunk.dtype
    )
    upto, block, after = block_masks(half)
    ahead, alive, _ = offsets(lengths, seq * pos + sent * half, most)

    forget[...] = jnp.zeros_like(forget)
    live = seq * pos + iota((req, pos), 1) < by_row(lengths, iota((req, pos), 0))
    for h in range(heads):
        gate = jnp.where(live, gates[h], 0.0)
        for c in range(pos // LANES):
            forget[c, pl.ds(h, req, stride=pad), :] = gate[:, c * LANES : (c + 1) * LANES]
    flat = jnp.concatenate([forget[c] for c in range(pos // LANES)], axis=1)
    total_ref[...] = jnp.broadcast_to(jnp.sum(flat, axis=1, keepdims=True), total_ref.shape)
    ends = iota((pos, slots), 1) >> SLOT_LOG
    begins = iota((pos, slots), 0) >> BLOCK_LOG
    last = iota((req * pad, slots), 1) & (SLOTS - 1) == SLOTS - 1

    for i, h in enumerate((own, sent)):
        slot, factor = plan(
            keep[:, lanes(h, half)],
            weight[:, lanes(h, half)],
            seq * pos + h * half,
            lengths,
            upto,
            block,
        )
        near = half // LANES
        inner = split_dot(
            jnp.concatenate([forget[h * near + c] for c in range(near)], axis=1), after
        )
        beyond = split_dot(
            flat, (begins > ends + h * (half // BLOCK)).astype(jnp.float32).astype(jnp.bfloat16)
        )
        spread = jnp.exp(inner)
        high = spread.astype(jnp.bfloat16).astype(jnp.float32)
        planes = three(inner) + (high, spread - high, jnp.ones_like(inner))
        found = []
        for r in range(req):
            chosen = select(slot, factor, r)
            stack = jnp.concatenate([x[r * pad : (r + 1) * pad] for x in planes], axis=0)
            found.append(dot_nt(stack.astype(jnp.bfloat16), chosen))
            if i == 0:
                for k in range(2):
                    slabs[2 * r + k].wait()
                made = dot(chosen, raw[r]).astype(jnp.bfloat16)
                for k, out in enumerate((out_k, out_v)):
                    rows[k, r] = made[:, k * channels : (k + 1) * channels]
                    stores.append(
                        pltpu.make_async_copy(
                            rows.at[k, r], out.at[r, lanes(own, slots), :], sem_o.at[2 * r + k]
                        )
                    )
                    stores[-1].start()
            elif r >= first:
                for k in range(2):
                    late_slabs[2 * (r - first) + k].wait()

                @pl.when((ahead[r] + alive[r] > FIRST) & (alive[r] > 0))
                def _(r=r, chosen=chosen):
                    at = pl.ds(pl.multiple_of(ahead[r] * SLOTS, SLOTS), slots)
                    made = dot(chosen, late[r - first]).astype(jnp.bfloat16)
                    for k in range(2):
                        chunk[k, at, :] = made[:, k * channels : (k + 1) * channels]
        at = [
            jnp.concatenate([x[p * pad : (p + 1) * pad] for x in found], axis=0) for p in range(6)
        ]
        filled = at[5] > 0.5
        kept = at[0] + at[1] + at[2]
        merged = jnp.log(jnp.where(filled, at[3] + at[4], 1.0))
        level_ref[i] = jnp.where(filled, jnp.where(last, merged, kept) + beyond, EMPTY_LOG)
        for k in range(heads):
            log_ref[k, :, lanes(h, slots)] = level_ref[i, pl.ds(k, req, stride=pad), :]
    second[...] = chunk[:, FIRST * SLOTS : (FIRST + SECOND) * SLOTS, :]
    for copy in stores:
        copy.wait()


def own_part(n_seq, lengths, keep, weight, forget, keys, values, early):
    req, pos, width = keys.shape
    heads = forget.shape[0]
    half, slots, pad = pos // 2, pos // 4, -(-heads // 8) * 8
    late = req - FIRST // (half // BLOCK)
    hbm = pl.BlockSpec(memory_space=pl.ANY)
    vmem = pl.BlockSpec(memory_space=pltpu.VMEM)
    whole = pltpu.HBM((req, 2 * slots, width), jnp.bfloat16)
    return pl.pallas_call(
        functools.partial(own_kernel, n_seq),
        out_shape=(
            whole,
            whole,
            pltpu.VMEM((2, req * slots, width), jnp.bfloat16),
            pltpu.VMEM((2, SECOND * SLOTS, width), jnp.bfloat16),
            pltpu.VMEM((2, req, slots, width), jnp.bfloat16),
            pltpu.VMEM((heads, req, 2 * slots), jnp.float32),
            pltpu.VMEM((2, req * pad, slots), jnp.float32),
            pltpu.VMEM((req * pad, LANES), jnp.float32),
        ),
        in_specs=[pl.BlockSpec(memory_space=pltpu.SMEM)] + [vmem] * 3 + [hbm] * 2 + [vmem],
        out_specs=(hbm, hbm, vmem, vmem, vmem, vmem, vmem, vmem),
        scratch_shapes=[
            pltpu.VMEM((req, half, 2 * width), jnp.bfloat16),
            pltpu.VMEM((late, half, 2 * width), jnp.bfloat16),
            pltpu.VMEM((pos // LANES, req * pad, LANES), jnp.float32),
            pltpu.VMEM((req, slots, width), jnp.bfloat16),
            pltpu.SemaphoreType.DMA((2 * late,)),
            pltpu.SemaphoreType.DMA((2 * req,)),
            pltpu.SemaphoreType.DMA((2 * req,)),
            pltpu.SemaphoreType.DMA((2,)),
        ],
        compiler_params=pltpu.CompilerParams(vmem_limit_bytes=VMEM_LIMIT),
        cost_estimate=LIGHT,
        name="compact_own",
    )(lengths, *near(keep, weight, forget), *far(keys, values), *near(early))


def attend_kernel(n_seq, n_grp, heads, *refs):
    lengths, route, own_rows, late, level, total = refs[:6]
    tokens, rest = refs[6 : 6 + n_grp], refs[6 + n_grp :]
    stats_ref, picked_ref, scores = rest
    _, sent = half_of("seq", n_seq)
    kinds, width = picked_ref.shape
    req = kinds // 4
    size = width // heads
    slots = own_rows.shape[2]
    pad = total.shape[0] // req
    start = lax.axis_index("seq") * (4 * slots) + sent * (2 * slots)
    ahead, _, _ = offsets(lengths, start, slots // SLOTS)

    def sent_part(i, r):
        at = pl.multiple_of(ahead[r] * SLOTS, SLOTS)
        return late[i, pl.ds(at, slots), :]

    shape = (kinds, kinds)
    to, frm = iota(shape, 0), iota(shape, 1)
    wanted = by_row(route, to % req)
    me = lax.axis_index("grp")
    picked = jnp.zeros((kinds, width), jnp.float32)
    for k in range(n_grp):
        source = lax.rem(me + n_grp - k, n_grp)
        hit = (to // req == frm // req) & (wanted == source * req + frm % req)
        picked = picked + dot(hit.astype(jnp.float32).astype(jnp.bfloat16), tokens[k][...])
    picked_ref[...] = picked

    lane, row = iota((pad, width), 1), iota((pad, width), 0)
    mine = (lane >= row * size) & (lane < (row + 1) * size)
    for r in range(req):
        query = jnp.where(mine, picked[r : r + 1, :], 0.0).astype(jnp.bfloat16)
        here = slice(r * pad, (r + 1) * pad)
        scores[here, :slots] = dot_nt(query, own_rows[0, r])
        scores[here, slots:] = dot_nt(query, sent_part(0, r))
    logit = scores[...] * (size**-0.5) + jnp.concatenate([level[0], level[1]], axis=1)
    top = jnp.max(logit, axis=1, keepdims=True)
    weights = jnp.exp(logit - top).astype(jnp.bfloat16).astype(jnp.float32)
    mass = jnp.sum(weights, axis=1, keepdims=True)

    def spread_out(column, r):
        return jnp.sum(
            jnp.where(mine, column[r * pad : (r + 1) * pad], 0.0), axis=0, keepdims=True
        )

    for r in range(req):
        w = weights[r * pad : (r + 1) * pad].astype(jnp.bfloat16)
        acc = dot(w[:, :slots], own_rows[1, r]) + dot(w[:, slots:], sent_part(1, r))
        acc = jnp.sum(jnp.where(mine, acc, 0.0), axis=0, keepdims=True)
        for p, x in enumerate((top, mass, total[:, :1])):
            stats_ref[p * req + r : p * req + r + 1, :] = spread_out(x, r)
        stats_ref[3 * req + r : 3 * req + r + 1, :] = acc


def attend_part(n_seq, n_grp, heads, lengths, route, own_rows, late, level, total, tokens):
    _, req, slots, width = own_rows.shape
    vmem = pl.BlockSpec(memory_space=pltpu.VMEM)
    small = pltpu.VMEM((4 * req, width), jnp.float32)
    return pl.pallas_call(
        functools.partial(attend_kernel, n_seq, n_grp, heads),
        out_shape=(small, small),
        in_specs=[pl.BlockSpec(memory_space=pltpu.SMEM)] * 2 + [vmem] * (4 + n_grp),
        out_specs=(vmem, vmem),
        scratch_shapes=[
            pltpu.VMEM((total.shape[0], 2 * slots), jnp.float32),
        ],
        compiler_params=pltpu.CompilerParams(vmem_limit_bytes=VMEM_LIMIT),
        cost_estimate=LIGHT,
        name="attend",
    )(lengths, route, *near(own_rows, late, level, total), *near(*tokens))


def merge_kernel(count, relative, size, *refs):
    stats, refs = refs[:count], refs[count:]
    picked_ref, weight_ref, _, later_ref, out_ref = refs
    req, width = later_ref.shape
    seq = lax.axis_index("seq")
    places = [lax.rem(seq + count - k, count) if relative else jnp.int32(k) for k in range(count)]
    tops, masses, totals, accs = [
        [ref[p * req : (p + 1) * req, :] for ref in stats] for p in range(4)
    ]

    def later(place):
        total = jnp.zeros_like(totals[0])
        for k in range(count):
            total = total + jnp.where(places[k] > place, totals[k], 0.0)
        return total

    tops = [tops[k] + later(places[k]) for k in range(count)]
    top = functools.reduce(jnp.maximum, tops)
    scales = [jnp.exp(t - top) for t in tops]
    mass = sum(s * x for s, x in zip(scales, masses))
    acc = sum(s * x for s, x in zip(scales, accs))
    query, key, value, gate = [picked_ref[p * req : (p + 1) * req, :] for p in range(4)]
    one, two = iota((width, width), 0), iota((width, width), 1)
    same = (one // size == two // size).astype(jnp.float32).astype(jnp.bfloat16)
    own = split_dot(query * key, same) * (size**-0.5)
    past = top + gate
    joint = jnp.maximum(past, own)
    scale, self_weight = jnp.exp(past - joint), jnp.exp(own - joint)
    attended = (scale * acc + self_weight * value) / (scale * mass + self_weight)
    later_ref[...] = later(seq)
    out_ref[...] = dot(attended.astype(jnp.bfloat16), weight_ref[...])


def merge_part(stats, relative, picked, out_weight, second, size):
    req, width = stats[0].shape[0] // 4, stats[0].shape[1]
    vmem = pl.BlockSpec(memory_space=pltpu.VMEM)
    return pl.pallas_call(
        functools.partial(merge_kernel, len(stats), relative, size),
        out_shape=(
            pltpu.VMEM((req, width), jnp.float32),
            pltpu.VMEM((req, out_weight.shape[1]), jnp.float32),
        ),
        in_specs=[vmem] * (len(stats) + 2) + [pl.BlockSpec(memory_space=pl.ANY)],
        out_specs=(vmem, vmem),
        compiler_params=pltpu.CompilerParams(vmem_limit_bytes=VMEM_LIMIT),
        cost_estimate=MERGE,
        name="merge_and_project",
    )(*near(*stats, picked, out_weight), second)


def sum_kernel(count, size, *refs):
    parts, (later_ref, log_ref, _, out, decay_ref) = refs[:count], refs[count:]
    me = lax.axis_index("head")
    total = jnp.zeros(out.shape, jnp.float32)
    for place in range(count):
        for k in range(count):
            total = total + jnp.where(lax.rem(me + count - k, count) == place, parts[k][...], 0.0)
    out[...] = total.astype(out.dtype)
    for h in range(log_ref.shape[0]):
        decay_ref[h] = jnp.exp(log_ref[h] + later_ref[:, h * size : h * size + 1])


def sum_part(parts, later, logs, placed, size):
    vmem = pl.BlockSpec(memory_space=pltpu.VMEM)
    return pl.pallas_call(
        functools.partial(sum_kernel, len(parts), size),
        out_shape=(
            pltpu.HBM(parts[0].shape, jnp.bfloat16),
            pltpu.HBM(logs.shape, jnp.float32),
        ),
        in_specs=[vmem] * (len(parts) + 3),
        out_specs=(vmem, vmem),
        compiler_params=pltpu.CompilerParams(vmem_limit_bytes=VMEM_LIMIT),
        cost_estimate=LIGHT,
        name="sum_heads_and_decay",
    )(*parts, later, logs, placed)


def place_kernel(n_seq, first, count, marked, *refs):
    parts, refs = refs[:count], refs[count:]
    lengths, _, _, out_k, out_v, *placed_ref, sem = refs
    _, sent = half_of("seq", n_seq)
    if marked:
        placed_ref[0][...] = jnp.zeros_like(placed_ref[0])
    req, rows, _ = out_k.shape
    slots = rows // 2
    most = slots // SLOTS
    seq = lax.axis_index("seq")
    if n_seq == 2:
        start = (1 - seq) * (4 * slots) + seq * (2 * slots)
    else:
        start = seq * (4 * slots) + sent * (2 * slots)
    ahead, live, _ = offsets(lengths, start, most)
    for phase in ("start", "wait"):
        begin = first
        for p, part in enumerate(parts):
            held = part.shape[1] // SLOTS
            for r in range(req):
                if begin >= (r + 1) * most:
                    continue
                low = jnp.clip(begin - ahead[r], 0, live[r])
                high = jnp.clip(begin + held - ahead[r], 0, live[r])
                size = pl.multiple_of((high - low) * SLOTS, SLOTS)

                @pl.when(high > low)
                def _(p=p, part=part, begin=begin, r=r, low=low, size=size):
                    src = pl.multiple_of((ahead[r] + low - begin) * SLOTS, SLOTS)
                    dst = pl.multiple_of(sent * slots + low * SLOTS, SLOTS)
                    for i, out in enumerate((out_k, out_v)):
                        copy = pltpu.make_async_copy(
                            part.at[i, pl.ds(src, size), :],
                            out.at[r, pl.ds(dst, size), :],
                            sem.at[p, i, r],
                        )
                        getattr(copy, phase)()

            begin += held


def place_part(n_seq, first, parts, lengths, out_k, out_v, marked=False):
    hbm = pl.BlockSpec(memory_space=pl.ANY)
    smem = pl.BlockSpec(memory_space=pltpu.SMEM)
    vmem = pl.BlockSpec(memory_space=pltpu.VMEM)
    shape = pltpu.HBM(out_k.shape, out_k.dtype)
    count = len(parts)
    return pl.pallas_call(
        functools.partial(place_kernel, n_seq, first, count, marked),
        out_shape=(shape, shape) + (pltpu.VMEM((8, LANES), jnp.float32),) * marked,
        in_specs=[vmem] * count + [smem, hbm, hbm],
        out_specs=(hbm, hbm) + (vmem,) * marked,
        scratch_shapes=[
            pltpu.SemaphoreType.DMA((count, 2, lengths.shape[0])),
        ],
        input_output_aliases={count + 1: 0, count + 2: 1},
        compiler_params=pltpu.CompilerParams(vmem_limit_bytes=VMEM_LIMIT),
        cost_estimate=LIGHT,
        name="place_received",
    )(*near(*parts), lengths, *far(out_k, out_v))


def others(value, axis):
    count = lax.axis_size(axis)
    return [value] + [
        lax.ppermute(value, axis, [(i, (i + k) % count) for i in range(count)])
        for k in range(1, count)
    ]


def swap(value, n_seq):
    return lax.ppermute(value, "seq", [(0, 1), (1, 0)]) if n_seq == 2 else value


def shards(
    keys, values, log_forget, keep, merge_weight, lengths, route, fresh, new_forget, out_weight
):
    req, pos, width = keys.shape
    heads = log_forget.shape[1]
    size = width // heads
    n_seq, n_grp = lax.axis_size("seq"), lax.axis_size("grp")
    early, packed, choice, held_lengths, held_route = first_part(
        n_seq,
        lengths,
        route,
        keep,
        merge_weight,
        fresh.reshape(3 * req, width),
        new_forget,
        keys,
        values,
    )
    exchange = functools.partial(swap, n_seq=n_seq)
    first_received = exchange(early)
    tokens = others(packed, "grp")
    out_k, out_v, late, next_rows, own_rows, logs, level, total = own_part(
        n_seq,
        held_lengths,
        keep,
        merge_weight,
        log_forget.transpose(1, 0, 2),
        keys,
        values,
        early,
    )
    end = (FIRST + SECOND) * SLOTS
    rest = late.shape[1] - end

    def finish(rows, early, next_rows, late, own_rows, logs, level, total, tokens, *others_in):
        out_weight, lengths, route, out_k, out_v = others_in
        second = exchange(next_rows)
        stats, picked = attend_part(
            n_seq, n_grp, heads, lengths, route, own_rows, late, level, total, tokens
        )
        if n_seq == 2:
            all_stats = others(stats, "seq")
        else:
            gathered = lax.all_gather(stats, "seq")
            all_stats = [gathered[i] for i in range(n_seq)]
        ends = [end, end + rows]
        if rows > 3 * LAST * SLOTS:
            ends.insert(1, end + rows - LAST * SLOTS)
        third = [exchange(late[:, low:high]) for low, high in zip(ends, ends[1:])]
        later, partial = merge_part(all_stats, n_seq == 2, picked, out_weight, second, size)
        out_k, out_v, placed = place_part(
            n_seq, 0, (early, second), lengths, out_k, out_v, marked=True
        )
        layer_out, decay = sum_part(others(partial, "head"), later, logs, placed, size)
        for low, part in zip(ends, third):
            out_k, out_v = place_part(n_seq, low // SLOTS, (part,), lengths, out_k, out_v)
        return decay, layer_out, out_k, out_v

    operands = (first_received, next_rows, late, own_rows, logs, level, total, tokens)
    operands += (out_weight, held_lengths, held_route, out_k, out_v)
    if n_seq == 2:
        branches = [
            functools.partial(finish, blocks * SLOTS) for blocks in SIZES + (rest // SLOTS,)
        ]
        decay, layer_out, out_k, out_v = lax.switch(choice[0], branches, *operands)
    else:
        decay, layer_out, out_k, out_v = finish(rest, *operands)
    if n_seq != 2:
        out_k, out_v = (
            lax.all_to_all(x, "seq", split_axis=1, concat_axis=1, tiled=True) for x in (out_k, out_v)
        )
    return out_k, out_v, decay.transpose(1, 0, 2), layer_out


def solution(mesh):
    return jax.shard_map(
        shards,
        mesh=mesh,
        in_specs=(
            P("grp", "seq", "head"),
            P("grp", "seq", "head"),
            P("grp", "head", "seq"),
            P("grp", "seq"),
            P("grp", "seq"),
            P("grp"),
            P("grp"),
            P(None, "grp", "head"),
            P("grp", "head"),
            P("head", "seq"),
        ),
        out_specs=(
            P("grp", "seq", "head"),
            P("grp", "seq", "head"),
            P("grp", "head", "seq"),
            P("grp", "seq"),
        ),
        check_vma=False,
    )
```

```python
import functools

import jax
import jax.numpy as jnp
from jax import lax
from jax.experimental import pallas as pl
from jax.experimental.pallas import tpu as pltpu
from jax.sharding import PartitionSpec as P

BLOCK = 64
SLOTS = 32
LANES = 128
BLOCK_LOG = BLOCK.bit_length() - 1
SLOT_LOG = SLOTS.bit_length() - 1
EMPTY_LOG = -10000.0
FIRST = 8
SECOND = 3
SIZES = (7, 9, 11, 13, 14, 15, 17, 19)
LAST = 4
SURE = 2
EAGER = 4
VMEM_LIMIT = 16 * 1024 * 1024


LIGHT = pl.CostEstimate(flops=1, bytes_accessed=1, transcendentals=0)
MERGE = pl.CostEstimate(flops=1 << 36, bytes_accessed=1, transcendentals=0)


def dot(a, b):
    return lax.dot_general(a, b, (((1,), (0,)), ((), ())), preferred_element_type=jnp.float32)


def dot_nt(a, b):
    return lax.dot_general(a, b, (((1,), (1,)), ((), ())), preferred_element_type=jnp.float32)


def iota(shape, dim):
    return lax.broadcasted_iota(jnp.int32, shape, dim)


def three(x):
    hi = x.astype(jnp.bfloat16).astype(jnp.float32)
    rest = x - hi
    mid = rest.astype(jnp.bfloat16).astype(jnp.float32)
    return hi, mid, rest - mid


def split_dot(x, ones):
    rows = x.shape[0]
    parts = dot(jnp.concatenate(three(x), axis=0).astype(jnp.bfloat16), ones)
    return parts[:rows] + parts[rows : 2 * rows] + parts[2 * rows :]


def half_of(axis, count):
    own = lax.axis_index(axis) if count == 2 else jnp.int32(0)
    return own, 1 - own


def by_row(ref, row):
    picked = jnp.zeros_like(row)
    for r in range(ref.shape[0]):
        picked = jnp.where(row == r, ref[r], picked)
    return picked


def live_blocks(lengths, r, start, most):
    return jnp.clip((lengths[r] - start) >> BLOCK_LOG, 0, most)


def offsets(lengths, start, most):
    total = jnp.int32(0)
    ahead, live = [], []
    for r in range(lengths.shape[0]):
        ahead.append(total)
        live.append(live_blocks(lengths, r, start, most))
        total = total + live[-1]
    return ahead, live, total


def mask(condition):
    return condition.astype(jnp.float32).astype(jnp.bfloat16)


def block_masks(width):
    one, two = iota((width, width), 0), iota((width, width), 1)
    same = (one ^ two) < BLOCK
    return mask(same & (one <= two)), mask(same), mask(same & (one > two))


def plan(keep, weight, start, len_ref, upto, block):
    rows, width = keep.shape
    kept = keep == 1
    rank = dot(keep.astype(jnp.float32).astype(jnp.bfloat16), upto) - 1.0
    weighted = jnp.where(kept, 0.0, weight)
    share = (weighted / split_dot(weighted, block)).astype(jnp.bfloat16).astype(jnp.float32)
    lane, row = iota((rows, width), 1), iota((rows, width), 0)
    slot = jnp.where(kept, rank.astype(jnp.int32), SLOTS - 1) + (lane >> BLOCK_LOG) * SLOTS
    slot = jnp.where(start + lane < by_row(len_ref, row), slot, -1)
    return slot, jnp.where(kept, 1.0, share)


def select(slot, factor, r):
    width = slot.shape[1]
    shape = (width // 2, width)
    hit = iota(shape, 0) == slot[r : r + 1, :]
    return jnp.where(hit, jnp.broadcast_to(factor[r : r + 1, :], shape), 0.0).astype(jnp.bfloat16)


def lanes(half, width):
    return pl.ds(pl.multiple_of(half * width, width), width)


def far(*arrays):
    return [pltpu.with_memory_space_constraint(x, pltpu.HBM) for x in arrays]


def near(*arrays):
    return [pltpu.with_memory_space_constraint(x, pltpu.VMEM) for x in arrays]


def fetch(pairs, sem):
    copies = [pltpu.make_async_copy(src, dst, sem.at[i]) for i, (src, dst) in enumerate(pairs)]
    for copy in copies:
        copy.start()
    return copies


def first_kernel(
    n_seq, len_hbm, route_hbm, keep_hbm, weight_hbm, fresh_hbm, gate_hbm, keys, values, *rest
):
    out, packed, size_ref, lengths, route, keep, weight, fresh, gates, raw, row_buf = rest[:11]
    sem_s, sem_t, sem_r = rest[11:]
    _, sent = half_of("seq", n_seq)
    req, width = keep.shape
    most = width // BLOCK
    small = fetch(
        [
            (len_hbm, lengths),
            (keep_hbm.at[:, lanes(sent, width)], keep),
            (weight_hbm.at[:, lanes(sent, width)], weight),
        ],
        sem_s,
    )

    channels = keys.shape[2]

    def slab(i, r):
        source = (keys, values)[i].at[r, lanes(sent, width), :]
        target = raw.at[r, :, pl.ds(i * channels, channels)]
        return pltpu.make_async_copy(source, target, sem_r.at[i, r])

    eager = min(EAGER, req)
    for r in range(eager):
        for i in range(2):
            slab(i, r).start()
    tokens = fetch([(fresh_hbm, fresh), (gate_hbm, gates), (route_hbm, route)], sem_t)
    row_buf[...] = jnp.zeros_like(row_buf)
    upto, block, _ = block_masks(width)
    for copy in small:
        copy.wait()
    start = lax.axis_index("seq") * (2 * width) + sent * width
    ahead, live, _ = offsets(lengths, start, most)
    needed = [(ahead[r] < FIRST) & (live[r] > 0) for r in range(req)]
    for r in range(eager, req):

        @pl.when(needed[r])
        def _(r=r):
            for i in range(2):
                slab(i, r).start()

    slot, factor = plan(keep[...], weight[...], start, lengths, upto, block)
    _, _, total = offsets(lengths, width, most)
    choice = jnp.int32(0)
    for size in SIZES:
        choice = choice + (total - FIRST - SECOND > size).astype(jnp.int32)
    size_ref[0] = choice

    def pack(r):
        chosen = select(slot, factor, r)
        at = pl.ds(pl.multiple_of(ahead[r] * SLOTS, SLOTS), most * SLOTS)
        if r >= eager:
            for i in range(2):
                slab(i, r).wait()
        rows = dot(chosen, raw[r]).astype(jnp.bfloat16)
        for i in range(2):
            row_buf[i, at, :] = rows[:, i * channels : (i + 1) * channels]

    for r in range(req):
        if r < eager:
            for i in range(2):
                slab(i, r).wait()
        if r < SURE:
            pack(r)
        else:
            pl.when(needed[r])(functools.partial(pack, r))

    for copy in tokens:
        copy.wait()
    new, gate = fresh[...].astype(jnp.float32), gates[...].astype(jnp.float32)
    heads = gate.shape[1]
    lane = iota((req, new.shape[1]), 1)
    size = new.shape[1] // heads
    spread = jnp.zeros((req, new.shape[1]), jnp.float32)
    for h in range(heads):
        inside = (lane >= h * size) & (lane < (h + 1) * size)
        spread = jnp.where(inside, gate[:, h : h + 1], spread)
    packed[...] = jnp.concatenate([new, spread], axis=0).astype(jnp.bfloat16)

    out[...] = row_buf[:, : FIRST * SLOTS, :]


def first_part(n_seq, lengths, route, keep, weight, fresh, gates, keys, values):
    req, pos, width = keys.shape
    half = pos // 2
    hbm = pl.BlockSpec(memory_space=pl.ANY)
    smem = pl.BlockSpec(memory_space=pltpu.SMEM)
    vmem = pl.BlockSpec(memory_space=pltpu.VMEM)
    return pl.pallas_call(
        functools.partial(first_kernel, n_seq),
        out_shape=(
            pltpu.VMEM((2, FIRST * SLOTS, width), jnp.bfloat16),
            pltpu.VMEM((fresh.shape[0] + req, width), jnp.bfloat16),
            jax.ShapeDtypeStruct((1,), jnp.int32),
            pltpu.SMEM(lengths.shape, jnp.int32),
            pltpu.SMEM(route.shape, jnp.int32),
        ),
        in_specs=[hbm] * 8,
        out_specs=(vmem, vmem, smem, smem, smem),
        scratch_shapes=[
            pltpu.VMEM((req, half), jnp.int32),
            pltpu.VMEM((req, half), jnp.float32),
            pltpu.VMEM(fresh.shape, fresh.dtype),
            pltpu.VMEM(gates.shape, gates.dtype),
            pltpu.VMEM((req, half, 2 * width), jnp.bfloat16),
            pltpu.VMEM((2, (FIRST - 1) * SLOTS + half // 2, width), jnp.bfloat16),
            pltpu.SemaphoreType.DMA((3,)),
            pltpu.SemaphoreType.DMA((3,)),
            pltpu.SemaphoreType.DMA((2, req)),
        ],
        compiler_params=pltpu.CompilerParams(vmem_limit_bytes=VMEM_LIMIT),
        cost_estimate=LIGHT,
        name="compact_first_sent",
    )(*far(lengths, route, keep, weight, fresh, gates, keys, values))


def own_kernel(
    n_seq, lengths, keep, weight, gates, keys, values, early, *rest
):
    out_k, out_v, chunk, second, rows, log_ref, level_ref, total_ref = rest[:8]
    raw, late, forget, zeros, sem_l, sem_r, sem_o, sem_z = rest[8:]
    own, sent = half_of("seq", n_seq)
    seq = lax.axis_index("seq")
    heads, req, pos = gates.shape
    half = pos // 2
    slots = half // 2
    most = half // BLOCK
    first = FIRST // most
    pad = forget.shape[1] // req
    both = ((0, keys), (1, values))
    channels = keys.shape[2]

    def part(i):
        return pl.ds(i * channels, channels)

    late_slabs = fetch(
        [
            (source.at[r, lanes(sent, half), :], late.at[r - first, :, part(i)])
            for r in range(first, req)
            for i, source in both
        ],
        sem_l,
    )
    slabs = fetch(
        [
            (source.at[r, lanes(own, half), :], raw.at[r, :, part(i)])
            for r in range(req)
            for i, source in both
        ],
        sem_r,
    )
    zeros[...] = jnp.zeros_like(zeros)
    stores = fetch([(zeros, out.at[:, lanes(sent, slots), :]) for out in (out_k, out_v)], sem_z)
    chunk[:, : FIRST * SLOTS, :] = early[...]
    chunk[:, FIRST * SLOTS :, :] = jnp.zeros(
        (2, chunk.shape[1] - FIRST * SLOTS, chunk.shape[2]), chunk.dtype
    )
    upto, block, after = block_masks(half)
    ahead, alive, _ = offsets(lengths, seq * pos + sent * half, most)

    forget[...] = jnp.zeros_like(forget)
    live = seq * pos + iota((req, pos), 1) < by_row(lengths, iota((req, pos), 0))
    for h in range(heads):
        gate = jnp.where(live, gates[h], 0.0)
        for c in range(pos // LANES):
            forget[c, pl.ds(h, req, stride=pad), :] = gate[:, c * LANES : (c + 1) * LANES]
    flat = jnp.concatenate([forget[c] for c in range(pos // LANES)], axis=1)
    total_ref[...] = jnp.broadcast_to(jnp.sum(flat, axis=1, keepdims=True), total_ref.shape)
    ends = iota((pos, slots), 1) >> SLOT_LOG
    begins = iota((pos, slots), 0) >> BLOCK_LOG
    last = iota((req * pad, slots), 1) & (SLOTS - 1) == SLOTS - 1

    for i, h in enumerate((own, sent)):
        slot, factor = plan(
            keep[:, lanes(h, half)],
            weight[:, lanes(h, half)],
            seq * pos + h * half,
            lengths,
            upto,
            block,
        )
        near = half // LANES
        inner = split_dot(
            jnp.concatenate([forget[h * near + c] for c in range(near)], axis=1), after
        )
        beyond = split_dot(
            flat, (begins > ends + h * (half // BLOCK)).astype(jnp.float32).astype(jnp.bfloat16)
        )
        spread = jnp.exp(inner)
        high = spread.astype(jnp.bfloat16).astype(jnp.float32)
        planes = three(inner) + (high, spread - high, jnp.ones_like(inner))
        found = []
        for r in range(req):
            chosen = select(slot, factor, r)
            stack = jnp.concatenate([x[r * pad : (r + 1) * pad] for x in planes], axis=0)
            found.append(dot_nt(stack.astype(jnp.bfloat16), chosen))
            if i == 0:
                for k in range(2):
                    slabs[2 * r + k].wait()
                made = dot(chosen, raw[r]).astype(jnp.bfloat16)
                for k, out in enumerate((out_k, out_v)):
                    rows[k, r] = made[:, k * channels : (k + 1) * channels]
                    stores.append(
                        pltpu.make_async_copy(
                            rows.at[k, r], out.at[r, lanes(own, slots), :], sem_o.at[2 * r + k]
                        )
                    )
                    stores[-1].start()
            elif r >= first:
                for k in range(2):
                    late_slabs[2 * (r - first) + k].wait()

                @pl.when((ahead[r] + alive[r] > FIRST) & (alive[r] > 0))
                def _(r=r, chosen=chosen):
                    at = pl.ds(pl.multiple_of(ahead[r] * SLOTS, SLOTS), slots)
                    made = dot(chosen, late[r - first]).astype(jnp.bfloat16)
                    for k in range(2):
                        chunk[k, at, :] = made[:, k * channels : (k + 1) * channels]
        at = [
            jnp.concatenate([x[p * pad : (p + 1) * pad] for x in found], axis=0) for p in range(6)
        ]
        filled = at[5] > 0.5
        kept = at[0] + at[1] + at[2]
        merged = jnp.log(jnp.where(filled, at[3] + at[4], 1.0))
        level_ref[i] = jnp.where(filled, jnp.where(last, merged, kept) + beyond, EMPTY_LOG)
        for k in range(heads):
            log_ref[k, :, lanes(h, slots)] = level_ref[i, pl.ds(k, req, stride=pad), :]
    second[...] = chunk[:, FIRST * SLOTS : (FIRST + SECOND) * SLOTS, :]
    for copy in stores:
        copy.wait()


def own_part(n_seq, lengths, keep, weight, forget, keys, values, early):
    req, pos, width = keys.shape
    heads = forget.shape[0]
    half, slots, pad = pos // 2, pos // 4, -(-heads // 8) * 8
    late = req - FIRST // (half // BLOCK)
    hbm = pl.BlockSpec(memory_space=pl.ANY)
    vmem = pl.BlockSpec(memory_space=pltpu.VMEM)
    whole = pltpu.HBM((req, 2 * slots, width), jnp.bfloat16)
    return pl.pallas_call(
        functools.partial(own_kernel, n_seq),
        out_shape=(
            whole,
            whole,
            pltpu.VMEM((2, req * slots, width), jnp.bfloat16),
            pltpu.VMEM((2, SECOND * SLOTS, width), jnp.bfloat16),
            pltpu.VMEM((2, req, slots, width), jnp.bfloat16),
            pltpu.VMEM((heads, req, 2 * slots), jnp.float32),
            pltpu.VMEM((2, req * pad, slots), jnp.float32),
            pltpu.VMEM((req * pad, LANES), jnp.float32),
        ),
        in_specs=[pl.BlockSpec(memory_space=pltpu.SMEM)] + [vmem] * 3 + [hbm] * 2 + [vmem],
        out_specs=(hbm, hbm, vmem, vmem, vmem, vmem, vmem, vmem),
        scratch_shapes=[
            pltpu.VMEM((req, half, 2 * width), jnp.bfloat16),
            pltpu.VMEM((late, half, 2 * width), jnp.bfloat16),
            pltpu.VMEM((pos // LANES, req * pad, LANES), jnp.float32),
            pltpu.VMEM((req, slots, width), jnp.bfloat16),
            pltpu.SemaphoreType.DMA((2 * late,)),
            pltpu.SemaphoreType.DMA((2 * req,)),
            pltpu.SemaphoreType.DMA((2 * req,)),
            pltpu.SemaphoreType.DMA((2,)),
        ],
        compiler_params=pltpu.CompilerParams(vmem_limit_bytes=VMEM_LIMIT),
        cost_estimate=LIGHT,
        name="compact_own",
    )(lengths, *near(keep, weight, forget), *far(keys, values), *near(early))


def attend_kernel(n_seq, n_grp, heads, *refs):
    lengths, route, own_rows, late, level, total = refs[:6]
    tokens, rest = refs[6 : 6 + n_grp], refs[6 + n_grp :]
    stats_ref, picked_ref, scores = rest
    _, sent = half_of("seq", n_seq)
    kinds, width = picked_ref.shape
    req = kinds // 4
    size = width // heads
    slots = own_rows.shape[2]
    pad = total.shape[0] // req
    start = lax.axis_index("seq") * (4 * slots) + sent * (2 * slots)
    ahead, _, _ = offsets(lengths, start, slots // SLOTS)

    def sent_part(i, r):
        at = pl.multiple_of(ahead[r] * SLOTS, SLOTS)
        return late[i, pl.ds(at, slots), :]

    shape = (kinds, kinds)
    to, frm = iota(shape, 0), iota(shape, 1)
    wanted = by_row(route, to % req)
    me = lax.axis_index("grp")
    picked = jnp.zeros((kinds, width), jnp.float32)
    for k in range(n_grp):
        source = lax.rem(me + n_grp - k, n_grp)
        hit = (to // req == frm // req) & (wanted == source * req + frm % req)
        picked = picked + dot(hit.astype(jnp.float32).astype(jnp.bfloat16), tokens[k][...])
    picked_ref[...] = picked

    lane, row = iota((pad, width), 1), iota((pad, width), 0)
    mine = (lane >= row * size) & (lane < (row + 1) * size)
    for r in range(req):
        query = jnp.where(mine, picked[r : r + 1, :], 0.0).astype(jnp.bfloat16)
        here = slice(r * pad, (r + 1) * pad)
        scores[here, :slots] = dot_nt(query, own_rows[0, r])
        scores[here, slots:] = dot_nt(query, sent_part(0, r))
    logit = scores[...] * (size**-0.5) + jnp.concatenate([level[0], level[1]], axis=1)
    top = jnp.max(logit, axis=1, keepdims=True)
    weights = jnp.exp(logit - top).astype(jnp.bfloat16).astype(jnp.float32)
    mass = jnp.sum(weights, axis=1, keepdims=True)

    def spread_out(column, r):
        return jnp.sum(
            jnp.where(mine, column[r * pad : (r + 1) * pad], 0.0), axis=0, keepdims=True
        )

    for r in range(req):
        w = weights[r * pad : (r + 1) * pad].astype(jnp.bfloat16)
        acc = dot(w[:, :slots], own_rows[1, r]) + dot(w[:, slots:], sent_part(1, r))
        acc = jnp.sum(jnp.where(mine, acc, 0.0), axis=0, keepdims=True)
        for p, x in enumerate((top, mass, total[:, :1])):
            stats_ref[p * req + r : p * req + r + 1, :] = spread_out(x, r)
        stats_ref[3 * req + r : 3 * req + r + 1, :] = acc


def attend_part(n_seq, n_grp, heads, lengths, route, own_rows, late, level, total, tokens):
    _, req, slots, width = own_rows.shape
    vmem = pl.BlockSpec(memory_space=pltpu.VMEM)
    small = pltpu.VMEM((4 * req, width), jnp.float32)
    return pl.pallas_call(
        functools.partial(attend_kernel, n_seq, n_grp, heads),
        out_shape=(small, small),
        in_specs=[pl.BlockSpec(memory_space=pltpu.SMEM)] * 2 + [vmem] * (4 + n_grp),
        out_specs=(vmem, vmem),
        scratch_shapes=[
            pltpu.VMEM((total.shape[0], 2 * slots), jnp.float32),
        ],
        compiler_params=pltpu.CompilerParams(vmem_limit_bytes=VMEM_LIMIT),
        cost_estimate=LIGHT,
        name="attend",
    )(lengths, route, *near(own_rows, late, level, total), *near(*tokens))


def merge_kernel(count, relative, size, *refs):
    stats, refs = refs[:count], refs[count:]
    picked_ref, weight_ref, _, later_ref, out_ref = refs
    req, width = later_ref.shape
    seq = lax.axis_index("seq")
    places = [lax.rem(seq + count - k, count) if relative else jnp.int32(k) for k in range(count)]
    tops, masses, totals, accs = [
        [ref[p * req : (p + 1) * req, :] for ref in stats] for p in range(4)
    ]

    def later(place):
        total = jnp.zeros_like(totals[0])
        for k in range(count):
            total = total + jnp.where(places[k] > place, totals[k], 0.0)
        return total

    tops = [tops[k] + later(places[k]) for k in range(count)]
    top = functools.reduce(jnp.maximum, tops)
    scales = [jnp.exp(t - top) for t in tops]
    mass = sum(s * x for s, x in zip(scales, masses))
    acc = sum(s * x for s, x in zip(scales, accs))
    query, key, value, gate = [picked_ref[p * req : (p + 1) * req, :] for p in range(4)]
    one, two = iota((width, width), 0), iota((width, width), 1)
    same = (one // size == two // size).astype(jnp.float32).astype(jnp.bfloat16)
    own = split_dot(query * key, same) * (size**-0.5)
    past = top + gate
    joint = jnp.maximum(past, own)
    scale, self_weight = jnp.exp(past - joint), jnp.exp(own - joint)
    attended = (scale * acc + self_weight * value) / (scale * mass + self_weight)
    later_ref[...] = later(seq)
    out_ref[...] = dot(attended.astype(jnp.bfloat16), weight_ref[...])


def merge_part(stats, relative, picked, out_weight, second, size):
    req, width = stats[0].shape[0] // 4, stats[0].shape[1]
    vmem = pl.BlockSpec(memory_space=pltpu.VMEM)
    return pl.pallas_call(
        functools.partial(merge_kernel, len(stats), relative, size),
        out_shape=(
            pltpu.VMEM((req, width), jnp.float32),
            pltpu.VMEM((req, out_weight.shape[1]), jnp.float32),
        ),
        in_specs=[vmem] * (len(stats) + 2) + [pl.BlockSpec(memory_space=pl.ANY)],
        out_specs=(vmem, vmem),
        compiler_params=pltpu.CompilerParams(vmem_limit_bytes=VMEM_LIMIT),
        cost_estimate=MERGE,
        name="merge_and_project",
    )(*near(*stats, picked, out_weight), second)


def sum_kernel(count, size, *refs):
    parts, (later_ref, log_ref, _, out, decay_ref) = refs[:count], refs[count:]
    me = lax.axis_index("head")
    total = jnp.zeros(out.shape, jnp.float32)
    for place in range(count):
        for k in range(count):
            total = total + jnp.where(lax.rem(me + count - k, count) == place, parts[k][...], 0.0)
    out[...] = total.astype(out.dtype)
    for h in range(log_ref.shape[0]):
        decay_ref[h] = jnp.exp(log_ref[h] + later_ref[:, h * size : h * size + 1])


def sum_part(parts, later, logs, placed, size):
    vmem = pl.BlockSpec(memory_space=pltpu.VMEM)
    return pl.pallas_call(
        functools.partial(sum_kernel, len(parts), size),
        out_shape=(
            pltpu.HBM(parts[0].shape, jnp.bfloat16),
            pltpu.HBM(logs.shape, jnp.float32),
        ),
        in_specs=[vmem] * (len(parts) + 3),
        out_specs=(vmem, vmem),
        compiler_params=pltpu.CompilerParams(vmem_limit_bytes=VMEM_LIMIT),
        cost_estimate=LIGHT,
        name="sum_heads_and_decay",
    )(*parts, later, logs, placed)


def place_kernel(n_seq, first, count, marked, *refs):
    parts, refs = refs[:count], refs[count:]
    lengths, _, _, out_k, out_v, *placed_ref, sem = refs
    _, sent = half_of("seq", n_seq)
    if marked:
        placed_ref[0][...] = jnp.zeros_like(placed_ref[0])
    req, rows, _ = out_k.shape
    slots = rows // 2
    most = slots // SLOTS
    seq = lax.axis_index("seq")
    if n_seq == 2:
        start = (1 - seq) * (4 * slots) + seq * (2 * slots)
    else:
        start = seq * (4 * slots) + sent * (2 * slots)
    ahead, live, _ = offsets(lengths, start, most)
    for phase in ("start", "wait"):
        begin = first
        for p, part in enumerate(parts):
            held = part.shape[1] // SLOTS
            for r in range(req):
                if begin >= (r + 1) * most:
                    continue
                low = jnp.clip(begin - ahead[r], 0, live[r])
                high = jnp.clip(begin + held - ahead[r], 0, live[r])
                size = pl.multiple_of((high - low) * SLOTS, SLOTS)

                @pl.when(high > low)
                def _(p=p, part=part, begin=begin, r=r, low=low, size=size):
                    src = pl.multiple_of((ahead[r] + low - begin) * SLOTS, SLOTS)
                    dst = pl.multiple_of(sent * slots + low * SLOTS, SLOTS)
                    for i, out in enumerate((out_k, out_v)):
                        copy = pltpu.make_async_copy(
                            part.at[i, pl.ds(src, size), :],
                            out.at[r, pl.ds(dst, size), :],
                            sem.at[p, i, r],
                        )
                        getattr(copy, phase)()

            begin += held


def place_part(n_seq, first, parts, lengths, out_k, out_v, marked=False):
    hbm = pl.BlockSpec(memory_space=pl.ANY)
    smem = pl.BlockSpec(memory_space=pltpu.SMEM)
    vmem = pl.BlockSpec(memory_space=pltpu.VMEM)
    shape = pltpu.HBM(out_k.shape, out_k.dtype)
    count = len(parts)
    return pl.pallas_call(
        functools.partial(place_kernel, n_seq, first, count, marked),
        out_shape=(shape, shape) + (pltpu.VMEM((8, LANES), jnp.float32),) * marked,
        in_specs=[vmem] * count + [smem, hbm, hbm],
        out_specs=(hbm, hbm) + (vmem,) * marked,
        scratch_shapes=[
            pltpu.SemaphoreType.DMA((count, 2, lengths.shape[0])),
        ],
        input_output_aliases={count + 1: 0, count + 2: 1},
        compiler_params=pltpu.CompilerParams(vmem_limit_bytes=VMEM_LIMIT),
        cost_estimate=LIGHT,
        name="place_received",
    )(*near(*parts), lengths, *far(out_k, out_v))


def others(value, axis):
    count = lax.axis_size(axis)
    return [value] + [
        lax.ppermute(value, axis, [(i, (i + k) % count) for i in range(count)])
        for k in range(1, count)
    ]


def swap(value, n_seq):
    return lax.ppermute(value, "seq", [(0, 1), (1, 0)]) if n_seq == 2 else value


def shards(
    keys, values, log_forget, keep, merge_weight, lengths, route, fresh, new_forget, out_weight
):
    req, pos, width = keys.shape
    heads = log_forget.shape[1]
    size = width // heads
    n_seq, n_grp = lax.axis_size("seq"), lax.axis_size("grp")
    early, packed, choice, held_lengths, held_route = first_part(
        n_seq,
        lengths,
        route,
        keep,
        merge_weight,
        fresh.reshape(3 * req, width),
        new_forget,
        keys,
        values,
    )
    exchange = functools.partial(swap, n_seq=n_seq)
    first_received = exchange(early)
    tokens = others(packed, "grp")
    out_k, out_v, late, next_rows, own_rows, logs, level, total = own_part(
        n_seq,
        held_lengths,
        keep,
        merge_weight,
        log_forget.transpose(1, 0, 2),
        keys,
        values,
        early,
    )
    end = (FIRST + SECOND) * SLOTS
    rest = late.shape[1] - end

    def finish(rows, early, next_rows, late, own_rows, logs, level, total, tokens, *others_in):
        out_weight, lengths, route, out_k, out_v = others_in
        second = exchange(next_rows)
        stats, picked = attend_part(
            n_seq, n_grp, heads, lengths, route, own_rows, late, level, total, tokens
        )
        if n_seq == 2:
            all_stats = others(stats, "seq")
        else:
            gathered = lax.all_gather(stats, "seq")
            all_stats = [gathered[i] for i in range(n_seq)]
        ends = [end, end + rows]
        if rows > 3 * LAST * SLOTS:
            ends.insert(1, end + rows - LAST * SLOTS)
        third = [exchange(late[:, low:high]) for low, high in zip(ends, ends[1:])]
        later, partial = merge_part(all_stats, n_seq == 2, picked, out_weight, second, size)
        out_k, out_v, placed = place_part(
            n_seq, 0, (early, second), lengths, out_k, out_v, marked=True
        )
        layer_out, decay = sum_part(others(partial, "head"), later, logs, placed, size)
        for low, part in zip(ends, third):
            out_k, out_v = place_part(n_seq, low // SLOTS, (part,), lengths, out_k, out_v)
        return decay, layer_out, out_k, out_v

    operands = (first_received, next_rows, late, own_rows, logs, level, total, tokens)
    operands += (out_weight, held_lengths, held_route, out_k, out_v)
    if n_seq == 2:
        branches = [
            functools.partial(finish, blocks * SLOTS) for blocks in SIZES + (rest // SLOTS,)
        ]
        decay, layer_out, out_k, out_v = lax.switch(choice[0], branches, *operands)
    else:
        decay, layer_out, out_k, out_v = finish(rest, *operands)
    if n_seq != 2:
        out_k, out_v = (
            lax.all_to_all(x, "seq", split_axis=1, concat_axis=1, tiled=True) for x in (out_k, out_v)
        )
    return out_k, out_v, decay.transpose(1, 0, 2), layer_out


def solution(mesh):
    return jax.shard_map(
        shards,
        mesh=mesh,
        in_specs=(
            P("grp", "seq", "head"),
            P("grp", "seq", "head"),
            P("grp", "head", "seq"),
            P("grp", "seq"),
            P("grp", "seq"),
            P("grp"),
            P("grp"),
            P(None, "grp", "head"),
            P("grp", "head"),
            P("head", "seq"),
        ),
        out_specs=(
            P("grp", "seq", "head"),
            P("grp", "seq", "head"),
            P("grp", "head", "seq"),
            P("grp", "seq"),
        ),
        check_vma=False,
    )
```
